32 devices in a mesh: heads: 4 (over y, core), blk: 8 (over z, x).
Axes of the slice: x: 2, y: 2, z: 4, core: 2. Of those that a mesh axis runs over, the one named last changes fastest.
Arguments:
- tokens: bfloat16 [4096, 2304], P(('blk', 'heads')), may hold values from -6 to 6
- cotangent: bfloat16 [4096, 2304], P(('blk', 'heads')), may hold values from -6 to 6
- norm_attn_in: float32 [2304], replicated, may hold values from -0.5 to 0.5
- w_query: bfloat16 [2304, 2048], P('blk', 'heads'), may hold values from -0.125 to 0.125
- w_key: bfloat16 [2304, 1024], P('blk', 'heads'), may hold values from -0.125 to 0.125
- w_value: bfloat16 [2304, 1024], P('blk', 'heads'), may hold values from -0.125 to 0.125
- w_out: bfloat16 [2048, 2304], P('heads', 'blk'), may hold values from -0.125 to 0.125
- norm_attn_out: float32 [2304], replicated, may hold values from -0.5 to 0.5
- norm_ff_in: float32 [2304], replicated, may hold values from -0.5 to 0.5
- w_gate: bfloat16 [2304, 9216], P('blk', 'heads'), may hold values from -0.125 to 0.125
- w_up: bfloat16 [2304, 9216], P('blk', 'heads'), may hold values from -0.125 to 0.125
- w_down: bfloat16 [9216, 2304], P('heads', 'blk'), may hold values from -0.0625 to 0.0625
- norm_ff_out: float32 [2304], replicated, may hold values from -0.5 to 0.5
- block_group: int32 [8], replicated, may hold values from 0 to 1, as said below
- block_role: int32 [8], replicated, may hold values from 0 to 3, as said below
Outputs:
- layer_out: bfloat16 [4096, 2304], P(('blk', 'heads'))
- input_grad: bfloat16 [4096, 2304], P(('blk', 'heads'))
- grad_norm_attn_in: float32 [2304], replicated
- grad_w_query: float32 [2304, 2048], P('blk', 'heads')
- grad_w_key: float32 [2304, 1024], P('blk', 'heads')
- grad_w_value: float32 [2304, 1024], P('blk', 'heads')
- grad_w_out: float32 [2048, 2304], P('heads', 'blk')
- grad_norm_attn_out: float32 [2304], replicated
- grad_norm_ff_in: float32 [2304], replicated
- grad_w_gate: float32 [2304, 9216], P('blk', 'heads')
- grad_w_up: float32 [2304, 9216], P('blk', 'heads')
- grad_w_down: float32 [9216, 2304], P('heads', 'blk')
- grad_norm_ff_out: float32 [2304], replicated
The draws below stay inside these ranges and needn't reach their ends.
Inputs may be any that keep to these rules, and one draw needn't show every extreme that they name: `block_group`: two groups of 4 blocks each; the first and the last block belong to the same group. `block_role`: within each group the roles are a permutation of 0 to 3; roles under 2 are the group's prompt blocks in order, the others its continuations.
All inputs are finite; a program needn't handle non-finite values.
Results may differ from the reference program's by a relative error of at most 0.03.
Values may be sent and summed in bfloat16 or wider, within the bound.
A program may use at most 192 MiB of HBM per device.

```python
import math
import jax
import jax.numpy as jnp
from jax import lax

D = 2304
HEADS = 8
KV_HEADS = 4
HEAD_DIM = 256
FF = 9216
BLOCK = 512
NBLK = 8
PROMPT_BLOCKS = 2
TOKENS = 4096


def layout(key, block_total):
    group_key, place_key, first_key, second_key = jax.random.split(key, 4)
    half_count = block_total // 2
    star_group = jax.random.randint(group_key, (), 0, 2).astype(jnp.int32)
    middle = jnp.concatenate([jnp.zeros((half_count - 2,), jnp.int32), jnp.ones((half_count,), jnp.int32)])
    middle = jax.random.permutation(place_key, middle)
    labels = jnp.concatenate([jnp.zeros((1,), jnp.int32), middle, jnp.zeros((1,), jnp.int32)])
    groups = jnp.where(labels == 0, star_group, 1 - star_group).astype(jnp.int32)
    first_rank = jnp.clip(jnp.cumsum((groups == 0).astype(jnp.int32)) - 1, 0, half_count - 1)
    second_rank = jnp.clip(jnp.cumsum((groups == 1).astype(jnp.int32)) - 1, 0, half_count - 1)
    first_order = jax.random.permutation(first_key, half_count).astype(jnp.int32)
    second_order = jax.random.permutation(second_key, half_count).astype(jnp.int32)
    role_values = jnp.where(groups == 0, first_order[first_rank], second_order[second_rank])
    return (groups, role_values.astype(jnp.int32))


def draw_block_group(key, part):
    return layout(key, NBLK)[0]


def draw_block_role(key, part):
    return layout(key, NBLK)[1]


def block_levels(own_key, dims, cuts, smallest, high):
    def one(position, shards_of):
        draws = jax.random.uniform(jax.random.fold_in(jax.random.fold_in(own_key, 6), position), (shards_of,), jnp.float32, smallest / len(cuts), high / len(cuts))
        return jnp.repeat(jnp.exp(draws), dims[position] // shards_of).reshape((-1,) + (1,) * (len(dims) - position - 1))

    loudness = one(*cuts[0])
    for cut in cuts[1:]:
        loudness = loudness * one(*cut)
    return loudness


def scatter_about(key, dims, spread, reach, cuts=(), kind=jnp.bfloat16):
    loudness = block_levels(key, dims, cuts, -0.22, 0.18) if cuts else 1.0
    entries = jax.random.normal(key, dims, jnp.float32) * spread * loudness
    return jnp.minimum(jnp.maximum(entries, -reach), reach).astype(kind)


def setup_inputs(seed: int = 0) -> dict:
    arg_keys = jax.random.split(jax.random.key(seed), 16)
    return {
        "tokens": scatter_about(arg_keys[0], (TOKENS, D), 1.0, 6.0, ((0, 32),)),
        "cotangent": scatter_about(arg_keys[1], (TOKENS, D), 1.0, 6.0, ((0, 32),)),
        "norm_attn_in": jnp.clip(jax.random.uniform(arg_keys[2], (D,), jnp.float32, -0.5, 0.5), -0.5, 0.5),
        "w_query": scatter_about(arg_keys[3], (D, HEADS * HEAD_DIM), D ** -0.5, 0.125, ((0, 8), (1, 4))),
        "w_key": scatter_about(arg_keys[4], (D, KV_HEADS * HEAD_DIM), D ** -0.5, 0.125, ((0, 8), (1, 4))),
        "w_value": scatter_about(arg_keys[5], (D, KV_HEADS * HEAD_DIM), D ** -0.5, 0.125, ((0, 8), (1, 4))),
        "w_out": scatter_about(arg_keys[6], (HEADS * HEAD_DIM, D), (HEADS * HEAD_DIM) ** -0.5, 0.125, ((0, 4), (1, 8))),
        "norm_attn_out": jnp.clip(jax.random.uniform(arg_keys[7], (D,), jnp.float32, -0.5, 0.5), -0.5, 0.5),
        "norm_ff_in": jnp.clip(jax.random.uniform(arg_keys[8], (D,), jnp.float32, -0.5, 0.5), -0.5, 0.5),
        "w_gate": scatter_about(arg_keys[9], (D, FF), D ** -0.5, 0.125, ((0, 8), (1, 4))),
        "w_up": scatter_about(arg_keys[10], (D, FF), D ** -0.5, 0.125, ((0, 8), (1, 4))),
        "w_down": scatter_about(arg_keys[11], (FF, D), FF ** -0.5, 0.0625, ((0, 4), (1, 8))),
        "norm_ff_out": jnp.clip(jax.random.uniform(arg_keys[12], (D,), jnp.float32, -0.5, 0.5), -0.5, 0.5),
        "block_group": draw_block_group(jax.random.fold_in(arg_keys[15], 71), 0),
        "block_role": draw_block_role(jax.random.fold_in(arg_keys[15], 71), 0),
    }


softcap = 50.0
epsilon = 1e-06
masked_low = -1e+30
highest = lax.Precision.HIGHEST

@jax.custom_vjp
def low(v):
    return lax.optimization_barrier(v.astype(jnp.bfloat16)).astype(jnp.float32)

@jax.custom_vjp
def low_back(v):
    return v

def low_keep(v):
    return (low(v), None)

def low_pass(kept, grad):
    return (grad,)

def back_keep(v):
    return (v, None)

def back_low(kept, grad):
    return (low(grad),)
low.defvjp(low_keep, low_pass)
low_back.defvjp(back_keep, back_low)

def normalize(values, weight_gain):
    factor = lax.rsqrt(lax.optimization_barrier(jnp.mean(values * values, axis=-1, keepdims=True)) + epsilon)
    return values * factor * (1.0 + weight_gain)

def rope_tables(positions):
    half_dim = HEAD_DIM // 2
    frequency = jnp.exp(jnp.arange(half_dim, dtype=jnp.float32) * (-2.0 * math.log(10000.0) / HEAD_DIM))
    angles = positions.astype(jnp.float32)[:, None] * frequency[None, :]
    return (jnp.cos(angles), jnp.sin(angles))

def rotate(tensor, cosine, sine_table):
    half_dim = tensor.shape[-1] // 2
    first_half = tensor[..., :half_dim]
    second_half = tensor[..., half_dim:]
    cos_wide = cosine[:, None, :]
    sin_wide = sine_table[:, None, :]
    return jnp.concatenate([first_half * cos_wide - second_half * sin_wide, second_half * cos_wide + first_half * sin_wide], axis=-1)

def attention(queries, key_rows, value_rows, group_tok, role_tok, inner_tok, block_group, block_role):
    repeat_count = HEADS // KV_HEADS
    wide_keys = jnp.repeat(key_rows, repeat_count, axis=1)
    wide_values = jnp.repeat(value_rows, repeat_count, axis=1)
    query_blocks = queries.reshape(NBLK, BLOCK, HEADS, HEAD_DIM)
    offsets = jnp.arange(BLOCK, dtype=jnp.int32)

    @jax.checkpoint
    def one_block(packed):
        block_queries, own_group, own_role = packed
        raw_scores = low_back(jnp.einsum('qhd,khd->qhk', block_queries, wide_keys, precision=highest))
        capped = softcap * jnp.tanh(raw_scores * HEAD_DIM ** (-0.5) / softcap)
        prompt_part = (role_tok[None, :] < PROMPT_BLOCKS) & (role_tok[None, :] < own_role)
        own_part = (role_tok[None, :] == own_role) & (inner_tok[None, :] <= offsets[:, None])
        allowed = ((group_tok[None, :] == own_group) & (prompt_part | own_part))[:, None, :]
        masked = jnp.where(allowed, capped, masked_low)
        peak_value = lax.optimization_barrier(jnp.max(masked, axis=-1, keepdims=True))
        weights = jnp.where(allowed, jnp.exp(capped - peak_value), 0.0)
        probabilities = weights / lax.optimization_barrier(jnp.sum(weights, axis=-1, keepdims=True))
        return jnp.einsum('qhk,khd->qhd', low(probabilities), wide_values, precision=highest)
    result = lax.map(one_block, (query_blocks, block_group, block_role))
    return result.reshape(TOKENS, HEADS, HEAD_DIM)

def reference(tokens, cotangent, norm_attn_in, w_query, w_key, w_value, w_out, norm_attn_out, norm_ff_in, w_gate, w_up, w_down, norm_ff_out, block_group, block_role):
    token_index = jnp.arange(TOKENS, dtype=jnp.int32)
    block_index = token_index // BLOCK
    group_tok = block_group[block_index]
    role_tok = block_role[block_index]
    inner_tok = token_index % BLOCK
    positions = jnp.where(role_tok < PROMPT_BLOCKS, role_tok * BLOCK, PROMPT_BLOCKS * BLOCK) + inner_tok
    cosine, sine_table = rope_tables(positions)

    def forward(token_f32, gain_one, query_w, key_w, value_w, out_w, gain_two, gain_three, gate_w, up_w, down_w, gain_four):
        normed_one = low(normalize(token_f32, gain_one))
        query_lin = low_back(jnp.dot(normed_one, query_w, precision=highest)).reshape(TOKENS, HEADS, HEAD_DIM)
        key_lin = low_back(jnp.dot(normed_one, key_w, precision=highest)).reshape(TOKENS, KV_HEADS, HEAD_DIM)
        value_rows = low(low_back(jnp.dot(normed_one, value_w, precision=highest))).reshape(TOKENS, KV_HEADS, HEAD_DIM)
        queries = low(rotate(query_lin, cosine, sine_table))
        key_rows = low(rotate(key_lin, cosine, sine_table))
        attended = attention(queries, key_rows, value_rows, group_tok, role_tok, inner_tok, block_group, block_role)
        attn_rows = low_back(low(attended)).reshape(TOKENS, HEADS * HEAD_DIM)
        attn_proj = low_back(jnp.dot(attn_rows, out_w, precision=highest))
        middle = token_f32 + normalize(attn_proj, gain_two)
        normed_two = low(normalize(middle, gain_three))
        gate_lin = low_back(jnp.dot(normed_two, gate_w, precision=highest))
        up_lin = low_back(jnp.dot(normed_two, up_w, precision=highest))
        hidden = low(jax.nn.gelu(gate_lin, approximate=True) * up_lin)
        ff_proj = low_back(jnp.dot(hidden, down_w, precision=highest))
        return middle + normalize(ff_proj, gain_four)
    primals = (tokens.astype(jnp.float32), norm_attn_in.astype(jnp.float32), w_query.astype(jnp.float32), w_key.astype(jnp.float32), w_value.astype(jnp.float32), w_out.astype(jnp.float32), norm_attn_out.astype(jnp.float32), norm_ff_in.astype(jnp.float32), w_gate.astype(jnp.float32), w_up.astype(jnp.float32), w_down.astype(jnp.float32), norm_ff_out.astype(jnp.float32))
    layer_out, pullback = jax.vjp(forward, *primals)
    grads = pullback(cotangent.astype(jnp.float32))
    return (layer_out.astype(jnp.bfloat16), grads[0].astype(jnp.bfloat16), grads[1], grads[2], grads[3], grads[4], grads[5], grads[6], grads[7], grads[8], grads[9], grads[10], grads[11])
```

```python
import functools
import math

import jax
import jax.numpy as jnp
from jax import lax
from jax.experimental import pallas as pl
from jax.experimental.pallas import tpu as pltpu
from jax.sharding import PartitionSpec as P

HEAD_DIM = 256


softcap = 50.0
epsilon = 1e-06
score_scale = HEAD_DIM ** (-0.5)
bf16 = jnp.bfloat16
f32 = jnp.float32


def contract(left_side, right_side, left_dim, right_dim):
    return lax.dot_general(
        left_side,
        right_side,
        (((left_dim,), (right_dim,)), ((), ())),
        preferred_element_type=f32,
    )


def factor_of(values):
    return lax.rsqrt(jnp.mean(values * values, axis=-1, keepdims=True) + epsilon)


def normalize(values, weight_gain):
    return values * factor_of(values) * (1.0 + weight_gain)


def normalize_back(values, weight_gain, upstream):
    factor = factor_of(values)
    unit = values * factor
    scaled = upstream * (1.0 + weight_gain)
    inner = jnp.mean(scaled * unit, axis=-1, keepdims=True)
    return (scaled - unit * inner) * factor, jnp.sum(upstream * unit, axis=0)


def rope_tables(positions):
    half_dim = HEAD_DIM // 2
    frequency = jnp.exp(
        jnp.arange(half_dim, dtype=f32) * (-2.0 * math.log(10000.0) / HEAD_DIM)
    )
    angles = positions.astype(f32)[:, None] * frequency[None, :]
    return (jnp.cos(angles), jnp.sin(angles))


def rotate(tensor, cosine, sine_table):
    half_dim = HEAD_DIM // 2
    first_half = tensor[..., :half_dim]
    second_half = tensor[..., half_dim:]
    return jnp.concatenate(
        [
            first_half * cosine - second_half * sine_table,
            second_half * cosine + first_half * sine_table,
        ],
        axis=-1,
    )


def swap_core(v):
    return lax.ppermute(v, "heads", [(i, i ^ 1) for i in range(4)])


def swap_y(v):
    return lax.ppermute(v, "heads", [(i, i ^ 2) for i in range(4)])


def swap_x(v):
    blocks = lax.axis_size("blk")
    return lax.ppermute(v, "blk", [(i, i ^ 1) for i in range(blocks)])


def pair_up(own, other, place, axis):
    first = jnp.where(place == 0, own, other)
    second = jnp.where(place == 0, other, own)
    return jnp.concatenate([first, second], axis=axis)


def shift_z(v, step, senders):
    pairs = []
    for z in senders:
        for x in range(2):
            pairs.append((2 * z + x, 2 * (z + step) + x))
    return lax.ppermute(v, "blk", pairs)


class Place:
    def __init__(self):
        self.blocks = lax.axis_size("blk")
        self.nz = self.blocks // 2
        self.b = lax.axis_index("blk")
        self.h = lax.axis_index("heads")
        self.z, self.x = self.b // 2, self.b % 2
        self.y, self.c = self.h // 2, self.h % 2


def gather_z(at, unit):
    nz = at.nz
    up, down = unit, unit
    ups, downs = [None], [None]
    for s in range(1, nz):
        up = shift_z(up, 1, range(s - 1, nz - 1))
        down = shift_z(down, -1, range(1, nz - s + 1))
        ups.append(up)
        downs.append(down)
    return [unit] + [jnp.where(at.z >= s, ups[s], downs[nz - s]) for s in range(1, nz)]


def scatter_z(at, parts):
    nz = at.nz
    up = down = None
    for t in range(1, nz):
        k = nz - t
        send_up = parts[nz - k].astype(f32)
        send_down = parts[k].astype(f32)
        if up is not None:
            send_up = send_up + up.astype(f32)
            send_down = send_down + down.astype(f32)
        up = shift_z(send_up.astype(bf16), 1, range(0, nz - k))
        down = shift_z(send_down.astype(bf16), -1, range(k, nz))
    return parts[0].astype(f32) + (up.astype(f32) + down.astype(f32))


def deal_z(at, parts):
    nz = at.nz
    got = [parts[0]]
    for s in range(1, nz):
        up = shift_z(parts[nz - s], s, range(0, nz - s))
        down = shift_z(parts[nz - s], s - nz, range(nz - s, nz))
        got.append(jnp.where(at.z >= s, up, down))
    return got


def turn(at, whole):
    return [
        lax.dynamic_index_in_dim(whole, (at.z - s) % at.nz, 0, keepdims=False)
        for s in range(at.nz)
    ]


def unturn(at, parts):
    whole = jnp.zeros((at.nz,) + parts[0].shape, parts[0].dtype)
    for s, part in enumerate(parts):
        whole = lax.dynamic_update_index_in_dim(whole, part, (at.z - s) % at.nz, 0)
    return whole


def gather_zx(at, unit):
    got = []
    for part in gather_z(at, unit):
        got.append(pair_up(part[None], swap_x(part)[None], at.x, 0))
    return unturn(at, got)


def gather_xz(at, unit):
    both = pair_up(unit[None], swap_x(unit)[None], at.x, 0)
    return unturn(at, gather_z(at, both))


def pick(pair, place):
    mine = jnp.where(place == 0, pair[0], pair[1])
    other = jnp.where(place == 0, pair[1], pair[0])
    return mine, other


def scatter_zx(at, parts):
    total = scatter_z(at, parts)
    mine, other = pick(total, at.x)
    return mine + swap_x(other.astype(bf16)).astype(f32)


def scatter_xz(at, parts):
    sums = []
    for part in parts:
        mine, other = pick(part, at.x)
        sums.append(mine.astype(f32) + swap_x(other.astype(bf16)).astype(f32))
    return scatter_z(at, sums)


def rows_to_block(at, own):
    both = pair_up(own, swap_core(own), at.c, 0)
    pair = pair_up(both[None], swap_y(both)[None], at.y, 0)
    return pair.reshape(4 * own.shape[0], own.shape[1])


def rows_from_block(at, partial_sum):
    rows = partial_sum.shape[0] // 4
    parts = partial_sum.reshape(2, 2, rows, partial_sum.shape[1])
    mine, other = pick(parts.swapaxes(0, 1), at.c)
    total = mine + swap_core(other.astype(bf16)).astype(f32)
    mine, other = pick(total, at.y)
    return mine + swap_y(other.astype(bf16)).astype(f32)


def spread_weight(at, shard):
    rows, units = shard.shape
    half = rows // 2
    keep, send = pick(shard.reshape(2, half, units), at.c)
    wide = pair_up(keep[None], swap_core(send)[None], at.c, 0)
    quarter = 2 * units // at.nz
    per_core = units // quarter
    pieces = wide.reshape(2, half, per_core, quarter).transpose(0, 2, 1, 3)
    pieces = pieces.reshape(at.nz, half, quarter)
    got = unturn(at, deal_z(at, turn(at, pieces)))
    got = pair_up(got[:, None], swap_x(got)[:, None], at.x, 1)
    got = pair_up(got, swap_y(got), at.y, 3)
    got = pair_up(got[:, :, None], swap_core(got)[:, :, None], at.c, 2)
    return got.reshape(at.blocks * rows, 2 * quarter)


def collect_weight(at, grad):
    depth, width = grad.shape
    half, quarter = depth // (2 * at.blocks), width // 2
    parts = grad.reshape(at.nz, 2, 2, half, width)
    mine, other = pick(parts.transpose(2, 0, 1, 3, 4), at.c)
    total = mine + swap_core(other.astype(bf16)).astype(f32)
    mine, other = pick((total[..., :quarter], total[..., quarter:]), at.y)
    total = mine + swap_y(other.astype(bf16)).astype(f32)
    mine, other = pick((total[:, 0], total[:, 1]), at.x)
    total = mine + swap_x(other.astype(bf16)).astype(f32)
    got = unturn(at, deal_z(at, turn(at, total.astype(bf16))))
    per_core = at.nz // 2
    wide = got.reshape(2, per_core, half, quarter).transpose(0, 2, 1, 3)
    wide = wide.reshape(2, half, per_core * quarter)
    mine, other = pick(wide, at.c)
    rows = pair_up(mine, swap_core(other), at.c, 0)
    return rows.astype(f32)


def sum_all(at, values):
    total = values
    for bit in (1, 2):
        total = total + lax.ppermute(total, "heads", [(i, i ^ bit) for i in range(4)])
    bit = 1
    while bit < at.blocks:
        total = total + lax.ppermute(total, "blk", [(i, i ^ bit) for i in range(at.blocks)])
        bit *= 2
    return total


class Permutes:
    def __init__(self, at):
        self.at = at
        self.block, self.blocks, self.nz = at.b, at.blocks, at.nz

    def start(self, own, attn_shard, ff_shards):
        at = self.at
        depth = own.shape[1]
        attn_full = gather_zx(at, attn_shard).reshape(depth, -1)
        return self.gather_heads(own), attn_full, [spread_weight(at, w) for w in ff_shards]

    def gather_heads(self, own):
        return rows_to_block(self.at, own)

    def scatter_heads(self, partial):
        return rows_from_block(self.at, partial)

    def gather_kv(self, own):
        whole = gather_zx(self.at, own)
        return whole.reshape((self.blocks,) + own.shape)

    def split(self, whole):
        return turn(self.at, whole.reshape((self.nz, whole.shape[0] // self.nz) + whole.shape[1:]))

    def scatter_kv(self, parts):
        return scatter_xz(self.at, self.split(parts))

    def gather_z(self, own):
        whole = unturn(self.at, gather_z(self.at, own))
        return whole.reshape(-1, own.shape[1])

    def scatter_z(self, partial):
        return scatter_z(self.at, self.split(partial))

    def scatter_attn(self, grad):
        rows = grad.shape[0] // self.blocks
        return scatter_xz(self.at, self.split(grad.reshape(self.blocks, rows, -1)))

    def collect(self, grads):
        return [collect_weight(self.at, g) for g in grads]


MESH = pl.DeviceIdType.MESH
anywhere = pl.BlockSpec(memory_space=pl.ANY)
in_vmem = pl.BlockSpec(memory_space=pltpu.VMEM)


def remote(src, dst, send_sem, recv_sem, target):
    return pltpu.make_async_remote_copy(
        src_ref=src,
        dst_ref=dst,
        send_sem=send_sem,
        recv_sem=recv_sem,
        device_id=target,
        device_id_type=MESH,
    )


class Spot:
    def __init__(self, nz):
        self.nz = nz
        h, b = lax.axis_index("heads"), lax.axis_index("blk")
        self.y, self.c = h // 2, h % 2
        self.z, self.x = b // 2, b % 2

    def device(self, z=None, x=None, y=None, c=None):
        z = self.z if z is None else z
        x = self.x if x is None else x
        y = self.y if y is None else y
        c = self.c if c is None else c
        return (2 * y + c, 2 * z + x)

    def greet(self, devices):
        barrier = pltpu.get_barrier_semaphore()
        for device in devices:
            pl.semaphore_signal(barrier, inc=1, device_id=device, device_id_type=MESH)
        pl.semaphore_wait(barrier, len(devices))

    def plane(self):
        found = []
        for dx, dy, dc in [(0, 0, 1), (1, 0, 0), (1, 0, 1), (0, 1, 0), (0, 1, 1), (1, 1, 0), (1, 1, 1)]:
            found.append(self.device(x=flip(self.x, dx), y=flip(self.y, dy), c=flip(self.c, dc)))
        return found

    def column(self, both_cores):
        found = []
        for s in range(1, self.nz):
            z = (self.z + s) % self.nz
            found.append(self.device(z=z))
            if both_cores:
                found.append(self.device(z=z, c=1 - self.c))
        return found


def flip(bit, by):
    return 1 - bit if by else bit


def add_rows(out, left, right, step=16):
    rows = left.shape[0]

    @pl.loop(0, rows // step)
    def _(i):
        at = pl.ds(pl.multiple_of(i * step, step), step)
        out[at, :] = (left[at, :].astype(f32) + right[at, :].astype(f32)).astype(out.dtype)


class LineGather:
    def __init__(self, spot, entry, sems):
        self.spot, self.entry = spot, entry
        self.send, self.recv = sems

    def copies(self, s):
        p, nz = self.spot, self.spot.nz
        up_at = lax.rem(p.z - s + 1 + nz, nz)
        down_at = lax.rem(p.z + s - 1, nz)
        up_z = lax.rem(p.z + 1, nz)
        down_z = lax.rem(p.z + nz - 1, nz)
        up = remote(
            self.entry(up_at), self.entry(up_at), self.send.at[0, s], self.recv.at[0, s], p.device(z=up_z)
        )
        down = remote(
            self.entry(down_at),
            self.entry(down_at),
            self.send.at[1, s],
            self.recv.at[1, s],
            p.device(z=down_z),
        )
        return (
            ((p.z >= s - 1) & (p.z < nz - 1), p.z >= s, up),
            ((p.z <= nz - s) & (p.z > 0), p.z <= nz - 1 - s, down),
        )

    def start(self, s):
        for sends, _, copy in self.copies(s):
            pl.when(sends)(copy.start)

    def arrive(self, s):
        for _, receives, copy in self.copies(s):
            pl.when(receives)(copy.wait_recv)

    def finish(self):
        for s in range(1, self.spot.nz):
            for sends, _, copy in self.copies(s):
                pl.when(sends)(copy.wait_send)

    def newest(self, s):
        p, nz = self.spot, self.spot.nz
        return (
            (p.z >= s, lax.rem(p.z - s + nz, nz)),
            (p.z <= nz - 1 - s, lax.rem(p.z + s, nz)),
        )


class LineScatter:
    def __init__(self, spot, parts, up, down, sems):
        self.spot, self.parts, self.up, self.down = spot, parts, up, down
        self.send, self.recv = sems

    def copies(self, t):
        p, nz = self.spot, self.spot.nz
        k = nz - t
        up_at, down_at = lax.rem(p.z + k, nz), lax.rem(p.z - k + nz, nz)
        up = remote(
            self.parts.at[up_at],
            self.up.at[t - 1],
            self.send.at[0, t],
            self.recv.at[0, t],
            p.device(z=lax.rem(p.z + 1, nz)),
        )
        down = remote(
            self.parts.at[down_at],
            self.down.at[t - 1],
            self.send.at[1, t],
            self.recv.at[1, t],
            p.device(z=lax.rem(p.z + nz - 1, nz)),
        )
        return (
            (p.z <= nz - 1 - k, (p.z >= 1) & (p.z <= t), up),
            (p.z >= k, (p.z <= nz - 2) & (p.z >= nz - 1 - t), down),
        )

    def start(self, t):
        for sends, _, copy in self.copies(t):
            pl.when(sends)(copy.start)

    def arrive(self, t):
        p, nz = self.spot, self.spot.nz
        k = nz - t
        for way, (_, receives, copy) in enumerate(self.copies(t)):

            @pl.when(receives)
            def _(way=way, copy=copy):
                copy.wait_recv()
                if t < nz - 1:
                    index = lax.rem(p.z + k - 1, nz) if way == 0 else lax.rem(p.z - k + 1 + nz, nz)
                    came = (self.up if way == 0 else self.down).at[t - 1]
                    add_rows(self.parts.at[index], self.parts.at[index], came)

    def finish(self):
        for t in range(1, self.spot.nz):
            for sends, _, copy in self.copies(t):
                pl.when(sends)(copy.wait_send)

    def total(self, out, step=16):
        p, last = self.spot, self.spot.nz - 2
        mine = self.parts.at[p.z]
        inner = (p.z > 0) & (p.z < p.nz - 1)

        @pl.when(p.z == 0)
        def _():
            add_rows(out, mine, self.down.at[last], step)

        @pl.when(p.z == p.nz - 1)
        def _():
            add_rows(out, mine, self.up.at[last], step)

        @pl.when(inner)
        def _():
            @pl.loop(0, out.shape[0] // step)
            def _(i):
                at = pl.ds(pl.multiple_of(i * step, step), step)
                sides = self.up[last, at, :].astype(f32) + self.down[last, at, :].astype(f32)
                out[at, :] = (mine[at, :].astype(f32) + sides).astype(out.dtype)


def core_copies(spot, entries, sems):
    send, recv = sems
    other = spot.device(c=1 - spot.c)
    return [remote(e, e, send.at[i], recv.at[i], other) for i, e in enumerate(entries)]


class PlaneGather:
    def __init__(self, spot, own, whole, sems, local_sem):
        self.spot, self.own, self.whole = spot, own, whole
        self.send, self.recv = sems
        self.local = pltpu.make_async_copy(own, whole.at[2 * spot.y + spot.c], local_sem)

    def copies(self):
        p = self.spot
        part = 2 * p.y + p.c
        found = []
        for i, (dx, dy) in enumerate([(1, 0), (0, 1), (1, 1), (0, 0)]):
            target = p.device(x=flip(p.x, dx), y=flip(p.y, dy), c=p.x)
            found.append(
                remote(self.own, self.whole.at[part], self.send.at[i], self.recv.at[part], target)
            )
        return found

    def start(self):
        p = self.spot
        *away, home = self.copies()
        for copy in away:
            copy.start()
        pl.when(p.c == p.x)(self.local.start)
        pl.when(p.c != p.x)(home.start)

    def finish(self):
        p = self.spot
        *away, home = self.copies()
        for copy in away:
            copy.wait_send()
        pl.when(p.c == p.x)(self.local.wait)
        pl.when(p.c != p.x)(home.wait_send)
        for part in range(4):
            copy = remote(
                self.own, self.whole.at[part], self.send.at[0], self.recv.at[part], p.device(c=1 - p.c)
            )
            mine = (p.c == p.x) & (part == 2 * p.y + p.c)
            pl.when(jnp.logical_not(mine))(copy.wait_recv)


def exclusive_or(z, i):
    low, high = lax.rem(z, 2), lax.rem(z // 2, 2)
    rest = z - 2 * high - low
    return rest + 2 * flip(high, i // 2) + flip(low, i % 2)


class Spread:
    def __init__(self, spot, shard, full, sems):
        self.spot, self.shard, self.full = spot, shard, full
        self.send, self.recv = sems
        self.quarter = full.shape[-1] // 2
        self.nz = spot.nz
        self.per_core = self.nz // 2

    def place(self, z, x, c, y):
        columns = pl.ds(pl.multiple_of(y * self.quarter, 128), self.quarter)
        return self.full.at[z, x, c, :, columns]


    def deal(self, piece, half):
        p = self.spot
        z = p.c * self.per_core + piece
        columns = pl.ds(piece * self.quarter, self.quarter)
        src = self.shard.at[half, :, columns]
        return z, remote(
            src,
            self.place(p.z, p.x, half, p.y),
            self.send.at[6 * self.nz + 2 * piece + half],
            self.recv.at[p.z],
            p.device(z=z, c=half),
        )

    def local(self, piece):
        p = self.spot
        columns = pl.ds(piece * self.quarter, self.quarter)
        return pltpu.make_async_copy(
            self.shard.at[p.c, :, columns],
            self.place(p.z, p.x, p.c, p.y),
            self.recv.at[p.z],
        )

    def start(self):
        p = self.spot
        for piece in range(self.per_core):
            for half in range(2):
                z, copy = self.deal(piece, half)
                here = (z == p.z) & (p.c == half)
                pl.when(jnp.logical_not(here))(copy.start)
                pl.when(here)(self.local(piece).start)

    def dealt(self, source):
        p = self.spot
        here = self.place(source, p.x, p.c, p.y)
        ours = (source == p.z) & (p.c == p.z // self.per_core)
        came = remote(here, here, self.send.at[0], self.recv.at[source], p.device(c=1 - p.c))
        pl.when(jnp.logical_not(ours))(came.wait_recv)
        pl.when(ours)(self.local(0).wait)

    def first(self, z):
        p = self.spot
        here = self.place(z, p.x, p.c, p.y)
        x = p.x + (1 - 2 * p.x) * (1 - p.c)
        y = p.y + (1 - 2 * p.y) * p.c
        return remote(
            here, here, self.send.at[self.nz + z], self.recv.at[self.nz + z], p.device(x=x, y=y)
        )

    def second(self, z, which):
        p = self.spot
        x, y = p.x, p.y
        if which:
            x = p.x + (1 - 2 * p.x) * (1 - p.c)
            y = p.y + (1 - 2 * p.y) * p.c
        here = self.place(z, x, p.c, y)
        tx = p.x + (1 - 2 * p.x) * p.c
        ty = p.y + (1 - 2 * p.y) * (1 - p.c)
        sem = 2 * self.nz + 2 * z + which
        return remote(here, here, self.send.at[sem], self.recv.at[sem], p.device(x=tx, y=ty))

    def across(self, z, x):
        p = self.spot
        here = self.full.at[z, x, p.c]
        sem = 4 * self.nz + 2 * z + x
        return remote(here, here, self.send.at[sem], self.recv.at[sem], p.device(c=1 - p.c))

    def finish(self):
        p = self.spot
        for piece in range(self.per_core):
            for half in range(2):
                z, copy = self.deal(piece, half)
                here = (z == p.z) & (p.c == half)
                pl.when(jnp.logical_not(here))(copy.wait_send)
        for z in range(self.nz):
            self.first(z).wait_send()
            for which in range(2):
                self.second(z, which).wait_send()
            for x in range(2):
                self.across(z, x).wait()


def start_kernel(nz, own, attn, gate, up, down, rows, attn_full, gate_full, up_full, down_full, *sems):
    (t_send, t_recv, a_send, a_recv, l_send, l_recv, x_send, x_recv, f_send, f_recv, local) = sems
    p = Spot(nz)
    p.greet(p.plane() + p.column(True))
    tokens = PlaneGather(p, own, rows, (t_send, t_recv), local.at[0])
    spreads = [
        Spread(p, shard, full, (f_send.at[i], f_recv.at[i]))
        for i, (shard, full) in enumerate(((gate, gate_full), (up, up_full), (down, down_full)))
    ]
    line = LineGather(p, lambda z: attn_full.at[z, p.c], (l_send, l_recv))
    keep = pltpu.make_async_copy(attn, attn_full.at[p.z, p.c], local.at[1])
    trade = remote(
        attn, attn_full.at[p.z, p.x], a_send, a_recv, p.device(x=1 - p.x, c=1 - p.c)
    )
    same = p.c == p.x
    pl.when(same)(keep.start)
    pl.when(jnp.logical_not(same))(trade.start)
    tokens.start()
    spreads[0].start()
    pl.when(same)(keep.wait)
    pl.when(jnp.logical_not(same))(trade.wait_recv)
    line.start(1)
    across = core_copies(p, [attn_full.at[z, p.c] for z in range(nz)], (x_send, x_recv))

    def stage_first(spread, i):
        z = exclusive_or(p.z, i)
        spread.dealt(z)
        spread.first(z).start()
        spread.second(z, 0).start()

    def stage_second(spread, i):
        z = exclusive_or(p.z, i)
        spread.first(z).wait_recv()
        spread.second(z, 1).start()

    def stage_core(spread, i):
        z = exclusive_or(p.z, i)
        for which in range(2):
            spread.second(z, which).wait_recv()
        for x in range(2):
            spread.across(z, x).start()

    spreads[1].start()
    stage_first(spreads[0], 0)
    line.arrive(1)
    line.start(2)
    for i in range(1, nz):
        stage_first(spreads[0], i)
    spreads[2].start()
    line.arrive(2)
    line.start(3)
    for i in range(nz):
        stage_first(spreads[1], i)
        stage_second(spreads[0], i)
    line.arrive(3)
    for copy in across:
        copy.start()
    for i in range(nz):
        stage_first(spreads[2], i)
        stage_core(spreads[0], i)
        stage_second(spreads[1], i)
    for i in range(nz):
        stage_second(spreads[2], i)
        stage_core(spreads[1], i)
    for i in range(nz):
        stage_core(spreads[2], i)
    tokens.finish()
    pl.when(jnp.logical_not(same))(trade.wait_send)
    line.finish()
    for copy in across:
        copy.wait()
    for spread in spreads:
        spread.finish()


def gather_kv_kernel(nz, own, full, send, recv, x_send, x_recv, local):
    p = Spot(nz)
    p.greet([p.device(c=1 - p.c)] + p.column(False))
    line = LineGather(p, lambda z: full.at[z, p.c], (send, recv))
    keep = pltpu.make_async_copy(own, full.at[p.z, p.c], local)
    keep.start()
    keep.wait()
    line.start(1)
    across = core_copies(p, [full.at[z, p.c] for z in range(nz)], (x_send, x_recv))
    for s in range(2, nz):
        line.arrive(s - 1)
        line.start(s)
    line.arrive(nz - 1)
    for copy in across:
        copy.start()
    line.finish()
    for copy in across:
        copy.wait()


def gather_heads_kernel(nz, own, whole, send, recv, local):
    p = Spot(nz)
    p.greet(p.plane())
    tokens = PlaneGather(p, own, whole, (send, recv), local)
    tokens.start()
    tokens.finish()


def scatter_heads_kernel(nz, parts, out, came, send, recv):
    p = Spot(nz)
    p.greet(p.plane())
    head = 2 * p.y + p.x

    def copy_to(part, slot):
        y, c = part // 2, part % 2
        return remote(
            parts.at[part], came.at[head], send.at[part], recv.at[slot], p.device(x=p.c, y=y, c=c)
        )

    ours = 2 * p.y + p.c
    for part in range(4):
        here = (p.x == p.c) & (part == ours)
        pl.when(jnp.logical_not(here))(copy_to(part, head).start)
    for part in range(4):
        here = (p.x == p.c) & (part == ours)
        pl.when(jnp.logical_not(here))(copy_to(part, head).wait_send)
        arrived = remote(
            parts.at[part], came.at[part], send.at[part], recv.at[part], p.device(c=1 - p.c)
        )
        mine = (p.x == p.c) & (part == head)
        pl.when(jnp.logical_not(mine))(arrived.wait_recv)

    @pl.when(p.x == p.c)
    def _():
        came[head] = parts[ours]

    rows = out.shape[0]

    @pl.loop(0, rows // 16)
    def _(i):
        at = pl.ds(pl.multiple_of(i * 16, 16), 16)
        low = came[0, at, :].astype(f32) + came[1, at, :].astype(f32)
        out[at, :] = low + (came[2, at, :].astype(f32) + came[3, at, :].astype(f32))


def gather_z_kernel(nz, own, full, send, recv, local):
    p = Spot(nz)
    p.greet(p.column(False))
    line = LineGather(p, lambda z: full.at[z], (send, recv))
    keep = pltpu.make_async_copy(own, full.at[p.z], local)
    keep.start()
    keep.wait()
    line.start(1)
    for s in range(2, nz):
        line.arrive(s - 1)
        line.start(s)
    line.arrive(nz - 1)
    line.finish()


def scatter_z_kernel(nz, given, out, parts, up, down, send, recv, local):
    p = Spot(nz)
    p.greet(p.column(False))
    bring = pltpu.make_async_copy(given, parts, local)
    bring.start()
    bring.wait()
    line = LineScatter(p, parts, up, down, (send, recv))
    for t in range(1, nz):
        line.start(t)
        line.arrive(t)
    line.total(out)
    line.finish()


def scatter_pair_kernel(nz, trade_back, given, out, parts, came, up, down, *sems):
    (x_send, x_recv, send, recv, local, b_send, b_recv) = sems
    p = Spot(nz)
    found = [p.device(c=1 - p.c)] + p.column(False)
    if trade_back:
        found.append(p.device(x=1 - p.x, c=1 - p.c))
    p.greet(found)
    order = [nz - 1, 0] + list(range(1, nz - 1))
    away = [
        remote(given.at[z, 1 - p.c], came.at[z], x_send.at[z], x_recv.at[z], p.device(c=1 - p.c))
        for z in range(nz)
    ]
    bring = [pltpu.make_async_copy(given.at[z, p.c], parts.at[z], local.at[z]) for z in range(nz)]
    for z in order:
        away[z].start()
        bring[z].start()
    line = LineScatter(p, parts, up, down, (send, recv))
    for z in order:
        away[z].wait_recv()
        bring[z].wait()
        add_rows(parts.at[z], parts.at[z], came.at[z])
    for t in range(1, nz):
        line.start(t)
        line.arrive(t)
    if not trade_back:
        line.total(out)
    else:
        line.total(came.at[0])
        away[0].wait_send()
        same = p.c == p.x
        back = remote(came.at[0], out, b_send, b_recv, p.device(x=1 - p.x, c=1 - p.c))
        keep = pltpu.make_async_copy(came.at[0], out, b_recv)
        pl.when(same)(keep.start)
        pl.when(jnp.logical_not(same))(back.start)
        pl.when(same)(keep.wait)
        pl.when(jnp.logical_not(same))(back.wait)
    for z in range(1 if trade_back else 0, nz):
        away[z].wait_send()
    line.finish()


def collect_kernel(nz, given, out, mine, came, first_in, second_in, *sems):
    (l_send, c_send, c_recv, f_send, f_recv, s_send, s_recv, d_send, d_recv) = sems
    p = Spot(nz)
    p.greet(p.plane() + p.column(True))
    half, quarter = given.shape[3], given.shape[4] // 2
    other_core = p.device(c=1 - p.c)
    order = [exclusive_or(p.z, i) for i in (3, 2, 1, 0)]

    def bring(z, x):
        return pltpu.make_async_copy(given.at[z, x, p.c], mine.at[z, x], l_send.at[2 * z + x])

    def across(z, x):
        sem = 2 * z + x
        return remote(
            given.at[z, x, 1 - p.c], came.at[z, x], c_send.at[sem], c_recv.at[sem], other_core
        )

    def columns(y):
        return pl.ds(pl.multiple_of(y * quarter, 128), quarter)

    fx = p.x + (1 - 2 * p.x) * p.c
    fy = p.y + (1 - 2 * p.y) * (1 - p.c)
    sx = p.x + (1 - 2 * p.x) * (1 - p.c)
    sy = p.y + (1 - 2 * p.y) * p.c

    def first(z, which):
        x, y = fx, fy
        if which:
            x = fx + (1 - 2 * fx) * (1 - p.c)
            y = fy + (1 - 2 * fy) * p.c
        sem = 2 * z + which
        return remote(
            mine.at[z, x, :, columns(y)],
            first_in.at[z, which],
            f_send.at[sem],
            f_recv.at[sem],
            p.device(x=fx, y=fy),
        )

    def second(z):
        return remote(
            mine.at[z, sx, :, columns(sy)],
            second_in.at[z],
            s_send.at[z],
            s_recv.at[z],
            p.device(x=sx, y=sy),
        )

    per_core = nz // 2

    def out_at(z, half_of):
        return out.at[half_of, :, pl.ds(pl.multiple_of(lax.rem(z, per_core) * quarter, 128), quarter)]

    owner = p.z // per_core

    def deal(z):
        return remote(
            mine.at[z, p.x, :, columns(p.y)],
            out_at(p.z, p.c),
            d_send.at[z],
            d_recv.at[2 * lax.rem(p.z, per_core) + p.c],
            p.device(z=z, c=owner),
        )

    def keep(z):
        return pltpu.make_async_copy(
            mine.at[z, p.x, :, columns(p.y)],
            out_at(p.z, p.c),
            d_recv.at[2 * lax.rem(p.z, per_core) + p.c],
        )

    for z in order:
        for x in range(2):
            across(z, x).start()
            bring(z, x).start()

    def summed_over_core(z):
        for x in range(2):
            across(z, x).wait_recv()
            bring(z, x).wait()
            add_rows(mine.at[z, x], mine.at[z, x], came.at[z, x])
        for which in range(2):
            first(z, which).start()

    def summed_over_first(z):
        for which in (1, 0):
            x, y = p.x, p.y
            if which:
                x, y = sx, sy
            first(z, which).wait_recv()
            place = mine.at[z, x, :, columns(y)]
            add_rows(place, place, first_in.at[z, which])
            if which:
                second(z).start()

    def summed_over_second(z):
        second(z).wait_recv()
        place = mine.at[z, p.x, :, columns(p.y)]
        add_rows(place, place, second_in.at[z])
        here = (z == p.z) & (p.c == owner)
        pl.when(jnp.logical_not(here))(deal(z).start)
        pl.when(here)(keep(z).start)

    for i in range(nz + 2):
        if i < nz:
            summed_over_core(order[i])
        if 0 <= i - 1 < nz:
            summed_over_first(order[i - 1])
        if 0 <= i - 2 < nz:
            summed_over_second(order[i - 2])
    for piece in range(per_core):
        for half_of in range(2):
            z = p.c * per_core + piece
            place = out_at(z, half_of)
            arrived = remote(
                place, place, d_send.at[0], d_recv.at[2 * piece + half_of], other_core
            )
            ours = (z == p.z) & (p.c == half_of)
            pl.when(jnp.logical_not(ours))(arrived.wait_recv)
    for z in range(nz):
        here = (z == p.z) & (p.c == owner)
        pl.when(jnp.logical_not(here))(deal(z).wait_send)
        pl.when(here)(keep(z).wait)
        second(z).wait_send()
        for which in range(2):
            first(z, which).wait_send()
        for x in range(2):
            across(z, x).wait_send()


class Kernels:
    def __init__(self, at):
        self.at = at
        self.blocks, self.nz = at.blocks, at.nz
        self.block = 2 * at.z + at.c
        self.number = 0

    def call(self, body, out_shape, scratch, vmem=(), out_vmem=(), sent=0):
        def run(*operands):
            self.number += 1
            many = isinstance(out_shape, list)
            specs = [in_vmem if i in out_vmem else anywhere for i in range(len(out_shape) if many else 1)]
            return pl.pallas_call(
                body,
                out_shape=out_shape,
                in_specs=[in_vmem if i in vmem else anywhere for i in range(len(operands))],
                out_specs=specs if many else specs[0],
                scratch_shapes=scratch,
                compiler_params=pltpu.CompilerParams(
                    collective_id=self.number, has_side_effects=True, vmem_limit_bytes=48 * 2**20
                ),
                cost_estimate=pl.CostEstimate(
                    flops=0, bytes_accessed=sent, transcendentals=0, remote_bytes_transferred=sent
                ),
            )(*operands)

        return run

    def start(self, own, attn_shard, ff_shards):
        nz = self.nz
        rows, depth = own.shape
        shard_rows, attn_columns = attn_shard.shape
        units = ff_shards[0].shape[1]
        half, width = shard_rows // 2, 4 * units // nz
        dma = pltpu.SemaphoreType.DMA
        full = jax.ShapeDtypeStruct((nz, 2, 2, half, width), bf16)
        outs = [
            jax.ShapeDtypeStruct((4, rows, depth), bf16),
            jax.ShapeDtypeStruct((nz, 2, shard_rows, attn_columns), bf16),
            full, full, full,
        ]
        count = 6 * nz + nz
        scratch = [
            dma((4,)), dma((4,)), dma, dma, dma((2, nz)), dma((2, nz)), dma((nz,)), dma((nz,)),
            dma((3, count)), dma((3, count)), dma((2,)),
        ]
        rows_out, attn_full, *ff = self.call(
            functools.partial(start_kernel, nz), outs, scratch, sent=20_000_000
        )(own, attn_shard, *[w.reshape(2, half, units) for w in ff_shards])
        return (
            rows_out.reshape(4 * rows, depth),
            attn_full.reshape(depth, attn_columns),
            [w.reshape(depth, width) for w in ff],
        )

    def gather_heads(self, own):
        dma = pltpu.SemaphoreType.DMA
        out = jax.ShapeDtypeStruct((4,) + own.shape, bf16)
        whole = self.call(
            functools.partial(gather_heads_kernel, self.nz), out, [dma((4,)), dma((4,)), dma]
        )(own)
        return whole.reshape(-1, own.shape[1])

    def scatter_heads(self, partial):
        dma = pltpu.SemaphoreType.DMA
        rows, depth = partial.shape[0] // 4, partial.shape[1]
        out = jax.ShapeDtypeStruct((rows, depth), f32)
        scratch = [pltpu.VMEM((4, rows, depth), bf16), dma((4,)), dma((4,))]
        return self.call(
            functools.partial(scatter_heads_kernel, self.nz), out, scratch, vmem=(0,), out_vmem=(0,)
        )(partial.reshape(4, rows, depth))

    def gather_kv(self, own):
        dma = pltpu.SemaphoreType.DMA
        nz = self.nz
        out = jax.ShapeDtypeStruct((nz, 2) + own.shape, bf16)
        scratch = [dma((2, nz)), dma((2, nz)), dma((nz,)), dma((nz,)), dma]
        whole = self.call(functools.partial(gather_kv_kernel, nz), out, scratch)(own)
        return whole.reshape((self.blocks,) + own.shape)

    def gather_z(self, own):
        dma = pltpu.SemaphoreType.DMA
        nz = self.nz
        out = jax.ShapeDtypeStruct((nz,) + own.shape, bf16)
        scratch = [dma((2, nz)), dma((2, nz)), dma]
        whole = self.call(functools.partial(gather_z_kernel, nz), out, scratch)(own)
        return whole.reshape(-1, own.shape[1])

    def scatter_z(self, partial):
        dma = pltpu.SemaphoreType.DMA
        nz = self.nz
        rows, depth = partial.shape[0] // nz, partial.shape[1]
        out = jax.ShapeDtypeStruct((rows, depth), f32)
        line = pltpu.VMEM((nz - 1, rows, depth), bf16)
        scratch = [pltpu.VMEM((nz, rows, depth), bf16), line, line, dma((2, nz)), dma((2, nz)), dma]
        return self.call(
            functools.partial(scatter_z_kernel, nz), out, scratch, out_vmem=(0,)
        )(partial.reshape(nz, rows, depth))

    def scatter_pair(self, given, trade_back):
        dma = pltpu.SemaphoreType.DMA
        nz = self.nz
        _, _, rows, width = given.shape
        out = jax.ShapeDtypeStruct((rows, width), bf16)
        whole = pltpu.VMEM((nz, rows, width), bf16)
        line = pltpu.VMEM((nz - 1, rows, width), bf16)
        scratch = [
            whole, whole, line, line,
            dma((nz,)), dma((nz,)), dma((2, nz)), dma((2, nz)), dma((nz,)), dma, dma,
        ]
        return self.call(
            functools.partial(scatter_pair_kernel, nz, trade_back), out, scratch, out_vmem=(0,)
        )(given)

    def scatter_kv(self, parts):
        return self.scatter_pair(parts.reshape((self.nz, 2) + parts.shape[1:]), False).astype(f32)

    def scatter_attn(self, grad):
        given = grad.reshape(self.nz, 2, grad.shape[0] // self.blocks, grad.shape[1])
        return self.scatter_pair(given, True).astype(f32)

    def collect(self, grads):
        dma = pltpu.SemaphoreType.DMA
        nz = self.nz
        depth, width = grads[0].shape
        half, quarter = depth // (4 * nz), width // 2
        out = jax.ShapeDtypeStruct((2, half, nz // 2 * quarter), bf16)
        whole = pltpu.VMEM((nz, 2, half, width), bf16)
        scratch = [
            whole,
            whole,
            pltpu.VMEM((nz, 2, half, quarter), bf16),
            pltpu.VMEM((nz, half, quarter), bf16),
            dma((2 * nz,)), dma((2 * nz,)), dma((2 * nz,)), dma((2 * nz,)), dma((2 * nz,)),
            dma((nz,)), dma((nz,)), dma((nz,)), dma((nz,)),
        ]
        run = self.call(functools.partial(collect_kernel, nz), out, scratch)
        found = []
        for grad in grads:
            shard = run(grad.reshape(nz, 2, 2, half, width))
            found.append(shard.reshape(2 * half, -1).astype(f32))
        return found


def causal_mask(rows):
    shape = (rows, rows)
    return lax.broadcasted_iota(jnp.int32, shape, 1) <= lax.broadcasted_iota(jnp.int32, shape, 0)


def forward_kernel(kinds, q_ref, kv_ref, out_ref, exact_ref, inv_ref, acc, total):
    step, last = pl.program_id(0), pl.num_programs(0) - 1
    heads, rows, dim = q_ref.shape
    kind = kinds[step]

    @pl.when(step == 0)
    def _():
        acc[...] = jnp.zeros_like(acc)
        total[...] = jnp.zeros_like(total)

    def work(own):
        for head in range(heads):
            raw = contract(q_ref[head], kv_ref[0, :, :dim], 1, 1)
            weights = jnp.exp(softcap * jnp.tanh(raw * (score_scale / softcap)))
            if own:
                weights = jnp.where(causal_mask(rows), weights, 0.0)
            total[head] += jnp.sum(weights, axis=-1, keepdims=True)
            acc[head] += contract(weights.astype(bf16), kv_ref[0, :, dim:], 1, 0)

    @pl.when(kind == 1)
    def _():
        work(False)

    @pl.when(kind == 2)
    def _():
        work(True)

    @pl.when(step == last)
    def _():
        for head in range(heads):
            inverse = 1.0 / total[head]
            value = acc[head] * inverse
            inv_ref[head] = inverse
            exact_ref[:, head * dim : (head + 1) * dim] = value
            out_ref[:, head * dim : (head + 1) * dim] = value.astype(bf16)


def whole2(step, kinds):
    return (0, 0)


def whole3(step, kinds):
    return (0, 0, 0)


def by_step(step, kinds):
    return (step, 0, 0)


def attend(kinds, queries, all_kv):
    heads, rows, dim = queries.shape
    return pl.pallas_call(
        forward_kernel,
        grid_spec=pltpu.PrefetchScalarGridSpec(
            num_scalar_prefetch=1,
            grid=(all_kv.shape[0],),
            in_specs=[
                pl.BlockSpec((heads, rows, dim), whole3),
                pl.BlockSpec((1, rows, 2 * dim), by_step),
            ],
            out_specs=[
                pl.BlockSpec((rows, heads * dim), whole2),
                pl.BlockSpec((rows, heads * dim), whole2),
                pl.BlockSpec((heads, rows, 1), whole3),
            ],
            scratch_shapes=[
                pltpu.VMEM((heads, rows, dim), f32),
                pltpu.VMEM((heads, rows, 1), f32),
            ],
        ),
        out_shape=[
            jax.ShapeDtypeStruct((rows, heads * dim), bf16),
            jax.ShapeDtypeStruct((rows, heads * dim), f32),
            jax.ShapeDtypeStruct((heads, rows, 1), f32),
        ],
        compiler_params=pltpu.CompilerParams(vmem_limit_bytes=40 * 2**20),
        cost_estimate=pl.CostEstimate(
            flops=3 * 4 * heads * rows * rows * dim,
            bytes_accessed=8 * rows * dim * heads,
            transcendentals=6 * heads * rows * rows,
        ),
    )(kinds, queries, all_kv)


def backward_kernel(kinds, q_ref, kv_ref, up_ref, exact_ref, inv_ref, dq_ref, dkv_ref):
    step = pl.program_id(0)
    heads, rows, dim = q_ref.shape
    kind = kinds[step]

    @pl.when(step == 0)
    def _():
        dq_ref[...] = jnp.zeros_like(dq_ref)

    def work(own):
        dk = jnp.zeros((rows, dim), f32)
        dv = jnp.zeros((rows, dim), f32)
        for head in range(heads):
            columns = slice(head * dim, (head + 1) * dim)
            up = up_ref[:, columns]
            delta = jnp.sum(up.astype(f32) * exact_ref[:, columns], axis=-1, keepdims=True)
            raw = contract(q_ref[head], kv_ref[0, :, :dim], 1, 1)
            bounded = jnp.tanh(raw * (score_scale / softcap))
            probs = jnp.exp(softcap * bounded) * inv_ref[head]
            if own:
                probs = jnp.where(causal_mask(rows), probs, 0.0)
            d_probs = contract(up, kv_ref[0, :, dim:], 1, 1)
            d_raw = probs * (d_probs - delta) * ((1.0 - bounded * bounded) * score_scale)
            d_raw = d_raw.astype(bf16)
            dq_ref[head] += contract(d_raw, kv_ref[0, :, :dim], 1, 0)
            dk += contract(d_raw, q_ref[head], 0, 0)
            dv += contract(probs.astype(bf16), up, 0, 0)
        dkv_ref[0, :, :dim] = dk.astype(bf16)
        dkv_ref[0, :, dim:] = dv.astype(bf16)

    @pl.when(kind == 1)
    def _():
        work(False)

    @pl.when(kind == 0)
    def _():
        dkv_ref[...] = jnp.zeros_like(dkv_ref)

    @pl.when(kind == 2)
    def _():
        work(True)


def attend_back(kinds, queries, all_kv, upstream, exact, inverse):
    heads, rows, dim = queries.shape
    blocks = all_kv.shape[0]
    return pl.pallas_call(
        backward_kernel,
        grid_spec=pltpu.PrefetchScalarGridSpec(
            num_scalar_prefetch=1,
            grid=(blocks,),
            in_specs=[
                pl.BlockSpec((heads, rows, dim), whole3),
                pl.BlockSpec((1, rows, 2 * dim), by_step),
                pl.BlockSpec((rows, heads * dim), whole2),
                pl.BlockSpec((rows, heads * dim), whole2),
                pl.BlockSpec((heads, rows, 1), whole3),
            ],
            out_specs=[
                pl.BlockSpec((heads, rows, dim), whole3),
                pl.BlockSpec((1, rows, 2 * dim), by_step),
            ],
        ),
        out_shape=[
            jax.ShapeDtypeStruct((heads, rows, dim), f32),
            jax.ShapeDtypeStruct((blocks, rows, 2 * dim), bf16),
        ],
        compiler_params=pltpu.CompilerParams(vmem_limit_bytes=40 * 2**20),
        cost_estimate=pl.CostEstimate(
            flops=3 * 10 * heads * rows * rows * dim,
            bytes_accessed=16 * rows * dim * heads,
            transcendentals=6 * heads * rows * rows,
        ),
    )(kinds, queries, all_kv, upstream, exact, inverse)


def on_device(
    tokens,
    cotangent,
    norm_attn_in,
    w_query,
    w_key,
    w_value,
    w_out,
    norm_attn_out,
    norm_ff_in,
    w_gate,
    w_up,
    w_down,
    norm_ff_out,
    block_group,
    block_role,
):
    at = Place()
    own_rows, depth = tokens.shape
    shard_rows, units = w_gate.shape
    regular = at.nz == 4 and shard_rows % 32 == 0 and (2 * units // at.nz) % 128 == 0
    comm = Kernels(at) if regular else Permutes(at)
    blocks = at.blocks
    block_len = own_rows * lax.axis_size("heads")
    prompt_len = blocks // 4
    block_ids = jnp.arange(blocks, dtype=jnp.int32)
    my_group = jnp.sum(jnp.where(block_ids == comm.block, block_group, 0))
    my_role = jnp.sum(jnp.where(block_ids == comm.block, block_role, 0))
    positions = jnp.where(
        my_role < prompt_len, my_role * block_len, prompt_len * block_len
    ) + jnp.arange(block_len, dtype=jnp.int32)
    cosine, sine_table = rope_tables(positions)
    prompt = (block_group == my_group) & (block_role < prompt_len) & (block_role < my_role)
    kinds = jnp.where(block_ids == comm.block, 2, prompt.astype(jnp.int32)).astype(jnp.int32)

    token_f32 = tokens.astype(f32)
    heads_width = w_query.shape[1]
    qkv_width = heads_width + 2 * HEAD_DIM
    attn_shard = jnp.concatenate([w_query, w_key, w_value, w_out.T], axis=1)
    normed_one, attn_full, (gate_full, up_full, down_full) = comm.start(
        normalize(token_f32, norm_attn_in).astype(bf16), attn_shard, (w_gate, w_up, w_down.T)
    )
    qkv_full, out_full = attn_full[:, :qkv_width], attn_full[:, qkv_width:]
    qkv_lin = jnp.dot(normed_one, qkv_full, preferred_element_type=f32)
    queries = jnp.stack(
        [
            rotate(qkv_lin[:, :HEAD_DIM], cosine, sine_table),
            rotate(qkv_lin[:, HEAD_DIM:heads_width], cosine, sine_table),
        ]
    ).astype(bf16)
    own_kv = jnp.concatenate(
        [
            rotate(qkv_lin[:, heads_width : heads_width + HEAD_DIM], cosine, sine_table),
            qkv_lin[:, heads_width + HEAD_DIM :],
        ],
        axis=1,
    ).astype(bf16)
    all_kv = comm.gather_kv(own_kv)
    attn_rows, attended, inverse = attend(kinds, queries, all_kv)
    attn_proj = comm.scatter_heads(contract(attn_rows, out_full, 1, 1).astype(bf16))
    middle = token_f32 + normalize(attn_proj, norm_attn_out)

    normed_two = comm.gather_z(normalize(middle, norm_ff_in).astype(bf16))
    gate_lin = jnp.dot(normed_two, gate_full, preferred_element_type=f32)
    up_lin = jnp.dot(normed_two, up_full, preferred_element_type=f32)
    hidden = (jax.nn.gelu(gate_lin, approximate=True) * up_lin).astype(bf16)
    ff_proj = comm.scatter_z(contract(hidden, down_full, 1, 1).astype(bf16))
    layer_out = middle + normalize(ff_proj, norm_ff_out)

    upstream = cotangent.astype(f32)
    d_ff, grad_ff_out = normalize_back(ff_proj, norm_ff_out, upstream)
    d_ff_rows = comm.gather_z(d_ff.astype(bf16))
    d_hidden = contract(d_ff_rows, down_full, 1, 0)
    _, glu_back = jax.vjp(
        lambda gate_in, up_in: jax.nn.gelu(gate_in, approximate=True) * up_in, gate_lin, up_lin
    )
    d_gate, d_up = glu_back(d_hidden)
    d_gate = d_gate.astype(bf16)
    d_up = d_up.astype(bf16)
    d_partial = contract(d_gate, gate_full, 1, 1) + contract(d_up, up_full, 1, 1)
    d_normed_two = comm.scatter_z(d_partial.astype(bf16))

    d_middle_part, grad_ff_in = normalize_back(middle, norm_ff_in, d_normed_two)
    d_middle = upstream + d_middle_part
    d_proj, grad_attn_out = normalize_back(attn_proj, norm_attn_out, d_middle)
    d_proj_rows = comm.gather_heads(d_proj.astype(bf16))
    d_attended = contract(d_proj_rows, out_full, 1, 0).astype(bf16)
    d_query, d_kv_parts = attend_back(kinds, queries, all_kv, d_attended, attended, inverse)
    d_kv = comm.scatter_kv(d_kv_parts)
    d_qkv_lin = jnp.concatenate(
        [
            rotate(d_query[0], cosine, -sine_table),
            rotate(d_query[1], cosine, -sine_table),
            rotate(d_kv[:, :HEAD_DIM], cosine, -sine_table),
            d_kv[:, HEAD_DIM:],
        ],
        axis=1,
    ).astype(bf16)
    d_normed_one = comm.scatter_heads(contract(d_qkv_lin, qkv_full, 1, 1).astype(bf16))
    grad_attn = comm.scatter_attn(
        jnp.concatenate(
            [contract(normed_one, d_qkv_lin, 0, 0), contract(d_proj_rows, attn_rows, 0, 0)], axis=1
        ).astype(bf16)
    )
    grad_gate, grad_up, grad_down = comm.collect(
        [
            contract(normed_two, d_gate, 0, 0).astype(bf16),
            contract(normed_two, d_up, 0, 0).astype(bf16),
            contract(d_ff_rows, hidden, 0, 0).astype(bf16),
        ]
    )
    d_token_part, grad_attn_in = normalize_back(token_f32, norm_attn_in, d_normed_one)
    input_grad = (d_middle + d_token_part).astype(bf16)
    gains = sum_all(at, jnp.stack([grad_attn_in, grad_attn_out, grad_ff_in, grad_ff_out]))
    return (
        layer_out.astype(bf16),
        input_grad,
        gains[0],
        grad_attn[:, :heads_width],
        grad_attn[:, heads_width : heads_width + HEAD_DIM],
        grad_attn[:, heads_width + HEAD_DIM : qkv_width],
        grad_attn[:, qkv_width:].T,
        gains[1],
        gains[2],
        grad_gate,
        grad_up,
        grad_down.T,
        gains[3],
    )


def solution(mesh):
    rows, weight, turned = P(("blk", "heads"), None), P("blk", "heads"), P("heads", "blk")
    return jax.shard_map(
        on_device,
        mesh=mesh,
        in_specs=(
            rows, rows, P(), weight, weight, weight, turned, P(), P(), weight, weight, turned,
            P(), P(), P(),
        ),
        out_specs=(
            rows, rows, P(), weight, weight, weight, turned, P(), P(), weight, weight, turned, P(),
        ),
        check_vma=False,
    )
```

```python
import math

import jax
import jax.numpy as jnp
from jax import lax
from jax.experimental import pallas as pl
from jax.experimental.pallas import tpu as pltpu
from jax.sharding import PartitionSpec as P

HEAD_DIM = 256


softcap = 50.0
epsilon = 1e-06
score_scale = HEAD_DIM ** (-0.5)
bf16 = jnp.bfloat16
f32 = jnp.float32


def contract(left_side, right_side, left_dim, right_dim):
    return lax.dot_general(
        left_side,
        right_side,
        (((left_dim,), (right_dim,)), ((), ())),
        preferred_element_type=f32,
    )


def factor_of(values):
    return lax.rsqrt(jnp.mean(values * values, axis=-1, keepdims=True) + epsilon)


def normalize(values, weight_gain):
    return values * factor_of(values) * (1.0 + weight_gain)


def normalize_back(values, weight_gain, upstream):
    factor = factor_of(values)
    unit = values * factor
    scaled = upstream * (1.0 + weight_gain)
    inner = jnp.mean(scaled * unit, axis=-1, keepdims=True)
    return (scaled - unit * inner) * factor, jnp.sum(upstream * unit, axis=0)


def rope_tables(positions):
    half_dim = HEAD_DIM // 2
    frequency = jnp.exp(
        jnp.arange(half_dim, dtype=f32) * (-2.0 * math.log(10000.0) / HEAD_DIM)
    )
    angles = positions.astype(f32)[:, None] * frequency[None, :]
    return (jnp.cos(angles), jnp.sin(angles))


def rotate(tensor, cosine, sine_table):
    half_dim = HEAD_DIM // 2
    first_half = tensor[..., :half_dim]
    second_half = tensor[..., half_dim:]
    return jnp.concatenate(
        [
            first_half * cosine - second_half * sine_table,
            second_half * cosine + first_half * sine_table,
        ],
        axis=-1,
    )


def swap_core(v):
    return lax.ppermute(v, "heads", [(i, i ^ 1) for i in range(4)])


def swap_y(v):
    return lax.ppermute(v, "heads", [(i, i ^ 2) for i in range(4)])


def swap_x(v):
    blocks = lax.axis_size("blk")
    return lax.ppermute(v, "blk", [(i, i ^ 1) for i in range(blocks)])


def pair_up(own, other, place, axis):
    first = jnp.where(place == 0, own, other)
    second = jnp.where(place == 0, other, own)
    return jnp.concatenate([first, second], axis=axis)


def shift_z(v, step, senders):
    pairs = []
    for z in senders:
        for x in range(2):
            pairs.append((2 * z + x, 2 * (z + step) + x))
    return lax.ppermute(v, "blk", pairs)


class Place:
    def __init__(self):
        self.blocks = lax.axis_size("blk")
        self.nz = self.blocks // 2
        self.b = lax.axis_index("blk")
        self.h = lax.axis_index("heads")
        self.z, self.x = self.b // 2, self.b % 2
        self.y, self.c = self.h // 2, self.h % 2


def gather_z(at, unit):
    nz = at.nz
    up, down = unit, unit
    ups, downs = [None], [None]
    for s in range(1, nz):
        up = shift_z(up, 1, range(s - 1, nz - 1))
        down = shift_z(down, -1, range(1, nz - s + 1))
        ups.append(up)
        downs.append(down)
    return [unit] + [jnp.where(at.z >= s, ups[s], downs[nz - s]) for s in range(1, nz)]


def scatter_z(at, parts):
    nz = at.nz
    up = down = None
    for t in range(1, nz):
        k = nz - t
        send_up = parts[nz - k].astype(f32)
        send_down = parts[k].astype(f32)
        if up is not None:
            send_up = send_up + up.astype(f32)
            send_down = send_down + down.astype(f32)
        up = shift_z(send_up.astype(bf16), 1, range(0, nz - k))
        down = shift_z(send_down.astype(bf16), -1, range(k, nz))
    return parts[0].astype(f32) + (up.astype(f32) + down.astype(f32))


def deal_z(at, parts):
    nz = at.nz
    got = [parts[0]]
    for s in range(1, nz):
        up = shift_z(parts[nz - s], s, range(0, nz - s))
        down = shift_z(parts[nz - s], s - nz, range(nz - s, nz))
        got.append(jnp.where(at.z >= s, up, down))
    return got


def turn(at, whole):
    return [
        lax.dynamic_index_in_dim(whole, (at.z - s) % at.nz, 0, keepdims=False)
        for s in range(at.nz)
    ]


def unturn(at, parts):
    whole = jnp.zeros((at.nz,) + parts[0].shape, parts[0].dtype)
    for s, part in enumerate(parts):
        whole = lax.dynamic_update_index_in_dim(whole, part, (at.z - s) % at.nz, 0)
    return whole


def gather_zx(at, unit):
    got = []
    for part in gather_z(at, unit):
        got.append(pair_up(part[None], swap_x(part)[None], at.x, 0))
    return unturn(at, got)


def gather_xz(at, unit):
    both = pair_up(unit[None], swap_x(unit)[None], at.x, 0)
    return unturn(at, gather_z(at, both))


def pick(pair, place):
    mine = jnp.where(place == 0, pair[0], pair[1])
    other = jnp.where(place == 0, pair[1], pair[0])
    return mine, other


def scatter_zx(at, parts):
    total = scatter_z(at, parts)
    mine, other = pick(total, at.x)
    return mine + swap_x(other.astype(bf16)).astype(f32)


def scatter_xz(at, parts):
    sums = []
    for part in parts:
        mine, other = pick(part, at.x)
        sums.append(mine.astype(f32) + swap_x(other.astype(bf16)).astype(f32))
    return scatter_z(at, sums)


def rows_to_block(at, own):
    both = pair_up(own, swap_core(own), at.c, 0)
    pair = pair_up(both[None], swap_y(both)[None], at.y, 0)
    return pair.reshape(4 * own.shape[0], own.shape[1])


def rows_from_block(at, partial_sum):
    rows = partial_sum.shape[0] // 4
    parts = partial_sum.reshape(2, 2, rows, partial_sum.shape[1])
    mine, other = pick(parts.swapaxes(0, 1), at.c)
    total = mine + swap_core(other.astype(bf16)).astype(f32)
    mine, other = pick(total, at.y)
    return mine + swap_y(other.astype(bf16)).astype(f32)


def spread_weight(at, shard):
    rows, units = shard.shape
    half = rows // 2
    keep, send = pick(shard.reshape(2, half, units), at.c)
    wide = pair_up(keep[None], swap_core(send)[None], at.c, 0)
    quarter = 2 * units // at.nz
    per_core = units // quarter
    pieces = wide.reshape(2, half, per_core, quarter).transpose(0, 2, 1, 3)
    pieces = pieces.reshape(at.nz, half, quarter)
    got = unturn(at, deal_z(at, turn(at, pieces)))
    got = pair_up(got[:, None], swap_x(got)[:, None], at.x, 1)
    got = pair_up(got, swap_y(got), at.y, 3)
    got = pair_up(got[:, :, None], swap_core(got)[:, :, None], at.c, 2)
    return got.reshape(at.blocks * rows, 2 * quarter)


def collect_weight(at, grad):
    depth, width = grad.shape
    half, quarter = depth // (2 * at.blocks), width // 2
    parts = grad.reshape(at.nz, 2, 2, half, width)
    mine, other = pick(parts.transpose(2, 0, 1, 3, 4), at.c)
    total = mine + swap_core(other.astype(bf16)).astype(f32)
    mine, other = pick((total[..., :quarter], total[..., quarter:]), at.y)
    total = mine + swap_y(other.astype(bf16)).astype(f32)
    mine, other = pick((total[:, 0], total[:, 1]), at.x)
    total = mine + swap_x(other.astype(bf16)).astype(f32)
    got = unturn(at, deal_z(at, turn(at, total.astype(bf16))))
    per_core = at.nz // 2
    wide = got.reshape(2, per_core, half, quarter).transpose(0, 2, 1, 3)
    wide = wide.reshape(2, half, per_core * quarter)
    mine, other = pick(wide, at.c)
    rows = pair_up(mine, swap_core(other), at.c, 0)
    return rows.astype(f32)


def sum_all(at, values):
    total = values
    for bit in (1, 2):
        total = total + lax.ppermute(total, "heads", [(i, i ^ bit) for i in range(4)])
    bit = 1
    while bit < at.blocks:
        total = total + lax.ppermute(total, "blk", [(i, i ^ bit) for i in range(at.blocks)])
        bit *= 2
    return total


class Permutes:
    def __init__(self, at):
        self.at = at
        self.block, self.blocks, self.nz = at.b, at.blocks, at.nz

    def split(self, whole):
        return turn(self.at, whole.reshape((self.nz, whole.shape[0] // self.nz) + whole.shape[1:]))

    def start(self, own, attn_shard, gate, up):
        at = self.at
        attn_full = gather_zx(at, attn_shard).reshape(own.shape[1], -1)
        return rows_to_block(at, own), attn_full, spread_weight(at, gate), spread_weight(at, up)

    def scatter_heads_deal(self, partial, down):
        return rows_from_block(self.at, partial), spread_weight(self.at, down)

    def gather_kv(self, own):
        return gather_zx(self.at, own).reshape((self.blocks,) + own.shape)

    def gather_z_copy(self, own, pieces):
        return self.gather_z(own), pieces

    def gather_z(self, own):
        whole = unturn(self.at, gather_z(self.at, own))
        return whole.reshape(-1, own.shape[1])

    def scatter_z(self, partial):
        return scatter_z(self.at, self.split(partial))

    def scatter_z_sums(self, partial, grad):
        return self.scatter_z(partial), collect_weight(self.at, grad)

    def gather_heads_back(self, own, sums):
        return rows_to_block(self.at, own), sums

    def scatter_kv_sums(self, parts, grad):
        return scatter_xz(self.at, self.split(parts)), collect_weight(self.at, grad)

    def scatter_heads_back(self, partial, sums):
        return rows_from_block(self.at, partial), sums

    def finish(self, attn_grad, grad, gains):
        rows = attn_grad.shape[0] // self.blocks
        attn = scatter_xz(self.at, self.split(attn_grad.reshape(self.blocks, rows, -1)))
        return attn, collect_weight(self.at, grad), sum_all(self.at, gains)


MESH = pl.DeviceIdType.MESH
DMA = pltpu.SemaphoreType.DMA
anywhere = pl.BlockSpec(memory_space=pl.ANY)
in_vmem = pl.BlockSpec(memory_space=pltpu.VMEM)


def remote(src, dst, send_sem, recv_sem, target):
    return pltpu.make_async_remote_copy(
        src_ref=src,
        dst_ref=dst,
        send_sem=send_sem,
        recv_sem=recv_sem,
        device_id=target,
        device_id_type=MESH,
    )


def flip(bit, by):
    return 1 - bit if by else bit


def exclusive_or(z, i):
    low, high = lax.rem(z, 2), lax.rem(z // 2, 2)
    rest = z - 2 * high - low
    return rest + 2 * flip(high, i // 2) + flip(low, i % 2)


class Spot:
    def __init__(self, nz):
        self.nz = nz
        h, b = lax.axis_index("heads"), lax.axis_index("blk")
        self.y, self.c = h // 2, h % 2
        self.z, self.x = b // 2, b % 2

    def device(self, z=None, x=None, y=None, c=None):
        z = self.z if z is None else z
        x = self.x if x is None else x
        y = self.y if y is None else y
        c = self.c if c is None else c
        return (2 * y + c, 2 * z + x)

    def partner(self):
        return self.device(c=1 - self.c)

    def greet(self):
        found = []
        for dx, dy, dc in [(0, 0, 1), (1, 0, 0), (1, 0, 1), (0, 1, 0), (0, 1, 1), (1, 1, 0), (1, 1, 1)]:
            found.append(self.device(x=flip(self.x, dx), y=flip(self.y, dy), c=flip(self.c, dc)))
        for s in range(1, self.nz):
            z = lax.rem(self.z + s, self.nz)
            found += [self.device(z=z), self.device(z=z, c=1 - self.c)]
        barrier = pltpu.get_barrier_semaphore()
        for device in found:
            pl.semaphore_signal(barrier, inc=1, device_id=device, device_id_type=MESH)
        pl.semaphore_wait(barrier, len(found))


def add_rows(out, left, right, step=16):
    rows = left.shape[0]

    @pl.loop(0, rows // step)
    def _(i):
        at = pl.ds(pl.multiple_of(i * step, step), step)
        out[at, :] = (left[at, :].astype(f32) + right[at, :].astype(f32)).astype(out.dtype)


class LineGather:
    def __init__(self, spot, entry, send, recv):
        self.spot, self.entry = spot, entry
        self.send, self.recv = send, recv

    def copies(self, s):
        p, nz = self.spot, self.spot.nz
        up_at = lax.rem(p.z - s + 1 + nz, nz)
        down_at = lax.rem(p.z + s - 1, nz)
        up = remote(
            self.entry(up_at),
            self.entry(up_at),
            self.send.at[0, s],
            self.recv.at[0, s],
            p.device(z=lax.rem(p.z + 1, nz)),
        )
        down = remote(
            self.entry(down_at),
            self.entry(down_at),
            self.send.at[1, s],
            self.recv.at[1, s],
            p.device(z=lax.rem(p.z + nz - 1, nz)),
        )
        return (
            ((p.z >= s - 1) & (p.z < nz - 1), p.z >= s, up),
            ((p.z <= nz - s) & (p.z > 0), p.z <= nz - 1 - s, down),
        )

    def start(self, s):
        for sends, _, copy in self.copies(s):
            pl.when(sends)(copy.start)

    def arrive(self, s):
        for _, receives, copy in self.copies(s):
            pl.when(receives)(copy.wait_recv)

    def finish(self):
        for s in range(1, self.spot.nz):
            for sends, _, copy in self.copies(s):
                pl.when(sends)(copy.wait_send)

    def newest(self, s):
        p, nz = self.spot, self.spot.nz
        return (
            (p.z >= s, lax.rem(p.z - s + nz, nz)),
            (p.z <= nz - 1 - s, lax.rem(p.z + s, nz)),
        )


class LineScatter:
    def __init__(self, spot, parts, up, down, send, recv):
        self.spot, self.parts, self.up, self.down = spot, parts, up, down
        self.send, self.recv = send, recv

    def copies(self, t):
        p, nz = self.spot, self.spot.nz
        k = nz - t
        up = remote(
            self.parts.at[lax.rem(p.z + k, nz)],
            self.up.at[t - 1],
            self.send.at[0, t],
            self.recv.at[0, t],
            p.device(z=lax.rem(p.z + 1, nz)),
        )
        down = remote(
            self.parts.at[lax.rem(p.z - k + nz, nz)],
            self.down.at[t - 1],
            self.send.at[1, t],
            self.recv.at[1, t],
            p.device(z=lax.rem(p.z + nz - 1, nz)),
        )
        return (
            (p.z <= nz - 1 - k, (p.z >= 1) & (p.z <= t), up),
            (p.z >= k, (p.z <= nz - 2) & (p.z >= nz - 1 - t), down),
        )

    def start(self, t):
        for sends, _, copy in self.copies(t):
            pl.when(sends)(copy.start)

    def arrive(self, t):
        p, nz = self.spot, self.spot.nz
        k = nz - t
        for way, (_, receives, copy) in enumerate(self.copies(t)):

            @pl.when(receives)
            def _(way=way, copy=copy):
                copy.wait_recv()
                if t < nz - 1:
                    index = lax.rem(p.z + k - 1, nz) if way == 0 else lax.rem(p.z - k + 1 + nz, nz)
                    came = (self.up if way == 0 else self.down).at[t - 1]
                    add_rows(self.parts.at[index], self.parts.at[index], came)

    def finish(self):
        for t in range(1, self.spot.nz):
            for sends, _, copy in self.copies(t):
                pl.when(sends)(copy.wait_send)

    def total(self, out, step=16):
        p, last = self.spot, self.spot.nz - 2
        mine = self.parts.at[p.z]
        inner = (p.z > 0) & (p.z < p.nz - 1)

        @pl.when(p.z == 0)
        def _():
            add_rows(out, mine, self.down.at[last], step)

        @pl.when(p.z == p.nz - 1)
        def _():
            add_rows(out, mine, self.up.at[last], step)

        @pl.when(inner)
        def _():
            @pl.loop(0, out.shape[0] // step)
            def _(i):
                at = pl.ds(pl.multiple_of(i * step, step), step)
                sides = self.up[last, at, :].astype(f32) + self.down[last, at, :].astype(f32)
                out[at, :] = (mine[at, :].astype(f32) + sides).astype(out.dtype)


class Task:
    ins = ()
    outs = ()
    scratch = ()
    vmem_ins = ()
    vmem_outs = ()

    def steps(self, p, ins, outs, scratch):
        raise NotImplementedError


class PlaneGather(Task):
    vmem_ins = (0,)
    vmem_outs = (0,)

    def __init__(self, own):
        self.ins = (own,)
        self.outs = (jax.ShapeDtypeStruct((4,) + own.shape, bf16),)
        self.scratch = (DMA((4,)), DMA((4,)), DMA)

    def steps(self, p, ins, outs, scratch):
        (own,), (whole,), (send, recv, local) = ins, outs, scratch
        part = 2 * p.y + p.c
        keep = pltpu.make_async_copy(own, whole.at[part], local)
        copies = []
        for i, (dx, dy) in enumerate([(1, 0), (0, 1), (1, 1), (0, 0)]):
            target = p.device(x=flip(p.x, dx), y=flip(p.y, dy), c=p.x)
            copies.append(remote(own, whole.at[part], send.at[i], recv.at[part], target))
        *away, home = copies
        for copy in away:
            copy.start()
        pl.when(p.c == p.x)(keep.start)
        pl.when(p.c != p.x)(home.start)
        yield
        for copy in away:
            copy.wait_send()
        pl.when(p.c == p.x)(keep.wait)
        pl.when(p.c != p.x)(home.wait_send)
        for slot in range(4):
            came = remote(own, whole.at[slot], send.at[0], recv.at[slot], p.partner())
            mine = (p.c == p.x) & (part == slot)
            pl.when(jnp.logical_not(mine))(came.wait_recv)


class PlaneScatter(Task):
    vmem_ins = (0,)
    vmem_outs = (0,)

    def __init__(self, partial):
        rows, depth = partial.shape[0] // 4, partial.shape[1]
        self.ins = (partial.reshape(4, rows, depth),)
        self.outs = (jax.ShapeDtypeStruct((rows, depth), f32),)
        self.scratch = (pltpu.VMEM((4, rows, depth), bf16), DMA((4,)), DMA((4,)))

    def steps(self, p, ins, outs, scratch):
        (parts,), (out,), (came, send, recv) = ins, outs, scratch
        head, ours = 2 * p.y + p.x, 2 * p.y + p.c

        def copy_to(part):
            target = p.device(x=p.c, y=part // 2, c=part % 2)
            return remote(parts.at[part], came.at[head], send.at[part], recv.at[head], target)

        for part in range(4):
            here = (p.x == p.c) & (part == ours)
            pl.when(jnp.logical_not(here))(copy_to(part).start)
        yield
        for part in range(4):
            here = (p.x == p.c) & (part == ours)
            pl.when(jnp.logical_not(here))(copy_to(part).wait_send)
            arrived = remote(parts.at[part], came.at[part], send.at[part], recv.at[part], p.partner())
            mine = (p.x == p.c) & (part == head)
            pl.when(jnp.logical_not(mine))(arrived.wait_recv)

        @pl.when(p.x == p.c)
        def _():
            came[head] = parts[ours]

        @pl.loop(0, out.shape[0] // 16)
        def _(i):
            at = pl.ds(pl.multiple_of(i * 16, 16), 16)
            low = came[0, at, :].astype(f32) + came[1, at, :].astype(f32)
            out[at, :] = low + (came[2, at, :].astype(f32) + came[3, at, :].astype(f32))


class PairGather(Task):
    vmem_ins = (0,)
    vmem_outs = (0,)

    def __init__(self, nz, own, trade):
        self.trade = trade
        self.ins = (own,)
        self.outs = (jax.ShapeDtypeStruct((nz, 2) + own.shape, bf16),)
        self.scratch = (DMA((2, nz)), DMA((2, nz)), DMA((nz,)), DMA((nz,)), DMA, DMA, DMA)

    def steps(self, p, ins, outs, scratch):
        (own,), (full,), (send, recv, x_send, x_recv, t_send, t_recv, local) = ins, outs, scratch
        nz = p.nz
        keep = pltpu.make_async_copy(own, full.at[p.z, p.c], local)
        line = LineGather(p, lambda z: full.at[z, p.c], send, recv)

        def across(z):
            here = full.at[z, p.c]
            return remote(here, here, x_send.at[z], x_recv.at[z], p.partner())

        if self.trade:
            same = p.c == p.x
            move = remote(own, full.at[p.z, p.x], t_send, t_recv, p.device(x=1 - p.x, c=1 - p.c))
            pl.when(same)(keep.start)
            pl.when(jnp.logical_not(same))(move.start)
            yield
            pl.when(same)(keep.wait)
            pl.when(jnp.logical_not(same))(move.wait_recv)
        else:
            keep.start()
            keep.wait()
        line.start(1)
        across(p.z).start()
        yield
        for s in range(1, nz):
            line.arrive(s)
            if s < nz - 1:
                line.start(s + 1)
            for came, z in line.newest(s):
                pl.when(came)(across(z).start)
            yield
        line.finish()
        if self.trade:
            pl.when(jnp.logical_not(same))(move.wait_send)
        for z in range(nz):
            across(z).wait()


class ZGather(Task):
    vmem_ins = (0,)
    vmem_outs = (0,)

    def __init__(self, nz, own):
        self.ins = (own,)
        self.outs = (jax.ShapeDtypeStruct((nz,) + own.shape, bf16),)
        self.scratch = (DMA((2, nz)), DMA((2, nz)), DMA)

    def steps(self, p, ins, outs, scratch):
        (own,), (full,), (send, recv, local) = ins, outs, scratch
        line = LineGather(p, lambda z: full.at[z], send, recv)
        keep = pltpu.make_async_copy(own, full.at[p.z], local)
        keep.start()
        keep.wait()
        line.start(1)
        yield
        for s in range(1, p.nz):
            line.arrive(s)
            if s < p.nz - 1:
                line.start(s + 1)
            yield
        line.finish()


class ZScatter(Task):
    vmem_outs = (0,)

    def __init__(self, nz, partial):
        rows, depth = partial.shape[0] // nz, partial.shape[1]
        self.ins = (partial.reshape(nz, rows, depth),)
        self.outs = (jax.ShapeDtypeStruct((rows, depth), f32),)
        line = pltpu.VMEM((nz - 1, rows, depth), bf16)
        self.scratch = (
            pltpu.VMEM((nz, rows, depth), bf16), line, line, DMA((2, nz)), DMA((2, nz)), DMA
        )

    def steps(self, p, ins, outs, scratch):
        (given,), (out,), (parts, up, down, send, recv, local) = ins, outs, scratch
        bring = pltpu.make_async_copy(given, parts, local)
        bring.start()
        bring.wait()
        line = LineScatter(p, parts, up, down, send, recv)
        line.start(1)
        yield
        for t in range(1, p.nz):
            line.arrive(t)
            if t < p.nz - 1:
                line.start(t + 1)
            yield
        line.total(out)
        line.finish()


class PairScatter(Task):
    vmem_outs = (0,)

    def __init__(self, nz, given, trade):
        _, _, rows, width = given.shape
        self.trade = trade
        self.ins = (given,)
        self.outs = (jax.ShapeDtypeStruct((rows, width), bf16),)
        whole = pltpu.VMEM((nz, rows, width), bf16)
        line = pltpu.VMEM((nz - 1, rows, width), bf16)
        self.scratch = (
            whole, whole, line, line,
            DMA((nz,)), DMA((nz,)), DMA((2, nz)), DMA((2, nz)), DMA((nz,)), DMA, DMA, DMA,
        )

    def steps(self, p, ins, outs, scratch):
        (given,), (out,) = ins, outs
        parts, came, up, down, x_send, x_recv, send, recv, local, b_send, b_recv, b_local = scratch
        nz = p.nz
        order = [exclusive_or(p.z, i) for i in (3, 2, 1, 0)]

        def away(z):
            return remote(given.at[z, 1 - p.c], came.at[z], x_send.at[z], x_recv.at[z], p.partner())

        def bring(z):
            return pltpu.make_async_copy(given.at[z, p.c], parts.at[z], local.at[z])

        for z in order:
            away(z).start()
            bring(z).start()
        yield
        for z in order:
            away(z).wait_recv()
            bring(z).wait()
            add_rows(parts.at[z], parts.at[z], came.at[z])
        line = LineScatter(p, parts, up, down, send, recv)
        line.start(1)
        yield
        for t in range(1, nz):
            line.arrive(t)
            if t < nz - 1:
                line.start(t + 1)
            yield
        if not self.trade:
            line.total(out)
        else:
            line.total(came.at[0])
            same = p.c == p.x
            back = remote(came.at[0], out, b_send, b_recv, p.device(x=1 - p.x, c=1 - p.c))
            keep = pltpu.make_async_copy(came.at[0], out, b_local)
            pl.when(same)(keep.start)
            pl.when(jnp.logical_not(same))(back.start)
            yield
            pl.when(same)(keep.wait)
            pl.when(jnp.logical_not(same))(back.wait)
        for z in order:
            away(z).wait_send()
        line.finish()


class Deal:
    def __init__(self, p, shard, place, quarter, send, recv):
        self.p, self.shard, self.place, self.quarter = p, shard, place, quarter
        self.send, self.recv = send, recv
        self.per_core = p.nz // 2

    def piece(self, piece, half):
        columns = pl.ds(piece * self.quarter, self.quarter)
        return self.shard.at[half, :, columns]

    def away(self, piece, half):
        p = self.p
        z = p.c * self.per_core + piece
        return z, remote(
            self.piece(piece, half),
            self.place(p.z, half),
            self.send.at[2 * piece + half],
            self.recv.at[p.z],
            p.device(z=z, c=half),
        )

    def local(self, piece):
        p = self.p
        columns = pl.ds(piece * self.quarter, self.quarter)
        return pltpu.make_async_copy(
            self.shard.at[p.c, :, columns], self.place(p.z, p.c), self.recv.at[p.z]
        )

    def start(self, in_plane):
        p = self.p
        for piece in range(self.per_core):
            for half in range(2):
                z, copy = self.away(piece, half)
                if in_plane:
                    pl.when((z == p.z) & (p.c != half))(copy.start)
                    pl.when((z == p.z) & (p.c == half))(self.local(piece).start)
                else:
                    pl.when(z != p.z)(copy.start)

    def arrive(self, source):
        p = self.p
        here = self.place(source, p.c)
        ours = (source == p.z) & (p.c == p.z // self.per_core)
        came = remote(here, here, self.send.at[0], self.recv.at[source], p.partner())
        pl.when(jnp.logical_not(ours))(came.wait_recv)
        pl.when(ours)(self.local(0).wait)

    def finish(self):
        p = self.p
        for piece in range(self.per_core):
            for half in range(2):
                z, copy = self.away(piece, half)
                here = (z == p.z) & (p.c == half)
                pl.when(jnp.logical_not(here))(copy.wait_send)


class DealTask(Task):
    vmem_outs = (0,)

    def __init__(self, nz, shard):
        rows, units = shard.shape
        self.ins = (shard.reshape(2, rows // 2, units),)
        self.outs = (jax.ShapeDtypeStruct((nz, rows // 2, 2 * units // nz), bf16),)
        self.scratch = (DMA((nz,)), DMA((nz,)))

    def steps(self, p, ins, outs, scratch):
        (shard,), (pieces,), (send, recv) = ins, outs, scratch
        deal = Deal(p, shard, lambda z, half: pieces.at[z], pieces.shape[-1], send, recv)
        deal.start(False)
        deal.start(True)
        yield
        for i in range(p.nz):
            deal.arrive(exclusive_or(p.z, i))
        deal.finish()


class Copies(Task):
    vmem_outs = (0,)

    def __init__(self, nz, given, dealt):
        self.dealt = dealt
        if dealt:
            _, half, quarter = given.shape
            self.ins = (given,)
        else:
            rows, units = given.shape
            half, quarter = rows // 2, 2 * units // nz
            self.ins = (given.reshape(2, half, units),)
        self.quarter = quarter
        self.outs = (jax.ShapeDtypeStruct((nz, 2, 2, half, 2 * quarter), bf16),)
        self.scratch = (
            DMA((nz,)), DMA((nz,)), DMA((nz,)), DMA((nz,)), DMA((nz, 2)), DMA((nz, 2)),
            DMA((nz, 2)), DMA((nz, 2)),
        )

    def steps(self, p, ins, outs, scratch):
        (given,), (full,) = ins, outs
        d_send, d_recv, f_send, f_recv, s_send, s_recv, x_send, x_recv = scratch
        nz, quarter = p.nz, self.quarter

        def place(z, x, c, y):
            columns = pl.ds(pl.multiple_of(y * quarter, 128), quarter)
            return full.at[z, x, c, :, columns]

        fx, fy = p.x + (1 - 2 * p.x) * (1 - p.c), p.y + (1 - 2 * p.y) * p.c
        sx, sy = p.x + (1 - 2 * p.x) * p.c, p.y + (1 - 2 * p.y) * (1 - p.c)

        def own(z):
            return given.at[z] if self.dealt else place(z, p.x, p.c, p.y)

        def first(z):
            target = p.device(x=fx, y=fy)
            return remote(own(z), place(z, p.x, p.c, p.y), f_send.at[z], f_recv.at[z], target)

        def second(z, which):
            x, y = (fx, fy) if which else (p.x, p.y)
            here = place(z, x, p.c, y)
            src = here if which else own(z)
            target = p.device(x=sx, y=sy)
            return remote(src, here, s_send.at[z, which], s_recv.at[z, which], target)

        def across(z, x):
            here = full.at[z, x, p.c]
            return remote(here, here, x_send.at[z, x], x_recv.at[z, x], p.partner())

        def keep(z):
            return pltpu.make_async_copy(given.at[z], place(z, p.x, p.c, p.y), d_send.at[z])

        order = [exclusive_or(p.z, i) for i in range(nz)]
        if self.dealt:
            for z in order:
                first(z).start()
                second(z, 0).start()
                keep(z).start()
            for z in order:
                keep(z).wait()
            yield
        else:
            deal = Deal(
                p, given, lambda z, half: place(z, p.x, half, p.y), quarter, d_send, d_recv
            )
            deal.start(True)
            yield
            deal.arrive(order[0])
            first(order[0]).start()
            second(order[0], 0).start()
            yield
            deal.start(False)
            yield
            for z in order[1:]:
                deal.arrive(z)
                first(z).start()
                second(z, 0).start()
                yield
        for z in order:
            first(z).wait_recv()
            second(z, 1).start()
            yield
        for z in order:
            second(z, 0).wait_recv()
            second(z, 1).wait_recv()
            across(z, 0).start()
            across(z, 1).start()
            yield
        for z in range(nz):
            first(z).wait_send()
            for i in range(2):
                second(z, i).wait_send()
                across(z, i).wait()
        if not self.dealt:
            deal.finish()


class DealBack:
    def __init__(self, p, source, out, quarter, send, recv):
        self.p, self.source, self.out, self.quarter = p, source, out, quarter
        self.send, self.recv = send, recv
        self.per_core = p.nz // 2
        self.owner = p.z // self.per_core

    def out_at(self, z, half):
        start = pl.multiple_of(lax.rem(z, self.per_core) * self.quarter, 128)
        return self.out.at[half, :, pl.ds(start, self.quarter)]

    def away(self, z):
        p = self.p
        return remote(
            self.source(z),
            self.out_at(p.z, p.c),
            self.send.at[z],
            self.recv.at[2 * lax.rem(p.z, self.per_core) + p.c],
            p.device(z=z, c=self.owner),
        )

    def keep(self, z):
        p = self.p
        return pltpu.make_async_copy(
            self.source(z),
            self.out_at(p.z, p.c),
            self.recv.at[2 * lax.rem(p.z, self.per_core) + p.c],
        )

    def start(self, z):
        p = self.p
        here = (z == p.z) & (p.c == self.owner)
        pl.when(jnp.logical_not(here))(self.away(z).start)
        pl.when(here)(self.keep(z).start)

    def finish(self):
        p = self.p
        for piece in range(self.per_core):
            for half in range(2):
                z = p.c * self.per_core + piece
                place = self.out_at(z, half)
                came = remote(
                    place, place, self.send.at[0], self.recv.at[2 * piece + half], p.partner()
                )
                ours = (z == p.z) & (p.c == half)
                pl.when(jnp.logical_not(ours))(came.wait_recv)
        for z in range(p.nz):
            here = (z == p.z) & (p.c == self.owner)
            pl.when(jnp.logical_not(here))(self.away(z).wait_send)
            pl.when(here)(self.keep(z).wait)


class DealBackTask(Task):
    vmem_outs = (0,)

    def __init__(self, nz, sums):
        _, half, quarter = sums.shape
        self.ins = (sums,)
        self.outs = (jax.ShapeDtypeStruct((2, half, nz // 2 * quarter), bf16),)
        self.scratch = (DMA((nz,)), DMA((nz,)))

    def steps(self, p, ins, outs, scratch):
        (sums,), (out,), (send, recv) = ins, outs, scratch
        deal = DealBack(p, lambda z: sums.at[z], out, sums.shape[-1], send, recv)
        for i in (3, 2, 1, 0):
            deal.start(exclusive_or(p.z, i))
        yield
        deal.finish()


class Sums(Task):
    def __init__(self, nz, grad, deal):
        depth, width = grad.shape
        half, quarter = depth // (4 * nz), width // 2
        self.deal = deal
        self.ins = (grad.reshape(nz, 2, 2, half, width),)
        if deal:
            self.outs = (jax.ShapeDtypeStruct((2, half, nz // 2 * quarter), bf16),)
        else:
            self.outs = (jax.ShapeDtypeStruct((nz, half, quarter), bf16),)
            self.vmem_outs = (0,)
        whole = pltpu.VMEM((nz, 2, half, width), bf16)
        self.scratch = (
            whole,
            whole,
            pltpu.VMEM((nz, 2, half, quarter), bf16),
            pltpu.VMEM((nz, half, quarter), bf16),
            DMA((nz, 2)), DMA((nz, 2)), DMA((nz, 2)), DMA((nz, 2)), DMA((nz, 2)),
            DMA((nz,)), DMA((nz,)), DMA((nz,)), DMA((nz,)),
        )

    def steps(self, p, ins, outs, scratch):
        (given,), (out,) = ins, outs
        mine, came, first_in, second_in, *sems = scratch
        local, c_send, c_recv, f_send, f_recv, s_send, s_recv, d_send, d_recv = sems
        nz, quarter = p.nz, given.shape[4] // 2
        order = [exclusive_or(p.z, i) for i in (3, 2, 1, 0)]

        def bring(z, x):
            return pltpu.make_async_copy(given.at[z, x, p.c], mine.at[z, x], local.at[z, x])

        def across(z, x):
            src = given.at[z, x, 1 - p.c]
            return remote(src, came.at[z, x], c_send.at[z, x], c_recv.at[z, x], p.partner())

        def place(z, x, y):
            return mine.at[z, x, :, pl.ds(pl.multiple_of(y * quarter, 128), quarter)]

        fx, fy = p.x + (1 - 2 * p.x) * p.c, p.y + (1 - 2 * p.y) * (1 - p.c)
        sx, sy = p.x + (1 - 2 * p.x) * (1 - p.c), p.y + (1 - 2 * p.y) * p.c

        def first(z, which):
            x, y = (1 - p.x, 1 - p.y) if which else (fx, fy)
            target = p.device(x=fx, y=fy)
            return remote(
                place(z, x, y), first_in.at[z, which], f_send.at[z, which], f_recv.at[z, which], target
            )

        def second(z):
            target = p.device(x=sx, y=sy)
            return remote(place(z, sx, sy), second_in.at[z], s_send.at[z], s_recv.at[z], target)

        back = DealBack(p, lambda z: place(z, p.x, p.y), out, quarter, d_send, d_recv)
        for z in order:
            for x in range(2):
                across(z, x).start()
                bring(z, x).start()
        yield
        for z in order:
            for x in range(2):
                across(z, x).wait_recv()
                bring(z, x).wait()
                add_rows(mine.at[z, x], mine.at[z, x], came.at[z, x])
            for which in (1, 0):
                first(z, which).start()
            yield
        for i in range(nz + 1):
            if i < nz:
                z = order[i]
                for which in (1, 0):
                    at = place(z, sx, sy) if which else place(z, p.x, p.y)
                    first(z, which).wait_recv()
                    add_rows(at, at, first_in.at[z, which])
                    if which:
                        second(z).start()
                yield
            if i >= 1:
                z = order[i - 1]
                second(z).wait_recv()
                at = place(z, p.x, p.y)
                if self.deal:
                    add_rows(at, at, second_in.at[z])
                    back.start(z)
                else:
                    add_rows(out.at[z], at, second_in.at[z])
                yield
        if self.deal:
            back.finish()
        for z in range(nz):
            second(z).wait_send()
            for i in range(2):
                first(z, i).wait_send()
                across(z, i).wait_send()


class SumAll(Task):
    vmem_ins = (0,)
    vmem_outs = (0,)

    def __init__(self, values):
        self.ins = (values,)
        self.outs = (jax.ShapeDtypeStruct(values.shape, f32),)
        stage = pltpu.VMEM((5,) + values.shape, f32)
        self.scratch = (stage, stage, DMA((5,)), DMA((5,)))

    def steps(self, p, ins, outs, scratch):
        (given,), (out,), (stage, came, send, recv) = ins, outs, scratch
        targets = [
            p.partner(),
            p.device(y=1 - p.y),
            p.device(x=1 - p.x),
            p.device(z=exclusive_or(p.z, 1)),
            p.device(z=exclusive_or(p.z, 2)),
        ]
        stage[0] = given[...]
        for i, target in enumerate(targets):
            copy = remote(stage.at[i], came.at[i], send.at[i], recv.at[i], target)
            copy.start()
            yield
            copy.wait()
            total = stage[i] + came[i]
            if i < 4:
                stage[i + 1] = total
            else:
                out[...] = total


def run_tasks(nz, number, tasks, order=""):
    counts = [(len(t.ins), len(t.outs), len(t.scratch)) for t in tasks]

    def split(refs, which):
        found = []
        for count in counts:
            found.append(refs[: count[which]])
            refs = refs[count[which] :]
        return found, refs

    def body(*refs):
        ins, refs = split(refs, 0)
        outs, refs = split(refs, 1)
        scratch, refs = split(refs, 2)
        p = Spot(nz)
        p.greet()
        running = [t.steps(p, *given) for t, *given in zip(tasks, ins, outs, scratch)]
        done = [False] * len(tasks)
        for digit in order:
            i = int(digit)
            if not done[i]:
                done[i] = next(running[i], "end") == "end"
        while not all(done):
            for i, steps in enumerate(running):
                if not done[i]:
                    done[i] = next(steps, "end") == "end"

    sent = sum(x.size * 2 for t in tasks for x in t.ins)
    held = [s for t in tasks for s in t.scratch if getattr(s, "memory_space", None) == pltpu.VMEM]
    held += [t.ins[i] for t in tasks for i in t.vmem_ins] + [t.outs[i] for t in tasks for i in t.vmem_outs]
    vmem = sum(math.prod(s.shape) * jnp.dtype(s.dtype).itemsize for s in held)
    results = pl.pallas_call(
        body,
        out_shape=[o for t in tasks for o in t.outs],
        in_specs=[in_vmem if i in t.vmem_ins else anywhere for t in tasks for i in range(len(t.ins))],
        out_specs=[
            in_vmem if i in t.vmem_outs else anywhere for t in tasks for i in range(len(t.outs))
        ],
        scratch_shapes=[s for t in tasks for s in t.scratch],
        compiler_params=pltpu.CompilerParams(
            collective_id=number, has_side_effects=True, vmem_limit_bytes=vmem + 4 * 2**20
        ),
        cost_estimate=pl.CostEstimate(
            flops=0, bytes_accessed=sent, transcendentals=0, remote_bytes_transferred=sent
        ),
    )(*[x for t in tasks for x in t.ins])
    found, _ = split(list(results), 1)
    return [f[0] for f in found]


START_ORDER = "10231223" + "13222" + "12222" + "3331" + "2222" + "33333333"


class Kernels:
    def __init__(self, at):
        self.at = at
        self.blocks, self.nz = at.blocks, at.nz
        self.block = 2 * at.z + at.c
        self.number = 0

    def run(self, tasks, order=""):
        self.number += 1
        return run_tasks(self.nz, self.number, tasks, order)

    def flat(self, whole):
        return whole.reshape(-1, whole.shape[-1])

    def start(self, own, attn_shard, gate, up):
        nz = self.nz
        tasks = [
            PlaneGather(own),
            PairGather(nz, attn_shard, True),
            Copies(nz, gate, False),
            Copies(nz, up, False),
        ]
        found = self.run(tasks, START_ORDER)
        return [self.flat(w) for w in found]

    def scatter_heads_deal(self, partial, down):
        return self.run([PlaneScatter(partial), DealTask(self.nz, down)], "10")

    def gather_kv(self, own):
        (whole,) = self.run([PairGather(self.nz, own, False)])
        return whole.reshape((self.blocks,) + own.shape)

    def gather_z_copy(self, own, pieces):
        return [
            self.flat(w) for w in self.run([ZGather(self.nz, own), Copies(self.nz, pieces, True)], "01001111011110")
        ]

    def gather_z(self, own):
        return self.flat(self.run([ZGather(self.nz, own)])[0])

    def scatter_z(self, partial):
        return self.run([ZScatter(self.nz, partial)])[0]

    def scatter_z_sums(self, partial, grad):
        return self.run([ZScatter(self.nz, partial), Sums(self.nz, grad, False)], "1011110" + "11110" + "11110")

    def gather_heads_back(self, own, sums):
        rows, shard = self.run([PlaneGather(own), DealBackTask(self.nz, sums)], "01")
        return self.flat(rows), self.flat(shard)

    def scatter_kv_sums(self, parts, grad):
        given = parts.reshape((self.nz, 2) + parts.shape[1:])
        kv, sums = self.run([PairScatter(self.nz, given, False), Sums(self.nz, grad, False)], "10" + "11" + "0" + "110" + "11110" + "11110")
        return kv.astype(f32), sums

    def scatter_heads_back(self, partial, sums):
        rows, shard = self.run([PlaneScatter(partial), DealBackTask(self.nz, sums)], "01")
        return rows, self.flat(shard)

    def finish(self, attn_grad, grad, gains):
        rows = attn_grad.shape[0] // self.blocks
        given = attn_grad.reshape(self.nz, 2, rows, attn_grad.shape[1])
        attn, shard, total = self.run(
            [
                PairScatter(self.nz, given, True),
                Sums(self.nz, grad, True),
                SumAll(gains.reshape(8, -1)),
            ],
            "01012" + "1121" + "0" + "1121" + "0" + "1121" + "0" + "1121",
        )
        return attn, self.flat(shard), total.reshape(gains.shape)


def causal_mask(rows):
    shape = (rows, rows)
    return lax.broadcasted_iota(jnp.int32, shape, 1) <= lax.broadcasted_iota(jnp.int32, shape, 0)


def forward_kernel(kinds, q_ref, kv_ref, out_ref, exact_ref, inv_ref, acc, total):
    step, last = pl.program_id(0), pl.num_programs(0) - 1
    heads, rows, dim = q_ref.shape
    kind = kinds[step]

    @pl.when(step == 0)
    def _():
        acc[...] = jnp.zeros_like(acc)
        total[...] = jnp.zeros_like(total)

    def work(own):
        for head in range(heads):
            raw = contract(q_ref[head], kv_ref[0, :, :dim], 1, 1)
            weights = jnp.exp(softcap * jnp.tanh(raw * (score_scale / softcap)))
            if own:
                weights = jnp.where(causal_mask(rows), weights, 0.0)
            total[head] += jnp.sum(weights, axis=-1, keepdims=True)
            acc[head] += contract(weights.astype(bf16), kv_ref[0, :, dim:], 1, 0)

    @pl.when(kind == 1)
    def _():
        work(False)

    @pl.when(kind == 2)
    def _():
        work(True)

    @pl.when(step == last)
    def _():
        for head in range(heads):
            inverse = 1.0 / total[head]
            value = acc[head] * inverse
            inv_ref[head] = inverse
            exact_ref[:, head * dim : (head + 1) * dim] = value
            out_ref[:, head * dim : (head + 1) * dim] = value.astype(bf16)


def whole2(step, kinds):
    return (0, 0)


def whole3(step, kinds):
    return (0, 0, 0)


def by_step(step, kinds):
    return (step, 0, 0)


def attend(kinds, queries, all_kv):
    heads, rows, dim = queries.shape
    return pl.pallas_call(
        forward_kernel,
        grid_spec=pltpu.PrefetchScalarGridSpec(
            num_scalar_prefetch=1,
            grid=(all_kv.shape[0],),
            in_specs=[
                pl.BlockSpec((heads, rows, dim), whole3),
                pl.BlockSpec((1, rows, 2 * dim), by_step),
            ],
            out_specs=[
                pl.BlockSpec((rows, heads * dim), whole2),
                pl.BlockSpec((rows, heads * dim), whole2),
                pl.BlockSpec((heads, rows, 1), whole3),
            ],
            scratch_shapes=[
                pltpu.VMEM((heads, rows, dim), f32),
                pltpu.VMEM((heads, rows, 1), f32),
            ],
        ),
        out_shape=[
            jax.ShapeDtypeStruct((rows, heads * dim), bf16),
            jax.ShapeDtypeStruct((rows, heads * dim), f32),
            jax.ShapeDtypeStruct((heads, rows, 1), f32),
        ],
        compiler_params=pltpu.CompilerParams(vmem_limit_bytes=40 * 2**20),
        cost_estimate=pl.CostEstimate(
            flops=3 * 4 * heads * rows * rows * dim,
            bytes_accessed=8 * rows * dim * heads,
            transcendentals=6 * heads * rows * rows,
        ),
    )(kinds, queries, all_kv)


def backward_kernel(kinds, q_ref, kv_ref, up_ref, exact_ref, inv_ref, dq_ref, dkv_ref):
    step = pl.program_id(0)
    heads, rows, dim = q_ref.shape
    kind = kinds[step]

    @pl.when(step == 0)
    def _():
        dq_ref[...] = jnp.zeros_like(dq_ref)

    def work(own):
        dk = jnp.zeros((rows, dim), f32)
        dv = jnp.zeros((rows, dim), f32)
        for head in range(heads):
            columns = slice(head * dim, (head + 1) * dim)
            up = up_ref[:, columns]
            delta = jnp.sum(up.astype(f32) * exact_ref[:, columns], axis=-1, keepdims=True)
            raw = contract(q_ref[head], kv_ref[0, :, :dim], 1, 1)
            bounded = jnp.tanh(raw * (score_scale / softcap))
            probs = jnp.exp(softcap * bounded) * inv_ref[head]
            if own:
                probs = jnp.where(causal_mask(rows), probs, 0.0)
            d_probs = contract(up, kv_ref[0, :, dim:], 1, 1)
            d_raw = probs * (d_probs - delta) * ((1.0 - bounded * bounded) * score_scale)
            d_raw = d_raw.astype(bf16)
            dq_ref[head] += contract(d_raw, kv_ref[0, :, :dim], 1, 0)
            dk += contract(d_raw, q_ref[head], 0, 0)
            dv += contract(probs.astype(bf16), up, 0, 0)
        dkv_ref[0, :, :dim] = dk.astype(bf16)
        dkv_ref[0, :, dim:] = dv.astype(bf16)

    @pl.when(kind == 1)
    def _():
        work(False)

    @pl.when(kind == 0)
    def _():
        dkv_ref[...] = jnp.zeros_like(dkv_ref)

    @pl.when(kind == 2)
    def _():
        work(True)


def attend_back(kinds, queries, all_kv, upstream, exact, inverse):
    heads, rows, dim = queries.shape
    blocks = all_kv.shape[0]
    return pl.pallas_call(
        backward_kernel,
        grid_spec=pltpu.PrefetchScalarGridSpec(
            num_scalar_prefetch=1,
            grid=(blocks,),
            in_specs=[
                pl.BlockSpec((heads, rows, dim), whole3),
                pl.BlockSpec((1, rows, 2 * dim), by_step),
                pl.BlockSpec((rows, heads * dim), whole2),
                pl.BlockSpec((rows, heads * dim), whole2),
                pl.BlockSpec((heads, rows, 1), whole3),
            ],
            out_specs=[
                pl.BlockSpec((heads, rows, dim), whole3),
                pl.BlockSpec((1, rows, 2 * dim), by_step),
            ],
        ),
        out_shape=[
            jax.ShapeDtypeStruct((heads, rows, dim), f32),
            jax.ShapeDtypeStruct((blocks, rows, 2 * dim), bf16),
        ],
        compiler_params=pltpu.CompilerParams(vmem_limit_bytes=40 * 2**20),
        cost_estimate=pl.CostEstimate(
            flops=3 * 10 * heads * rows * rows * dim,
            bytes_accessed=16 * rows * dim * heads,
            transcendentals=6 * heads * rows * rows,
        ),
    )(kinds, queries, all_kv, upstream, exact, inverse)


def on_device(
    tokens,
    cotangent,
    norm_attn_in,
    w_query,
    w_key,
    w_value,
    w_out,
    norm_attn_out,
    norm_ff_in,
    w_gate,
    w_up,
    w_down,
    norm_ff_out,
    block_group,
    block_role,
):
    at = Place()
    own_rows, depth = tokens.shape
    shard_rows, units = w_gate.shape
    regular = at.nz == 4 and shard_rows % 32 == 0 and (2 * units // at.nz) % 128 == 0
    comm = Kernels(at) if regular else Permutes(at)
    blocks = at.blocks
    block_len = own_rows * lax.axis_size("heads")
    prompt_len = blocks // 4
    block_ids = jnp.arange(blocks, dtype=jnp.int32)
    my_group = jnp.sum(jnp.where(block_ids == comm.block, block_group, 0))
    my_role = jnp.sum(jnp.where(block_ids == comm.block, block_role, 0))
    positions = jnp.where(
        my_role < prompt_len, my_role * block_len, prompt_len * block_len
    ) + jnp.arange(block_len, dtype=jnp.int32)
    cosine, sine_table = rope_tables(positions)
    prompt = (block_group == my_group) & (block_role < prompt_len) & (block_role < my_role)
    kinds = jnp.where(block_ids == comm.block, 2, prompt.astype(jnp.int32)).astype(jnp.int32)

    token_f32 = tokens.astype(f32)
    heads_width = w_query.shape[1]
    qkv_width = heads_width + 2 * HEAD_DIM
    attn_shard = jnp.concatenate([w_query, w_key, w_value, w_out.T], axis=1)
    normed_one, attn_full, gate_full, up_full = comm.start(
        normalize(token_f32, norm_attn_in).astype(bf16), attn_shard, w_gate, w_up
    )
    qkv_full, out_full = attn_full[:, :qkv_width], attn_full[:, qkv_width:]
    qkv_lin = jnp.dot(normed_one, qkv_full, preferred_element_type=f32)
    queries = jnp.stack(
        [
            rotate(qkv_lin[:, :HEAD_DIM], cosine, sine_table),
            rotate(qkv_lin[:, HEAD_DIM:heads_width], cosine, sine_table),
        ]
    ).astype(bf16)
    own_kv = jnp.concatenate(
        [
            rotate(qkv_lin[:, heads_width : heads_width + HEAD_DIM], cosine, sine_table),
            qkv_lin[:, heads_width + HEAD_DIM :],
        ],
        axis=1,
    ).astype(bf16)
    all_kv = comm.gather_kv(own_kv)
    attn_rows, attended, inverse = attend(kinds, queries, all_kv)
    attn_proj, down_pieces = comm.scatter_heads_deal(
        contract(attn_rows, out_full, 1, 1).astype(bf16), w_down.T
    )
    middle = token_f32 + normalize(attn_proj, norm_attn_out)

    normed_two, down_full = comm.gather_z_copy(
        normalize(middle, norm_ff_in).astype(bf16), down_pieces
    )
    gate_lin = jnp.dot(normed_two, gate_full, preferred_element_type=f32)
    up_lin = jnp.dot(normed_two, up_full, preferred_element_type=f32)
    hidden = (jax.nn.gelu(gate_lin, approximate=True) * up_lin).astype(bf16)
    ff_proj = comm.scatter_z(contract(hidden, down_full, 1, 1).astype(bf16))
    layer_out = middle + normalize(ff_proj, norm_ff_out)

    upstream = cotangent.astype(f32)
    d_ff, grad_ff_out = normalize_back(ff_proj, norm_ff_out, upstream)
    d_ff_rows = comm.gather_z(d_ff.astype(bf16))
    d_hidden = contract(d_ff_rows, down_full, 1, 0)
    _, glu_back = jax.vjp(
        lambda gate_in, up_in: jax.nn.gelu(gate_in, approximate=True) * up_in, gate_lin, up_lin
    )
    d_gate, d_up = glu_back(d_hidden)
    d_gate = d_gate.astype(bf16)
    d_up = d_up.astype(bf16)
    d_partial = contract(d_gate, gate_full, 1, 1) + contract(d_up, up_full, 1, 1)
    d_normed_two, down_sums = comm.scatter_z_sums(
        d_partial.astype(bf16), contract(d_ff_rows, hidden, 0, 0).astype(bf16)
    )

    d_middle_part, grad_ff_in = normalize_back(middle, norm_ff_in, d_normed_two)
    d_middle = upstream + d_middle_part
    d_proj, grad_attn_out = normalize_back(attn_proj, norm_attn_out, d_middle)
    d_proj_rows, grad_down = comm.gather_heads_back(d_proj.astype(bf16), down_sums)
    d_attended = contract(d_proj_rows, out_full, 1, 0).astype(bf16)
    d_query, d_kv_parts = attend_back(kinds, queries, all_kv, d_attended, attended, inverse)
    d_kv, gate_sums = comm.scatter_kv_sums(
        d_kv_parts, contract(normed_two, d_gate, 0, 0).astype(bf16)
    )
    d_qkv_lin = jnp.concatenate(
        [
            rotate(d_query[0], cosine, -sine_table),
            rotate(d_query[1], cosine, -sine_table),
            rotate(d_kv[:, :HEAD_DIM], cosine, -sine_table),
            d_kv[:, HEAD_DIM:],
        ],
        axis=1,
    ).astype(bf16)
    d_normed_one, grad_gate = comm.scatter_heads_back(
        contract(d_qkv_lin, qkv_full, 1, 1).astype(bf16), gate_sums
    )
    d_token_part, grad_attn_in = normalize_back(token_f32, norm_attn_in, d_normed_one)
    input_grad = (d_middle + d_token_part).astype(bf16)
    grad_attn, grad_up, gains = comm.finish(
        jnp.concatenate(
            [contract(normed_one, d_qkv_lin, 0, 0), contract(d_proj_rows, attn_rows, 0, 0)], axis=1
        ).astype(bf16),
        contract(normed_two, d_up, 0, 0).astype(bf16),
        jnp.stack([grad_attn_in, grad_attn_out, grad_ff_in, grad_ff_out]),
    )
    grad_attn, grad_gate, grad_up = [g.astype(f32) for g in (grad_attn, grad_gate, grad_up)]
    return (
        layer_out.astype(bf16),
        input_grad,
        gains[0],
        grad_attn[:, :heads_width],
        grad_attn[:, heads_width : heads_width + HEAD_DIM],
        grad_attn[:, heads_width + HEAD_DIM : qkv_width],
        grad_attn[:, qkv_width:].T,
        gains[1],
        gains[2],
        grad_gate,
        grad_up,
        grad_down.astype(f32).T,
        gains[3],
    )


def solution(mesh):
    rows, weight, turned = P(("blk", "heads"), None), P("blk", "heads"), P("heads", "blk")
    return jax.shard_map(
        on_device,
        mesh=mesh,
        in_specs=(
            rows, rows, P(), weight, weight, weight, turned, P(), P(), weight, weight, turned,
            P(), P(), P(),
        ),
        out_specs=(
            rows, rows, P(), weight, weight, weight, turned, P(), P(), weight, weight, turned, P(),
        ),
        check_vma=False,
    )
```

```python
import math

import jax
import jax.numpy as jnp
from jax import lax
from jax.experimental import pallas as pl
from jax.experimental.pallas import tpu as pltpu
from jax.sharding import PartitionSpec as P

HEAD_DIM = 256


softcap = 50.0
epsilon = 1e-06
score_scale = HEAD_DIM ** (-0.5)
bf16 = jnp.bfloat16
f32 = jnp.float32


def contract(left_side, right_side, left_dim, right_dim):
    return lax.dot_general(
        left_side,
        right_side,
        (((left_dim,), (right_dim,)), ((), ())),
        preferred_element_type=f32,
    )


def factor_of(values):
    return lax.rsqrt(jnp.mean(values * values, axis=-1, keepdims=True) + epsilon)


def normalize(values, weight_gain):
    return values * factor_of(values) * (1.0 + weight_gain)


def normalize_back(values, weight_gain, upstream):
    factor = factor_of(values)
    unit = values * factor
    scaled = upstream * (1.0 + weight_gain)
    inner = jnp.mean(scaled * unit, axis=-1, keepdims=True)
    return (scaled - unit * inner) * factor, jnp.sum(upstream * unit, axis=0)


def rope_tables(positions):
    half_dim = HEAD_DIM // 2
    frequency = jnp.exp(
        jnp.arange(half_dim, dtype=f32) * (-2.0 * math.log(10000.0) / HEAD_DIM)
    )
    angles = positions.astype(f32)[:, None] * frequency[None, :]
    return (jnp.cos(angles), jnp.sin(angles))


def rotate(tensor, cosine, sine_table):
    half_dim = HEAD_DIM // 2
    first_half = tensor[..., :half_dim]
    second_half = tensor[..., half_dim:]
    return jnp.concatenate(
        [
            first_half * cosine - second_half * sine_table,
            second_half * cosine + first_half * sine_table,
        ],
        axis=-1,
    )


def swap_core(v):
    return lax.ppermute(v, "heads", [(i, i ^ 1) for i in range(4)])


def swap_y(v):
    return lax.ppermute(v, "heads", [(i, i ^ 2) for i in range(4)])


def swap_x(v):
    blocks = lax.axis_size("blk")
    return lax.ppermute(v, "blk", [(i, i ^ 1) for i in range(blocks)])


def pair_up(own, other, place, axis):
    first = jnp.where(place == 0, own, other)
    second = jnp.where(place == 0, other, own)
    return jnp.concatenate([first, second], axis=axis)


def shift_z(v, step, senders):
    pairs = []
    for z in senders:
        for x in range(2):
            pairs.append((2 * z + x, 2 * (z + step) + x))
    return lax.ppermute(v, "blk", pairs)


class Place:
    def __init__(self):
        self.blocks = lax.axis_size("blk")
        self.nz = self.blocks // 2
        self.b = lax.axis_index("blk")
        self.h = lax.axis_index("heads")
        self.z, self.x = self.b // 2, self.b % 2
        self.y, self.c = self.h // 2, self.h % 2


def gather_z(at, unit):
    nz = at.nz
    up, down = unit, unit
    ups, downs = [None], [None]
    for s in range(1, nz):
        up = shift_z(up, 1, range(s - 1, nz - 1))
        down = shift_z(down, -1, range(1, nz - s + 1))
        ups.append(up)
        downs.append(down)
    return [unit] + [jnp.where(at.z >= s, ups[s], downs[nz - s]) for s in range(1, nz)]


def scatter_z(at, parts):
    nz = at.nz
    up = down = None
    for t in range(1, nz):
        k = nz - t
        send_up = parts[nz - k].astype(f32)
        send_down = parts[k].astype(f32)
        if up is not None:
            send_up = send_up + up.astype(f32)
            send_down = send_down + down.astype(f32)
        up = shift_z(send_up.astype(bf16), 1, range(0, nz - k))
        down = shift_z(send_down.astype(bf16), -1, range(k, nz))
    return parts[0].astype(f32) + (up.astype(f32) + down.astype(f32))


def deal_z(at, parts):
    nz = at.nz
    got = [parts[0]]
    for s in range(1, nz):
        up = shift_z(parts[nz - s], s, range(0, nz - s))
        down = shift_z(parts[nz - s], s - nz, range(nz - s, nz))
        got.append(jnp.where(at.z >= s, up, down))
    return got


def turn(at, whole):
    return [
        lax.dynamic_index_in_dim(whole, (at.z - s) % at.nz, 0, keepdims=False)
        for s in range(at.nz)
    ]


def unturn(at, parts):
    whole = jnp.zeros((at.nz,) + parts[0].shape, parts[0].dtype)
    for s, part in enumerate(parts):
        whole = lax.dynamic_update_index_in_dim(whole, part, (at.z - s) % at.nz, 0)
    return whole


def gather_zx(at, unit):
    got = []
    for part in gather_z(at, unit):
        got.append(pair_up(part[None], swap_x(part)[None], at.x, 0))
    return unturn(at, got)


def gather_xz(at, unit):
    both = pair_up(unit[None], swap_x(unit)[None], at.x, 0)
    return unturn(at, gather_z(at, both))


def pick(pair, place):
    mine = jnp.where(place == 0, pair[0], pair[1])
    other = jnp.where(place == 0, pair[1], pair[0])
    return mine, other


def scatter_zx(at, parts):
    total = scatter_z(at, parts)
    mine, other = pick(total, at.x)
    return mine + swap_x(other.astype(bf16)).astype(f32)


def scatter_xz(at, parts):
    sums = []
    for part in parts:
        mine, other = pick(part, at.x)
        sums.append(mine.astype(f32) + swap_x(other.astype(bf16)).astype(f32))
    return scatter_z(at, sums)


def rows_to_block(at, own):
    both = pair_up(own, swap_core(own), at.c, 0)
    pair = pair_up(both[None], swap_y(both)[None], at.y, 0)
    return pair.reshape(4 * own.shape[0], own.shape[1])


def rows_from_block(at, partial_sum):
    rows = partial_sum.shape[0] // 4
    parts = partial_sum.reshape(2, 2, rows, partial_sum.shape[1])
    mine, other = pick(parts.swapaxes(0, 1), at.c)
    total = mine + swap_core(other.astype(bf16)).astype(f32)
    mine, other = pick(total, at.y)
    return mine + swap_y(other.astype(bf16)).astype(f32)


def spread_weight(at, shard):
    rows, units = shard.shape
    half = rows // 2
    keep, send = pick(shard.reshape(2, half, units), at.c)
    wide = pair_up(keep[None], swap_core(send)[None], at.c, 0)
    quarter = 2 * units // at.nz
    per_core = units // quarter
    pieces = wide.reshape(2, half, per_core, quarter).transpose(0, 2, 1, 3)
    pieces = pieces.reshape(at.nz, half, quarter)
    got = unturn(at, deal_z(at, turn(at, pieces)))
    got = pair_up(got[:, None], swap_x(got)[:, None], at.x, 1)
    got = pair_up(got, swap_y(got), at.y, 3)
    got = pair_up(got[:, :, None], swap_core(got)[:, :, None], at.c, 2)
    return got.reshape(at.blocks * rows, 2 * quarter)


def collect_weight(at, grad):
    depth, width = grad.shape
    half, quarter = depth // (2 * at.blocks), width // 2
    parts = grad.reshape(at.nz, 2, 2, half, width)
    mine, other = pick(parts.transpose(2, 0, 1, 3, 4), at.c)
    total = mine + swap_core(other.astype(bf16)).astype(f32)
    mine, other = pick((total[..., :quarter], total[..., quarter:]), at.y)
    total = mine + swap_y(other.astype(bf16)).astype(f32)
    mine, other = pick((total[:, 0], total[:, 1]), at.x)
    total = mine + swap_x(other.astype(bf16)).astype(f32)
    got = unturn(at, deal_z(at, turn(at, total.astype(bf16))))
    per_core = at.nz // 2
    wide = got.reshape(2, per_core, half, quarter).transpose(0, 2, 1, 3)
    wide = wide.reshape(2, half, per_core * quarter)
    mine, other = pick(wide, at.c)
    rows = pair_up(mine, swap_core(other), at.c, 0)
    return rows.astype(f32)


def sum_all(at, values):
    total = values
    for bit in (1, 2):
        total = total + lax.ppermute(total, "heads", [(i, i ^ bit) for i in range(4)])
    bit = 1
    while bit < at.blocks:
        total = total + lax.ppermute(total, "blk", [(i, i ^ bit) for i in range(at.blocks)])
        bit *= 2
    return total


class Permutes:
    def __init__(self, at):
        self.at = at
        self.block, self.blocks, self.nz = at.b, at.blocks, at.nz

    def split(self, whole):
        return turn(self.at, whole.reshape((self.nz, whole.shape[0] // self.nz) + whole.shape[1:]))

    def start(self, own, attn_shard, gate, up, down):
        at = self.at
        attn_full = gather_zx(at, attn_shard).reshape(own.shape[1], -1)
        weights = [spread_weight(at, w) for w in (gate, up, down)]
        return [rows_to_block(at, own), attn_full] + weights

    def gather_kv(self, own, down):
        return gather_zx(self.at, own).reshape((self.blocks,) + own.shape), down

    def scatter_heads(self, partial):
        return rows_from_block(self.at, partial)

    def gather_z(self, own):
        whole = unturn(self.at, gather_z(self.at, own))
        return whole.reshape(-1, own.shape[1])

    def scatter_z(self, partial):
        return scatter_z(self.at, self.split(partial))

    def feed_forward(self, own, cotangent, gain, gate, up, down):
        normed = self.gather_z(own)
        gate_lin = jnp.dot(normed, gate, preferred_element_type=f32)
        up_lin = jnp.dot(normed, up, preferred_element_type=f32)
        hidden = (jax.nn.gelu(gate_lin, approximate=True) * up_lin).astype(bf16)
        ff_proj = self.scatter_z(contract(hidden, down, 1, 1).astype(bf16))
        d_ff, _ = normalize_back(ff_proj, gain, cotangent.astype(f32))
        d_ff_rows = self.gather_z(d_ff.astype(bf16))
        d_hidden = contract(d_ff_rows, down, 1, 0)
        _, glu_back = jax.vjp(
            lambda gate_in, up_in: jax.nn.gelu(gate_in, approximate=True) * up_in, gate_lin, up_lin
        )
        d_gate, d_up = [d.astype(bf16) for d in glu_back(d_hidden)]
        d_partial = contract(d_gate, gate, 1, 1) + contract(d_up, up, 1, 1)
        d_normed = self.scatter_z(d_partial.astype(bf16))
        grads = [
            contract(left, right, 0, 0).astype(bf16)
            for left, right in ((normed, d_gate), (normed, d_up), (d_ff_rows, hidden))
        ]
        return [ff_proj, d_normed] + grads

    def gather_heads(self, own):
        return rows_to_block(self.at, own)

    def scatter_pairs(self, grad):
        rows = grad.shape[0] // self.blocks
        return scatter_xz(self.at, self.split(grad.reshape(self.blocks, rows, -1)))

    def scatter_kv_sums(self, parts, out_grad, grad):
        kv = scatter_xz(self.at, self.split(parts))
        return kv, self.scatter_pairs(out_grad), collect_weight(self.at, grad)

    def scatter_heads_back(self, partial, sums):
        return rows_from_block(self.at, partial), sums

    def finish(self, qkv_grad, gate_grad, up_grad, gains):
        gate, up = collect_weight(self.at, gate_grad), collect_weight(self.at, up_grad)
        return self.scatter_pairs(qkv_grad), gate, up, sum_all(self.at, gains)


MESH = pl.DeviceIdType.MESH
DMA = pltpu.SemaphoreType.DMA
anywhere = pl.BlockSpec(memory_space=pl.ANY)
in_vmem = pl.BlockSpec(memory_space=pltpu.VMEM)


def remote(src, dst, send_sem, recv_sem, target):
    return pltpu.make_async_remote_copy(
        src_ref=src,
        dst_ref=dst,
        send_sem=send_sem,
        recv_sem=recv_sem,
        device_id=target,
        device_id_type=MESH,
    )


def flip(bit, by):
    return 1 - bit if by else bit


def exclusive_or(z, i):
    low, high = lax.rem(z, 2), lax.rem(z // 2, 2)
    rest = z - 2 * high - low
    return rest + 2 * flip(high, i // 2) + flip(low, i % 2)


class Spot:
    def __init__(self, nz):
        self.nz = nz
        h, b = lax.axis_index("heads"), lax.axis_index("blk")
        self.y, self.c = h // 2, h % 2
        self.z, self.x = b // 2, b % 2

    def device(self, z=None, x=None, y=None, c=None):
        z = self.z if z is None else z
        x = self.x if x is None else x
        y = self.y if y is None else y
        c = self.c if c is None else c
        return (2 * y + c, 2 * z + x)

    def partner(self):
        return self.device(c=1 - self.c)

    def greet(self):
        found = []
        for dx, dy, dc in [(0, 0, 1), (1, 0, 0), (1, 0, 1), (0, 1, 0), (0, 1, 1), (1, 1, 0), (1, 1, 1)]:
            found.append(self.device(x=flip(self.x, dx), y=flip(self.y, dy), c=flip(self.c, dc)))
        for s in range(1, self.nz):
            z = lax.rem(self.z + s, self.nz)
            found += [self.device(z=z), self.device(z=z, c=1 - self.c)]
        barrier = pltpu.get_barrier_semaphore()
        for device in found:
            pl.semaphore_signal(barrier, inc=1, device_id=device, device_id_type=MESH)
        pl.semaphore_wait(barrier, len(found))


def add_rows(out, left, right, step=16):
    rows = left.shape[0]

    @pl.loop(0, rows // step)
    def _(i):
        at = pl.ds(pl.multiple_of(i * step, step), step)
        out[at, :] = (left[at, :].astype(f32) + right[at, :].astype(f32)).astype(out.dtype)


class LineGather:
    def __init__(self, spot, entry, send, recv):
        self.spot, self.entry = spot, entry
        self.send, self.recv = send, recv

    def copies(self, s):
        p, nz = self.spot, self.spot.nz
        up_at = lax.rem(p.z - s + 1 + nz, nz)
        down_at = lax.rem(p.z + s - 1, nz)
        up = remote(
            self.entry(up_at),
            self.entry(up_at),
            self.send.at[0, s],
            self.recv.at[0, s],
            p.device(z=lax.rem(p.z + 1, nz)),
        )
        down = remote(
            self.entry(down_at),
            self.entry(down_at),
            self.send.at[1, s],
            self.recv.at[1, s],
            p.device(z=lax.rem(p.z + nz - 1, nz)),
        )
        return (
            ((p.z >= s - 1) & (p.z < nz - 1), p.z >= s, up),
            ((p.z <= nz - s) & (p.z > 0), p.z <= nz - 1 - s, down),
        )

    def start(self, s):
        for sends, _, copy in self.copies(s):
            pl.when(sends)(copy.start)

    def arrive(self, s):
        for _, receives, copy in self.copies(s):
            pl.when(receives)(copy.wait_recv)

    def finish(self):
        for s in range(1, self.spot.nz):
            for sends, _, copy in self.copies(s):
                pl.when(sends)(copy.wait_send)

    def newest(self, s):
        p, nz = self.spot, self.spot.nz
        return (
            (p.z >= s, lax.rem(p.z - s + nz, nz)),
            (p.z <= nz - 1 - s, lax.rem(p.z + s, nz)),
        )


class LineScatter:
    def __init__(self, spot, parts, up, down, send, recv):
        self.spot, self.parts, self.up, self.down = spot, parts, up, down
        self.send, self.recv = send, recv

    def copies(self, t):
        p, nz = self.spot, self.spot.nz
        k = nz - t
        up = remote(
            self.parts(lax.rem(p.z + k, nz)),
            self.up.at[t - 1],
            self.send.at[0, t],
            self.recv.at[0, t],
            p.device(z=lax.rem(p.z + 1, nz)),
        )
        down = remote(
            self.parts(lax.rem(p.z - k + nz, nz)),
            self.down.at[t - 1],
            self.send.at[1, t],
            self.recv.at[1, t],
            p.device(z=lax.rem(p.z + nz - 1, nz)),
        )
        return (
            (p.z <= nz - 1 - k, (p.z >= 1) & (p.z <= t), up),
            (p.z >= k, (p.z <= nz - 2) & (p.z >= nz - 1 - t), down),
        )

    def start(self, t):
        for sends, _, copy in self.copies(t):
            pl.when(sends)(copy.start)

    def arrive(self, t):
        p, nz = self.spot, self.spot.nz
        k = nz - t
        for way, (_, receives, copy) in enumerate(self.copies(t)):

            @pl.when(receives)
            def _(way=way, copy=copy):
                copy.wait_recv()
                if t < nz - 1:
                    index = lax.rem(p.z + k - 1, nz) if way == 0 else lax.rem(p.z - k + 1 + nz, nz)
                    came = (self.up if way == 0 else self.down).at[t - 1]
                    add_rows(self.parts(index), self.parts(index), came)

    def finish(self):
        for t in range(1, self.spot.nz):
            for sends, _, copy in self.copies(t):
                pl.when(sends)(copy.wait_send)

    def total(self, out, step=16):
        p, last = self.spot, self.spot.nz - 2
        mine = self.parts(p.z)
        inner = (p.z > 0) & (p.z < p.nz - 1)

        @pl.when(p.z == 0)
        def _():
            add_rows(out, mine, self.down.at[last], step)

        @pl.when(p.z == p.nz - 1)
        def _():
            add_rows(out, mine, self.up.at[last], step)

        @pl.when(inner)
        def _():
            @pl.loop(0, out.shape[0] // step)
            def _(i):
                at = pl.ds(pl.multiple_of(i * step, step), step)
                sides = self.up[last, at, :].astype(f32) + self.down[last, at, :].astype(f32)
                out[at, :] = (mine[at, :].astype(f32) + sides).astype(out.dtype)


class Task:
    ins = ()
    outs = ()
    scratch = ()
    vmem_ins = ()
    vmem_outs = ()
    spare = 5

    def steps(self, p, ins, outs, scratch):
        raise NotImplementedError


class PlaneGather(Task):
    vmem_ins = (0,)
    vmem_outs = (0,)

    def __init__(self, own):
        self.ins = (own,)
        self.outs = (jax.ShapeDtypeStruct((4,) + own.shape, bf16),)
        self.scratch = (DMA((4,)), DMA((4,)), DMA)

    def steps(self, p, ins, outs, scratch):
        (own,), (whole,), (send, recv, local) = ins, outs, scratch
        part = 2 * p.y + p.c
        keep = pltpu.make_async_copy(own, whole.at[part], local)
        copies = []
        for i, (dx, dy) in enumerate([(1, 0), (0, 1), (1, 1), (0, 0)]):
            target = p.device(x=flip(p.x, dx), y=flip(p.y, dy), c=p.x)
            copies.append(remote(own, whole.at[part], send.at[i], recv.at[part], target))
        *away, home = copies
        for copy in away:
            copy.start()
        pl.when(p.c == p.x)(keep.start)
        pl.when(p.c != p.x)(home.start)
        yield
        for copy in away:
            copy.wait_send()
        pl.when(p.c == p.x)(keep.wait)
        pl.when(p.c != p.x)(home.wait_send)
        for slot in range(4):
            came = remote(own, whole.at[slot], send.at[0], recv.at[slot], p.partner())
            mine = (p.c == p.x) & (part == slot)
            pl.when(jnp.logical_not(mine))(came.wait_recv)


class PlaneScatter(Task):
    vmem_ins = (0,)
    vmem_outs = (0,)

    def __init__(self, partial):
        rows, depth = partial.shape[0] // 4, partial.shape[1]
        self.ins = (partial.reshape(4, rows, depth),)
        self.outs = (jax.ShapeDtypeStruct((rows, depth), f32),)
        self.scratch = (pltpu.VMEM((4, rows, depth), bf16), DMA((4,)), DMA((4,)))

    def steps(self, p, ins, outs, scratch):
        (parts,), (out,), (came, send, recv) = ins, outs, scratch
        head, ours = 2 * p.y + p.x, 2 * p.y + p.c

        def copy_to(part):
            target = p.device(x=p.c, y=part // 2, c=part % 2)
            return remote(parts.at[part], came.at[head], send.at[part], recv.at[head], target)

        for part in range(4):
            here = (p.x == p.c) & (part == ours)
            pl.when(jnp.logical_not(here))(copy_to(part).start)
        yield
        for part in range(4):
            here = (p.x == p.c) & (part == ours)
            pl.when(jnp.logical_not(here))(copy_to(part).wait_send)
            arrived = remote(parts.at[part], came.at[part], send.at[part], recv.at[part], p.partner())
            mine = (p.x == p.c) & (part == head)
            pl.when(jnp.logical_not(mine))(arrived.wait_recv)

        @pl.when(p.x == p.c)
        def _():
            came[head] = parts[ours]

        @pl.loop(0, out.shape[0] // 16)
        def _(i):
            at = pl.ds(pl.multiple_of(i * 16, 16), 16)
            low = came[0, at, :].astype(f32) + came[1, at, :].astype(f32)
            out[at, :] = low + (came[2, at, :].astype(f32) + came[3, at, :].astype(f32))


class PairGather(Task):
    vmem_ins = (0,)
    vmem_outs = (0,)

    def __init__(self, nz, own, trade):
        self.trade = trade
        self.ins = (own,)
        self.outs = (jax.ShapeDtypeStruct((nz, 2) + own.shape, bf16),)
        self.scratch = (DMA((2, nz)), DMA((2, nz)), DMA((nz,)), DMA((nz,)), DMA, DMA, DMA)

    def steps(self, p, ins, outs, scratch):
        (own,), (full,), (send, recv, x_send, x_recv, t_send, t_recv, local) = ins, outs, scratch
        nz = p.nz
        keep = pltpu.make_async_copy(own, full.at[p.z, p.c], local)
        line = LineGather(p, lambda z: full.at[z, p.c], send, recv)

        def across(z):
            here = full.at[z, p.c]
            return remote(here, here, x_send.at[z], x_recv.at[z], p.partner())

        if self.trade:
            same = p.c == p.x
            move = remote(own, full.at[p.z, p.x], t_send, t_recv, p.device(x=1 - p.x, c=1 - p.c))
            pl.when(same)(keep.start)
            pl.when(jnp.logical_not(same))(move.start)
            yield
            pl.when(same)(keep.wait)
            pl.when(jnp.logical_not(same))(move.wait_recv)
        else:
            keep.start()
            keep.wait()
        line.start(1)
        across(p.z).start()
        yield
        for s in range(1, nz):
            line.arrive(s)
            if s < nz - 1:
                line.start(s + 1)
            for came, z in line.newest(s):
                pl.when(came)(across(z).start)
            yield
        line.finish()
        if self.trade:
            pl.when(jnp.logical_not(same))(move.wait_send)
        for z in range(nz):
            across(z).wait()


class ZGather(Task):
    vmem_ins = (0,)
    vmem_outs = (0,)

    def __init__(self, nz, own):
        self.ins = (own,)
        self.outs = (jax.ShapeDtypeStruct((nz,) + own.shape, bf16),)
        self.scratch = (DMA((2, nz)), DMA((2, nz)), DMA)

    def steps(self, p, ins, outs, scratch):
        (own,), (full,), (send, recv, local) = ins, outs, scratch
        line = LineGather(p, lambda z: full.at[z], send, recv)
        keep = pltpu.make_async_copy(own, full.at[p.z], local)
        keep.start()
        keep.wait()
        line.start(1)
        yield
        for s in range(1, p.nz):
            line.arrive(s)
            if s < p.nz - 1:
                line.start(s + 1)
            yield
        line.finish()


class ZScatter(Task):
    vmem_outs = (0,)

    def __init__(self, nz, partial):
        rows, depth = partial.shape[0] // nz, partial.shape[1]
        self.ins = (partial.reshape(nz, rows, depth),)
        self.outs = (jax.ShapeDtypeStruct((rows, depth), f32),)
        line = pltpu.VMEM((nz - 1, rows, depth), bf16)
        self.scratch = (
            pltpu.VMEM((nz, rows, depth), bf16), line, line, DMA((2, nz)), DMA((2, nz)), DMA
        )

    def steps(self, p, ins, outs, scratch):
        (given,), (out,), (parts, up, down, send, recv, local) = ins, outs, scratch
        bring = pltpu.make_async_copy(given, parts, local)
        bring.start()
        bring.wait()
        line = LineScatter(p, lambda z: parts.at[z], up, down, send, recv)
        line.start(1)
        yield
        for t in range(1, p.nz):
            line.arrive(t)
            if t < p.nz - 1:
                line.start(t + 1)
            yield
        line.total(out)
        line.finish()


class PairScatter(Task):
    vmem_outs = (0,)

    def __init__(self, nz, given, trade):
        _, _, rows, width = given.shape
        self.trade = trade
        self.ins = (given,)
        self.outs = (jax.ShapeDtypeStruct((rows, width), bf16),)
        whole = pltpu.VMEM((nz, rows, width), bf16)
        line = pltpu.VMEM((nz - 1, rows, width), bf16)
        self.scratch = (
            whole, whole, line, line,
            DMA((nz,)), DMA((nz,)), DMA((2, nz)), DMA((2, nz)), DMA((nz,)), DMA, DMA, DMA,
        )

    def steps(self, p, ins, outs, scratch):
        (given,), (out,) = ins, outs
        parts, came, up, down, x_send, x_recv, send, recv, local, b_send, b_recv, b_local = scratch
        nz = p.nz
        order = [exclusive_or(p.z, i) for i in (3, 2, 1, 0)]

        def away(z):
            return remote(given.at[z, 1 - p.c], came.at[z], x_send.at[z], x_recv.at[z], p.partner())

        def bring(z):
            return pltpu.make_async_copy(given.at[z, p.c], parts.at[z], local.at[z])

        for z in order:
            away(z).start()
            bring(z).start()
        yield
        for z in order:
            away(z).wait_recv()
            bring(z).wait()
            add_rows(parts.at[z], parts.at[z], came.at[z])
        line = LineScatter(p, lambda z: parts.at[z], up, down, send, recv)
        line.start(1)
        yield
        for t in range(1, nz):
            line.arrive(t)
            if t < nz - 1:
                line.start(t + 1)
            yield
        if not self.trade:
            line.total(out)
        else:
            line.total(came.at[0])
            same = p.c == p.x
            back = remote(came.at[0], out, b_send, b_recv, p.device(x=1 - p.x, c=1 - p.c))
            keep = pltpu.make_async_copy(came.at[0], out, b_local)
            pl.when(same)(keep.start)
            pl.when(jnp.logical_not(same))(back.start)
            yield
            pl.when(same)(keep.wait)
            pl.when(jnp.logical_not(same))(back.wait)
        for z in order:
            away(z).wait_send()
        line.finish()


class Deal:
    def __init__(self, p, shard, place, quarter, send, recv):
        self.p, self.shard, self.place, self.quarter = p, shard, place, quarter
        self.send, self.recv = send, recv
        self.per_core = p.nz // 2

    def piece(self, piece, half):
        columns = pl.ds(piece * self.quarter, self.quarter)
        return self.shard.at[half, :, columns]

    def away(self, piece, half):
        p = self.p
        z = p.c * self.per_core + piece
        return z, remote(
            self.piece(piece, half),
            self.place(p.z, half),
            self.send.at[2 * piece + half],
            self.recv.at[p.z],
            p.device(z=z, c=half),
        )

    def local(self, piece):
        p = self.p
        columns = pl.ds(piece * self.quarter, self.quarter)
        return pltpu.make_async_copy(
            self.shard.at[p.c, :, columns], self.place(p.z, p.c), self.recv.at[p.z]
        )

    def start(self, in_plane):
        p = self.p
        for piece in range(self.per_core):
            for half in range(2):
                z, copy = self.away(piece, half)
                if in_plane:
                    pl.when((z == p.z) & (p.c != half))(copy.start)
                    pl.when((z == p.z) & (p.c == half))(self.local(piece).start)
                else:
                    pl.when(z != p.z)(copy.start)

    def arrive(self, source):
        p = self.p
        here = self.place(source, p.c)
        ours = (source == p.z) & (p.c == p.z // self.per_core)
        came = remote(here, here, self.send.at[0], self.recv.at[source], p.partner())
        pl.when(jnp.logical_not(ours))(came.wait_recv)
        pl.when(ours)(self.local(0).wait)

    def finish(self):
        p = self.p
        for piece in range(self.per_core):
            for half in range(2):
                z, copy = self.away(piece, half)
                here = (z == p.z) & (p.c == half)
                pl.when(jnp.logical_not(here))(copy.wait_send)


class DealTask(Task):
    vmem_outs = (0,)

    def __init__(self, nz, shard):
        rows, units = shard.shape
        self.ins = (shard.reshape(2, rows // 2, units),)
        self.outs = (jax.ShapeDtypeStruct((nz, rows // 2, 2 * units // nz), bf16),)
        self.scratch = (DMA((nz,)), DMA((nz,)))

    def steps(self, p, ins, outs, scratch):
        (shard,), (pieces,), (send, recv) = ins, outs, scratch
        deal = Deal(p, shard, lambda z, half: pieces.at[z], pieces.shape[-1], send, recv)
        deal.start(False)
        deal.start(True)
        yield
        for i in range(p.nz):
            deal.arrive(exclusive_or(p.z, i))
        deal.finish()


class Copies(Task):
    vmem_outs = (0,)

    def __init__(self, nz, given, dealt):
        self.dealt = dealt
        if dealt:
            _, half, quarter = given.shape
            self.ins = (given,)
        else:
            rows, units = given.shape
            half, quarter = rows // 2, 2 * units // nz
            self.ins = (given.reshape(2, half, units),)
        self.quarter = quarter
        self.outs = (jax.ShapeDtypeStruct((nz, 2, 2, half, 2 * quarter), bf16),)
        self.scratch = (
            DMA((nz,)), DMA((nz,)), DMA((nz,)), DMA((nz,)), DMA((nz, 2)), DMA((nz, 2)),
            DMA((nz, 2)), DMA((nz, 2)),
        )

    def steps(self, p, ins, outs, scratch):
        (given,), (full,) = ins, outs
        d_send, d_recv, f_send, f_recv, s_send, s_recv, x_send, x_recv = scratch
        nz, quarter = p.nz, self.quarter

        def place(z, x, c, y):
            columns = pl.ds(pl.multiple_of(y * quarter, 128), quarter)
            return full.at[z, x, c, :, columns]

        fx, fy = p.x + (1 - 2 * p.x) * (1 - p.c), p.y + (1 - 2 * p.y) * p.c
        sx, sy = p.x + (1 - 2 * p.x) * p.c, p.y + (1 - 2 * p.y) * (1 - p.c)

        def own(z):
            return given.at[z] if self.dealt else place(z, p.x, p.c, p.y)

        def first(z):
            target = p.device(x=fx, y=fy)
            return remote(own(z), place(z, p.x, p.c, p.y), f_send.at[z], f_recv.at[z], target)

        def second(z, which):
            x, y = (fx, fy) if which else (p.x, p.y)
            here = place(z, x, p.c, y)
            src = here if which else own(z)
            target = p.device(x=sx, y=sy)
            return remote(src, here, s_send.at[z, which], s_recv.at[z, which], target)

        def across(z, x):
            here = full.at[z, x, p.c]
            return remote(here, here, x_send.at[z, x], x_recv.at[z, x], p.partner())

        def keep(z):
            return pltpu.make_async_copy(given.at[z], place(z, p.x, p.c, p.y), d_send.at[z])

        order = [exclusive_or(p.z, i) for i in range(nz)]
        if self.dealt:
            for z in order:
                first(z).start()
                second(z, 0).start()
                keep(z).start()
            for z in order:
                keep(z).wait()
            yield
        else:
            deal = Deal(
                p, given, lambda z, half: place(z, p.x, half, p.y), quarter, d_send, d_recv
            )
            deal.start(True)
            yield
            deal.arrive(order[0])
            first(order[0]).start()
            second(order[0], 0).start()
            yield
            deal.start(False)
            yield
            for z in order[1:]:
                deal.arrive(z)
                first(z).start()
                second(z, 0).start()
                yield
        for z in order:
            first(z).wait_recv()
            second(z, 1).start()
            yield
        for z in order:
            second(z, 0).wait_recv()
            second(z, 1).wait_recv()
            across(z, 0).start()
            across(z, 1).start()
            yield
        for z in range(nz):
            first(z).wait_send()
            for i in range(2):
                second(z, i).wait_send()
                across(z, i).wait()
        if not self.dealt:
            deal.finish()


class DealBack:
    def __init__(self, p, source, out, quarter, send, recv):
        self.p, self.source, self.out, self.quarter = p, source, out, quarter
        self.send, self.recv = send, recv
        self.per_core = p.nz // 2
        self.owner = p.z // self.per_core

    def out_at(self, z, half):
        start = pl.multiple_of(lax.rem(z, self.per_core) * self.quarter, 128)
        return self.out.at[half, :, pl.ds(start, self.quarter)]

    def away(self, z):
        p = self.p
        return remote(
            self.source(z),
            self.out_at(p.z, p.c),
            self.send.at[z],
            self.recv.at[2 * lax.rem(p.z, self.per_core) + p.c],
            p.device(z=z, c=self.owner),
        )

    def keep(self, z):
        p = self.p
        return pltpu.make_async_copy(
            self.source(z),
            self.out_at(p.z, p.c),
            self.recv.at[2 * lax.rem(p.z, self.per_core) + p.c],
        )

    def start(self, z):
        p = self.p
        here = (z == p.z) & (p.c == self.owner)
        pl.when(jnp.logical_not(here))(self.away(z).start)
        pl.when(here)(self.keep(z).start)

    def finish(self):
        p = self.p
        for piece in range(self.per_core):
            for half in range(2):
                z = p.c * self.per_core + piece
                place = self.out_at(z, half)
                came = remote(
                    place, place, self.send.at[0], self.recv.at[2 * piece + half], p.partner()
                )
                ours = (z == p.z) & (p.c == half)
                pl.when(jnp.logical_not(ours))(came.wait_recv)
        for z in range(p.nz):
            here = (z == p.z) & (p.c == self.owner)
            pl.when(jnp.logical_not(here))(self.away(z).wait_send)
            pl.when(here)(self.keep(z).wait)


class DealBackTask(Task):
    vmem_outs = (0,)

    def __init__(self, nz, sums):
        _, half, quarter = sums.shape
        self.ins = (sums,)
        self.outs = (jax.ShapeDtypeStruct((2, half, nz // 2 * quarter), bf16),)
        self.scratch = (DMA((nz,)), DMA((nz,)))

    def steps(self, p, ins, outs, scratch):
        (sums,), (out,), (send, recv) = ins, outs, scratch
        deal = DealBack(p, lambda z: sums.at[z], out, sums.shape[-1], send, recv)
        for i in (3, 2, 1, 0):
            deal.start(exclusive_or(p.z, i))
        yield
        deal.finish()


class Sums(Task):
    def __init__(self, nz, grad, deal):
        depth, width = grad.shape
        half, quarter = depth // (4 * nz), width // 2
        self.deal = deal
        self.ins = (grad.reshape(nz, 2, 2, half, width),)
        if deal:
            self.outs = (jax.ShapeDtypeStruct((2, half, nz // 2 * quarter), bf16),)
        else:
            self.outs = (jax.ShapeDtypeStruct((nz, half, quarter), bf16),)
            self.vmem_outs = (0,)
        whole = pltpu.VMEM((nz, 2, half, width), bf16)
        self.scratch = (
            whole,
            whole,
            pltpu.VMEM((nz, 2, half, quarter), bf16),
            pltpu.VMEM((nz, half, quarter), bf16),
            DMA((nz, 2)), DMA((nz, 2)), DMA((nz, 2)), DMA((nz, 2)), DMA((nz, 2)),
            DMA((nz,)), DMA((nz,)), DMA((nz,)), DMA((nz,)),
        )

    def steps(self, p, ins, outs, scratch):
        (given,), (out,) = ins, outs
        mine, came, first_in, second_in, *sems = scratch
        local, c_send, c_recv, f_send, f_recv, s_send, s_recv, d_send, d_recv = sems
        nz, quarter = p.nz, given.shape[4] // 2
        order = [exclusive_or(p.z, i) for i in (3, 2, 1, 0)]

        def bring(z, x):
            return pltpu.make_async_copy(given.at[z, x, p.c], mine.at[z, x], local.at[z, x])

        def across(z, x):
            src = given.at[z, x, 1 - p.c]
            return remote(src, came.at[z, x], c_send.at[z, x], c_recv.at[z, x], p.partner())

        def place(z, x, y):
            return mine.at[z, x, :, pl.ds(pl.multiple_of(y * quarter, 128), quarter)]

        fx, fy = p.x + (1 - 2 * p.x) * p.c, p.y + (1 - 2 * p.y) * (1 - p.c)
        sx, sy = p.x + (1 - 2 * p.x) * (1 - p.c), p.y + (1 - 2 * p.y) * p.c

        def first(z, which):
            x, y = (1 - p.x, 1 - p.y) if which else (fx, fy)
            target = p.device(x=fx, y=fy)
            return remote(
                place(z, x, y), first_in.at[z, which], f_send.at[z, which], f_recv.at[z, which], target
            )

        def second(z):
            target = p.device(x=sx, y=sy)
            return remote(place(z, sx, sy), second_in.at[z], s_send.at[z], s_recv.at[z], target)

        back = DealBack(p, lambda z: place(z, p.x, p.y), out, quarter, d_send, d_recv)
        for z in order:
            for x in range(2):
                across(z, x).start()
                bring(z, x).start()
        yield
        for z in order:
            for x in range(2):
                across(z, x).wait_recv()
                bring(z, x).wait()
                add_rows(mine.at[z, x], mine.at[z, x], came.at[z, x])
            for which in (1, 0):
                first(z, which).start()
            yield
        for i in range(nz + 1):
            if i < nz:
                z = order[i]
                for which in (1, 0):
                    at = place(z, sx, sy) if which else place(z, p.x, p.y)
                    first(z, which).wait_recv()
                    add_rows(at, at, first_in.at[z, which])
                    if which:
                        second(z).start()
                yield
            if i >= 1:
                z = order[i - 1]
                second(z).wait_recv()
                at = place(z, p.x, p.y)
                if self.deal:
                    add_rows(at, at, second_in.at[z])
                    back.start(z)
                else:
                    add_rows(out.at[z], at, second_in.at[z])
                yield
        if self.deal:
            back.finish()
        for z in range(nz):
            second(z).wait_send()
            for i in range(2):
                first(z, i).wait_send()
                across(z, i).wait_send()


class FeedForward(Task):
    vmem_ins = (0, 1, 2)
    vmem_outs = (0, 1)
    spare = 10

    def __init__(self, nz, own, cotangent, gain, gate, up, down):
        rows, depth = own.shape
        units = gate.shape[1]
        self.rows, self.depth, self.units = rows, depth, units
        self.ins = (own, cotangent, gain.reshape(1, depth), gate, up, down)
        wide = jax.ShapeDtypeStruct((depth, units), bf16)
        exact = jax.ShapeDtypeStruct((rows, depth), f32)
        self.outs = (exact, exact, wide, wide, wide)
        weight = pltpu.VMEM((depth, units), bf16)
        tokens = pltpu.VMEM((nz * rows, depth), bf16)
        inner = pltpu.VMEM((nz * rows, units), bf16)
        line = pltpu.VMEM((2, nz - 1, rows // 2, depth), bf16)
        self.scratch = (
            weight, weight, weight, tokens, tokens, inner, inner, inner, tokens, line, line,
            DMA((8, 2, nz)), DMA((8, 2, nz)), DMA((8,)),
        )

    def steps(self, p, ins, outs, scratch):
        own, cotangent, gain, gate_in, up_in, down_in = ins
        ff_out, dn_out, grad_gate, grad_up, grad_down = outs
        gate, up, down, normed, d_ff, hidden, gated, upped, parts, above, below, send, recv, local = scratch
        nz, depth, units = p.nz, self.depth, self.units
        part = self.rows // 2
        half_rows = nz * part
        tile = 768 if units % 768 == 0 and depth % 768 == 0 else 128

        def entry(buffer, half):
            return lambda z: buffer.at[pl.ds(pl.multiple_of(half * half_rows + z * part, part), part)]

        gathers, scatters = [], []
        for i, buffer in enumerate((normed, d_ff)):
            for half in range(2):
                k = 4 * i + half
                gathers.append(LineGather(p, entry(buffer, half), send.at[k], recv.at[k]))
                scatters.append(
                    LineScatter(
                        p, entry(parts, half), above.at[half], below.at[half], send.at[k + 2], recv.at[k + 2]
                    )
                )

        loads = [
            pltpu.make_async_copy(src, dst, local.at[i])
            for i, (src, dst) in enumerate(((gate_in, gate), (up_in, up), (down_in, down)))
        ]

        def gelu(v):
            bent = jnp.tanh(math.sqrt(2.0 / math.pi) * (v + 0.044715 * (v * v * v)))
            return 0.5 * v * (1.0 + bent), bent

        def columns(i):
            return pl.ds(pl.multiple_of(i * tile, 128), tile)

        def hide(half, low, high):
            rows = slice(half * half_rows, (half + 1) * half_rows)

            @pl.loop(low, high)
            def _(i):
                at = columns(i)
                gate_lin = jnp.dot(normed[rows, :], gate[:, at], preferred_element_type=f32)
                up_lin = jnp.dot(normed[rows, :], up[:, at], preferred_element_type=f32)
                hidden[rows, at] = (gelu(gate_lin)[0] * up_lin).astype(bf16)
                gated[rows, at] = gate_lin.astype(bf16)
                upped[rows, at] = up_lin.astype(bf16)

        def project(half):
            rows = slice(half * half_rows, (half + 1) * half_rows)

            @pl.loop(0, depth // tile)
            def _(i):
                at = columns(i)
                parts[rows, at] = contract(hidden[rows, :], down[at, :], 1, 1).astype(bf16)

        def hide_back(half, low, high):
            rows = slice(half * half_rows, (half + 1) * half_rows)

            @pl.loop(low, high)
            def _(i):
                at = columns(i)
                d_hidden = jnp.dot(d_ff[rows, :], down[:, at], preferred_element_type=f32)
                v, u = gated[rows, at].astype(f32), upped[rows, at].astype(f32)
                value, bent = gelu(v)
                slope = 0.5 * (1.0 + bent) + (0.5 * math.sqrt(2.0 / math.pi)) * v * (
                    1.0 - bent * bent
                ) * (1.0 + (3.0 * 0.044715) * (v * v))
                gated[rows, at] = (d_hidden * u * slope).astype(bf16)
                upped[rows, at] = (d_hidden * value).astype(bf16)

        def project_back(half):
            rows = slice(half * half_rows, (half + 1) * half_rows)

            @pl.loop(0, depth // tile)
            def _(i):
                at = columns(i)
                total = contract(gated[rows, :], gate[at, :], 1, 1)
                parts[rows, at] = (total + contract(upped[rows, :], up[at, :], 1, 1)).astype(bf16)

        def turn_back(half):
            start = half * half_rows + p.z * part

            @pl.loop(0, part // 16)
            def _(i):
                at = pl.ds(pl.multiple_of(half * part + i * 16, 16), 16)
                values = ff_out[at, :]
                scaled = cotangent[at, :].astype(f32) * (1.0 + gain[...])
                factor = factor_of(values)
                unit = values * factor
                mean = jnp.mean(scaled * unit, axis=-1, keepdims=True)
                here = pl.ds(pl.multiple_of(start + i * 16, 16), 16)
                d_ff[here, :] = ((scaled - unit * mean) * factor).astype(bf16)

        def weigh(left, right, out, low, high):
            @pl.loop(low, high)
            def _(i):
                at = pl.ds(pl.multiple_of(i * 256, 128), 256)
                out[at, :] = contract(left[:, at], right[...], 0, 0).astype(bf16)

        def store(i, src, dst):
            return pltpu.make_async_copy(src, dst, local.at[3 + i])

        blocks = depth // 256
        tiles = units // tile
        one, two, one_back, two_back = gathers
        sum_one, sum_two, sum_one_back, sum_two_back = scatters
        keep = [
            pltpu.make_async_copy(own.at[pl.ds(half * part, part)], entry(normed, half)(p.z), local.at[6 + half])
            for half in range(2)
        ]
        keep[0].start()
        keep[1].start()
        for load in loads:
            load.start()
        keep[0].wait()
        one.start(1)
        keep[1].wait()
        for s in range(1, nz):
            one.arrive(s)
            if s < nz - 1:
                one.start(s + 1)
            if s == nz - 2:
                two.start(1)
        for load in loads:
            load.wait()
        hide(0, 0, 1)
        two.arrive(1)
        two.start(2)
        hide(0, 1, tiles)
        two.arrive(2)
        two.start(3)
        project(0)
        sum_one.start(1)
        two.arrive(3)
        hide(1, 0, 1)
        sum_one.arrive(1)
        sum_one.start(2)
        hide(1, 1, tiles)
        sum_one.arrive(2)
        sum_one.start(3)
        project(1)
        sum_two.start(1)
        sum_one.arrive(3)
        sum_one.total(ff_out.at[pl.ds(0, part)])
        turn_back(0)
        one_back.start(1)
        sum_two.arrive(1)
        sum_two.start(2)
        one_back.arrive(1)
        one_back.start(2)
        sum_two.arrive(2)
        sum_two.start(3)
        one_back.arrive(2)
        one_back.start(3)
        sum_two.arrive(3)
        sum_two.total(ff_out.at[pl.ds(part, part)])
        turn_back(1)
        two_back.start(1)
        one_back.arrive(3)
        sum_one.finish()
        hide_back(0, 0, 1)
        two_back.arrive(1)
        two_back.start(2)
        hide_back(0, 1, tiles)
        two_back.arrive(2)
        two_back.start(3)
        project_back(0)
        sum_one_back.start(1)
        two_back.arrive(3)
        hide_back(1, 0, 1)
        sum_one_back.arrive(1)
        sum_one_back.start(2)
        hide_back(1, 1, tiles)
        sum_one_back.arrive(2)
        sum_one_back.start(3)
        sum_two.finish()
        project_back(1)
        sum_two_back.start(1)
        weigh(d_ff, hidden, down, 0, blocks)
        store(0, down, grad_down).start()
        sum_one_back.arrive(3)
        sum_two_back.arrive(1)
        sum_two_back.start(2)
        sum_one_back.total(dn_out.at[pl.ds(0, part)])
        weigh(normed, gated, gate, 0, blocks)
        store(1, gate, grad_gate).start()
        sum_two_back.arrive(2)
        sum_two_back.start(3)
        weigh(normed, upped, up, 0, blocks)
        store(2, up, grad_up).start()
        sum_two_back.arrive(3)
        sum_two_back.total(dn_out.at[pl.ds(part, part)])
        for gather in gathers:
            gather.finish()
        sum_one_back.finish()
        sum_two_back.finish()
        store(0, down, grad_down).wait()
        store(1, gate, grad_gate).wait()
        store(2, up, grad_up).wait()
        yield


class SumAll(Task):
    vmem_ins = (0,)
    vmem_outs = (0,)

    def __init__(self, values):
        self.ins = (values,)
        self.outs = (jax.ShapeDtypeStruct(values.shape, f32),)
        stage = pltpu.VMEM((5,) + values.shape, f32)
        self.scratch = (stage, stage, DMA((5,)), DMA((5,)))

    def steps(self, p, ins, outs, scratch):
        (given,), (out,), (stage, came, send, recv) = ins, outs, scratch
        targets = [
            p.partner(),
            p.device(y=1 - p.y),
            p.device(x=1 - p.x),
            p.device(z=exclusive_or(p.z, 1)),
            p.device(z=exclusive_or(p.z, 2)),
        ]
        stage[0] = given[...]
        for i, target in enumerate(targets):
            copy = remote(stage.at[i], came.at[i], send.at[i], recv.at[i], target)
            copy.start()
            yield
            copy.wait()
            total = stage[i] + came[i]
            if i < 4:
                stage[i + 1] = total
            else:
                out[...] = total


def run_tasks(nz, number, tasks, order=""):
    counts = [(len(t.ins), len(t.outs), len(t.scratch)) for t in tasks]

    def split(refs, which):
        found = []
        for count in counts:
            found.append(refs[: count[which]])
            refs = refs[count[which] :]
        return found, refs

    def body(*refs):
        ins, refs = split(refs, 0)
        outs, refs = split(refs, 1)
        scratch, refs = split(refs, 2)
        p = Spot(nz)
        p.greet()
        running = [t.steps(p, *given) for t, *given in zip(tasks, ins, outs, scratch)]
        done = [False] * len(tasks)
        for digit in order:
            i = int(digit)
            if not done[i]:
                done[i] = next(running[i], "end") == "end"
        while not all(done):
            for i, steps in enumerate(running):
                if not done[i]:
                    done[i] = next(steps, "end") == "end"

    sent = sum(x.size * 2 for t in tasks for x in t.ins)
    spare = max(t.spare for t in tasks) * 2**20
    held = [s for t in tasks for s in t.scratch if getattr(s, "memory_space", None) == pltpu.VMEM]
    held += [t.ins[i] for t in tasks for i in t.vmem_ins] + [t.outs[i] for t in tasks for i in t.vmem_outs]
    vmem = sum(math.prod(s.shape) * jnp.dtype(s.dtype).itemsize for s in held)
    results = pl.pallas_call(
        body,
        out_shape=[o for t in tasks for o in t.outs],
        in_specs=[in_vmem if i in t.vmem_ins else anywhere for t in tasks for i in range(len(t.ins))],
        out_specs=[
            in_vmem if i in t.vmem_outs else anywhere for t in tasks for i in range(len(t.outs))
        ],
        scratch_shapes=[s for t in tasks for s in t.scratch],
        compiler_params=pltpu.CompilerParams(
            collective_id=number, has_side_effects=True, vmem_limit_bytes=vmem + spare
        ),
        cost_estimate=pl.CostEstimate(
            flops=0, bytes_accessed=sent, transcendentals=0, remote_bytes_transferred=sent
        ),
    )(*[x for t in tasks for x in t.ins])
    found, _ = split(list(results), 1)
    return found[0] if len(tasks) == 1 else [f[0] for f in found]


START_ORDER = "10231223" + "132224" + "12222" + "3331" + "2222" + "33333333"
FINISH_ORDER = "01203111" + "1112" + "03112" + "11220" + "3112" + "2220" + "32222"
KV_ORDER = "0120" + "12" + "2" + "20" + "12222" + "01" + "222201" + "2222"


class Kernels:
    def __init__(self, at):
        self.at = at
        self.blocks, self.nz = at.blocks, at.nz
        self.block = 2 * at.z + at.c
        self.number = 0

    def run(self, tasks, order=""):
        self.number += 1
        return run_tasks(self.nz, self.number, tasks, order)

    def flat(self, whole):
        return whole.reshape(-1, whole.shape[-1])

    def start(self, own, attn_shard, gate, up, down):
        nz = self.nz
        tasks = [
            PlaneGather(own),
            PairGather(nz, attn_shard, True),
            Copies(nz, gate, False),
            Copies(nz, up, False),
            DealTask(nz, down),
        ]
        *found, pieces = self.run(tasks, START_ORDER)
        return [self.flat(w) for w in found] + [pieces]

    def gather_kv(self, own, pieces):
        whole, down = self.run(
            [PairGather(self.nz, own, False), Copies(self.nz, pieces, True)], "010011110111"
        )
        return whole.reshape((self.blocks,) + own.shape), self.flat(down)

    def scatter_heads(self, partial):
        return self.run([PlaneScatter(partial)])[0]

    def feed_forward(self, own, cotangent, gain, gate, up, down):
        task = FeedForward(self.nz, own, cotangent, gain, gate, up, down)
        self.number += 1
        return run_tasks(self.nz, self.number, [task])

    def gather_heads(self, own):
        return self.flat(self.run([PlaneGather(own)])[0])

    def scatter_kv_sums(self, parts, out_grad, grad):
        nz = self.nz
        given = parts.reshape((nz, 2) + parts.shape[1:])
        rows = out_grad.shape[0] // self.blocks
        out_given = out_grad.reshape(nz, 2, rows, out_grad.shape[1])
        kv, out, sums = self.run(
            [PairScatter(nz, given, False), PairScatter(nz, out_given, True), Sums(nz, grad, False)],
            KV_ORDER,
        )
        return kv.astype(f32), out, sums

    def scatter_heads_back(self, partial, sums):
        rows, shard = self.run([PlaneScatter(partial), DealBackTask(self.nz, sums)], "01")
        return rows, self.flat(shard)

    def finish(self, qkv_grad, gate_grad, up_grad, gains):
        rows = qkv_grad.shape[0] // self.blocks
        given = qkv_grad.reshape(self.nz, 2, rows, qkv_grad.shape[1])
        qkv, gate, up, total = self.run(
            [
                PairScatter(self.nz, given, True),
                Sums(self.nz, gate_grad, True),
                Sums(self.nz, up_grad, True),
                SumAll(gains.reshape(8, -1)),
            ],
            FINISH_ORDER,
        )
        return qkv, self.flat(gate), self.flat(up), total.reshape(gains.shape)


def causal_mask(rows):
    shape = (rows, rows)
    return lax.broadcasted_iota(jnp.int32, shape, 1) <= lax.broadcasted_iota(jnp.int32, shape, 0)


def forward_kernel(kinds, q_ref, kv_ref, out_ref, exact_ref, inv_ref, acc, total):
    step, last = pl.program_id(0), pl.num_programs(0) - 1
    heads, rows, dim = q_ref.shape
    kind = kinds[step]

    @pl.when(step == 0)
    def _():
        acc[...] = jnp.zeros_like(acc)
        total[...] = jnp.zeros_like(total)

    def work(own):
        for head in range(heads):
            raw = contract(q_ref[head], kv_ref[0, :, :dim], 1, 1)
            weights = jnp.exp(softcap * jnp.tanh(raw * (score_scale / softcap)))
            if own:
                weights = jnp.where(causal_mask(rows), weights, 0.0)
            total[head] += jnp.sum(weights, axis=-1, keepdims=True)
            acc[head] += contract(weights.astype(bf16), kv_ref[0, :, dim:], 1, 0)

    @pl.when(kind == 1)
    def _():
        work(False)

    @pl.when(kind == 2)
    def _():
        work(True)

    @pl.when(step == last)
    def _():
        for head in range(heads):
            inverse = 1.0 / total[head]
            value = acc[head] * inverse
            inv_ref[head] = inverse
            exact_ref[:, head * dim : (head + 1) * dim] = value
            out_ref[:, head * dim : (head + 1) * dim] = value.astype(bf16)


def whole2(step, kinds):
    return (0, 0)


def whole3(step, kinds):
    return (0, 0, 0)


def by_step(step, kinds):
    return (step, 0, 0)


def attend(kinds, queries, all_kv):
    heads, rows, dim = queries.shape
    return pl.pallas_call(
        forward_kernel,
        grid_spec=pltpu.PrefetchScalarGridSpec(
            num_scalar_prefetch=1,
            grid=(all_kv.shape[0],),
            in_specs=[
                pl.BlockSpec((heads, rows, dim), whole3),
                pl.BlockSpec((1, rows, 2 * dim), by_step),
            ],
            out_specs=[
                pl.BlockSpec((rows, heads * dim), whole2),
                pl.BlockSpec((rows, heads * dim), whole2),
                pl.BlockSpec((heads, rows, 1), whole3),
            ],
            scratch_shapes=[
                pltpu.VMEM((heads, rows, dim), f32),
                pltpu.VMEM((heads, rows, 1), f32),
            ],
        ),
        out_shape=[
            jax.ShapeDtypeStruct((rows, heads * dim), bf16),
            jax.ShapeDtypeStruct((rows, heads * dim), f32),
            jax.ShapeDtypeStruct((heads, rows, 1), f32),
        ],
        compiler_params=pltpu.CompilerParams(vmem_limit_bytes=40 * 2**20),
        cost_estimate=pl.CostEstimate(
            flops=3 * 4 * heads * rows * rows * dim,
            bytes_accessed=8 * rows * dim * heads,
            transcendentals=6 * heads * rows * rows,
        ),
    )(kinds, queries, all_kv)


def backward_kernel(kinds, q_ref, kv_ref, up_ref, exact_ref, inv_ref, dq_ref, dkv_ref):
    step = pl.program_id(0)
    heads, rows, dim = q_ref.shape
    kind = kinds[step]

    @pl.when(step == 0)
    def _():
        dq_ref[...] = jnp.zeros_like(dq_ref)

    def work(own):
        dk = jnp.zeros((rows, dim), f32)
        dv = jnp.zeros((rows, dim), f32)
        for head in range(heads):
            columns = slice(head * dim, (head + 1) * dim)
            up = up_ref[:, columns]
            delta = jnp.sum(up.astype(f32) * exact_ref[:, columns], axis=-1, keepdims=True)
            raw = contract(q_ref[head], kv_ref[0, :, :dim], 1, 1)
            bounded = jnp.tanh(raw * (score_scale / softcap))
            probs = jnp.exp(softcap * bounded) * inv_ref[head]
            if own:
                probs = jnp.where(causal_mask(rows), probs, 0.0)
            d_probs = contract(up, kv_ref[0, :, dim:], 1, 1)
            d_raw = probs * (d_probs - delta) * ((1.0 - bounded * bounded) * score_scale)
            d_raw = d_raw.astype(bf16)
            dq_ref[head] += contract(d_raw, kv_ref[0, :, :dim], 1, 0)
            dk += contract(d_raw, q_ref[head], 0, 0)
            dv += contract(probs.astype(bf16), up, 0, 0)
        dkv_ref[0, :, :dim] = dk.astype(bf16)
        dkv_ref[0, :, dim:] = dv.astype(bf16)

    @pl.when(kind == 1)
    def _():
        work(False)

    @pl.when(kind == 0)
    def _():
        dkv_ref[...] = jnp.zeros_like(dkv_ref)

    @pl.when(kind == 2)
    def _():
        work(True)


def attend_back(kinds, queries, all_kv, upstream, exact, inverse):
    heads, rows, dim = queries.shape
    blocks = all_kv.shape[0]
    return pl.pallas_call(
        backward_kernel,
        grid_spec=pltpu.PrefetchScalarGridSpec(
            num_scalar_prefetch=1,
            grid=(blocks,),
            in_specs=[
                pl.BlockSpec((heads, rows, dim), whole3),
                pl.BlockSpec((1, rows, 2 * dim), by_step),
                pl.BlockSpec((rows, heads * dim), whole2),
                pl.BlockSpec((rows, heads * dim), whole2),
                pl.BlockSpec((heads, rows, 1), whole3),
            ],
            out_specs=[
                pl.BlockSpec((heads, rows, dim), whole3),
                pl.BlockSpec((1, rows, 2 * dim), by_step),
            ],
        ),
        out_shape=[
            jax.ShapeDtypeStruct((heads, rows, dim), f32),
            jax.ShapeDtypeStruct((blocks, rows, 2 * dim), bf16),
        ],
        compiler_params=pltpu.CompilerParams(vmem_limit_bytes=40 * 2**20),
        cost_estimate=pl.CostEstimate(
            flops=3 * 10 * heads * rows * rows * dim,
            bytes_accessed=16 * rows * dim * heads,
            transcendentals=6 * heads * rows * rows,
        ),
    )(kinds, queries, all_kv, upstream, exact, inverse)


def on_device(
    tokens,
    cotangent,
    norm_attn_in,
    w_query,
    w_key,
    w_value,
    w_out,
    norm_attn_out,
    norm_ff_in,
    w_gate,
    w_up,
    w_down,
    norm_ff_out,
    block_group,
    block_role,
):
    at = Place()
    own_rows, depth = tokens.shape
    shard_rows, units = w_gate.shape
    regular = at.nz == 4 and shard_rows % 32 == 0 and (2 * units // at.nz) % 128 == 0
    comm = Kernels(at) if regular else Permutes(at)
    blocks = at.blocks
    block_len = own_rows * lax.axis_size("heads")
    prompt_len = blocks // 4
    block_ids = jnp.arange(blocks, dtype=jnp.int32)
    my_group = jnp.sum(jnp.where(block_ids == comm.block, block_group, 0))
    my_role = jnp.sum(jnp.where(block_ids == comm.block, block_role, 0))
    positions = jnp.where(
        my_role < prompt_len, my_role * block_len, prompt_len * block_len
    ) + jnp.arange(block_len, dtype=jnp.int32)
    cosine, sine_table = rope_tables(positions)
    prompt = (block_group == my_group) & (block_role < prompt_len) & (block_role < my_role)
    kinds = jnp.where(block_ids == comm.block, 2, prompt.astype(jnp.int32)).astype(jnp.int32)

    token_f32 = tokens.astype(f32)
    heads_width = w_query.shape[1]
    qkv_width = heads_width + 2 * HEAD_DIM
    attn_shard = jnp.concatenate([w_query, w_key, w_value, w_out.T], axis=1)
    normed_one, attn_full, gate_full, up_full, down_pieces = comm.start(
        normalize(token_f32, norm_attn_in).astype(bf16), attn_shard, w_gate, w_up, w_down.T
    )
    qkv_full, out_full = attn_full[:, :qkv_width], attn_full[:, qkv_width:]
    qkv_lin = jnp.dot(normed_one, qkv_full, preferred_element_type=f32)
    queries = jnp.stack(
        [
            rotate(qkv_lin[:, :HEAD_DIM], cosine, sine_table),
            rotate(qkv_lin[:, HEAD_DIM:heads_width], cosine, sine_table),
        ]
    ).astype(bf16)
    own_kv = jnp.concatenate(
        [
            rotate(qkv_lin[:, heads_width : heads_width + HEAD_DIM], cosine, sine_table),
            qkv_lin[:, heads_width + HEAD_DIM :],
        ],
        axis=1,
    ).astype(bf16)
    all_kv, down_full = comm.gather_kv(own_kv, down_pieces)
    attn_rows, attended, inverse = attend(kinds, queries, all_kv)
    attn_proj = comm.scatter_heads(contract(attn_rows, out_full, 1, 1).astype(bf16))
    middle = token_f32 + normalize(attn_proj, norm_attn_out)

    ff_proj, d_normed_two, gate_sum, up_sum, down_sum = comm.feed_forward(
        normalize(middle, norm_ff_in).astype(bf16), cotangent, norm_ff_out, gate_full, up_full, down_full
    )
    layer_out = middle + normalize(ff_proj, norm_ff_out)
    upstream = cotangent.astype(f32)
    _, grad_ff_out = normalize_back(ff_proj, norm_ff_out, upstream)

    d_middle_part, grad_ff_in = normalize_back(middle, norm_ff_in, d_normed_two)
    d_middle = upstream + d_middle_part
    d_proj, grad_attn_out = normalize_back(attn_proj, norm_attn_out, d_middle)
    d_proj_rows = comm.gather_heads(d_proj.astype(bf16))
    d_attended = contract(d_proj_rows, out_full, 1, 0).astype(bf16)
    d_query, d_kv_parts = attend_back(kinds, queries, all_kv, d_attended, attended, inverse)
    d_kv, grad_out, down_sums = comm.scatter_kv_sums(
        d_kv_parts, contract(d_proj_rows, attn_rows, 0, 0).astype(bf16), down_sum
    )
    d_qkv_lin = jnp.concatenate(
        [
            rotate(d_query[0], cosine, -sine_table),
            rotate(d_query[1], cosine, -sine_table),
            rotate(d_kv[:, :HEAD_DIM], cosine, -sine_table),
            d_kv[:, HEAD_DIM:],
        ],
        axis=1,
    ).astype(bf16)
    d_normed_one, grad_down = comm.scatter_heads_back(
        contract(d_qkv_lin, qkv_full, 1, 1).astype(bf16), down_sums
    )
    d_token_part, grad_attn_in = normalize_back(token_f32, norm_attn_in, d_normed_one)
    input_grad = (d_middle + d_token_part).astype(bf16)
    grad_qkv, grad_gate, grad_up, gains = comm.finish(
        contract(normed_one, d_qkv_lin, 0, 0).astype(bf16),
        gate_sum,
        up_sum,
        jnp.stack([grad_attn_in, grad_attn_out, grad_ff_in, grad_ff_out]),
    )
    grad_qkv, grad_gate, grad_up = [g.astype(f32) for g in (grad_qkv, grad_gate, grad_up)]
    return (
        layer_out.astype(bf16),
        input_grad,
        gains[0],
        grad_qkv[:, :heads_width],
        grad_qkv[:, heads_width : heads_width + HEAD_DIM],
        grad_qkv[:, heads_width + HEAD_DIM :],
        grad_out.astype(f32).T,
        gains[1],
        gains[2],
        grad_gate,
        grad_up,
        grad_down.astype(f32).T,
        gains[3],
    )


def solution(mesh):
    rows, weight, turned = P(("blk", "heads"), None), P("blk", "heads"), P("heads", "blk")
    return jax.shard_map(
        on_device,
        mesh=mesh,
        in_specs=(
            rows, rows, P(), weight, weight, weight, turned, P(), P(), weight, weight, turned,
            P(), P(), P(),
        ),
        out_specs=(
            rows, rows, P(), weight, weight, weight, turned, P(), P(), weight, weight, turned, P(),
        ),
        check_vma=False,
    )
```

```python
import math

import jax
import jax.numpy as jnp
from jax import lax
from jax.experimental import pallas as pl
from jax.experimental.pallas import tpu as pltpu
from jax.sharding import PartitionSpec as P

HEAD_DIM = 256


softcap = 50.0
epsilon = 1e-06
score_scale = HEAD_DIM ** (-0.5)
bf16 = jnp.bfloat16
f32 = jnp.float32


def contract(left_side, right_side, left_dim, right_dim):
    return lax.dot_general(
        left_side,
        right_side,
        (((left_dim,), (right_dim,)), ((), ())),
        preferred_element_type=f32,
    )


def factor_of(values):
    return lax.rsqrt(jnp.mean(values * values, axis=-1, keepdims=True) + epsilon)


def normalize(values, weight_gain):
    return values * factor_of(values) * (1.0 + weight_gain)


def normalize_back(values, weight_gain, upstream):
    factor = factor_of(values)
    unit = values * factor
    scaled = upstream * (1.0 + weight_gain)
    inner = jnp.mean(scaled * unit, axis=-1, keepdims=True)
    return (scaled - unit * inner) * factor, jnp.sum(upstream * unit, axis=0)


def rotate(tensor, cosine, sine_table):
    half_dim = HEAD_DIM // 2
    first_half = tensor[..., :half_dim]
    second_half = tensor[..., half_dim:]
    return jnp.concatenate(
        [
            first_half * cosine - second_half * sine_table,
            second_half * cosine + first_half * sine_table,
        ],
        axis=-1,
    )


def swap_core(v):
    return lax.ppermute(v, "heads", [(i, i ^ 1) for i in range(4)])


def swap_y(v):
    return lax.ppermute(v, "heads", [(i, i ^ 2) for i in range(4)])


def swap_x(v):
    blocks = lax.axis_size("blk")
    return lax.ppermute(v, "blk", [(i, i ^ 1) for i in range(blocks)])


def pair_up(own, other, place, axis):
    first = jnp.where(place == 0, own, other)
    second = jnp.where(place == 0, other, own)
    return jnp.concatenate([first, second], axis=axis)


def shift_z(v, step, senders):
    pairs = []
    for z in senders:
        for x in range(2):
            pairs.append((2 * z + x, 2 * (z + step) + x))
    return lax.ppermute(v, "blk", pairs)


class Place:
    def __init__(self):
        self.blocks = lax.axis_size("blk")
        self.nz = self.blocks // 2
        self.b = lax.axis_index("blk")
        self.h = lax.axis_index("heads")
        self.z, self.x = self.b // 2, self.b % 2
        self.y, self.c = self.h // 2, self.h % 2


def gather_z(at, unit):
    nz = at.nz
    up, down = unit, unit
    ups, downs = [None], [None]
    for s in range(1, nz):
        up = shift_z(up, 1, range(s - 1, nz - 1))
        down = shift_z(down, -1, range(1, nz - s + 1))
        ups.append(up)
        downs.append(down)
    return [unit] + [jnp.where(at.z >= s, ups[s], downs[nz - s]) for s in range(1, nz)]


def scatter_z(at, parts):
    nz = at.nz
    up = down = None
    for t in range(1, nz):
        k = nz - t
        send_up = parts[nz - k].astype(f32)
        send_down = parts[k].astype(f32)
        if up is not None:
            send_up = send_up + up.astype(f32)
            send_down = send_down + down.astype(f32)
        up = shift_z(send_up.astype(bf16), 1, range(0, nz - k))
        down = shift_z(send_down.astype(bf16), -1, range(k, nz))
    return parts[0].astype(f32) + (up.astype(f32) + down.astype(f32))


def deal_z(at, parts):
    nz = at.nz
    got = [parts[0]]
    for s in range(1, nz):
        up = shift_z(parts[nz - s], s, range(0, nz - s))
        down = shift_z(parts[nz - s], s - nz, range(nz - s, nz))
        got.append(jnp.where(at.z >= s, up, down))
    return got


def turn(at, whole):
    return [
        lax.dynamic_index_in_dim(whole, (at.z - s) % at.nz, 0, keepdims=False)
        for s in range(at.nz)
    ]


def unturn(at, parts):
    whole = jnp.zeros((at.nz,) + parts[0].shape, parts[0].dtype)
    for s, part in enumerate(parts):
        whole = lax.dynamic_update_index_in_dim(whole, part, (at.z - s) % at.nz, 0)
    return whole


def gather_zx(at, unit):
    got = []
    for part in gather_z(at, unit):
        got.append(pair_up(part[None], swap_x(part)[None], at.x, 0))
    return unturn(at, got)


def gather_xz(at, unit):
    both = pair_up(unit[None], swap_x(unit)[None], at.x, 0)
    return unturn(at, gather_z(at, both))


def pick(pair, place):
    mine = jnp.where(place == 0, pair[0], pair[1])
    other = jnp.where(place == 0, pair[1], pair[0])
    return mine, other


def scatter_zx(at, parts):
    total = scatter_z(at, parts)
    mine, other = pick(total, at.x)
    return mine + swap_x(other.astype(bf16)).astype(f32)


def scatter_xz(at, parts):
    sums = []
    for part in parts:
        mine, other = pick(part, at.x)
        sums.append(mine.astype(f32) + swap_x(other.astype(bf16)).astype(f32))
    return scatter_z(at, sums)


def rows_to_block(at, own):
    both = pair_up(own, swap_core(own), at.c, 0)
    pair = pair_up(both[None], swap_y(both)[None], at.y, 0)
    return pair.reshape(4 * own.shape[0], own.shape[1])


def rows_from_block(at, partial_sum):
    rows = partial_sum.shape[0] // 4
    parts = partial_sum.reshape(2, 2, rows, partial_sum.shape[1])
    mine, other = pick(parts.swapaxes(0, 1), at.c)
    total = mine + swap_core(other.astype(bf16)).astype(f32)
    mine, other = pick(total, at.y)
    return mine + swap_y(other.astype(bf16)).astype(f32)


def spread_weight(at, shard):
    rows, units = shard.shape
    half = rows // 2
    keep, send = pick(shard.reshape(2, half, units), at.c)
    wide = pair_up(keep[None], swap_core(send)[None], at.c, 0)
    quarter = 2 * units // at.nz
    per_core = units // quarter
    pieces = wide.reshape(2, half, per_core, quarter).transpose(0, 2, 1, 3)
    pieces = pieces.reshape(at.nz, half, quarter)
    got = unturn(at, deal_z(at, turn(at, pieces)))
    got = pair_up(got[:, None], swap_x(got)[:, None], at.x, 1)
    got = pair_up(got, swap_y(got), at.y, 3)
    got = pair_up(got[:, :, None], swap_core(got)[:, :, None], at.c, 2)
    return got.reshape(at.blocks * rows, 2 * quarter)


def collect_weight(at, grad):
    depth, width = grad.shape
    half, quarter = depth // (2 * at.blocks), width // 2
    parts = grad.reshape(at.nz, 2, 2, half, width)
    mine, other = pick(parts.transpose(2, 0, 1, 3, 4), at.c)
    total = mine + swap_core(other.astype(bf16)).astype(f32)
    mine, other = pick((total[..., :quarter], total[..., quarter:]), at.y)
    total = mine + swap_y(other.astype(bf16)).astype(f32)
    mine, other = pick((total[:, 0], total[:, 1]), at.x)
    total = mine + swap_x(other.astype(bf16)).astype(f32)
    got = unturn(at, deal_z(at, turn(at, total.astype(bf16))))
    per_core = at.nz // 2
    wide = got.reshape(2, per_core, half, quarter).transpose(0, 2, 1, 3)
    wide = wide.reshape(2, half, per_core * quarter)
    mine, other = pick(wide, at.c)
    rows = pair_up(mine, swap_core(other), at.c, 0)
    return rows.astype(f32)


def sum_all(at, values):
    total = values
    for bit in (1, 2):
        total = total + lax.ppermute(total, "heads", [(i, i ^ bit) for i in range(4)])
    bit = 1
    while bit < at.blocks:
        total = total + lax.ppermute(total, "blk", [(i, i ^ bit) for i in range(at.blocks)])
        bit *= 2
    return total


class Permutes:
    def __init__(self, at):
        self.at = at
        self.block, self.blocks, self.nz = at.b, at.blocks, at.nz

    def split(self, whole):
        return turn(self.at, whole.reshape((self.nz, whole.shape[0] // self.nz) + whole.shape[1:]))

    def start(self, own, qkv_shard, gate, up):
        at = self.at
        qkv_full = gather_zx(at, qkv_shard).reshape(own.shape[1], -1)
        return rows_to_block(at, own), qkv_full, spread_weight(at, gate), spread_weight(at, up)

    def gather_kv(self, own, out_shard, up):
        out_full = gather_zx(self.at, out_shard).reshape(-1, out_shard.shape[1])
        return gather_zx(self.at, own).reshape((self.blocks,) + own.shape), out_full, up

    def scatter_heads(self, partial, down):
        return rows_from_block(self.at, partial), spread_weight(self.at, down)

    def gather_z(self, own):
        whole = unturn(self.at, gather_z(self.at, own))
        return whole.reshape(-1, own.shape[1])

    def scatter_z(self, partial):
        return scatter_z(self.at, self.split(partial))

    def feed_forward(self, own, cotangent, gain, gate, up, down):
        normed = self.gather_z(own)
        gate_lin = jnp.dot(normed, gate, preferred_element_type=f32)
        up_lin = jnp.dot(normed, up, preferred_element_type=f32)
        hidden = (jax.nn.gelu(gate_lin, approximate=True) * up_lin).astype(bf16)
        ff_proj = self.scatter_z(contract(hidden, down, 1, 1).astype(bf16))
        d_ff, _ = normalize_back(ff_proj, gain, cotangent.astype(f32))
        d_ff_rows = self.gather_z(d_ff.astype(bf16))
        d_hidden = contract(d_ff_rows, down, 1, 0)
        _, glu_back = jax.vjp(
            lambda gate_in, up_in: jax.nn.gelu(gate_in, approximate=True) * up_in, gate_lin, up_lin
        )
        d_gate, d_up = [d.astype(bf16) for d in glu_back(d_hidden)]
        d_partial = contract(d_gate, gate, 1, 1) + contract(d_up, up, 1, 1)
        d_normed = self.scatter_z(d_partial.astype(bf16))
        grads = [
            contract(left, right, 0, 0).astype(bf16)
            for left, right in ((normed, d_gate), (normed, d_up), (d_ff_rows, hidden))
        ]
        return [ff_proj, d_normed] + grads

    def gather_heads(self, own):
        return rows_to_block(self.at, own)

    def scatter_pairs(self, grad):
        rows = grad.shape[0] // self.blocks
        return scatter_xz(self.at, self.split(grad.reshape(self.blocks, rows, -1)))

    def scatter_kv_sums(self, parts, out_grad, grad):
        kv = scatter_xz(self.at, self.split(parts))
        return kv, self.scatter_pairs(out_grad), collect_weight(self.at, grad)

    def scatter_heads_back(self, partial, sums):
        return rows_from_block(self.at, partial), sums

    def finish(self, qkv_grad, gate_grad, up_grad, gains):
        gate, up = collect_weight(self.at, gate_grad), collect_weight(self.at, up_grad)
        return self.scatter_pairs(qkv_grad), gate, up, sum_all(self.at, gains)


MESH = pl.DeviceIdType.MESH
DMA = pltpu.SemaphoreType.DMA
anywhere = pl.BlockSpec(memory_space=pl.ANY)
in_vmem = pl.BlockSpec(memory_space=pltpu.VMEM)


def remote(src, dst, send_sem, recv_sem, target):
    return pltpu.make_async_remote_copy(
        src_ref=src,
        dst_ref=dst,
        send_sem=send_sem,
        recv_sem=recv_sem,
        device_id=target,
        device_id_type=MESH,
    )


def flip(bit, by):
    return 1 - bit if by else bit


def exclusive_or(z, i):
    low, high = lax.rem(z, 2), lax.rem(z // 2, 2)
    rest = z - 2 * high - low
    return rest + 2 * flip(high, i // 2) + flip(low, i % 2)


class Spot:
    def __init__(self, nz):
        self.nz = nz
        h, b = lax.axis_index("heads"), lax.axis_index("blk")
        self.y, self.c = h // 2, h % 2
        self.z, self.x = b // 2, b % 2

    def device(self, z=None, x=None, y=None, c=None):
        z = self.z if z is None else z
        x = self.x if x is None else x
        y = self.y if y is None else y
        c = self.c if c is None else c
        return (2 * y + c, 2 * z + x)

    def partner(self):
        return self.device(c=1 - self.c)

    def greet(self):
        found = []
        for dx, dy, dc in [(0, 0, 1), (1, 0, 0), (1, 0, 1), (0, 1, 0), (0, 1, 1), (1, 1, 0), (1, 1, 1)]:
            found.append(self.device(x=flip(self.x, dx), y=flip(self.y, dy), c=flip(self.c, dc)))
        for s in range(1, self.nz):
            z = lax.rem(self.z + s, self.nz)
            found += [self.device(z=z), self.device(z=z, c=1 - self.c)]
        barrier = pltpu.get_barrier_semaphore()
        for device in found:
            pl.semaphore_signal(barrier, inc=1, device_id=device, device_id_type=MESH)
        pl.semaphore_wait(barrier, len(found))


def row_step(rows):
    return next(step for step in (48, 32, 16) if rows % step == 0)


def add_rows(out, left, right):
    rows = left.shape[0]
    step = row_step(rows)

    @pl.loop(0, rows // step)
    def _(i):
        at = pl.ds(pl.multiple_of(i * step, step), step)
        out[at, :] = (left[at, :].astype(f32) + right[at, :].astype(f32)).astype(out.dtype)


class LineGather:
    def __init__(self, spot, entry, send, recv):
        self.spot, self.entry = spot, entry
        self.send, self.recv = send, recv

    def copies(self, s):
        p, nz = self.spot, self.spot.nz
        up_at = lax.rem(p.z - s + 1 + nz, nz)
        down_at = lax.rem(p.z + s - 1, nz)
        up = remote(
            self.entry(up_at),
            self.entry(up_at),
            self.send.at[0, s],
            self.recv.at[0, s],
            p.device(z=lax.rem(p.z + 1, nz)),
        )
        down = remote(
            self.entry(down_at),
            self.entry(down_at),
            self.send.at[1, s],
            self.recv.at[1, s],
            p.device(z=lax.rem(p.z + nz - 1, nz)),
        )
        return (
            ((p.z >= s - 1) & (p.z < nz - 1), p.z >= s, up),
            ((p.z <= nz - s) & (p.z > 0), p.z <= nz - 1 - s, down),
        )

    def start(self, s):
        for sends, _, copy in self.copies(s):
            pl.when(sends)(copy.start)

    def arrive(self, s):
        for _, receives, copy in self.copies(s):
            pl.when(receives)(copy.wait_recv)

    def finish(self):
        for s in range(1, self.spot.nz):
            for sends, _, copy in self.copies(s):
                pl.when(sends)(copy.wait_send)

    def newest(self, s):
        p, nz = self.spot, self.spot.nz
        return (
            (p.z >= s, lax.rem(p.z - s + nz, nz)),
            (p.z <= nz - 1 - s, lax.rem(p.z + s, nz)),
        )


class LineScatter:
    def __init__(self, spot, parts, up, down, send, recv):
        self.spot, self.parts, self.up, self.down = spot, parts, up, down
        self.send, self.recv = send, recv

    def copies(self, t):
        p, nz = self.spot, self.spot.nz
        k = nz - t
        up = remote(
            self.parts(lax.rem(p.z + k, nz)),
            self.up.at[t - 1],
            self.send.at[0, t],
            self.recv.at[0, t],
            p.device(z=lax.rem(p.z + 1, nz)),
        )
        down = remote(
            self.parts(lax.rem(p.z - k + nz, nz)),
            self.down.at[t - 1],
            self.send.at[1, t],
            self.recv.at[1, t],
            p.device(z=lax.rem(p.z + nz - 1, nz)),
        )
        return (
            (p.z <= nz - 1 - k, (p.z >= 1) & (p.z <= t), up),
            (p.z >= k, (p.z <= nz - 2) & (p.z >= nz - 1 - t), down),
        )

    def start(self, t):
        for sends, _, copy in self.copies(t):
            pl.when(sends)(copy.start)

    def arrive(self, t):
        p, nz = self.spot, self.spot.nz
        k = nz - t
        for way, (_, receives, copy) in enumerate(self.copies(t)):

            @pl.when(receives)
            def _(way=way, copy=copy):
                copy.wait_recv()
                if t < nz - 1:
                    index = lax.rem(p.z + k - 1, nz) if way == 0 else lax.rem(p.z - k + 1 + nz, nz)
                    came = (self.up if way == 0 else self.down).at[t - 1]
                    add_rows(self.parts(index), self.parts(index), came)

    def finish(self):
        for t in range(1, self.spot.nz):
            for sends, _, copy in self.copies(t):
                pl.when(sends)(copy.wait_send)

    def total(self, out):
        p, last = self.spot, self.spot.nz - 2
        mine = self.parts(p.z)
        inner = (p.z > 0) & (p.z < p.nz - 1)

        @pl.when(p.z == 0)
        def _():
            add_rows(out, mine, self.down.at[last])

        @pl.when(p.z == p.nz - 1)
        def _():
            add_rows(out, mine, self.up.at[last])

        step = row_step(out.shape[0])

        @pl.when(inner)
        def _():
            @pl.loop(0, out.shape[0] // step)
            def _(i):
                at = pl.ds(pl.multiple_of(i * step, step), step)
                sides = self.up[last, at, :].astype(f32) + self.down[last, at, :].astype(f32)
                out[at, :] = (mine[at, :].astype(f32) + sides).astype(out.dtype)


class Task:
    ins = ()
    outs = ()
    scratch = ()
    vmem_ins = ()
    vmem_outs = ()
    spare = 5

    def steps(self, p, ins, outs, scratch):
        raise NotImplementedError


class PlaneGather(Task):
    vmem_ins = (0,)
    vmem_outs = (0,)

    def __init__(self, own):
        self.ins = (own,)
        self.outs = (jax.ShapeDtypeStruct((4,) + own.shape, bf16),)
        self.scratch = (DMA((4,)), DMA((4,)), DMA)

    def steps(self, p, ins, outs, scratch):
        (own,), (whole,), (send, recv, local) = ins, outs, scratch
        part = 2 * p.y + p.c
        keep = pltpu.make_async_copy(own, whole.at[part], local)
        copies = []
        for i, (dx, dy) in enumerate([(1, 0), (0, 1), (1, 1), (0, 0)]):
            target = p.device(x=flip(p.x, dx), y=flip(p.y, dy), c=p.x)
            copies.append(remote(own, whole.at[part], send.at[i], recv.at[part], target))
        *away, home = copies
        for copy in away:
            copy.start()
        pl.when(p.c == p.x)(keep.start)
        pl.when(p.c != p.x)(home.start)
        yield
        for copy in away:
            copy.wait_send()
        pl.when(p.c == p.x)(keep.wait)
        pl.when(p.c != p.x)(home.wait_send)
        for slot in range(4):
            came = remote(own, whole.at[slot], send.at[0], recv.at[slot], p.partner())
            mine = (p.c == p.x) & (part == slot)
            pl.when(jnp.logical_not(mine))(came.wait_recv)


class PlaneScatter(Task):
    vmem_ins = (0,)
    vmem_outs = (0,)

    def __init__(self, partial):
        rows, depth = partial.shape[0] // 4, partial.shape[1]
        self.ins = (partial.reshape(4, rows, depth),)
        self.outs = (jax.ShapeDtypeStruct((rows, depth), f32),)
        self.scratch = (pltpu.VMEM((4, rows, depth), bf16), DMA((4,)), DMA((4,)))

    def steps(self, p, ins, outs, scratch):
        (parts,), (out,), (came, send, recv) = ins, outs, scratch
        head, ours = 2 * p.y + p.x, 2 * p.y + p.c

        def copy_to(part):
            target = p.device(x=p.c, y=part // 2, c=part % 2)
            return remote(parts.at[part], came.at[head], send.at[part], recv.at[head], target)

        for part in range(4):
            here = (p.x == p.c) & (part == ours)
            pl.when(jnp.logical_not(here))(copy_to(part).start)
        yield
        for part in range(4):
            here = (p.x == p.c) & (part == ours)
            pl.when(jnp.logical_not(here))(copy_to(part).wait_send)
            arrived = remote(parts.at[part], came.at[part], send.at[part], recv.at[part], p.partner())
            mine = (p.x == p.c) & (part == head)
            pl.when(jnp.logical_not(mine))(arrived.wait_recv)

        @pl.when(p.x == p.c)
        def _():
            came[head] = parts[ours]

        @pl.loop(0, out.shape[0] // 16)
        def _(i):
            at = pl.ds(pl.multiple_of(i * 16, 16), 16)
            low = came[0, at, :].astype(f32) + came[1, at, :].astype(f32)
            out[at, :] = low + (came[2, at, :].astype(f32) + came[3, at, :].astype(f32))


class PairGather(Task):
    vmem_ins = (0,)
    vmem_outs = (0,)

    def __init__(self, nz, own, trade):
        self.trade = trade
        self.ins = (own,)
        self.outs = (jax.ShapeDtypeStruct((nz, 2) + own.shape, bf16),)
        self.scratch = (DMA((2, nz)), DMA((2, nz)), DMA((nz,)), DMA((nz,)), DMA, DMA, DMA)

    def steps(self, p, ins, outs, scratch):
        (own,), (full,), (send, recv, x_send, x_recv, t_send, t_recv, local) = ins, outs, scratch
        nz = p.nz
        keep = pltpu.make_async_copy(own, full.at[p.z, p.c], local)
        line = LineGather(p, lambda z: full.at[z, p.c], send, recv)

        def across(z):
            here = full.at[z, p.c]
            return remote(here, here, x_send.at[z], x_recv.at[z], p.partner())

        if self.trade:
            same = p.c == p.x
            move = remote(own, full.at[p.z, p.x], t_send, t_recv, p.device(x=1 - p.x, c=1 - p.c))
            pl.when(same)(keep.start)
            pl.when(jnp.logical_not(same))(move.start)
            yield
            pl.when(same)(keep.wait)
            pl.when(jnp.logical_not(same))(move.wait_recv)
        else:
            keep.start()
            keep.wait()
        line.start(1)
        across(p.z).start()
        yield
        for s in range(1, nz):
            line.arrive(s)
            if s < nz - 1:
                line.start(s + 1)
            for came, z in line.newest(s):
                pl.when(came)(across(z).start)
            yield
        line.finish()
        if self.trade:
            pl.when(jnp.logical_not(same))(move.wait_send)
        for z in range(nz):
            across(z).wait()


class ZGather(Task):
    vmem_ins = (0,)
    vmem_outs = (0,)

    def __init__(self, nz, own):
        self.ins = (own,)
        self.outs = (jax.ShapeDtypeStruct((nz,) + own.shape, bf16),)
        self.scratch = (DMA((2, nz)), DMA((2, nz)), DMA)

    def steps(self, p, ins, outs, scratch):
        (own,), (full,), (send, recv, local) = ins, outs, scratch
        line = LineGather(p, lambda z: full.at[z], send, recv)
        keep = pltpu.make_async_copy(own, full.at[p.z], local)
        keep.start()
        keep.wait()
        line.start(1)
        yield
        for s in range(1, p.nz):
            line.arrive(s)
            if s < p.nz - 1:
                line.start(s + 1)
            yield
        line.finish()


class ZScatter(Task):
    vmem_outs = (0,)

    def __init__(self, nz, partial):
        rows, depth = partial.shape[0] // nz, partial.shape[1]
        self.ins = (partial.reshape(nz, rows, depth),)
        self.outs = (jax.ShapeDtypeStruct((rows, depth), f32),)
        line = pltpu.VMEM((nz - 1, rows, depth), bf16)
        self.scratch = (
            pltpu.VMEM((nz, rows, depth), bf16), line, line, DMA((2, nz)), DMA((2, nz)), DMA
        )

    def steps(self, p, ins, outs, scratch):
        (given,), (out,), (parts, up, down, send, recv, local) = ins, outs, scratch
        bring = pltpu.make_async_copy(given, parts, local)
        bring.start()
        bring.wait()
        line = LineScatter(p, lambda z: parts.at[z], up, down, send, recv)
        line.start(1)
        yield
        for t in range(1, p.nz):
            line.arrive(t)
            if t < p.nz - 1:
                line.start(t + 1)
            yield
        line.total(out)
        line.finish()


class PairScatter(Task):
    vmem_outs = (0,)

    def __init__(self, nz, given, trade):
        _, _, rows, width = given.shape
        self.trade = trade
        self.ins = (given,)
        self.outs = (jax.ShapeDtypeStruct((rows, width), bf16),)
        whole = pltpu.VMEM((nz, rows, width), bf16)
        line = pltpu.VMEM((nz - 1, rows, width), bf16)
        self.scratch = (
            whole, whole, line, line,
            DMA((nz,)), DMA((nz,)), DMA((2, nz)), DMA((2, nz)), DMA((nz,)), DMA, DMA, DMA,
        )

    def steps(self, p, ins, outs, scratch):
        (given,), (out,) = ins, outs
        parts, came, up, down, x_send, x_recv, send, recv, local, b_send, b_recv, b_local = scratch
        nz = p.nz
        order = [exclusive_or(p.z, i) for i in (3, 2, 1, 0)]

        def away(z):
            return remote(given.at[z, 1 - p.c], came.at[z], x_send.at[z], x_recv.at[z], p.partner())

        def bring(z):
            return pltpu.make_async_copy(given.at[z, p.c], parts.at[z], local.at[z])

        for z in order:
            away(z).start()
            bring(z).start()
        yield
        for z in order:
            away(z).wait_recv()
            bring(z).wait()
            add_rows(parts.at[z], parts.at[z], came.at[z])
        line = LineScatter(p, lambda z: parts.at[z], up, down, send, recv)
        line.start(1)
        yield
        for t in range(1, nz):
            line.arrive(t)
            if t < nz - 1:
                line.start(t + 1)
            yield
        if not self.trade:
            line.total(out)
        else:
            line.total(came.at[0])
            same = p.c == p.x
            back = remote(came.at[0], out, b_send, b_recv, p.device(x=1 - p.x, c=1 - p.c))
            keep = pltpu.make_async_copy(came.at[0], out, b_local)
            pl.when(same)(keep.start)
            pl.when(jnp.logical_not(same))(back.start)
            yield
            pl.when(same)(keep.wait)
            pl.when(jnp.logical_not(same))(back.wait)
        for z in order:
            away(z).wait_send()
        line.finish()


class Deal:
    def __init__(self, p, shard, place, quarter, send, recv):
        self.p, self.shard, self.place, self.quarter = p, shard, place, quarter
        self.send, self.recv = send, recv
        self.per_core = p.nz // 2

    def piece(self, piece, half):
        columns = pl.ds(piece * self.quarter, self.quarter)
        return self.shard.at[half, :, columns]

    def away(self, piece, half):
        p = self.p
        z = p.c * self.per_core + piece
        return z, remote(
            self.piece(piece, half),
            self.place(p.z, half),
            self.send.at[2 * piece + half],
            self.recv.at[p.z],
            p.device(z=z, c=half),
        )

    def local(self, piece):
        p = self.p
        columns = pl.ds(piece * self.quarter, self.quarter)
        return pltpu.make_async_copy(
            self.shard.at[p.c, :, columns], self.place(p.z, p.c), self.recv.at[p.z]
        )

    def start(self, in_plane):
        p = self.p
        for piece in range(self.per_core):
            for half in range(2):
                z, copy = self.away(piece, half)
                if in_plane:
                    pl.when((z == p.z) & (p.c != half))(copy.start)
                    pl.when((z == p.z) & (p.c == half))(self.local(piece).start)
                else:
                    pl.when(z != p.z)(copy.start)

    def arrive(self, source):
        p = self.p
        here = self.place(source, p.c)
        ours = (source == p.z) & (p.c == p.z // self.per_core)
        came = remote(here, here, self.send.at[0], self.recv.at[source], p.partner())
        pl.when(jnp.logical_not(ours))(came.wait_recv)
        pl.when(ours)(self.local(0).wait)

    def finish(self):
        p = self.p
        for piece in range(self.per_core):
            for half in range(2):
                z, copy = self.away(piece, half)
                here = (z == p.z) & (p.c == half)
                pl.when(jnp.logical_not(here))(copy.wait_send)


class DealTask(Task):
    vmem_outs = (0,)

    def __init__(self, nz, shard):
        rows, units = shard.shape
        self.ins = (shard.reshape(2, rows // 2, units),)
        self.outs = (jax.ShapeDtypeStruct((nz, rows // 2, 2 * units // nz), bf16),)
        self.scratch = (DMA((nz,)), DMA((nz,)))

    def steps(self, p, ins, outs, scratch):
        (shard,), (pieces,), (send, recv) = ins, outs, scratch
        deal = Deal(p, shard, lambda z, half: pieces.at[z], pieces.shape[-1], send, recv)
        deal.start(False)
        deal.start(True)
        yield
        for i in range(p.nz):
            deal.arrive(exclusive_or(p.z, i))
        deal.finish()


class Copies(Task):
    vmem_outs = (0,)

    def __init__(self, nz, given, dealt):
        self.dealt = dealt
        if dealt:
            _, half, quarter = given.shape
            self.ins = (given,)
        else:
            rows, units = given.shape
            half, quarter = rows // 2, 2 * units // nz
            self.ins = (given.reshape(2, half, units),)
        self.outs = (jax.ShapeDtypeStruct((nz * 4 * half, 2 * quarter), bf16),)
        self.scratch = copy_sems(nz)

    def steps(self, p, ins, outs, scratch):
        return copy_steps(p, ins[0], outs[0], scratch, self.dealt)


def copy_sems(nz):
    one, two = DMA((nz,)), DMA((nz, 2))
    return (one, one, one, one, two, two, two, two)


def copy_steps(p, given, full, sems, dealt):
    d_send, d_recv, f_send, f_recv, s_send, s_recv, x_send, x_recv = sems
    nz = p.nz
    quarter, half = full.shape[1] // 2, full.shape[0] // (4 * nz)

    def strip(z, x, c):
        return pl.ds(pl.multiple_of(((z * 2 + x) * 2 + c) * half, half), half)

    def place(z, x, c, y):
        return full.at[strip(z, x, c), pl.ds(pl.multiple_of(y * quarter, 128), quarter)]

    fx, fy = p.x + (1 - 2 * p.x) * (1 - p.c), p.y + (1 - 2 * p.y) * p.c
    sx, sy = p.x + (1 - 2 * p.x) * p.c, p.y + (1 - 2 * p.y) * (1 - p.c)

    def own(z):
        return given.at[z] if dealt else place(z, p.x, p.c, p.y)

    def first(z):
        target = p.device(x=fx, y=fy)
        return remote(own(z), place(z, p.x, p.c, p.y), f_send.at[z], f_recv.at[z], target)

    def second(z, which):
        x, y = (fx, fy) if which else (p.x, p.y)
        here = place(z, x, p.c, y)
        src = here if which else own(z)
        target = p.device(x=sx, y=sy)
        return remote(src, here, s_send.at[z, which], s_recv.at[z, which], target)

    def across(z, x):
        here = full.at[strip(z, x, p.c)]
        return remote(here, here, x_send.at[z, x], x_recv.at[z, x], p.partner())

    def keep(z):
        return pltpu.make_async_copy(given.at[z], place(z, p.x, p.c, p.y), d_send.at[z])

    order = [exclusive_or(p.z, i) for i in range(nz)]
    if dealt:
        for z in order:
            first(z).start()
            second(z, 0).start()
            keep(z).start()
        for z in order:
            keep(z).wait()
        yield
    else:
        deal = Deal(p, given, lambda z, c: place(z, p.x, c, p.y), quarter, d_send, d_recv)
        deal.start(True)
        yield
        deal.arrive(order[0])
        first(order[0]).start()
        second(order[0], 0).start()
        yield
        deal.start(False)
        yield
        for z in order[1:]:
            deal.arrive(z)
            first(z).start()
            second(z, 0).start()
            yield
    for z in order:
        first(z).wait_recv()
        second(z, 1).start()
        yield
    for z in order:
        second(z, 0).wait_recv()
        second(z, 1).wait_recv()
        across(z, 0).start()
        across(z, 1).start()
        yield
    for z in range(nz):
        first(z).wait_send()
        for i in range(2):
            second(z, i).wait_send()
            across(z, i).wait()
    if not dealt:
        deal.finish()


class DealBack:
    def __init__(self, p, source, out, quarter, send, recv):
        self.p, self.source, self.out, self.quarter = p, source, out, quarter
        self.send, self.recv = send, recv
        self.per_core = p.nz // 2
        self.owner = p.z // self.per_core

    def out_at(self, z, half):
        start = pl.multiple_of(lax.rem(z, self.per_core) * self.quarter, 128)
        return self.out.at[half, :, pl.ds(start, self.quarter)]

    def away(self, z):
        p = self.p
        return remote(
            self.source(z),
            self.out_at(p.z, p.c),
            self.send.at[z],
            self.recv.at[2 * lax.rem(p.z, self.per_core) + p.c],
            p.device(z=z, c=self.owner),
        )

    def keep(self, z):
        p = self.p
        return pltpu.make_async_copy(
            self.source(z),
            self.out_at(p.z, p.c),
            self.recv.at[2 * lax.rem(p.z, self.per_core) + p.c],
        )

    def start(self, z):
        p = self.p
        here = (z == p.z) & (p.c == self.owner)
        pl.when(jnp.logical_not(here))(self.away(z).start)
        pl.when(here)(self.keep(z).start)

    def finish(self):
        p = self.p
        for piece in range(self.per_core):
            for half in range(2):
                z = p.c * self.per_core + piece
                place = self.out_at(z, half)
                came = remote(
                    place, place, self.send.at[0], self.recv.at[2 * piece + half], p.partner()
                )
                ours = (z == p.z) & (p.c == half)
                pl.when(jnp.logical_not(ours))(came.wait_recv)
        for z in range(p.nz):
            here = (z == p.z) & (p.c == self.owner)
            pl.when(jnp.logical_not(here))(self.away(z).wait_send)
            pl.when(here)(self.keep(z).wait)


class DealBackTask(Task):
    vmem_outs = (0,)

    def __init__(self, nz, sums):
        _, half, quarter = sums.shape
        self.ins = (sums,)
        self.outs = (jax.ShapeDtypeStruct((2, half, nz // 2 * quarter), bf16),)
        self.scratch = (DMA((nz,)), DMA((nz,)))

    def steps(self, p, ins, outs, scratch):
        (sums,), (out,), (send, recv) = ins, outs, scratch
        deal = DealBack(p, lambda z: sums.at[z], out, sums.shape[-1], send, recv)
        for i in (3, 2, 1, 0):
            deal.start(exclusive_or(p.z, i))
        yield
        deal.finish()


class Sums(Task):
    def __init__(self, nz, grad, deal):
        depth, width = grad.shape
        half, quarter = depth // (4 * nz), width // 2
        self.deal = deal
        self.ins = (grad.reshape(nz, 2, 2, half, width),)
        if deal:
            self.outs = (jax.ShapeDtypeStruct((2, half, nz // 2 * quarter), bf16),)
        else:
            self.outs = (jax.ShapeDtypeStruct((nz, half, quarter), bf16),)
            self.vmem_outs = (0,)
        whole = pltpu.VMEM((nz, 2, half, width), bf16)
        self.scratch = (
            whole,
            whole,
            pltpu.VMEM((nz, 2, half, quarter), bf16),
            pltpu.VMEM((nz, half, quarter), bf16),
            DMA((nz, 2)), DMA((nz, 2)), DMA((nz, 2)), DMA((nz, 2)), DMA((nz, 2)),
            DMA((nz,)), DMA((nz,)), DMA((nz,)), DMA((nz,)),
        )

    def steps(self, p, ins, outs, scratch):
        (given,), (out,) = ins, outs
        mine, came, first_in, second_in, *sems = scratch
        local, c_send, c_recv, f_send, f_recv, s_send, s_recv, d_send, d_recv = sems
        nz, quarter = p.nz, given.shape[4] // 2
        order = [exclusive_or(p.z, i) for i in (3, 2, 1, 0)]

        def bring(z, x):
            return pltpu.make_async_copy(given.at[z, x, p.c], mine.at[z, x], local.at[z, x])

        def across(z, x):
            src = given.at[z, x, 1 - p.c]
            return remote(src, came.at[z, x], c_send.at[z, x], c_recv.at[z, x], p.partner())

        def place(z, x, y):
            return mine.at[z, x, :, pl.ds(pl.multiple_of(y * quarter, 128), quarter)]

        fx, fy = p.x + (1 - 2 * p.x) * p.c, p.y + (1 - 2 * p.y) * (1 - p.c)
        sx, sy = p.x + (1 - 2 * p.x) * (1 - p.c), p.y + (1 - 2 * p.y) * p.c

        def first(z, which):
            x, y = (1 - p.x, 1 - p.y) if which else (fx, fy)
            target = p.device(x=fx, y=fy)
            return remote(
                place(z, x, y), first_in.at[z, which], f_send.at[z, which], f_recv.at[z, which], target
            )

        def second(z):
            target = p.device(x=sx, y=sy)
            return remote(place(z, sx, sy), second_in.at[z], s_send.at[z], s_recv.at[z], target)

        back = DealBack(p, lambda z: place(z, p.x, p.y), out, quarter, d_send, d_recv)
        for z in order:
            for x in range(2):
                across(z, x).start()
                bring(z, x).start()
        yield
        for z in order:
            for x in range(2):
                across(z, x).wait_recv()
                bring(z, x).wait()
                add_rows(mine.at[z, x], mine.at[z, x], came.at[z, x])
            for which in (1, 0):
                first(z, which).start()
            yield
        for i in range(nz + 1):
            if i < nz:
                z = order[i]
                for which in (1, 0):
                    at = place(z, sx, sy) if which else place(z, p.x, p.y)
                    first(z, which).wait_recv()
                    add_rows(at, at, first_in.at[z, which])
                    if which:
                        second(z).start()
                yield
            if i >= 1:
                z = order[i - 1]
                second(z).wait_recv()
                at = place(z, p.x, p.y)
                if self.deal:
                    add_rows(at, at, second_in.at[z])
                    back.start(z)
                else:
                    add_rows(out.at[z], at, second_in.at[z])
                yield
        if self.deal:
            back.finish()
        for z in range(nz):
            second(z).wait_send()
            for i in range(2):
                first(z, i).wait_send()
                across(z, i).wait_send()


class FeedForward(Task):
    vmem_ins = (0, 1, 2)
    vmem_outs = (0, 1)
    spare = 10

    def __init__(self, nz, own, cotangent, gain, gate, up, down_pieces):
        rows, depth = own.shape
        units = gate.shape[1]
        self.rows, self.depth, self.units = rows, depth, units
        self.ins = (own, cotangent, gain.reshape(1, depth), gate, up, down_pieces)
        wide = jax.ShapeDtypeStruct((depth, units), bf16)
        exact = jax.ShapeDtypeStruct((rows, depth), f32)
        self.outs = (exact, exact, wide, wide, wide)
        weight = pltpu.VMEM((depth, units), bf16)
        tokens = pltpu.VMEM((nz * rows, depth), bf16)
        inner = pltpu.VMEM((nz * rows, units), bf16)
        line = pltpu.VMEM((2, nz - 1, rows // 2, depth), bf16)
        self.scratch = (
            weight, weight, weight, tokens, tokens, inner, inner, inner, tokens, line, line,
            DMA((8, 2, nz)), DMA((8, 2, nz)), DMA((8,)), *copy_sems(nz),
        )

    def steps(self, p, ins, outs, scratch):
        own, cotangent, gain, gate_in, up_in, down_in = ins
        ff_out, dn_out, grad_gate, grad_up, grad_down = outs
        gate, up, down, normed, d_ff, hidden, gated, upped, parts, above, below, *sems = scratch
        send, recv, local, *down_sems = sems
        copies = copy_steps(p, down_in, down, down_sems, True)
        nz, depth, units = p.nz, self.depth, self.units
        part = self.rows // 2
        half_rows = nz * part
        tile = units // 3

        def entry(buffer, half):
            return lambda z: buffer.at[pl.ds(pl.multiple_of(half * half_rows + z * part, part), part)]

        gathers, scatters = [], []
        for i, buffer in enumerate((normed, d_ff)):
            for half in range(2):
                k = 4 * i + half
                gathers.append(LineGather(p, entry(buffer, half), send.at[k], recv.at[k]))
                scatters.append(
                    LineScatter(
                        p, entry(parts, half), above.at[half], below.at[half], send.at[k + 2], recv.at[k + 2]
                    )
                )

        loads = [
            pltpu.make_async_copy(src, dst, local.at[i])
            for i, (src, dst) in enumerate(((gate_in, gate), (up_in, up)))
        ]

        def gelu(v):
            bent = jnp.tanh(math.sqrt(2.0 / math.pi) * (v + 0.044715 * (v * v * v)))
            return 0.5 * v * (1.0 + bent), bent

        def columns(i):
            return pl.ds(pl.multiple_of(i * tile, 128), tile)

        def hide(half, low, high):
            rows = slice(half * half_rows, (half + 1) * half_rows)

            @pl.loop(low, high)
            def _(i):
                at = columns(i)
                gate_lin = jnp.dot(normed[rows, :], gate[:, at], preferred_element_type=f32)
                up_lin = jnp.dot(normed[rows, :], up[:, at], preferred_element_type=f32)
                hidden[rows, at] = (gelu(gate_lin)[0] * up_lin).astype(bf16)
                gated[rows, at] = gate_lin.astype(bf16)
                upped[rows, at] = up_lin.astype(bf16)

        def project(half):
            rows = slice(half * half_rows, (half + 1) * half_rows)

            @pl.loop(0, depth // tile)
            def _(i):
                at = columns(i)
                parts[rows, at] = contract(hidden[rows, :], down[at, :], 1, 1).astype(bf16)

        def hide_back(half, low, high):
            rows = slice(half * half_rows, (half + 1) * half_rows)

            @pl.loop(low, high)
            def _(i):
                at = columns(i)
                d_hidden = jnp.dot(d_ff[rows, :], down[:, at], preferred_element_type=f32)
                v, u = gated[rows, at].astype(f32), upped[rows, at].astype(f32)
                value, bent = gelu(v)
                slope = 0.5 * (1.0 + bent) + (0.5 * math.sqrt(2.0 / math.pi)) * v * (
                    1.0 - bent * bent
                ) * (1.0 + (3.0 * 0.044715) * (v * v))
                gated[rows, at] = (d_hidden * u * slope).astype(bf16)
                upped[rows, at] = (d_hidden * value).astype(bf16)

        def project_back(half):
            rows = slice(half * half_rows, (half + 1) * half_rows)

            @pl.loop(0, depth // tile)
            def _(i):
                at = columns(i)
                total = contract(gated[rows, :], gate[at, :], 1, 1)
                parts[rows, at] = (total + contract(upped[rows, :], up[at, :], 1, 1)).astype(bf16)

        def turn_back(half):
            start = half * half_rows + p.z * part

            @pl.loop(0, part // 16)
            def _(i):
                at = pl.ds(pl.multiple_of(half * part + i * 16, 16), 16)
                values = ff_out[at, :]
                scaled = cotangent[at, :].astype(f32) * (1.0 + gain[...])
                factor = factor_of(values)
                unit = values * factor
                mean = jnp.mean(scaled * unit, axis=-1, keepdims=True)
                here = pl.ds(pl.multiple_of(start + i * 16, 16), 16)
                d_ff[here, :] = ((scaled - unit * mean) * factor).astype(bf16)

        def weigh(left, right, out, low, high):
            @pl.loop(low, high)
            def _(i):
                at = pl.ds(pl.multiple_of(i * 256, 128), 256)
                out[at, :] = contract(left[:, at], right[...], 0, 0).astype(bf16)

        def store(i, src, dst):
            return pltpu.make_async_copy(src, dst, local.at[3 + i])

        blocks = depth // 256
        one, two, one_back, two_back = gathers
        sum_one, sum_two, sum_one_back, sum_two_back = scatters
        keep = [
            pltpu.make_async_copy(own.at[pl.ds(half * part, part)], entry(normed, half)(p.z), local.at[6 + half])
            for half in range(2)
        ]
        keep[0].start()
        keep[1].start()
        keep[0].wait()
        one.start(1)
        keep[1].wait()
        next(copies)
        for load in loads:
            load.start()
        one.arrive(1)
        one.start(2)
        two.start(1)
        one.arrive(2)
        one.start(3)
        for _ in range(nz):
            next(copies)
        one.arrive(3)
        two.arrive(1)
        two.start(2)
        for load in loads:
            load.wait()
        hide(0, 0, 1)
        two.arrive(2)
        two.start(3)
        hide(0, 1, 3)
        two.arrive(3)
        hide(1, 0, 1)
        for _ in copies:
            pass
        project(0)
        sum_one.start(1)
        hide(1, 1, 3)
        sum_one.arrive(1)
        sum_one.start(2)
        project(1)
        sum_two.start(1)
        sum_one.arrive(2)
        sum_one.start(3)
        sum_two.arrive(1)
        sum_two.start(2)
        sum_one.arrive(3)
        sum_one.total(ff_out.at[pl.ds(0, part)])
        turn_back(0)
        one_back.start(1)
        sum_two.arrive(2)
        sum_two.start(3)
        one_back.arrive(1)
        one_back.start(2)
        sum_two.arrive(3)
        sum_two.total(ff_out.at[pl.ds(part, part)])
        turn_back(1)
        one_back.arrive(2)
        one_back.start(3)
        two_back.start(1)
        one_back.arrive(3)
        hide_back(0, 0, 3)
        two_back.arrive(1)
        two_back.start(2)
        sum_one.finish()
        project_back(0)
        sum_one_back.start(1)
        two_back.arrive(2)
        two_back.start(3)
        two_back.arrive(3)
        hide_back(1, 0, 3)
        sum_one_back.arrive(1)
        sum_one_back.start(2)
        sum_two.finish()
        project_back(1)
        sum_two_back.start(1)
        weigh(d_ff, hidden, down, 0, blocks)
        store(0, down, grad_down).start()
        sum_one_back.arrive(2)
        sum_two_back.arrive(1)
        sum_two_back.start(2)
        sum_one_back.start(3)
        weigh(normed, gated, gate, 0, blocks)
        store(1, gate, grad_gate).start()
        sum_two_back.arrive(2)
        sum_two_back.start(3)
        weigh(normed, upped, up, 0, blocks)
        store(2, up, grad_up).start()
        sum_one_back.arrive(3)
        sum_one_back.total(dn_out.at[pl.ds(0, part)])
        sum_two_back.arrive(3)
        sum_two_back.total(dn_out.at[pl.ds(part, part)])
        for gather in gathers:
            gather.finish()
        sum_one_back.finish()
        sum_two_back.finish()
        store(0, down, grad_down).wait()
        store(1, gate, grad_gate).wait()
        store(2, up, grad_up).wait()
        yield


class SumAll(Task):
    vmem_ins = (0,)
    vmem_outs = (0,)

    def __init__(self, values):
        self.ins = (values,)
        self.outs = (jax.ShapeDtypeStruct(values.shape, f32),)
        stage = pltpu.VMEM((5,) + values.shape, f32)
        self.scratch = (stage, stage, DMA((5,)), DMA((5,)))

    def steps(self, p, ins, outs, scratch):
        (given,), (out,), (stage, came, send, recv) = ins, outs, scratch
        targets = [
            p.partner(),
            p.device(y=1 - p.y),
            p.device(x=1 - p.x),
            p.device(z=exclusive_or(p.z, 1)),
            p.device(z=exclusive_or(p.z, 2)),
        ]
        stage[0] = given[...]
        for i, target in enumerate(targets):
            copy = remote(stage.at[i], came.at[i], send.at[i], recv.at[i], target)
            copy.start()
            yield
            copy.wait()
            total = stage[i] + came[i]
            if i < 4:
                stage[i + 1] = total
            else:
                out[...] = total


def run_tasks(nz, number, tasks, order=""):
    counts = [(len(t.ins), len(t.outs), len(t.scratch)) for t in tasks]

    def split(refs, which):
        found = []
        for count in counts:
            found.append(refs[: count[which]])
            refs = refs[count[which] :]
        return found, refs

    def body(*refs):
        ins, refs = split(refs, 0)
        outs, refs = split(refs, 1)
        scratch, refs = split(refs, 2)
        p = Spot(nz)
        p.greet()
        running = [t.steps(p, *given) for t, *given in zip(tasks, ins, outs, scratch)]
        done = [False] * len(tasks)
        for digit in order:
            i = int(digit)
            if not done[i]:
                done[i] = next(running[i], "end") == "end"
        while not all(done):
            for i, steps in enumerate(running):
                if not done[i]:
                    done[i] = next(steps, "end") == "end"

    sent = sum(x.size * 2 for t in tasks for x in t.ins)
    spare = max(t.spare for t in tasks) * 2**20
    held = [s for t in tasks for s in t.scratch if getattr(s, "memory_space", None) == pltpu.VMEM]
    held += [t.ins[i] for t in tasks for i in t.vmem_ins] + [t.outs[i] for t in tasks for i in t.vmem_outs]
    vmem = sum(math.prod(s.shape) * jnp.dtype(s.dtype).itemsize for s in held)
    results = pl.pallas_call(
        body,
        out_shape=[o for t in tasks for o in t.outs],
        in_specs=[in_vmem if i in t.vmem_ins else anywhere for t in tasks for i in range(len(t.ins))],
        out_specs=[
            in_vmem if i in t.vmem_outs else anywhere for t in tasks for i in range(len(t.outs))
        ],
        scratch_shapes=[s for t in tasks for s in t.scratch],
        compiler_params=pltpu.CompilerParams(
            collective_id=number, has_side_effects=True, vmem_limit_bytes=vmem + spare
        ),
        cost_estimate=pl.CostEstimate(
            flops=0, bytes_accessed=sent, transcendentals=0, remote_bytes_transferred=sent
        ),
    )(*[x for t in tasks for x in t.ins])
    found, _ = split(list(results), 1)
    return found[0] if len(tasks) == 1 else [f[0] for f in found]


START_ORDER = "10212" + "23" + "1222" + "12222" + "3" + "12222"
FINISH_ORDER = "01203111" + "1112" + "03112" + "11220" + "3112" + "2220" + "32222"
KV_ORDER = "0120" + "12" + "2" + "20" + "12222" + "01" + "222201" + "2222"


class Kernels:
    def __init__(self, at):
        self.at = at
        self.blocks, self.nz = at.blocks, at.nz
        self.block = 2 * at.z + at.c
        self.number = 0

    def run(self, tasks, order=""):
        self.number += 1
        return run_tasks(self.nz, self.number, tasks, order)

    def flat(self, whole):
        return whole.reshape(-1, whole.shape[-1])

    def start(self, own, qkv_shard, gate, up):
        nz = self.nz
        tasks = [
            PlaneGather(own),
            PairGather(nz, qkv_shard, True),
            Copies(nz, gate, False),
            DealTask(nz, up),
        ]
        rows, qkv, gate_full, pieces = self.run(tasks, START_ORDER)
        return self.flat(rows), self.flat(qkv), gate_full, pieces

    def gather_kv(self, own, out_shard, pieces):
        nz = self.nz
        whole, out, up = self.run(
            [PairGather(nz, own, False), PairGather(nz, out_shard, True), Copies(nz, pieces, True)],
            "1021" + "0101" + "2222" + "01" + "2222",
        )
        return whole.reshape((self.blocks,) + own.shape), self.flat(out), up

    def scatter_heads(self, partial, down):
        return self.run([PlaneScatter(partial), DealTask(self.nz, down)], "01")

    def feed_forward(self, own, cotangent, gain, gate, up, down):
        task = FeedForward(self.nz, own, cotangent, gain, gate, up, down)
        self.number += 1
        return run_tasks(self.nz, self.number, [task])

    def gather_heads(self, own):
        return self.flat(self.run([PlaneGather(own)])[0])

    def scatter_kv_sums(self, parts, out_grad, grad):
        nz = self.nz
        given = parts.reshape((nz, 2) + parts.shape[1:])
        rows = out_grad.shape[0] // self.blocks
        out_given = out_grad.reshape(nz, 2, rows, out_grad.shape[1])
        kv, out, sums = self.run(
            [PairScatter(nz, given, False), PairScatter(nz, out_given, True), Sums(nz, grad, False)],
            KV_ORDER,
        )
        return kv, out, sums

    def scatter_heads_back(self, partial, sums):
        rows, shard = self.run([PlaneScatter(partial), DealBackTask(self.nz, sums)], "01")
        return rows, self.flat(shard)

    def finish(self, qkv_grad, gate_grad, up_grad, gains):
        rows = qkv_grad.shape[0] // self.blocks
        given = qkv_grad.reshape(self.nz, 2, rows, qkv_grad.shape[1])
        qkv, gate, up, total = self.run(
            [
                PairScatter(self.nz, given, True),
                Sums(self.nz, gate_grad, True),
                Sums(self.nz, up_grad, True),
                SumAll(gains.reshape(8, -1)),
            ],
            FINISH_ORDER,
        )
        return qkv, self.flat(gate), self.flat(up), total.reshape(gains.shape)


def project_kernel(info, normed_ref, weight_ref, q_ref, kv_ref, cos_ref, sin_ref):
    rows, half = cos_ref.shape
    dim = 2 * half
    heads = q_ref.shape[0]
    blocks = (info.shape[0] - 2) // 2
    me, prompts = info[2 * blocks], info[2 * blocks + 1]
    first = jnp.minimum(info[blocks + me], prompts) * rows
    positions = (lax.broadcasted_iota(jnp.int32, (rows, half), 0) + first).astype(f32)
    index = lax.broadcasted_iota(jnp.int32, (rows, half), 1).astype(f32)
    angles = positions * jnp.exp(index * (-2.0 * math.log(10000.0) / dim))
    cos_ref[...] = jnp.cos(angles)
    sin_ref[...] = jnp.sin(angles)
    for i in range(heads + 2):
        columns = slice(i * dim, (i + 1) * dim)
        linear = jnp.dot(normed_ref[...], weight_ref[:, columns], preferred_element_type=f32)
        if i <= heads:
            linear = rotate(linear, cos_ref[...], sin_ref[...])
        if i < heads:
            q_ref[i] = linear.astype(bf16)
        else:
            kv_ref[:, (i - heads) * dim : (i - heads + 1) * dim] = linear.astype(bf16)


def project(info, normed, weight):
    rows = normed.shape[0]
    heads = weight.shape[1] // HEAD_DIM - 2
    table = jax.ShapeDtypeStruct((rows, HEAD_DIM // 2), f32)
    return pl.pallas_call(
        project_kernel,
        in_specs=[pl.BlockSpec(memory_space=pltpu.SMEM), in_vmem, in_vmem],
        out_specs=[in_vmem] * 4,
        out_shape=[
            jax.ShapeDtypeStruct((heads, rows, HEAD_DIM), bf16),
            jax.ShapeDtypeStruct((rows, 2 * HEAD_DIM), bf16),
            table,
            table,
        ],
        compiler_params=pltpu.CompilerParams(vmem_limit_bytes=24 * 2**20),
        cost_estimate=pl.CostEstimate(
            flops=2 * rows * weight.size, bytes_accessed=2 * weight.size, transcendentals=0
        ),
    )(info, normed, weight)


def project_back_kernel(dq_ref, dkv_ref, cos_ref, sin_ref, weight_ref, lin_ref, out_ref):
    heads, rows, dim = dq_ref.shape
    cosine, sine = cos_ref[...], -sin_ref[...]
    for i in range(heads):
        lin_ref[:, i * dim : (i + 1) * dim] = rotate(dq_ref[i], cosine, sine).astype(bf16)
    start = heads * dim
    d_key = rotate(dkv_ref[:, :dim].astype(f32), cosine, sine)
    lin_ref[:, start : start + dim] = d_key.astype(bf16)
    lin_ref[:, start + dim :] = dkv_ref[:, dim:].astype(bf16)
    depth = weight_ref.shape[0]
    tile = 384

    @pl.loop(0, depth // tile)
    def _(i):
        at = pl.ds(pl.multiple_of(i * tile, 128), tile)
        out_ref[:, at] = contract(lin_ref[...], weight_ref[at, :], 1, 1).astype(bf16)


def project_back(d_query, d_kv, cosine, sine_table, weight):
    rows = d_kv.shape[0]
    depth, width = weight.shape
    return pl.pallas_call(
        project_back_kernel,
        in_specs=[in_vmem] * 5,
        out_specs=[in_vmem] * 2,
        out_shape=[
            jax.ShapeDtypeStruct((rows, width), bf16),
            jax.ShapeDtypeStruct((rows, depth), bf16),
        ],
        compiler_params=pltpu.CompilerParams(vmem_limit_bytes=24 * 2**20),
        cost_estimate=pl.CostEstimate(
            flops=2 * rows * weight.size, bytes_accessed=2 * weight.size, transcendentals=0
        ),
    )(d_query, d_kv, cosine, sine_table, weight)


def causal_mask(rows):
    shape = (rows, rows)
    return lax.broadcasted_iota(jnp.int32, shape, 1) <= lax.broadcasted_iota(jnp.int32, shape, 0)


def kind_of(info, step):
    blocks = pl.num_programs(0)
    me, prompts = info[2 * blocks], info[2 * blocks + 1]
    role = info[blocks + step]
    reads = (info[step] == info[me]) & (role < prompts) & (role < info[blocks + me])
    return jnp.where(step == me, 2, jnp.where(reads, 1, 0))


def forward_kernel(info, q_ref, kv_ref, out_ref, exact_ref, inv_ref, acc, total):
    step, last = pl.program_id(0), pl.num_programs(0) - 1
    heads, rows, dim = q_ref.shape
    kind = kind_of(info, step)

    @pl.when(step == 0)
    def _():
        acc[...] = jnp.zeros_like(acc)
        total[...] = jnp.zeros_like(total)

    def work(own):
        for head in range(heads):
            raw = contract(q_ref[head], kv_ref[0, :, :dim], 1, 1)
            weights = jnp.exp(softcap * jnp.tanh(raw * (score_scale / softcap)))
            if own:
                weights = jnp.where(causal_mask(rows), weights, 0.0)
            total[head] += jnp.sum(weights, axis=-1, keepdims=True)
            acc[head] += contract(weights.astype(bf16), kv_ref[0, :, dim:], 1, 0)

    @pl.when(kind == 1)
    def _():
        work(False)

    @pl.when(kind == 2)
    def _():
        work(True)

    @pl.when(step == last)
    def _():
        for head in range(heads):
            inverse = 1.0 / total[head]
            value = acc[head] * inverse
            inv_ref[head] = inverse
            exact_ref[:, head * dim : (head + 1) * dim] = value
            out_ref[:, head * dim : (head + 1) * dim] = value.astype(bf16)


def whole2(step, info):
    return (0, 0)


def whole3(step, info):
    return (0, 0, 0)


def by_step(step, info):
    return (step, 0, 0)


def attend(info, queries, all_kv):
    heads, rows, dim = queries.shape
    return pl.pallas_call(
        forward_kernel,
        grid_spec=pltpu.PrefetchScalarGridSpec(
            num_scalar_prefetch=1,
            grid=(all_kv.shape[0],),
            in_specs=[
                pl.BlockSpec((heads, rows, dim), whole3),
                pl.BlockSpec((1, rows, 2 * dim), by_step),
            ],
            out_specs=[
                pl.BlockSpec((rows, heads * dim), whole2),
                pl.BlockSpec((rows, heads * dim), whole2),
                pl.BlockSpec((heads, rows, 1), whole3),
            ],
            scratch_shapes=[
                pltpu.VMEM((heads, rows, dim), f32),
                pltpu.VMEM((heads, rows, 1), f32),
            ],
        ),
        out_shape=[
            jax.ShapeDtypeStruct((rows, heads * dim), bf16),
            jax.ShapeDtypeStruct((rows, heads * dim), f32),
            jax.ShapeDtypeStruct((heads, rows, 1), f32),
        ],
        compiler_params=pltpu.CompilerParams(vmem_limit_bytes=24 * 2**20),
        cost_estimate=pl.CostEstimate(
            flops=3 * 4 * heads * rows * rows * dim,
            bytes_accessed=8 * rows * dim * heads,
            transcendentals=6 * heads * rows * rows,
        ),
    )(info, queries, all_kv)


def backward_kernel(info, q_ref, kv_ref, up_ref, exact_ref, inv_ref, dq_ref, dkv_ref):
    step = pl.program_id(0)
    heads, rows, dim = q_ref.shape
    kind = kind_of(info, step)

    @pl.when(step == 0)
    def _():
        dq_ref[...] = jnp.zeros_like(dq_ref)

    def work(own):
        dk = jnp.zeros((rows, dim), f32)
        dv = jnp.zeros((rows, dim), f32)
        for head in range(heads):
            columns = slice(head * dim, (head + 1) * dim)
            up = up_ref[:, columns]
            delta = jnp.sum(up.astype(f32) * exact_ref[:, columns], axis=-1, keepdims=True)
            raw = contract(q_ref[head], kv_ref[0, :, :dim], 1, 1)
            bounded = jnp.tanh(raw * (score_scale / softcap))
            probs = jnp.exp(softcap * bounded) * inv_ref[head]
            if own:
                probs = jnp.where(causal_mask(rows), probs, 0.0)
            d_probs = contract(up, kv_ref[0, :, dim:], 1, 1)
            d_raw = probs * (d_probs - delta) * ((1.0 - bounded * bounded) * score_scale)
            d_raw = d_raw.astype(bf16)
            dq_ref[head] += contract(d_raw, kv_ref[0, :, :dim], 1, 0)
            dk += contract(d_raw, q_ref[head], 0, 0)
            dv += contract(probs.astype(bf16), up, 0, 0)
        dkv_ref[0, :, :dim] = dk.astype(bf16)
        dkv_ref[0, :, dim:] = dv.astype(bf16)

    @pl.when(kind == 1)
    def _():
        work(False)

    @pl.when(kind == 0)
    def _():
        dkv_ref[...] = jnp.zeros_like(dkv_ref)

    @pl.when(kind == 2)
    def _():
        work(True)


def attend_back(info, queries, all_kv, upstream, exact, inverse):
    heads, rows, dim = queries.shape
    blocks = all_kv.shape[0]
    return pl.pallas_call(
        backward_kernel,
        grid_spec=pltpu.PrefetchScalarGridSpec(
            num_scalar_prefetch=1,
            grid=(blocks,),
            in_specs=[
                pl.BlockSpec((heads, rows, dim), whole3),
                pl.BlockSpec((1, rows, 2 * dim), by_step),
                pl.BlockSpec((rows, heads * dim), whole2),
                pl.BlockSpec((rows, heads * dim), whole2),
                pl.BlockSpec((heads, rows, 1), whole3),
            ],
            out_specs=[
                pl.BlockSpec((heads, rows, dim), whole3),
                pl.BlockSpec((1, rows, 2 * dim), by_step),
            ],
        ),
        out_shape=[
            jax.ShapeDtypeStruct((heads, rows, dim), f32),
            jax.ShapeDtypeStruct((blocks, rows, 2 * dim), bf16),
        ],
        compiler_params=pltpu.CompilerParams(vmem_limit_bytes=24 * 2**20),
        cost_estimate=pl.CostEstimate(
            flops=3 * 10 * heads * rows * rows * dim,
            bytes_accessed=16 * rows * dim * heads,
            transcendentals=6 * heads * rows * rows,
        ),
    )(info, queries, all_kv, upstream, exact, inverse)


def on_device(
    tokens,
    cotangent,
    norm_attn_in,
    w_query,
    w_key,
    w_value,
    w_out,
    norm_attn_out,
    norm_ff_in,
    w_gate,
    w_up,
    w_down,
    norm_ff_out,
    block_group,
    block_role,
):
    at = Place()
    own_rows, depth = tokens.shape
    shard_rows, units = w_gate.shape
    regular = at.nz == 4 and shard_rows % 32 == 0 and units == depth and units % 768 == 0
    comm = Kernels(at) if regular else Permutes(at)
    blocks = at.blocks
    info = jnp.concatenate(
        [block_group, block_role, jnp.stack([comm.block, blocks // 4]).astype(jnp.int32)]
    )

    token_f32 = tokens.astype(f32)
    heads_width = w_query.shape[1]
    normed_one, qkv_full, gate_full, up_pieces = comm.start(
        normalize(token_f32, norm_attn_in).astype(bf16),
        jnp.concatenate([w_query, w_key, w_value], axis=1),
        w_gate,
        w_up,
    )
    queries, own_kv, cosine, sine_table = project(info, normed_one, qkv_full)
    all_kv, out_full, up_full = comm.gather_kv(own_kv, w_out.T, up_pieces)
    attn_rows, attended, inverse = attend(info, queries, all_kv)
    attn_proj, down_pieces = comm.scatter_heads(
        contract(attn_rows, out_full, 1, 1).astype(bf16), w_down.T
    )
    middle = token_f32 + normalize(attn_proj, norm_attn_out)

    ff_proj, d_normed_two, gate_sum, up_sum, down_sum = comm.feed_forward(
        normalize(middle, norm_ff_in).astype(bf16), cotangent, norm_ff_out, gate_full, up_full, down_pieces
    )
    layer_out = middle + normalize(ff_proj, norm_ff_out)
    upstream = cotangent.astype(f32)
    _, grad_ff_out = normalize_back(ff_proj, norm_ff_out, upstream)

    d_middle_part, grad_ff_in = normalize_back(middle, norm_ff_in, d_normed_two)
    d_middle = upstream + d_middle_part
    d_proj, grad_attn_out = normalize_back(attn_proj, norm_attn_out, d_middle)
    d_proj_rows = comm.gather_heads(d_proj.astype(bf16))
    d_attended = contract(d_proj_rows, out_full, 1, 0).astype(bf16)
    d_query, d_kv_parts = attend_back(info, queries, all_kv, d_attended, attended, inverse)
    d_kv, grad_out, down_sums = comm.scatter_kv_sums(
        d_kv_parts, contract(d_proj_rows, attn_rows, 0, 0).astype(bf16), down_sum
    )
    d_qkv_lin, d_partial = project_back(d_query, d_kv, cosine, sine_table, qkv_full)
    d_normed_one, grad_down = comm.scatter_heads_back(d_partial, down_sums)
    d_token_part, grad_attn_in = normalize_back(token_f32, norm_attn_in, d_normed_one)
    input_grad = (d_middle + d_token_part).astype(bf16)
    grad_qkv, grad_gate, grad_up, gains = comm.finish(
        contract(normed_one, d_qkv_lin, 0, 0).astype(bf16),
        gate_sum,
        up_sum,
        jnp.stack([grad_attn_in, grad_attn_out, grad_ff_in, grad_ff_out]),
    )
    grad_qkv, grad_gate, grad_up = [g.astype(f32) for g in (grad_qkv, grad_gate, grad_up)]
    return (
        layer_out.astype(bf16),
        input_grad,
        gains[0],
        grad_qkv[:, :heads_width],
        grad_qkv[:, heads_width : heads_width + HEAD_DIM],
        grad_qkv[:, heads_width + HEAD_DIM :],
        grad_out.astype(f32).T,
        gains[1],
        gains[2],
        grad_gate,
        grad_up,
        grad_down.astype(f32).T,
        gains[3],
    )


def solution(mesh):
    rows, weight, turned = P(("blk", "heads"), None), P("blk", "heads"), P("heads", "blk")
    return jax.shard_map(
        on_device,
        mesh=mesh,
        in_specs=(
            rows, rows, P(), weight, weight, weight, turned, P(), P(), weight, weight, turned,
            P(), P(), P(),
        ),
        out_specs=(
            rows, rows, P(), weight, weight, weight, turned, P(), P(), weight, weight, turned, P(),
        ),
        check_vma=False,
    )
```

```python
import math

import jax
import jax.numpy as jnp
from jax import lax
from jax.experimental import pallas as pl
from jax.experimental.pallas import tpu as pltpu
from jax.sharding import PartitionSpec as P

HEAD_DIM = 256


softcap = 50.0
epsilon = 1e-06
score_scale = HEAD_DIM ** (-0.5)
bf16 = jnp.bfloat16
f32 = jnp.float32


def contract(left_side, right_side, left_dim, right_dim):
    return lax.dot_general(
        left_side,
        right_side,
        (((left_dim,), (right_dim,)), ((), ())),
        preferred_element_type=f32,
    )


def factor_of(values):
    return lax.rsqrt(jnp.mean(values * values, axis=-1, keepdims=True) + epsilon)


def normalize(values, weight_gain):
    return values * factor_of(values) * (1.0 + weight_gain)


def normalize_back(values, weight_gain, upstream):
    factor = factor_of(values)
    unit = values * factor
    scaled = upstream * (1.0 + weight_gain)
    inner = jnp.mean(scaled * unit, axis=-1, keepdims=True)
    return (scaled - unit * inner) * factor, jnp.sum(upstream * unit, axis=0)


def rotate(tensor, cosine, sine_table):
    half_dim = HEAD_DIM // 2
    first_half = tensor[..., :half_dim]
    second_half = tensor[..., half_dim:]
    return jnp.concatenate(
        [
            first_half * cosine - second_half * sine_table,
            second_half * cosine + first_half * sine_table,
        ],
        axis=-1,
    )


def swap_core(v):
    return lax.ppermute(v, "heads", [(i, i ^ 1) for i in range(4)])


def swap_y(v):
    return lax.ppermute(v, "heads", [(i, i ^ 2) for i in range(4)])


def swap_x(v):
    blocks = lax.axis_size("blk")
    return lax.ppermute(v, "blk", [(i, i ^ 1) for i in range(blocks)])


def pair_up(own, other, place, axis):
    first = jnp.where(place == 0, own, other)
    second = jnp.where(place == 0, other, own)
    return jnp.concatenate([first, second], axis=axis)


def shift_z(v, step, senders):
    pairs = []
    for z in senders:
        for x in range(2):
            pairs.append((2 * z + x, 2 * (z + step) + x))
    return lax.ppermute(v, "blk", pairs)


class Place:
    def __init__(self):
        self.blocks = lax.axis_size("blk")
        self.nz = self.blocks // 2
        self.b = lax.axis_index("blk")
        self.h = lax.axis_index("heads")
        self.z, self.x = self.b // 2, self.b % 2
        self.y, self.c = self.h // 2, self.h % 2


def gather_z(at, unit):
    nz = at.nz
    up, down = unit, unit
    ups, downs = [None], [None]
    for s in range(1, nz):
        up = shift_z(up, 1, range(s - 1, nz - 1))
        down = shift_z(down, -1, range(1, nz - s + 1))
        ups.append(up)
        downs.append(down)
    return [unit] + [jnp.where(at.z >= s, ups[s], downs[nz - s]) for s in range(1, nz)]


def scatter_z(at, parts):
    nz = at.nz
    up = down = None
    for t in range(1, nz):
        k = nz - t
        send_up = parts[nz - k].astype(f32)
        send_down = parts[k].astype(f32)
        if up is not None:
            send_up = send_up + up.astype(f32)
            send_down = send_down + down.astype(f32)
        up = shift_z(send_up.astype(bf16), 1, range(0, nz - k))
        down = shift_z(send_down.astype(bf16), -1, range(k, nz))
    return parts[0].astype(f32) + (up.astype(f32) + down.astype(f32))


def deal_z(at, parts):
    nz = at.nz
    got = [parts[0]]
    for s in range(1, nz):
        up = shift_z(parts[nz - s], s, range(0, nz - s))
        down = shift_z(parts[nz - s], s - nz, range(nz - s, nz))
        got.append(jnp.where(at.z >= s, up, down))
    return got


def turn(at, whole):
    return [
        lax.dynamic_index_in_dim(whole, (at.z - s) % at.nz, 0, keepdims=False)
        for s in range(at.nz)
    ]


def unturn(at, parts):
    whole = jnp.zeros((at.nz,) + parts[0].shape, parts[0].dtype)
    for s, part in enumerate(parts):
        whole = lax.dynamic_update_index_in_dim(whole, part, (at.z - s) % at.nz, 0)
    return whole


def gather_zx(at, unit):
    got = []
    for part in gather_z(at, unit):
        got.append(pair_up(part[None], swap_x(part)[None], at.x, 0))
    return unturn(at, got)


def gather_xz(at, unit):
    both = pair_up(unit[None], swap_x(unit)[None], at.x, 0)
    return unturn(at, gather_z(at, both))


def pick(pair, place):
    mine = jnp.where(place == 0, pair[0], pair[1])
    other = jnp.where(place == 0, pair[1], pair[0])
    return mine, other


def scatter_zx(at, parts):
    total = scatter_z(at, parts)
    mine, other = pick(total, at.x)
    return mine + swap_x(other.astype(bf16)).astype(f32)


def scatter_xz(at, parts):
    sums = []
    for part in parts:
        mine, other = pick(part, at.x)
        sums.append(mine.astype(f32) + swap_x(other.astype(bf16)).astype(f32))
    return scatter_z(at, sums)


def rows_to_block(at, own):
    both = pair_up(own, swap_core(own), at.c, 0)
    pair = pair_up(both[None], swap_y(both)[None], at.y, 0)
    return pair.reshape(4 * own.shape[0], own.shape[1])


def rows_from_block(at, partial_sum):
    rows = partial_sum.shape[0] // 4
    parts = partial_sum.reshape(2, 2, rows, partial_sum.shape[1])
    mine, other = pick(parts.swapaxes(0, 1), at.c)
    total = mine + swap_core(other.astype(bf16)).astype(f32)
    mine, other = pick(total, at.y)
    return mine + swap_y(other.astype(bf16)).astype(f32)


def spread_weight(at, shard):
    rows, units = shard.shape
    half = rows // 2
    keep, send = pick(shard.reshape(2, half, units), at.c)
    wide = pair_up(keep[None], swap_core(send)[None], at.c, 0)
    quarter = 2 * units // at.nz
    per_core = units // quarter
    pieces = wide.reshape(2, half, per_core, quarter).transpose(0, 2, 1, 3)
    pieces = pieces.reshape(at.nz, half, quarter)
    got = unturn(at, deal_z(at, turn(at, pieces)))
    got = pair_up(got[:, None], swap_x(got)[:, None], at.x, 1)
    got = pair_up(got, swap_y(got), at.y, 3)
    got = pair_up(got[:, :, None], swap_core(got)[:, :, None], at.c, 2)
    return got.reshape(at.blocks * rows, 2 * quarter)


def collect_weight(at, grad):
    depth, width = grad.shape
    half, quarter = depth // (2 * at.blocks), width // 2
    parts = grad.reshape(at.nz, 2, 2, half, width)
    mine, other = pick(parts.transpose(2, 0, 1, 3, 4), at.c)
    total = mine + swap_core(other.astype(bf16)).astype(f32)
    mine, other = pick((total[..., :quarter], total[..., quarter:]), at.y)
    total = mine + swap_y(other.astype(bf16)).astype(f32)
    mine, other = pick((total[:, 0], total[:, 1]), at.x)
    total = mine + swap_x(other.astype(bf16)).astype(f32)
    got = unturn(at, deal_z(at, turn(at, total.astype(bf16))))
    per_core = at.nz // 2
    wide = got.reshape(2, per_core, half, quarter).transpose(0, 2, 1, 3)
    wide = wide.reshape(2, half, per_core * quarter)
    mine, other = pick(wide, at.c)
    rows = pair_up(mine, swap_core(other), at.c, 0)
    return rows.astype(f32)


def sum_all(at, values):
    total = values
    for bit in (1, 2):
        total = total + lax.ppermute(total, "heads", [(i, i ^ bit) for i in range(4)])
    bit = 1
    while bit < at.blocks:
        total = total + lax.ppermute(total, "blk", [(i, i ^ bit) for i in range(at.blocks)])
        bit *= 2
    return total


class Permutes:
    def __init__(self, at):
        self.at = at
        self.block, self.blocks, self.nz = at.b, at.blocks, at.nz

    def split(self, whole):
        return turn(self.at, whole.reshape((self.nz, whole.shape[0] // self.nz) + whole.shape[1:]))

    def start(self, own, qkv_shard, gate, up):
        at = self.at
        qkv_full = gather_zx(at, qkv_shard).reshape(own.shape[1], -1)
        return rows_to_block(at, own), qkv_full, spread_weight(at, gate), spread_weight(at, up)

    def gather_kv(self, own, out_shard, up):
        out_full = gather_zx(self.at, out_shard).reshape(-1, out_shard.shape[1])
        return gather_zx(self.at, own).reshape((self.blocks,) + own.shape), out_full, up

    def heads_forward(self, partial, tokens, gain_out, gain_in, down):
        summed = rows_from_block(self.at, partial)
        middle = tokens.astype(f32) + normalize(summed, gain_out)
        return summed, normalize(middle, gain_in).astype(bf16), spread_weight(self.at, down)

    def gather_z(self, own):
        whole = unturn(self.at, gather_z(self.at, own))
        return whole.reshape(-1, own.shape[1])

    def scatter_z(self, partial):
        return scatter_z(self.at, self.split(partial))

    def feed_forward(self, own, cotangent, gain, gate, up, down):
        normed = self.gather_z(own)
        gate_lin = jnp.dot(normed, gate, preferred_element_type=f32)
        up_lin = jnp.dot(normed, up, preferred_element_type=f32)
        hidden = (jax.nn.gelu(gate_lin, approximate=True) * up_lin).astype(bf16)
        ff_proj = self.scatter_z(contract(hidden, down, 1, 1).astype(bf16))
        d_ff, _ = normalize_back(ff_proj, gain, cotangent.astype(f32))
        d_ff_rows = self.gather_z(d_ff.astype(bf16))
        d_hidden = contract(d_ff_rows, down, 1, 0)
        _, glu_back = jax.vjp(
            lambda gate_in, up_in: jax.nn.gelu(gate_in, approximate=True) * up_in, gate_lin, up_lin
        )
        d_gate, d_up = [d.astype(bf16) for d in glu_back(d_hidden)]
        d_partial = contract(d_gate, gate, 1, 1) + contract(d_up, up, 1, 1)
        d_normed = self.scatter_z(d_partial.astype(bf16))
        grads = [
            contract(left, right, 0, 0).astype(bf16)
            for left, right in ((normed, d_gate), (normed, d_up), (d_ff_rows, hidden))
        ]
        return [ff_proj, d_normed] + grads

    def heads_backward(self, d_normed, projected, tokens, cotangent, gain_out, gain_in):
        middle = tokens.astype(f32) + normalize(projected, gain_out)
        part, by_in = normalize_back(middle, gain_in, d_normed)
        d_middle = cotangent.astype(f32) + part
        d_projected, by_out = normalize_back(projected, gain_out, d_middle)
        rows = rows_to_block(self.at, d_projected.astype(bf16))
        return rows, d_middle, jnp.stack([by_out, by_in])

    def scatter_pairs(self, grad):
        rows = grad.shape[0] // self.blocks
        return scatter_xz(self.at, self.split(grad.reshape(self.blocks, rows, -1)))

    def scatter_kv_sums(self, parts, out_grad, grad):
        kv = scatter_xz(self.at, self.split(parts))
        return kv, self.scatter_pairs(out_grad), collect_weight(self.at, grad)

    def scatter_heads_back(self, partial, sums):
        return rows_from_block(self.at, partial), sums

    def finish(self, qkv_grad, gate_grad, up_grad, gains):
        gate, up = collect_weight(self.at, gate_grad), collect_weight(self.at, up_grad)
        return self.scatter_pairs(qkv_grad), gate, up, sum_all(self.at, gains)


MESH = pl.DeviceIdType.MESH
DMA = pltpu.SemaphoreType.DMA
anywhere = pl.BlockSpec(memory_space=pl.ANY)
in_vmem = pl.BlockSpec(memory_space=pltpu.VMEM)


def remote(src, dst, send_sem, recv_sem, target):
    return pltpu.make_async_remote_copy(
        src_ref=src,
        dst_ref=dst,
        send_sem=send_sem,
        recv_sem=recv_sem,
        device_id=target,
        device_id_type=MESH,
    )


def flip(bit, by):
    return 1 - bit if by else bit


def exclusive_or(z, i):
    low, high = lax.rem(z, 2), lax.rem(z // 2, 2)
    rest = z - 2 * high - low
    return rest + 2 * flip(high, i // 2) + flip(low, i % 2)


class Spot:
    def __init__(self, nz):
        self.nz = nz
        h, b = lax.axis_index("heads"), lax.axis_index("blk")
        self.y, self.c = h // 2, h % 2
        self.z, self.x = b // 2, b % 2

    def device(self, z=None, x=None, y=None, c=None):
        z = self.z if z is None else z
        x = self.x if x is None else x
        y = self.y if y is None else y
        c = self.c if c is None else c
        return (2 * y + c, 2 * z + x)

    def partner(self):
        return self.device(c=1 - self.c)

    def greet(self):
        found = []
        for dx, dy, dc in [(0, 0, 1), (1, 0, 0), (1, 0, 1), (0, 1, 0), (0, 1, 1), (1, 1, 0), (1, 1, 1)]:
            found.append(self.device(x=flip(self.x, dx), y=flip(self.y, dy), c=flip(self.c, dc)))
        for s in range(1, self.nz):
            z = lax.rem(self.z + s, self.nz)
            found += [self.device(z=z), self.device(z=z, c=1 - self.c)]
        barrier = pltpu.get_barrier_semaphore()
        for device in found:
            pl.semaphore_signal(barrier, inc=1, device_id=device, device_id_type=MESH)
        pl.semaphore_wait(barrier, len(found))


def row_step(rows):
    return next(step for step in (48, 32, 16) if rows % step == 0)


def add_rows(out, left, right):
    rows = left.shape[0]
    step = row_step(rows)

    @pl.loop(0, rows // step)
    def _(i):
        at = pl.ds(pl.multiple_of(i * step, step), step)
        out[at, :] = (left[at, :].astype(f32) + right[at, :].astype(f32)).astype(out.dtype)


class LineGather:
    def __init__(self, spot, entry, send, recv):
        self.spot, self.entry = spot, entry
        self.send, self.recv = send, recv

    def copies(self, s):
        p, nz = self.spot, self.spot.nz
        up_at = lax.rem(p.z - s + 1 + nz, nz)
        down_at = lax.rem(p.z + s - 1, nz)
        up = remote(
            self.entry(up_at),
            self.entry(up_at),
            self.send.at[0, s],
            self.recv.at[0, s],
            p.device(z=lax.rem(p.z + 1, nz)),
        )
        down = remote(
            self.entry(down_at),
            self.entry(down_at),
            self.send.at[1, s],
            self.recv.at[1, s],
            p.device(z=lax.rem(p.z + nz - 1, nz)),
        )
        return (
            ((p.z >= s - 1) & (p.z < nz - 1), p.z >= s, up),
            ((p.z <= nz - s) & (p.z > 0), p.z <= nz - 1 - s, down),
        )

    def start(self, s):
        for sends, _, copy in self.copies(s):
            pl.when(sends)(copy.start)

    def arrive(self, s):
        for _, receives, copy in self.copies(s):
            pl.when(receives)(copy.wait_recv)

    def finish(self):
        for s in range(1, self.spot.nz):
            for sends, _, copy in self.copies(s):
                pl.when(sends)(copy.wait_send)

    def newest(self, s):
        p, nz = self.spot, self.spot.nz
        return (
            (p.z >= s, lax.rem(p.z - s + nz, nz)),
            (p.z <= nz - 1 - s, lax.rem(p.z + s, nz)),
        )


class LineScatter:
    def __init__(self, spot, parts, up, down, send, recv):
        self.spot, self.parts, self.up, self.down = spot, parts, up, down
        self.send, self.recv = send, recv

    def copies(self, t):
        p, nz = self.spot, self.spot.nz
        k = nz - t
        up = remote(
            self.parts(lax.rem(p.z + k, nz)),
            self.up.at[t - 1],
            self.send.at[0, t],
            self.recv.at[0, t],
            p.device(z=lax.rem(p.z + 1, nz)),
        )
        down = remote(
            self.parts(lax.rem(p.z - k + nz, nz)),
            self.down.at[t - 1],
            self.send.at[1, t],
            self.recv.at[1, t],
            p.device(z=lax.rem(p.z + nz - 1, nz)),
        )
        return (
            (p.z <= nz - 1 - k, (p.z >= 1) & (p.z <= t), up),
            (p.z >= k, (p.z <= nz - 2) & (p.z >= nz - 1 - t), down),
        )

    def start(self, t):
        for sends, _, copy in self.copies(t):
            pl.when(sends)(copy.start)

    def arrive(self, t):
        p, nz = self.spot, self.spot.nz
        k = nz - t
        for way, (_, receives, copy) in enumerate(self.copies(t)):

            @pl.when(receives)
            def _(way=way, copy=copy):
                copy.wait_recv()
                if t < nz - 1:
                    index = lax.rem(p.z + k - 1, nz) if way == 0 else lax.rem(p.z - k + 1 + nz, nz)
                    came = (self.up if way == 0 else self.down).at[t - 1]
                    add_rows(self.parts(index), self.parts(index), came)

    def finish(self):
        for t in range(1, self.spot.nz):
            for sends, _, copy in self.copies(t):
                pl.when(sends)(copy.wait_send)

    def total(self, out):
        p, last = self.spot, self.spot.nz - 2
        mine = self.parts(p.z)
        inner = (p.z > 0) & (p.z < p.nz - 1)

        @pl.when(p.z == 0)
        def _():
            add_rows(out, mine, self.down.at[last])

        @pl.when(p.z == p.nz - 1)
        def _():
            add_rows(out, mine, self.up.at[last])

        step = row_step(out.shape[0])

        @pl.when(inner)
        def _():
            @pl.loop(0, out.shape[0] // step)
            def _(i):
                at = pl.ds(pl.multiple_of(i * step, step), step)
                sides = self.up[last, at, :].astype(f32) + self.down[last, at, :].astype(f32)
                out[at, :] = (mine[at, :].astype(f32) + sides).astype(out.dtype)


class Task:
    ins = ()
    outs = ()
    scratch = ()
    vmem_ins = ()
    vmem_outs = ()
    spare = 5

    def steps(self, p, ins, outs, scratch):
        raise NotImplementedError


class PlaneGather(Task):
    vmem_ins = (0,)
    vmem_outs = (0,)

    def __init__(self, own):
        self.ins = (own,)
        self.outs = (jax.ShapeDtypeStruct((4,) + own.shape, bf16),)
        self.scratch = (DMA((6,)), DMA((4, 2)), DMA((2,)), DMA)

    def steps(self, p, ins, outs, scratch):
        (own,), (whole,), (send, recv, on_send, local) = ins, outs, scratch
        part, half = 2 * p.y + p.c, own.shape[0] // 2
        same = p.c == p.x

        def rows(of, i):
            return whole.at[of, pl.ds(i * half, half)]

        def piece(i):
            return own.at[pl.ds(i * half, half)]

        along = [
            remote(piece(i), rows(part, i), send.at[2 * k + i], recv.at[part, i], target)
            for k, target in enumerate((p.device(x=1 - p.x, c=p.x), p.device(y=1 - p.y, c=p.x)))
            for i in range(2)
        ]
        home = [
            remote(piece(i), rows(part, i), send.at[4 + i], recv.at[part, i], p.device(c=1 - p.c))
            for i in range(2)
        ]
        keep = pltpu.make_async_copy(own, whole.at[part], local)

        def passed(k, by_x):
            if by_x:
                here = rows(2 * p.y + k, 0)
                return remote(here, here, on_send.at[k], recv.at[2 * p.y + k, 0], p.device(y=1 - p.y))
            here = rows(2 * (1 - p.y) + k, 1)
            return remote(
                here, here, on_send.at[k], recv.at[2 * (1 - p.y) + k, 1], p.device(x=1 - p.x)
            )

        along[0].start()
        along[3].start()
        along[1].start()
        along[2].start()
        pl.when(same)(keep.start)
        for copy in home:
            pl.when(jnp.logical_not(same))(copy.start)
        yield
        for k in range(2):

            @pl.when(jnp.logical_not(same))
            def _(k=k):
                passed(k, True).wait_recv()
                passed(k, True).start()

            @pl.when(same)
            def _(k=k):
                passed(k, False).wait_recv()
                passed(k, False).start()

        yield
        for copy in along:
            copy.wait_send()
        pl.when(same)(keep.wait)
        for copy in home:
            pl.when(jnp.logical_not(same))(copy.wait_send)
        for k in range(2):
            pl.when(jnp.logical_not(same))(passed(k, True).wait_send)
            pl.when(same)(passed(k, False).wait_send)
        for slot in range(4):
            y, c = slot // 2, slot % 2
            for i in range(2):
                came = remote(rows(slot, i), rows(slot, i), send.at[0], recv.at[slot, i], p.partner())
                if i == 0:
                    waited = jnp.logical_not(same) & (p.y == y)
                else:
                    waited = same & (p.y != y)
                mine = same & (part == slot)
                pl.when(jnp.logical_not(waited | mine))(came.wait_recv)


class PlaneScatter(Task):
    vmem_ins = (0,)
    vmem_outs = (0,)

    def __init__(self, partial):
        rows, depth = partial.shape[0] // 4, partial.shape[1]
        self.ins = (partial.reshape(4, rows, depth),)
        self.outs = (jax.ShapeDtypeStruct((rows, depth), f32),)
        self.scratch = (pltpu.VMEM((4, rows, depth), bf16), DMA((4,)), DMA((4,)))

    def steps(self, p, ins, outs, scratch):
        (parts,), (out,), (came, send, recv) = ins, outs, scratch
        head, ours = 2 * p.y + p.x, 2 * p.y + p.c

        def copy_to(part):
            target = p.device(x=p.c, y=part // 2, c=part % 2)
            return remote(parts.at[part], came.at[head], send.at[part], recv.at[head], target)

        for part in range(4):
            here = (p.x == p.c) & (part == ours)
            pl.when(jnp.logical_not(here))(copy_to(part).start)
        yield
        for part in range(4):
            here = (p.x == p.c) & (part == ours)
            pl.when(jnp.logical_not(here))(copy_to(part).wait_send)
            arrived = remote(parts.at[part], came.at[part], send.at[part], recv.at[part], p.partner())
            mine = (p.x == p.c) & (part == head)
            pl.when(jnp.logical_not(mine))(arrived.wait_recv)

        @pl.when(p.x == p.c)
        def _():
            came[head] = parts[ours]

        @pl.loop(0, out.shape[0] // 16)
        def _(i):
            at = pl.ds(pl.multiple_of(i * 16, 16), 16)
            low = came[0, at, :].astype(f32) + came[1, at, :].astype(f32)
            out[at, :] = low + (came[2, at, :].astype(f32) + came[3, at, :].astype(f32))


class HeadsForward(PlaneScatter):
    vmem_ins = (0, 1, 2, 3)
    vmem_outs = (0, 1)

    def __init__(self, partial, tokens, gain_out, gain_in):
        super().__init__(partial)
        depth = tokens.shape[1]
        self.ins += (tokens, gain_out.reshape(1, depth), gain_in.reshape(1, depth))
        self.outs += (jax.ShapeDtypeStruct(tokens.shape, bf16),)

    def steps(self, p, ins, outs, scratch):
        partial, tokens, gain_out, gain_in = ins
        summed, normed = outs
        yield from super().steps(p, (partial,), (summed,), scratch)

        @pl.loop(0, normed.shape[0] // 16)
        def _(i):
            at = pl.ds(pl.multiple_of(i * 16, 16), 16)
            middle = tokens[at, :].astype(f32) + normalize(summed[at, :], gain_out[...])
            normed[at, :] = normalize(middle, gain_in[...]).astype(bf16)


class HeadsBackward(PlaneGather):
    vmem_ins = (0, 1, 2, 3, 4, 5)
    vmem_outs = (0, 1, 2)

    def __init__(self, d_normed, projected, tokens, cotangent, gain_out, gain_in):
        super().__init__(tokens)
        depth = tokens.shape[1]
        gains = (gain_out.reshape(1, depth), gain_in.reshape(1, depth))
        self.ins = (d_normed, projected, tokens, cotangent) + gains
        self.outs += (
            jax.ShapeDtypeStruct(tokens.shape, f32),
            jax.ShapeDtypeStruct((2, 16, depth), f32),
        )
        self.scratch += (pltpu.VMEM(tokens.shape, bf16),)

    def steps(self, p, ins, outs, scratch):
        d_normed, projected, tokens, cotangent, gain_out, gain_in = ins
        whole, d_middle, sums = outs
        *sems, own = scratch
        sums[...] = jnp.zeros_like(sums)

        def back(values, gain, upstream):
            factor = factor_of(values)
            unit = values * factor
            scaled = upstream * (1.0 + gain)
            inner = jnp.mean(scaled * unit, axis=-1, keepdims=True)
            return (scaled - unit * inner) * factor, upstream * unit

        @pl.loop(0, own.shape[0] // 16)
        def _(i):
            at = pl.ds(pl.multiple_of(i * 16, 16), 16)
            values = projected[at, :]
            middle = tokens[at, :].astype(f32) + normalize(values, gain_out[...])
            part, by_in = back(middle, gain_in[...], d_normed[at, :])
            total = cotangent[at, :].astype(f32) + part
            d_middle[at, :] = total
            d_values, by_out = back(values, gain_out[...], total)
            own[at, :] = d_values.astype(bf16)
            sums[0] += by_out
            sums[1] += by_in

        yield from super().steps(p, (own,), (whole,), sems)


class PairGather(Task):
    vmem_ins = (0,)
    vmem_outs = (0,)

    def __init__(self, nz, own, trade):
        self.trade = trade
        self.ins = (own,)
        self.outs = (jax.ShapeDtypeStruct((nz, 2) + own.shape, bf16),)
        self.scratch = (DMA((2, nz)), DMA((2, nz)), DMA((nz,)), DMA((nz,)), DMA, DMA, DMA)

    def steps(self, p, ins, outs, scratch):
        (own,), (full,), (send, recv, x_send, x_recv, t_send, t_recv, local) = ins, outs, scratch
        nz = p.nz
        keep = pltpu.make_async_copy(own, full.at[p.z, p.c], local)
        line = LineGather(p, lambda z: full.at[z, p.c], send, recv)

        def across(z):
            here = full.at[z, p.c]
            return remote(here, here, x_send.at[z], x_recv.at[z], p.partner())

        if self.trade:
            same = p.c == p.x
            move = remote(own, full.at[p.z, p.x], t_send, t_recv, p.device(x=1 - p.x, c=1 - p.c))
            pl.when(same)(keep.start)
            pl.when(jnp.logical_not(same))(move.start)
            yield
            pl.when(same)(keep.wait)
            pl.when(jnp.logical_not(same))(move.wait_recv)
        else:
            keep.start()
            keep.wait()
        line.start(1)
        across(p.z).start()
        yield
        for s in range(1, nz):
            line.arrive(s)
            if s < nz - 1:
                line.start(s + 1)
            for came, z in line.newest(s):
                pl.when(came)(across(z).start)
            yield
        line.finish()
        if self.trade:
            pl.when(jnp.logical_not(same))(move.wait_send)
        for z in range(nz):
            across(z).wait()


class ZGather(Task):
    vmem_ins = (0,)
    vmem_outs = (0,)

    def __init__(self, nz, own):
        self.ins = (own,)
        self.outs = (jax.ShapeDtypeStruct((nz,) + own.shape, bf16),)
        self.scratch = (DMA((2, nz)), DMA((2, nz)), DMA)

    def steps(self, p, ins, outs, scratch):
        (own,), (full,), (send, recv, local) = ins, outs, scratch
        line = LineGather(p, lambda z: full.at[z], send, recv)
        keep = pltpu.make_async_copy(own, full.at[p.z], local)
        keep.start()
        keep.wait()
        line.start(1)
        yield
        for s in range(1, p.nz):
            line.arrive(s)
            if s < p.nz - 1:
                line.start(s + 1)
            yield
        line.finish()


class ZScatter(Task):
    vmem_outs = (0,)

    def __init__(self, nz, partial):
        rows, depth = partial.shape[0] // nz, partial.shape[1]
        self.ins = (partial.reshape(nz, rows, depth),)
        self.outs = (jax.ShapeDtypeStruct((rows, depth), f32),)
        line = pltpu.VMEM((nz - 1, rows, depth), bf16)
        self.scratch = (
            pltpu.VMEM((nz, rows, depth), bf16), line, line, DMA((2, nz)), DMA((2, nz)), DMA
        )

    def steps(self, p, ins, outs, scratch):
        (given,), (out,), (parts, up, down, send, recv, local) = ins, outs, scratch
        bring = pltpu.make_async_copy(given, parts, local)
        bring.start()
        bring.wait()
        line = LineScatter(p, lambda z: parts.at[z], up, down, send, recv)
        line.start(1)
        yield
        for t in range(1, p.nz):
            line.arrive(t)
            if t < p.nz - 1:
                line.start(t + 1)
            yield
        line.total(out)
        line.finish()


class PairScatter(Task):
    vmem_outs = (0,)

    def __init__(self, nz, given, trade):
        _, _, rows, width = given.shape
        self.trade = trade
        self.ins = (given,)
        self.outs = (jax.ShapeDtypeStruct((rows, width), bf16),)
        whole = pltpu.VMEM((nz, rows, width), bf16)
        line = pltpu.VMEM((nz - 1, rows, width), bf16)
        self.scratch = (
            whole, whole, line, line,
            DMA((nz,)), DMA((nz,)), DMA((2, nz)), DMA((2, nz)), DMA((nz,)), DMA, DMA, DMA,
        )

    def steps(self, p, ins, outs, scratch):
        (given,), (out,) = ins, outs
        parts, came, up, down, x_send, x_recv, send, recv, local, b_send, b_recv, b_local = scratch
        nz = p.nz
        order = [exclusive_or(p.z, i) for i in (3, 2, 1, 0)]

        def away(z):
            return remote(given.at[z, 1 - p.c], came.at[z], x_send.at[z], x_recv.at[z], p.partner())

        def bring(z):
            return pltpu.make_async_copy(given.at[z, p.c], parts.at[z], local.at[z])

        for z in order:
            away(z).start()
            bring(z).start()
        yield
        for z in order:
            away(z).wait_recv()
            bring(z).wait()
            add_rows(parts.at[z], parts.at[z], came.at[z])
        line = LineScatter(p, lambda z: parts.at[z], up, down, send, recv)
        line.start(1)
        yield
        for t in range(1, nz):
            line.arrive(t)
            if t < nz - 1:
                line.start(t + 1)
            yield
        if not self.trade:
            line.total(out)
        else:
            line.total(came.at[0])
            same = p.c == p.x
            back = remote(came.at[0], out, b_send, b_recv, p.device(x=1 - p.x, c=1 - p.c))
            keep = pltpu.make_async_copy(came.at[0], out, b_local)
            pl.when(same)(keep.start)
            pl.when(jnp.logical_not(same))(back.start)
            yield
            pl.when(same)(keep.wait)
            pl.when(jnp.logical_not(same))(back.wait)
        for z in order:
            away(z).wait_send()
        line.finish()


class Deal:
    def __init__(self, p, shard, place, quarter, send, recv):
        self.p, self.shard, self.place, self.quarter = p, shard, place, quarter
        self.send, self.recv = send, recv
        self.per_core = p.nz // 2

    def piece(self, piece, half):
        columns = pl.ds(piece * self.quarter, self.quarter)
        return self.shard.at[half, :, columns]

    def away(self, piece, half):
        p = self.p
        z = p.c * self.per_core + piece
        return z, remote(
            self.piece(piece, half),
            self.place(p.z, half),
            self.send.at[2 * piece + half],
            self.recv.at[p.z],
            p.device(z=z, c=half),
        )

    def local(self, piece):
        p = self.p
        columns = pl.ds(piece * self.quarter, self.quarter)
        return pltpu.make_async_copy(
            self.shard.at[p.c, :, columns], self.place(p.z, p.c), self.recv.at[p.z]
        )

    def start(self, in_plane):
        p = self.p
        for piece in range(self.per_core):
            for half in range(2):
                z, copy = self.away(piece, half)
                if in_plane:
                    pl.when((z == p.z) & (p.c != half))(copy.start)
                    pl.when((z == p.z) & (p.c == half))(self.local(piece).start)
                else:
                    pl.when(z != p.z)(copy.start)

    def arrive(self, source):
        p = self.p
        here = self.place(source, p.c)
        ours = (source == p.z) & (p.c == p.z // self.per_core)
        came = remote(here, here, self.send.at[0], self.recv.at[source], p.partner())
        pl.when(jnp.logical_not(ours))(came.wait_recv)
        pl.when(ours)(self.local(0).wait)

    def finish(self):
        p = self.p
        for piece in range(self.per_core):
            for half in range(2):
                z, copy = self.away(piece, half)
                here = (z == p.z) & (p.c == half)
                pl.when(jnp.logical_not(here))(copy.wait_send)


class DealTask(Task):
    vmem_outs = (0,)

    def __init__(self, nz, shard):
        rows, units = shard.shape
        self.ins = (shard.reshape(2, rows // 2, units),)
        self.outs = (jax.ShapeDtypeStruct((nz, rows // 2, 2 * units // nz), bf16),)
        self.scratch = (DMA((nz,)), DMA((nz,)))

    def steps(self, p, ins, outs, scratch):
        (shard,), (pieces,), (send, recv) = ins, outs, scratch
        deal = Deal(p, shard, lambda z, half: pieces.at[z], pieces.shape[-1], send, recv)
        deal.start(False)
        deal.start(True)
        yield
        for i in range(p.nz):
            deal.arrive(exclusive_or(p.z, i))
        deal.finish()


class Copies(Task):
    def __init__(self, nz, given, dealt):
        self.dealt = dealt
        if dealt:
            _, half, quarter = given.shape
            self.ins = (given,)
        else:
            rows, units = given.shape
            half, quarter = rows // 2, 2 * units // nz
            self.ins = (given.reshape(2, half, units),)
        self.outs = (jax.ShapeDtypeStruct((nz * 4 * half, 2 * quarter), bf16),)
        self.scratch = (pltpu.VMEM(self.outs[0].shape, bf16), DMA, *copy_sems(nz))

    def steps(self, p, ins, outs, scratch):
        full, done, *sems = scratch
        yield from copy_steps(p, ins[0], full, sems, self.dealt)
        store = pltpu.make_async_copy(full, outs[0], done)
        store.start()
        yield
        store.wait()


def copy_sems(nz):
    one, two = DMA((nz,)), DMA((nz, 2))
    return (one, one, one, one, two, two, two, two)


def copy_steps(p, given, full, sems, dealt):
    d_send, d_recv, f_send, f_recv, s_send, s_recv, x_send, x_recv = sems
    nz = p.nz
    quarter, half = full.shape[1] // 2, full.shape[0] // (4 * nz)

    def strip(z, x, c):
        return pl.ds(pl.multiple_of(((z * 2 + x) * 2 + c) * half, half), half)

    def place(z, x, c, y):
        return full.at[strip(z, x, c), pl.ds(pl.multiple_of(y * quarter, 128), quarter)]

    fx, fy = p.x + (1 - 2 * p.x) * (1 - p.c), p.y + (1 - 2 * p.y) * p.c
    sx, sy = p.x + (1 - 2 * p.x) * p.c, p.y + (1 - 2 * p.y) * (1 - p.c)

    def own(z):
        return given.at[z] if dealt else place(z, p.x, p.c, p.y)

    def first(z):
        target = p.device(x=fx, y=fy)
        return remote(own(z), place(z, p.x, p.c, p.y), f_send.at[z], f_recv.at[z], target)

    def second(z, which):
        x, y = (fx, fy) if which else (p.x, p.y)
        here = place(z, x, p.c, y)
        src = here if which else own(z)
        target = p.device(x=sx, y=sy)
        return remote(src, here, s_send.at[z, which], s_recv.at[z, which], target)

    def across(z, x):
        here = full.at[strip(z, x, p.c)]
        return remote(here, here, x_send.at[z, x], x_recv.at[z, x], p.partner())

    def keep(z):
        return pltpu.make_async_copy(given.at[z], place(z, p.x, p.c, p.y), d_send.at[z])

    order = [exclusive_or(p.z, i) for i in range(nz)]
    if dealt:
        for z in order:
            first(z).start()
            second(z, 0).start()
            keep(z).start()
        for z in order:
            keep(z).wait()
        yield
    else:
        deal = Deal(p, given, lambda z, c: place(z, p.x, c, p.y), quarter, d_send, d_recv)
        deal.start(True)
        yield
        deal.arrive(order[0])
        first(order[0]).start()
        second(order[0], 0).start()
        yield
        deal.start(False)
        yield
        for z in order[1:]:
            deal.arrive(z)
            first(z).start()
            second(z, 0).start()
            yield
    for z in order:
        first(z).wait_recv()
        second(z, 1).start()
        yield
    for z in order:
        second(z, 0).wait_recv()
        second(z, 1).wait_recv()
        across(z, 0).start()
        across(z, 1).start()
        yield
    for z in range(nz):
        first(z).wait_send()
        for i in range(2):
            second(z, i).wait_send()
            across(z, i).wait()
    if not dealt:
        deal.finish()


class DealBack:
    def __init__(self, p, source, out, quarter, send, recv):
        self.p, self.source, self.out, self.quarter = p, source, out, quarter
        self.send, self.recv = send, recv
        self.per_core = p.nz // 2
        self.owner = p.z // self.per_core

    def out_at(self, z, half):
        start = pl.multiple_of(lax.rem(z, self.per_core) * self.quarter, 128)
        return self.out.at[half, :, pl.ds(start, self.quarter)]

    def away(self, z):
        p = self.p
        return remote(
            self.source(z),
            self.out_at(p.z, p.c),
            self.send.at[z],
            self.recv.at[2 * lax.rem(p.z, self.per_core) + p.c],
            p.device(z=z, c=self.owner),
        )

    def keep(self, z):
        p = self.p
        return pltpu.make_async_copy(
            self.source(z),
            self.out_at(p.z, p.c),
            self.recv.at[2 * lax.rem(p.z, self.per_core) + p.c],
        )

    def start(self, z):
        p = self.p
        here = (z == p.z) & (p.c == self.owner)
        pl.when(jnp.logical_not(here))(self.away(z).start)
        pl.when(here)(self.keep(z).start)

    def finish(self):
        p = self.p
        for piece in range(self.per_core):
            for half in range(2):
                z = p.c * self.per_core + piece
                place = self.out_at(z, half)
                came = remote(
                    place, place, self.send.at[0], self.recv.at[2 * piece + half], p.partner()
                )
                ours = (z == p.z) & (p.c == half)
                pl.when(jnp.logical_not(ours))(came.wait_recv)
        for z in range(p.nz):
            here = (z == p.z) & (p.c == self.owner)
            pl.when(jnp.logical_not(here))(self.away(z).wait_send)
            pl.when(here)(self.keep(z).wait)


class DealBackTask(Task):
    vmem_outs = (0,)

    def __init__(self, nz, sums):
        _, half, quarter = sums.shape
        self.ins = (sums,)
        self.outs = (jax.ShapeDtypeStruct((2, half, nz // 2 * quarter), bf16),)
        self.scratch = (DMA((nz,)), DMA((nz,)))

    def steps(self, p, ins, outs, scratch):
        (sums,), (out,), (send, recv) = ins, outs, scratch
        deal = DealBack(p, lambda z: sums.at[z], out, sums.shape[-1], send, recv)
        for i in (3, 2, 1, 0):
            deal.start(exclusive_or(p.z, i))
        yield
        deal.finish()


class Sums(Task):
    def __init__(self, nz, grad, deal):
        depth, width = grad.shape
        half, quarter = depth // (4 * nz), width // 2
        self.deal = deal
        self.ins = (grad.reshape(nz, 2, 2, half, width),)
        if deal:
            self.outs = (jax.ShapeDtypeStruct((2, half, nz // 2 * quarter), bf16),)
        else:
            self.outs = (jax.ShapeDtypeStruct((nz, half, quarter), bf16),)
            self.vmem_outs = (0,)
        whole = pltpu.VMEM((nz, 2, half, width), bf16)
        self.scratch = (
            whole,
            whole,
            pltpu.VMEM((nz, 2, half, quarter), bf16),
            pltpu.VMEM((nz, half, quarter), bf16),
            DMA((nz, 2)), DMA((nz, 2)), DMA((nz, 2)), DMA((nz, 2)), DMA((nz, 2)),
            DMA((nz,)), DMA((nz,)), DMA((nz,)), DMA((nz,)),
        )

    def steps(self, p, ins, outs, scratch):
        (given,), (out,) = ins, outs
        mine, came, first_in, second_in, *sems = scratch
        local, c_send, c_recv, f_send, f_recv, s_send, s_recv, d_send, d_recv = sems
        nz, quarter = p.nz, given.shape[4] // 2
        order = [exclusive_or(p.z, i) for i in (3, 2, 1, 0)]

        def bring(z, x):
            return pltpu.make_async_copy(given.at[z, x, p.c], mine.at[z, x], local.at[z, x])

        def across(z, x):
            src = given.at[z, x, 1 - p.c]
            return remote(src, came.at[z, x], c_send.at[z, x], c_recv.at[z, x], p.partner())

        def place(z, x, y):
            return mine.at[z, x, :, pl.ds(pl.multiple_of(y * quarter, 128), quarter)]

        fx, fy = p.x + (1 - 2 * p.x) * p.c, p.y + (1 - 2 * p.y) * (1 - p.c)
        sx, sy = p.x + (1 - 2 * p.x) * (1 - p.c), p.y + (1 - 2 * p.y) * p.c

        def first(z, which):
            x, y = (1 - p.x, 1 - p.y) if which else (fx, fy)
            target = p.device(x=fx, y=fy)
            return remote(
                place(z, x, y), first_in.at[z, which], f_send.at[z, which], f_recv.at[z, which], target
            )

        def second(z):
            target = p.device(x=sx, y=sy)
            return remote(place(z, sx, sy), second_in.at[z], s_send.at[z], s_recv.at[z], target)

        back = DealBack(p, lambda z: place(z, p.x, p.y), out, quarter, d_send, d_recv)
        for z in order:
            for x in range(2):
                across(z, x).start()
                bring(z, x).start()
        yield
        def over_core(z):
            for x in range(2):
                across(z, x).wait_recv()
                bring(z, x).wait()
                add_rows(mine.at[z, x], mine.at[z, x], came.at[z, x])
            for which in (1, 0):
                first(z, which).start()

        def over_first(z):
            for which in (1, 0):
                at = place(z, sx, sy) if which else place(z, p.x, p.y)
                first(z, which).wait_recv()
                add_rows(at, at, first_in.at[z, which])
                if which:
                    second(z).start()

        def over_second(z):
            second(z).wait_recv()
            at = place(z, p.x, p.y)
            if self.deal:
                add_rows(at, at, second_in.at[z])
                back.start(z)
            else:
                add_rows(out.at[z], at, second_in.at[z])

        over_core(order[0])
        yield
        for i in range(nz + 1):
            if i + 1 < nz:
                over_core(order[i + 1])
                yield
            if i < nz:
                over_first(order[i])
                yield
            if i >= 1:
                over_second(order[i - 1])
                yield
        if self.deal:
            back.finish()
        for z in range(nz):
            second(z).wait_send()
            for i in range(2):
                first(z, i).wait_send()
                across(z, i).wait_send()


class FeedForward(Task):
    vmem_ins = (0, 1, 2)
    vmem_outs = (0, 1)
    spare = 10

    def __init__(self, nz, own, cotangent, gain, gate, up, down_pieces):
        rows, depth = own.shape
        units = gate.shape[1]
        self.rows, self.depth, self.units = rows, depth, units
        self.ins = (own, cotangent, gain.reshape(1, depth), gate, up, down_pieces)
        wide = jax.ShapeDtypeStruct((depth, units), bf16)
        exact = jax.ShapeDtypeStruct((rows, depth), f32)
        self.outs = (exact, exact, wide, wide, wide)
        weight = pltpu.VMEM((depth, units), bf16)
        tokens = pltpu.VMEM((nz * rows, depth), bf16)
        inner = pltpu.VMEM((nz * rows, units), bf16)
        line = pltpu.VMEM((2, nz - 1, rows // 2, depth), bf16)
        self.scratch = (
            weight, weight, weight, tokens, tokens, inner, inner, inner, tokens, line, line,
            DMA((8, 2, nz)), DMA((8, 2, nz)), DMA((8,)), *copy_sems(nz),
        )

    def steps(self, p, ins, outs, scratch):
        own, cotangent, gain, gate_in, up_in, down_in = ins
        ff_out, dn_out, grad_gate, grad_up, grad_down = outs
        gate, up, down, normed, d_ff, hidden, gated, upped, parts, above, below, *sems = scratch
        send, recv, local, *down_sems = sems
        copies = copy_steps(p, down_in, down, down_sems, True)
        nz, depth, units = p.nz, self.depth, self.units
        part = self.rows // 2
        half_rows = nz * part
        tile = units // 3

        def entry(buffer, half):
            return lambda z: buffer.at[pl.ds(pl.multiple_of(half * half_rows + z * part, part), part)]

        gathers, scatters = [], []
        for i, buffer in enumerate((normed, d_ff)):
            for half in range(2):
                k = 4 * i + half
                gathers.append(LineGather(p, entry(buffer, half), send.at[k], recv.at[k]))
                scatters.append(
                    LineScatter(
                        p, entry(parts, half), above.at[half], below.at[half], send.at[k + 2], recv.at[k + 2]
                    )
                )

        loads = [
            pltpu.make_async_copy(src, dst, local.at[i])
            for i, (src, dst) in enumerate(((gate_in, gate), (up_in, up)))
        ]

        def gelu(v):
            bent = jnp.tanh(math.sqrt(2.0 / math.pi) * (v + 0.044715 * (v * v * v)))
            return 0.5 * v * (1.0 + bent), bent

        def columns(i):
            return pl.ds(pl.multiple_of(i * tile, 128), tile)

        def hide(half, low, high):
            rows = slice(half * half_rows, (half + 1) * half_rows)

            @pl.loop(low, high)
            def _(i):
                at = columns(i)
                gate_lin = jnp.dot(normed[rows, :], gate[:, at], preferred_element_type=f32)
                up_lin = jnp.dot(normed[rows, :], up[:, at], preferred_element_type=f32)
                hidden[rows, at] = (gelu(gate_lin)[0] * up_lin).astype(bf16)
                gated[rows, at] = gate_lin.astype(bf16)
                upped[rows, at] = up_lin.astype(bf16)

        def project(half):
            rows = slice(half * half_rows, (half + 1) * half_rows)

            @pl.loop(0, depth // tile)
            def _(i):
                at = columns(i)
                parts[rows, at] = contract(hidden[rows, :], down[at, :], 1, 1).astype(bf16)

        def hide_back(half, low, high):
            rows = slice(half * half_rows, (half + 1) * half_rows)

            @pl.loop(low, high)
            def _(i):
                at = columns(i)
                d_hidden = jnp.dot(d_ff[rows, :], down[:, at], preferred_element_type=f32)
                v, u = gated[rows, at].astype(f32), upped[rows, at].astype(f32)
                value, bent = gelu(v)
                slope = 0.5 * (1.0 + bent) + (0.5 * math.sqrt(2.0 / math.pi)) * v * (
                    1.0 - bent * bent
                ) * (1.0 + (3.0 * 0.044715) * (v * v))
                gated[rows, at] = (d_hidden * u * slope).astype(bf16)
                upped[rows, at] = (d_hidden * value).astype(bf16)

        def project_back(half):
            rows = slice(half * half_rows, (half + 1) * half_rows)

            @pl.loop(0, depth // tile)
            def _(i):
                at = columns(i)
                total = contract(gated[rows, :], gate[at, :], 1, 1)
                parts[rows, at] = (total + contract(upped[rows, :], up[at, :], 1, 1)).astype(bf16)

        def turn_back(half):
            start = half * half_rows + p.z * part

            @pl.loop(0, part // 16)
            def _(i):
                at = pl.ds(pl.multiple_of(half * part + i * 16, 16), 16)
                values = ff_out[at, :]
                scaled = cotangent[at, :].astype(f32) * (1.0 + gain[...])
                factor = factor_of(values)
                unit = values * factor
                mean = jnp.mean(scaled * unit, axis=-1, keepdims=True)
                here = pl.ds(pl.multiple_of(start + i * 16, 16), 16)
                d_ff[here, :] = ((scaled - unit * mean) * factor).astype(bf16)

        def weigh(left, right, out, low, high):
            @pl.loop(low, high)
            def _(i):
                at = pl.ds(pl.multiple_of(i * 256, 128), 256)
                out[at, :] = contract(left[:, at], right[...], 0, 0).astype(bf16)

        def store(i, src, dst):
            return pltpu.make_async_copy(src, dst, local.at[3 + i])

        blocks = depth // 256
        one, two, one_back, two_back = gathers
        sum_one, sum_two, sum_one_back, sum_two_back = scatters
        keep = [
            pltpu.make_async_copy(own.at[pl.ds(half * part, part)], entry(normed, half)(p.z), local.at[6 + half])
            for half in range(2)
        ]
        keep[0].start()
        keep[1].start()
        keep[0].wait()
        one.start(1)
        keep[1].wait()
        next(copies)
        for load in loads:
            load.start()
        one.arrive(1)
        one.start(2)
        two.start(1)
        one.arrive(2)
        one.start(3)
        for _ in range(nz):
            next(copies)
        one.arrive(3)
        two.arrive(1)
        two.start(2)
        for load in loads:
            load.wait()
        hide(0, 0, 1)
        two.arrive(2)
        two.start(3)
        hide(0, 1, 3)
        two.arrive(3)
        hide(1, 0, 1)
        for _ in copies:
            pass
        project(0)
        sum_one.start(1)
        hide(1, 1, 3)
        sum_one.arrive(1)
        sum_one.start(2)
        project(1)
        sum_two.start(1)
        sum_one.arrive(2)
        sum_one.start(3)
        sum_two.arrive(1)
        sum_two.start(2)
        sum_one.arrive(3)
        sum_one.total(ff_out.at[pl.ds(0, part)])
        turn_back(0)
        one_back.start(1)
        sum_two.arrive(2)
        sum_two.start(3)
        one_back.arrive(1)
        one_back.start(2)
        sum_two.arrive(3)
        sum_two.total(ff_out.at[pl.ds(part, part)])
        turn_back(1)
        one_back.arrive(2)
        one_back.start(3)
        two_back.start(1)
        one_back.arrive(3)
        hide_back(0, 0, 3)
        two_back.arrive(1)
        two_back.start(2)
        sum_one.finish()
        project_back(0)
        sum_one_back.start(1)
        two_back.arrive(2)
        two_back.start(3)
        two_back.arrive(3)
        hide_back(1, 0, 3)
        sum_one_back.arrive(1)
        sum_one_back.start(2)
        sum_two.finish()
        project_back(1)
        sum_two_back.start(1)
        weigh(d_ff, hidden, down, 0, blocks)
        store(0, down, grad_down).start()
        sum_one_back.arrive(2)
        sum_two_back.arrive(1)
        sum_two_back.start(2)
        sum_one_back.start(3)
        weigh(normed, gated, gate, 0, blocks)
        store(1, gate, grad_gate).start()
        sum_two_back.arrive(2)
        sum_two_back.start(3)
        weigh(normed, upped, up, 0, blocks)
        store(2, up, grad_up).start()
        sum_one_back.arrive(3)
        sum_one_back.total(dn_out.at[pl.ds(0, part)])
        sum_two_back.arrive(3)
        sum_two_back.total(dn_out.at[pl.ds(part, part)])
        for gather in gathers:
            gather.finish()
        sum_one_back.finish()
        sum_two_back.finish()
        store(0, down, grad_down).wait()
        store(1, gate, grad_gate).wait()
        store(2, up, grad_up).wait()
        yield


class SumAll(Task):
    vmem_ins = (0,)
    vmem_outs = (0,)

    def __init__(self, values):
        self.ins = (values,)
        self.outs = (jax.ShapeDtypeStruct(values.shape, f32),)
        stage = pltpu.VMEM((5,) + values.shape, f32)
        self.scratch = (stage, stage, DMA((5,)), DMA((5,)))

    def steps(self, p, ins, outs, scratch):
        (given,), (out,), (stage, came, send, recv) = ins, outs, scratch
        targets = [
            p.partner(),
            p.device(y=1 - p.y),
            p.device(x=1 - p.x),
            p.device(z=exclusive_or(p.z, 1)),
            p.device(z=exclusive_or(p.z, 2)),
        ]
        stage[0] = given[...]
        for i, target in enumerate(targets):
            copy = remote(stage.at[i], came.at[i], send.at[i], recv.at[i], target)
            copy.start()
            yield
            copy.wait()
            total = stage[i] + came[i]
            if i < 4:
                stage[i + 1] = total
            else:
                out[...] = total


def run_tasks(nz, number, tasks, order="", every=False):
    counts = [(len(t.ins), len(t.outs), len(t.scratch)) for t in tasks]

    def split(refs, which):
        found = []
        for count in counts:
            found.append(refs[: count[which]])
            refs = refs[count[which] :]
        return found, refs

    def body(*refs):
        ins, refs = split(refs, 0)
        outs, refs = split(refs, 1)
        scratch, refs = split(refs, 2)
        p = Spot(nz)
        p.greet()
        running = [t.steps(p, *given) for t, *given in zip(tasks, ins, outs, scratch)]
        done = [False] * len(tasks)
        for digit in order:
            i = int(digit)
            if not done[i]:
                done[i] = next(running[i], "end") == "end"
        while not all(done):
            for i, steps in enumerate(running):
                if not done[i]:
                    done[i] = next(steps, "end") == "end"

    sent = sum(x.size * 2 for t in tasks for x in t.ins)
    spare = max(t.spare for t in tasks) * 2**20
    held = [s for t in tasks for s in t.scratch if getattr(s, "memory_space", None) == pltpu.VMEM]
    held += [t.ins[i] for t in tasks for i in t.vmem_ins] + [t.outs[i] for t in tasks for i in t.vmem_outs]
    vmem = sum(math.prod(s.shape) * jnp.dtype(s.dtype).itemsize for s in held)
    results = pl.pallas_call(
        body,
        out_shape=[o for t in tasks for o in t.outs],
        in_specs=[in_vmem if i in t.vmem_ins else anywhere for t in tasks for i in range(len(t.ins))],
        out_specs=[
            in_vmem if i in t.vmem_outs else anywhere for t in tasks for i in range(len(t.outs))
        ],
        scratch_shapes=[s for t in tasks for s in t.scratch],
        compiler_params=pltpu.CompilerParams(
            collective_id=number, has_side_effects=True, vmem_limit_bytes=vmem + spare
        ),
        cost_estimate=pl.CostEstimate(
            flops=0, bytes_accessed=sent, transcendentals=0, remote_bytes_transferred=sent
        ),
    )(*[x for t in tasks for x in t.ins])
    found, _ = split(list(results), 1)
    if every:
        return found
    return found[0] if len(tasks) == 1 else [f[0] for f in found]


START_ORDER = "10212" + "230" + "1222" + "12222" + "22223" + "21"
FINISH_ORDER = "0103111101131101132220113222022322222"
KV_ORDER = "0120" + "12" + "222" + "021" + "2222" + "01" + "222" + "01" + "2"


class Kernels:
    def __init__(self, at):
        self.at = at
        self.blocks, self.nz = at.blocks, at.nz
        self.block = 2 * at.z + at.c
        self.number = 0

    def run(self, tasks, order=""):
        self.number += 1
        return run_tasks(self.nz, self.number, tasks, order)

    def flat(self, whole):
        return whole.reshape(-1, whole.shape[-1])

    def start(self, own, qkv_shard, gate, up):
        nz = self.nz
        tasks = [
            PlaneGather(own),
            PairGather(nz, qkv_shard, True),
            Copies(nz, gate, False),
            DealTask(nz, up),
        ]
        rows, qkv, gate_full, pieces = self.run(tasks, START_ORDER)
        return self.flat(rows), self.flat(qkv), gate_full, pieces

    def gather_kv(self, own, out_shard, pieces):
        nz = self.nz
        whole, out, up = self.run(
            [PairGather(nz, own, False), PairGather(nz, out_shard, True), Copies(nz, pieces, True)],
            "1021" + "012" + "0222" + "1" + "2222" + "02" + "1",
        )
        return whole.reshape((self.blocks,) + own.shape), self.flat(out), up

    def heads_forward(self, partial, tokens, gain_out, gain_in, down):
        task = HeadsForward(partial, tokens, gain_out, gain_in)
        self.number += 1
        (summed, normed), (pieces,) = run_tasks(
            self.nz, self.number, [task, DealTask(self.nz, down)], "01", True
        )
        return summed, normed, pieces

    def feed_forward(self, own, cotangent, gain, gate, up, down):
        task = FeedForward(self.nz, own, cotangent, gain, gate, up, down)
        self.number += 1
        return run_tasks(self.nz, self.number, [task])

    def heads_backward(self, *given):
        whole, d_middle, sums = self.run([HeadsBackward(*given)])
        return self.flat(whole), d_middle, jnp.sum(sums, axis=1)

    def scatter_kv_sums(self, parts, out_grad, grad):
        nz = self.nz
        given = parts.reshape((nz, 2) + parts.shape[1:])
        rows = out_grad.shape[0] // self.blocks
        out_given = out_grad.reshape(nz, 2, rows, out_grad.shape[1])
        kv, out, sums = self.run(
            [PairScatter(nz, given, False), PairScatter(nz, out_given, True), Sums(nz, grad, False)],
            KV_ORDER,
        )
        return kv, out, sums

    def scatter_heads_back(self, partial, sums):
        rows, shard = self.run([PlaneScatter(partial), DealBackTask(self.nz, sums)], "01")
        return rows, self.flat(shard)

    def finish(self, qkv_grad, gate_grad, up_grad, gains):
        rows = qkv_grad.shape[0] // self.blocks
        given = qkv_grad.reshape(self.nz, 2, rows, qkv_grad.shape[1])
        qkv, gate, up, total = self.run(
            [
                PairScatter(self.nz, given, True),
                Sums(self.nz, gate_grad, True),
                Sums(self.nz, up_grad, True),
                SumAll(gains.reshape(8, -1)),
            ],
            FINISH_ORDER,
        )
        return qkv, self.flat(gate), self.flat(up), total.reshape(gains.shape)


def project_kernel(info, normed_ref, weight_ref, q_ref, kv_ref, cos_ref, sin_ref):
    rows, half = cos_ref.shape
    dim = 2 * half
    heads = q_ref.shape[0]
    blocks = (info.shape[0] - 2) // 2
    me, prompts = info[2 * blocks], info[2 * blocks + 1]
    first = jnp.minimum(info[blocks + me], prompts) * rows
    positions = (lax.broadcasted_iota(jnp.int32, (rows, half), 0) + first).astype(f32)
    index = lax.broadcasted_iota(jnp.int32, (rows, half), 1).astype(f32)
    angles = positions * jnp.exp(index * (-2.0 * math.log(10000.0) / dim))
    cos_ref[...] = jnp.cos(angles)
    sin_ref[...] = jnp.sin(angles)
    for i in range(heads + 2):
        columns = slice(i * dim, (i + 1) * dim)
        linear = jnp.dot(normed_ref[...], weight_ref[:, columns], preferred_element_type=f32)
        if i <= heads:
            linear = rotate(linear, cos_ref[...], sin_ref[...])
        if i < heads:
            q_ref[i] = linear.astype(bf16)
        else:
            kv_ref[:, (i - heads) * dim : (i - heads + 1) * dim] = linear.astype(bf16)


def project(info, normed, weight):
    rows = normed.shape[0]
    heads = weight.shape[1] // HEAD_DIM - 2
    table = jax.ShapeDtypeStruct((rows, HEAD_DIM // 2), f32)
    return pl.pallas_call(
        project_kernel,
        in_specs=[pl.BlockSpec(memory_space=pltpu.SMEM), in_vmem, in_vmem],
        out_specs=[in_vmem] * 4,
        out_shape=[
            jax.ShapeDtypeStruct((heads, rows, HEAD_DIM), bf16),
            jax.ShapeDtypeStruct((rows, 2 * HEAD_DIM), bf16),
            table,
            table,
        ],
        compiler_params=pltpu.CompilerParams(vmem_limit_bytes=24 * 2**20),
        cost_estimate=pl.CostEstimate(
            flops=2 * rows * weight.size, bytes_accessed=2 * weight.size, transcendentals=0
        ),
    )(info, normed, weight)


def project_back_kernel(dq_ref, dkv_ref, cos_ref, sin_ref, weight_ref, lin_ref, out_ref):
    heads, rows, dim = dq_ref.shape
    cosine, sine = cos_ref[...], -sin_ref[...]
    for i in range(heads):
        lin_ref[:, i * dim : (i + 1) * dim] = rotate(dq_ref[i], cosine, sine).astype(bf16)
    start = heads * dim
    d_key = rotate(dkv_ref[:, :dim].astype(f32), cosine, sine)
    lin_ref[:, start : start + dim] = d_key.astype(bf16)
    lin_ref[:, start + dim :] = dkv_ref[:, dim:].astype(bf16)
    depth = weight_ref.shape[0]
    tile = 384

    @pl.loop(0, depth // tile)
    def _(i):
        at = pl.ds(pl.multiple_of(i * tile, 128), tile)
        out_ref[:, at] = contract(lin_ref[...], weight_ref[at, :], 1, 1).astype(bf16)


def project_back(d_query, d_kv, cosine, sine_table, weight):
    rows = d_kv.shape[0]
    depth, width = weight.shape
    return pl.pallas_call(
        project_back_kernel,
        in_specs=[in_vmem] * 5,
        out_specs=[in_vmem] * 2,
        out_shape=[
            jax.ShapeDtypeStruct((rows, width), bf16),
            jax.ShapeDtypeStruct((rows, depth), bf16),
        ],
        compiler_params=pltpu.CompilerParams(vmem_limit_bytes=24 * 2**20),
        cost_estimate=pl.CostEstimate(
            flops=2 * rows * weight.size, bytes_accessed=2 * weight.size, transcendentals=0
        ),
    )(d_query, d_kv, cosine, sine_table, weight)


def causal_mask(rows):
    shape = (rows, rows)
    return lax.broadcasted_iota(jnp.int32, shape, 1) <= lax.broadcasted_iota(jnp.int32, shape, 0)


def kind_of(info, step):
    blocks = pl.num_programs(0)
    me, prompts = info[2 * blocks], info[2 * blocks + 1]
    role = info[blocks + step]
    reads = (info[step] == info[me]) & (role < prompts) & (role < info[blocks + me])
    return jnp.where(step == me, 2, jnp.where(reads, 1, 0))


def forward_kernel(info, q_ref, kv_ref, out_ref, exact_ref, inv_ref, acc, total):
    step, last = pl.program_id(0), pl.num_programs(0) - 1
    heads, rows, dim = q_ref.shape
    kind = kind_of(info, step)

    @pl.when(step == 0)
    def _():
        acc[...] = jnp.zeros_like(acc)
        total[...] = jnp.zeros_like(total)

    def work(own):
        for head in range(heads):
            raw = contract(q_ref[head], kv_ref[0, :, :dim], 1, 1)
            weights = jnp.exp(softcap * jnp.tanh(raw * (score_scale / softcap)))
            if own:
                weights = jnp.where(causal_mask(rows), weights, 0.0)
            total[head] += jnp.sum(weights, axis=-1, keepdims=True)
            acc[head] += contract(weights.astype(bf16), kv_ref[0, :, dim:], 1, 0)

    @pl.when(kind == 1)
    def _():
        work(False)

    @pl.when(kind == 2)
    def _():
        work(True)

    @pl.when(step == last)
    def _():
        for head in range(heads):
            inverse = 1.0 / total[head]
            value = acc[head] * inverse
            inv_ref[head] = inverse
            exact_ref[:, head * dim : (head + 1) * dim] = value
            out_ref[:, head * dim : (head + 1) * dim] = value.astype(bf16)


def whole2(step, info):
    return (0, 0)


def whole3(step, info):
    return (0, 0, 0)


def by_step(step, info):
    return (step, 0, 0)


def attend(info, queries, all_kv):
    heads, rows, dim = queries.shape
    return pl.pallas_call(
        forward_kernel,
        grid_spec=pltpu.PrefetchScalarGridSpec(
            num_scalar_prefetch=1,
            grid=(all_kv.shape[0],),
            in_specs=[
                pl.BlockSpec((heads, rows, dim), whole3),
                pl.BlockSpec((1, rows, 2 * dim), by_step),
            ],
            out_specs=[
                pl.BlockSpec((rows, heads * dim), whole2),
                pl.BlockSpec((rows, heads * dim), whole2),
                pl.BlockSpec((heads, rows, 1), whole3),
            ],
            scratch_shapes=[
                pltpu.VMEM((heads, rows, dim), f32),
                pltpu.VMEM((heads, rows, 1), f32),
            ],
        ),
        out_shape=[
            jax.ShapeDtypeStruct((rows, heads * dim), bf16),
            jax.ShapeDtypeStruct((rows, heads * dim), f32),
            jax.ShapeDtypeStruct((heads, rows, 1), f32),
        ],
        compiler_params=pltpu.CompilerParams(vmem_limit_bytes=24 * 2**20),
        cost_estimate=pl.CostEstimate(
            flops=3 * 4 * heads * rows * rows * dim,
            bytes_accessed=8 * rows * dim * heads,
            transcendentals=6 * heads * rows * rows,
        ),
    )(info, queries, all_kv)


def backward_kernel(info, q_ref, kv_ref, up_ref, exact_ref, inv_ref, dq_ref, dkv_ref):
    step = pl.program_id(0)
    heads, rows, dim = q_ref.shape
    kind = kind_of(info, step)

    @pl.when(step == 0)
    def _():
        dq_ref[...] = jnp.zeros_like(dq_ref)

    def work(own):
        dk = jnp.zeros((rows, dim), f32)
        dv = jnp.zeros((rows, dim), f32)
        for head in range(heads):
            columns = slice(head * dim, (head + 1) * dim)
            up = up_ref[:, columns]
            delta = jnp.sum(up.astype(f32) * exact_ref[:, columns], axis=-1, keepdims=True)
            raw = contract(q_ref[head], kv_ref[0, :, :dim], 1, 1)
            bounded = jnp.tanh(raw * (score_scale / softcap))
            probs = jnp.exp(softcap * bounded) * inv_ref[head]
            if own:
                probs = jnp.where(causal_mask(rows), probs, 0.0)
            d_probs = contract(up, kv_ref[0, :, dim:], 1, 1)
            d_raw = probs * (d_probs - delta) * ((1.0 - bounded * bounded) * score_scale)
            d_raw = d_raw.astype(bf16)
            dq_ref[head] += contract(d_raw, kv_ref[0, :, :dim], 1, 0)
            dk += contract(d_raw, q_ref[head], 0, 0)
            dv += contract(probs.astype(bf16), up, 0, 0)
        dkv_ref[0, :, :dim] = dk.astype(bf16)
        dkv_ref[0, :, dim:] = dv.astype(bf16)

    @pl.when(kind == 1)
    def _():
        work(False)

    @pl.when(kind == 0)
    def _():
        dkv_ref[...] = jnp.zeros_like(dkv_ref)

    @pl.when(kind == 2)
    def _():
        work(True)


def attend_back(info, queries, all_kv, upstream, exact, inverse):
    heads, rows, dim = queries.shape
    blocks = all_kv.shape[0]
    return pl.pallas_call(
        backward_kernel,
        grid_spec=pltpu.PrefetchScalarGridSpec(
            num_scalar_prefetch=1,
            grid=(blocks,),
            in_specs=[
                pl.BlockSpec((heads, rows, dim), whole3),
                pl.BlockSpec((1, rows, 2 * dim), by_step),
                pl.BlockSpec((rows, heads * dim), whole2),
                pl.BlockSpec((rows, heads * dim), whole2),
                pl.BlockSpec((heads, rows, 1), whole3),
            ],
            out_specs=[
                pl.BlockSpec((heads, rows, dim), whole3),
                pl.BlockSpec((1, rows, 2 * dim), by_step),
            ],
        ),
        out_shape=[
            jax.ShapeDtypeStruct((heads, rows, dim), f32),
            jax.ShapeDtypeStruct((blocks, rows, 2 * dim), bf16),
        ],
        compiler_params=pltpu.CompilerParams(vmem_limit_bytes=24 * 2**20),
        cost_estimate=pl.CostEstimate(
            flops=3 * 10 * heads * rows * rows * dim,
            bytes_accessed=16 * rows * dim * heads,
            transcendentals=6 * heads * rows * rows,
        ),
    )(info, queries, all_kv, upstream, exact, inverse)


def on_device(
    tokens,
    cotangent,
    norm_attn_in,
    w_query,
    w_key,
    w_value,
    w_out,
    norm_attn_out,
    norm_ff_in,
    w_gate,
    w_up,
    w_down,
    norm_ff_out,
    block_group,
    block_role,
):
    at = Place()
    own_rows, depth = tokens.shape
    shard_rows, units = w_gate.shape
    regular = at.nz == 4 and shard_rows % 32 == 0 and units == depth and units % 768 == 0
    comm = Kernels(at) if regular else Permutes(at)
    blocks = at.blocks
    info = jnp.concatenate(
        [block_group, block_role, jnp.stack([comm.block, blocks // 4]).astype(jnp.int32)]
    )

    token_f32 = tokens.astype(f32)
    heads_width = w_query.shape[1]
    normed_one, qkv_full, gate_full, up_pieces = comm.start(
        normalize(token_f32, norm_attn_in).astype(bf16),
        jnp.concatenate([w_query, w_key, w_value], axis=1),
        w_gate,
        w_up,
    )
    queries, own_kv, cosine, sine_table = project(info, normed_one, qkv_full)
    all_kv, out_full, up_full = comm.gather_kv(own_kv, w_out.T, up_pieces)
    attn_rows, attended, inverse = attend(info, queries, all_kv)
    attn_proj, normed_two, down_pieces = comm.heads_forward(
        contract(attn_rows, out_full, 1, 1).astype(bf16), tokens, norm_attn_out, norm_ff_in, w_down.T
    )

    ff_proj, d_normed_two, gate_sum, up_sum, down_sum = comm.feed_forward(
        normed_two, cotangent, norm_ff_out, gate_full, up_full, down_pieces
    )
    middle = token_f32 + normalize(attn_proj, norm_attn_out)
    layer_out = middle + normalize(ff_proj, norm_ff_out)
    upstream = cotangent.astype(f32)
    _, grad_ff_out = normalize_back(ff_proj, norm_ff_out, upstream)

    d_proj_rows, d_middle, inner_gains = comm.heads_backward(
        d_normed_two, attn_proj, tokens, cotangent, norm_attn_out, norm_ff_in
    )
    d_attended = contract(d_proj_rows, out_full, 1, 0).astype(bf16)
    d_query, d_kv_parts = attend_back(info, queries, all_kv, d_attended, attended, inverse)
    d_kv, grad_out, down_sums = comm.scatter_kv_sums(
        d_kv_parts, contract(d_proj_rows, attn_rows, 0, 0).astype(bf16), down_sum
    )
    d_qkv_lin, d_partial = project_back(d_query, d_kv, cosine, sine_table, qkv_full)
    d_normed_one, grad_down = comm.scatter_heads_back(d_partial, down_sums)
    d_token_part, grad_attn_in = normalize_back(token_f32, norm_attn_in, d_normed_one)
    input_grad = (d_middle + d_token_part).astype(bf16)
    grad_qkv, grad_gate, grad_up, gains = comm.finish(
        contract(normed_one, d_qkv_lin, 0, 0).astype(bf16),
        gate_sum,
        up_sum,
        jnp.stack([grad_attn_in, inner_gains[0], inner_gains[1], grad_ff_out]),
    )
    grad_qkv, grad_gate, grad_up = [g.astype(f32) for g in (grad_qkv, grad_gate, grad_up)]
    return (
        layer_out.astype(bf16),
        input_grad,
        gains[0],
        grad_qkv[:, :heads_width],
        grad_qkv[:, heads_width : heads_width + HEAD_DIM],
        grad_qkv[:, heads_width + HEAD_DIM :],
        grad_out.astype(f32).T,
        gains[1],
        gains[2],
        grad_gate,
        grad_up,
        grad_down.astype(f32).T,
        gains[3],
    )


def solution(mesh):
    rows, weight, turned = P(("blk", "heads"), None), P("blk", "heads"), P("heads", "blk")
    return jax.shard_map(
        on_device,
        mesh=mesh,
        in_specs=(
            rows, rows, P(), weight, weight, weight, turned, P(), P(), weight, weight, turned,
            P(), P(), P(),
        ),
        out_specs=(
            rows, rows, P(), weight, weight, weight, turned, P(), P(), weight, weight, turned, P(),
        ),
        check_vma=False,
    )
```

```python
import math

import jax
import jax.numpy as jnp
from jax import lax
from jax.experimental import pallas as pl
from jax.experimental.pallas import tpu as pltpu
from jax.sharding import PartitionSpec as P

HEAD_DIM = 256


softcap = 50.0
epsilon = 1e-06
score_scale = HEAD_DIM ** (-0.5)
bf16 = jnp.bfloat16
f32 = jnp.float32


def contract(left_side, right_side, left_dim, right_dim):
    return lax.dot_general(
        left_side,
        right_side,
        (((left_dim,), (right_dim,)), ((), ())),
        preferred_element_type=f32,
    )


def factor_of(values):
    return lax.rsqrt(jnp.mean(values * values, axis=-1, keepdims=True) + epsilon)


def normalize(values, weight_gain):
    return values * factor_of(values) * (1.0 + weight_gain)


def normalize_back(values, weight_gain, upstream):
    factor = factor_of(values)
    unit = values * factor
    scaled = upstream * (1.0 + weight_gain)
    inner = jnp.mean(scaled * unit, axis=-1, keepdims=True)
    return (scaled - unit * inner) * factor, jnp.sum(upstream * unit, axis=0)


def rotate(tensor, cosine, sine_table):
    half_dim = HEAD_DIM // 2
    first_half = tensor[..., :half_dim]
    second_half = tensor[..., half_dim:]
    return jnp.concatenate(
        [
            first_half * cosine - second_half * sine_table,
            second_half * cosine + first_half * sine_table,
        ],
        axis=-1,
    )


def swap_core(v):
    return lax.ppermute(v, "heads", [(i, i ^ 1) for i in range(4)])


def swap_y(v):
    return lax.ppermute(v, "heads", [(i, i ^ 2) for i in range(4)])


def swap_x(v):
    blocks = lax.axis_size("blk")
    return lax.ppermute(v, "blk", [(i, i ^ 1) for i in range(blocks)])


def pair_up(own, other, place, axis):
    first = jnp.where(place == 0, own, other)
    second = jnp.where(place == 0, other, own)
    return jnp.concatenate([first, second], axis=axis)


def shift_z(v, step, senders):
    pairs = []
    for z in senders:
        for x in range(2):
            pairs.append((2 * z + x, 2 * (z + step) + x))
    return lax.ppermute(v, "blk", pairs)


class Place:
    def __init__(self):
        self.blocks = lax.axis_size("blk")
        self.nz = self.blocks // 2
        self.b = lax.axis_index("blk")
        self.h = lax.axis_index("heads")
        self.z, self.x = self.b // 2, self.b % 2
        self.y, self.c = self.h // 2, self.h % 2


def gather_z(at, unit):
    nz = at.nz
    up, down = unit, unit
    ups, downs = [None], [None]
    for s in range(1, nz):
        up = shift_z(up, 1, range(s - 1, nz - 1))
        down = shift_z(down, -1, range(1, nz - s + 1))
        ups.append(up)
        downs.append(down)
    return [unit] + [jnp.where(at.z >= s, ups[s], downs[nz - s]) for s in range(1, nz)]


def scatter_z(at, parts):
    nz = at.nz
    up = down = None
    for t in range(1, nz):
        k = nz - t
        send_up = parts[nz - k].astype(f32)
        send_down = parts[k].astype(f32)
        if up is not None:
            send_up = send_up + up.astype(f32)
            send_down = send_down + down.astype(f32)
        up = shift_z(send_up.astype(bf16), 1, range(0, nz - k))
        down = shift_z(send_down.astype(bf16), -1, range(k, nz))
    return parts[0].astype(f32) + (up.astype(f32) + down.astype(f32))


def deal_z(at, parts):
    nz = at.nz
    got = [parts[0]]
    for s in range(1, nz):
        up = shift_z(parts[nz - s], s, range(0, nz - s))
        down = shift_z(parts[nz - s], s - nz, range(nz - s, nz))
        got.append(jnp.where(at.z >= s, up, down))
    return got


def turn(at, whole):
    return [
        lax.dynamic_index_in_dim(whole, (at.z - s) % at.nz, 0, keepdims=False)
        for s in range(at.nz)
    ]


def unturn(at, parts):
    whole = jnp.zeros((at.nz,) + parts[0].shape, parts[0].dtype)
    for s, part in enumerate(parts):
        whole = lax.dynamic_update_index_in_dim(whole, part, (at.z - s) % at.nz, 0)
    return whole


def gather_zx(at, unit):
    got = []
    for part in gather_z(at, unit):
        got.append(pair_up(part[None], swap_x(part)[None], at.x, 0))
    return unturn(at, got)


def gather_xz(at, unit):
    both = pair_up(unit[None], swap_x(unit)[None], at.x, 0)
    return unturn(at, gather_z(at, both))


def pick(pair, place):
    mine = jnp.where(place == 0, pair[0], pair[1])
    other = jnp.where(place == 0, pair[1], pair[0])
    return mine, other


def scatter_zx(at, parts):
    total = scatter_z(at, parts)
    mine, other = pick(total, at.x)
    return mine + swap_x(other.astype(bf16)).astype(f32)


def scatter_xz(at, parts):
    sums = []
    for part in parts:
        mine, other = pick(part, at.x)
        sums.append(mine.astype(f32) + swap_x(other.astype(bf16)).astype(f32))
    return scatter_z(at, sums)


def rows_to_block(at, own):
    both = pair_up(own, swap_core(own), at.c, 0)
    pair = pair_up(both[None], swap_y(both)[None], at.y, 0)
    return pair.reshape(4 * own.shape[0], own.shape[1])


def rows_from_block(at, partial_sum):
    rows = partial_sum.shape[0] // 4
    parts = partial_sum.reshape(2, 2, rows, partial_sum.shape[1])
    mine, other = pick(parts.swapaxes(0, 1), at.c)
    total = mine + swap_core(other.astype(bf16)).astype(f32)
    mine, other = pick(total, at.y)
    return mine + swap_y(other.astype(bf16)).astype(f32)


def spread_weight(at, shard):
    rows, units = shard.shape
    half = rows // 2
    keep, send = pick(shard.reshape(2, half, units), at.c)
    wide = pair_up(keep[None], swap_core(send)[None], at.c, 0)
    quarter = 2 * units // at.nz
    per_core = units // quarter
    pieces = wide.reshape(2, half, per_core, quarter).transpose(0, 2, 1, 3)
    pieces = pieces.reshape(at.nz, half, quarter)
    got = unturn(at, deal_z(at, turn(at, pieces)))
    got = pair_up(got[:, None], swap_x(got)[:, None], at.x, 1)
    got = pair_up(got, swap_y(got), at.y, 3)
    got = pair_up(got[:, :, None], swap_core(got)[:, :, None], at.c, 2)
    return got.reshape(at.blocks * rows, 2 * quarter)


def collect_weight(at, grad):
    depth, width = grad.shape
    half, quarter = depth // (2 * at.blocks), width // 2
    parts = grad.reshape(at.nz, 2, 2, half, width)
    mine, other = pick(parts.transpose(2, 0, 1, 3, 4), at.c)
    total = mine + swap_core(other.astype(bf16)).astype(f32)
    mine, other = pick((total[..., :quarter], total[..., quarter:]), at.y)
    total = mine + swap_y(other.astype(bf16)).astype(f32)
    mine, other = pick((total[:, 0], total[:, 1]), at.x)
    total = mine + swap_x(other.astype(bf16)).astype(f32)
    got = unturn(at, deal_z(at, turn(at, total.astype(bf16))))
    per_core = at.nz // 2
    wide = got.reshape(2, per_core, half, quarter).transpose(0, 2, 1, 3)
    wide = wide.reshape(2, half, per_core * quarter)
    mine, other = pick(wide, at.c)
    rows = pair_up(mine, swap_core(other), at.c, 0)
    return rows.astype(f32)


def sum_all(at, values):
    total = values
    for bit in (1, 2):
        total = total + lax.ppermute(total, "heads", [(i, i ^ bit) for i in range(4)])
    bit = 1
    while bit < at.blocks:
        total = total + lax.ppermute(total, "blk", [(i, i ^ bit) for i in range(at.blocks)])
        bit *= 2
    return total


class Permutes:
    def __init__(self, at):
        self.at = at
        self.block, self.blocks, self.nz = at.b, at.blocks, at.nz

    def split(self, whole):
        return turn(self.at, whole.reshape((self.nz, whole.shape[0] // self.nz) + whole.shape[1:]))

    def start(self, own, qkv_shard, gate, up):
        at = self.at
        qkv_full = gather_zx(at, qkv_shard).reshape(own.shape[1], -1)
        return rows_to_block(at, own), qkv_full, spread_weight(at, gate), spread_weight(at, up)

    def gather_kv(self, own, out_shard, up):
        out_full = gather_zx(self.at, out_shard).reshape(-1, out_shard.shape[1])
        return gather_zx(self.at, own).reshape((self.blocks,) + own.shape), out_full, up

    def heads_forward(self, partial, tokens, gain_out, gain_in, down):
        summed = rows_from_block(self.at, partial)
        middle = tokens.astype(f32) + normalize(summed, gain_out)
        return summed, normalize(middle, gain_in).astype(bf16), spread_weight(self.at, down)

    def gather_z(self, own):
        whole = unturn(self.at, gather_z(self.at, own))
        return whole.reshape(-1, own.shape[1])

    def scatter_z(self, partial):
        return scatter_z(self.at, self.split(partial))

    def feed_forward(self, own, cotangent, gain, gate, up, down):
        normed = self.gather_z(own)
        gate_lin = jnp.dot(normed, gate, preferred_element_type=f32)
        up_lin = jnp.dot(normed, up, preferred_element_type=f32)
        hidden = (jax.nn.gelu(gate_lin, approximate=True) * up_lin).astype(bf16)
        ff_proj = self.scatter_z(contract(hidden, down, 1, 1).astype(bf16))
        d_ff, _ = normalize_back(ff_proj, gain, cotangent.astype(f32))
        d_ff_rows = self.gather_z(d_ff.astype(bf16))
        d_hidden = contract(d_ff_rows, down, 1, 0)
        _, glu_back = jax.vjp(
            lambda gate_in, up_in: jax.nn.gelu(gate_in, approximate=True) * up_in, gate_lin, up_lin
        )
        d_gate, d_up = [d.astype(bf16) for d in glu_back(d_hidden)]
        d_partial = contract(d_gate, gate, 1, 1) + contract(d_up, up, 1, 1)
        d_normed = self.scatter_z(d_partial.astype(bf16))
        grads = [
            contract(left, right, 0, 0).astype(bf16)
            for left, right in ((normed, d_gate), (normed, d_up), (d_ff_rows, hidden))
        ]
        return [ff_proj, d_normed] + grads

    def heads_backward(self, d_normed, projected, tokens, cotangent, gain_out, gain_in):
        middle = tokens.astype(f32) + normalize(projected, gain_out)
        part, by_in = normalize_back(middle, gain_in, d_normed)
        d_middle = cotangent.astype(f32) + part
        d_projected, by_out = normalize_back(projected, gain_out, d_middle)
        rows = rows_to_block(self.at, d_projected.astype(bf16))
        return rows, d_middle, jnp.stack([by_out, by_in])

    def scatter_pairs(self, grad):
        rows = grad.shape[0] // self.blocks
        return scatter_xz(self.at, self.split(grad.reshape(self.blocks, rows, -1)))

    def scatter_kv_sums(self, parts, out_grad, grad):
        kv = scatter_xz(self.at, self.split(parts))
        return kv, self.scatter_pairs(out_grad), collect_weight(self.at, grad)

    def scatter_heads_back(self, partial, sums):
        return rows_from_block(self.at, partial), sums

    def finish(self, qkv_grad, gate_grad, up_grad, gains):
        gate, up = collect_weight(self.at, gate_grad), collect_weight(self.at, up_grad)
        return self.scatter_pairs(qkv_grad), gate, up, sum_all(self.at, gains)


MESH = pl.DeviceIdType.MESH
DMA = pltpu.SemaphoreType.DMA
anywhere = pl.BlockSpec(memory_space=pl.ANY)
in_vmem = pl.BlockSpec(memory_space=pltpu.VMEM)


def remote(src, dst, send_sem, recv_sem, target):
    return pltpu.make_async_remote_copy(
        src_ref=src,
        dst_ref=dst,
        send_sem=send_sem,
        recv_sem=recv_sem,
        device_id=target,
        device_id_type=MESH,
    )


def flip(bit, by):
    return 1 - bit if by else bit


def exclusive_or(z, i):
    low, high = lax.rem(z, 2), lax.rem(z // 2, 2)
    rest = z - 2 * high - low
    return rest + 2 * flip(high, i // 2) + flip(low, i % 2)


class Spot:
    def __init__(self, nz):
        self.nz = nz
        h, b = lax.axis_index("heads"), lax.axis_index("blk")
        self.y, self.c = h // 2, h % 2
        self.z, self.x = b // 2, b % 2

    def device(self, z=None, x=None, y=None, c=None):
        z = self.z if z is None else z
        x = self.x if x is None else x
        y = self.y if y is None else y
        c = self.c if c is None else c
        return (2 * y + c, 2 * z + x)

    def partner(self):
        return self.device(c=1 - self.c)

    def greet(self):
        found = []
        for dx, dy, dc in [(0, 0, 1), (1, 0, 0), (1, 0, 1), (0, 1, 0), (0, 1, 1), (1, 1, 0), (1, 1, 1)]:
            found.append(self.device(x=flip(self.x, dx), y=flip(self.y, dy), c=flip(self.c, dc)))
        for s in range(1, self.nz):
            z = lax.rem(self.z + s, self.nz)
            found += [self.device(z=z), self.device(z=z, c=1 - self.c)]
        barrier = pltpu.get_barrier_semaphore()
        for device in found:
            pl.semaphore_signal(barrier, inc=1, device_id=device, device_id_type=MESH)
        pl.semaphore_wait(barrier, len(found))


def row_step(rows):
    return next(step for step in (48, 32, 16) if rows % step == 0)


def add_rows(out, left, right):
    rows = left.shape[0]
    step = row_step(rows)

    @pl.loop(0, rows // step)
    def _(i):
        at = pl.ds(pl.multiple_of(i * step, step), step)
        out[at, :] = (left[at, :].astype(f32) + right[at, :].astype(f32)).astype(out.dtype)


class LineGather:
    def __init__(self, spot, entry, send, recv):
        self.spot, self.entry = spot, entry
        self.send, self.recv = send, recv

    def copies(self, s):
        p, nz = self.spot, self.spot.nz
        up_at = lax.rem(p.z - s + 1 + nz, nz)
        down_at = lax.rem(p.z + s - 1, nz)
        up = remote(
            self.entry(up_at),
            self.entry(up_at),
            self.send.at[0, s],
            self.recv.at[0, s],
            p.device(z=lax.rem(p.z + 1, nz)),
        )
        down = remote(
            self.entry(down_at),
            self.entry(down_at),
            self.send.at[1, s],
            self.recv.at[1, s],
            p.device(z=lax.rem(p.z + nz - 1, nz)),
        )
        return (
            ((p.z >= s - 1) & (p.z < nz - 1), p.z >= s, up),
            ((p.z <= nz - s) & (p.z > 0), p.z <= nz - 1 - s, down),
        )

    def start(self, s):
        for sends, _, copy in self.copies(s):
            pl.when(sends)(copy.start)

    def arrive(self, s):
        for _, receives, copy in self.copies(s):
            pl.when(receives)(copy.wait_recv)

    def finish(self):
        for s in range(1, self.spot.nz):
            for sends, _, copy in self.copies(s):
                pl.when(sends)(copy.wait_send)

    def newest(self, s):
        p, nz = self.spot, self.spot.nz
        return (
            (p.z >= s, lax.rem(p.z - s + nz, nz)),
            (p.z <= nz - 1 - s, lax.rem(p.z + s, nz)),
        )


class LineScatter:
    def __init__(self, spot, parts, up, down, send, recv):
        self.spot, self.parts, self.up, self.down = spot, parts, up, down
        self.send, self.recv = send, recv

    def copies(self, t):
        p, nz = self.spot, self.spot.nz
        k = nz - t
        up = remote(
            self.parts(lax.rem(p.z + k, nz)),
            self.up.at[t - 1],
            self.send.at[0, t],
            self.recv.at[0, t],
            p.device(z=lax.rem(p.z + 1, nz)),
        )
        down = remote(
            self.parts(lax.rem(p.z - k + nz, nz)),
            self.down.at[t - 1],
            self.send.at[1, t],
            self.recv.at[1, t],
            p.device(z=lax.rem(p.z + nz - 1, nz)),
        )
        return (
            (p.z <= nz - 1 - k, (p.z >= 1) & (p.z <= t), up),
            (p.z >= k, (p.z <= nz - 2) & (p.z >= nz - 1 - t), down),
        )

    def start(self, t):
        for sends, _, copy in self.copies(t):
            pl.when(sends)(copy.start)

    def arrive(self, t):
        p, nz = self.spot, self.spot.nz
        k = nz - t
        for way, (_, receives, copy) in enumerate(self.copies(t)):

            @pl.when(receives)
            def _(way=way, copy=copy):
                copy.wait_recv()
                if t < nz - 1:
                    index = lax.rem(p.z + k - 1, nz) if way == 0 else lax.rem(p.z - k + 1 + nz, nz)
                    came = (self.up if way == 0 else self.down).at[t - 1]
                    add_rows(self.parts(index), self.parts(index), came)

    def finish(self):
        for t in range(1, self.spot.nz):
            for sends, _, copy in self.copies(t):
                pl.when(sends)(copy.wait_send)

    def total(self, out):
        p, last = self.spot, self.spot.nz - 2
        mine = self.parts(p.z)
        inner = (p.z > 0) & (p.z < p.nz - 1)

        @pl.when(p.z == 0)
        def _():
            add_rows(out, mine, self.down.at[last])

        @pl.when(p.z == p.nz - 1)
        def _():
            add_rows(out, mine, self.up.at[last])

        step = row_step(out.shape[0])

        @pl.when(inner)
        def _():
            @pl.loop(0, out.shape[0] // step)
            def _(i):
                at = pl.ds(pl.multiple_of(i * step, step), step)
                sides = self.up[last, at, :].astype(f32) + self.down[last, at, :].astype(f32)
                out[at, :] = (mine[at, :].astype(f32) + sides).astype(out.dtype)


class Task:
    ins = ()
    outs = ()
    scratch = ()
    vmem_ins = ()
    vmem_outs = ()
    spare = 5

    def steps(self, p, ins, outs, scratch):
        raise NotImplementedError


class PlaneGather(Task):
    vmem_ins = (0,)
    vmem_outs = (0,)

    def __init__(self, own):
        self.ins = (own,)
        self.outs = (jax.ShapeDtypeStruct((4,) + own.shape, bf16),)
        self.scratch = (DMA((6,)), DMA((4, 2)), DMA((2,)), DMA)

    def steps(self, p, ins, outs, scratch):
        (own,), (whole,), (send, recv, on_send, local) = ins, outs, scratch
        part, half = 2 * p.y + p.c, own.shape[0] // 2
        same = p.c == p.x

        def rows(of, i):
            return whole.at[of, pl.ds(i * half, half)]

        def piece(i):
            return own.at[pl.ds(i * half, half)]

        along = [
            remote(piece(i), rows(part, i), send.at[2 * k + i], recv.at[part, i], target)
            for k, target in enumerate((p.device(x=1 - p.x, c=p.x), p.device(y=1 - p.y, c=p.x)))
            for i in range(2)
        ]
        home = [
            remote(piece(i), rows(part, i), send.at[4 + i], recv.at[part, i], p.device(c=1 - p.c))
            for i in range(2)
        ]
        keep = pltpu.make_async_copy(own, whole.at[part], local)

        def passed(k, by_x):
            if by_x:
                here = rows(2 * p.y + k, 0)
                return remote(here, here, on_send.at[k], recv.at[2 * p.y + k, 0], p.device(y=1 - p.y))
            here = rows(2 * (1 - p.y) + k, 1)
            return remote(
                here, here, on_send.at[k], recv.at[2 * (1 - p.y) + k, 1], p.device(x=1 - p.x)
            )

        along[0].start()
        along[3].start()
        along[1].start()
        along[2].start()
        pl.when(same)(keep.start)
        for copy in home:
            pl.when(jnp.logical_not(same))(copy.start)
        yield
        for k in range(2):

            @pl.when(jnp.logical_not(same))
            def _(k=k):
                passed(k, True).wait_recv()
                passed(k, True).start()

            @pl.when(same)
            def _(k=k):
                passed(k, False).wait_recv()
                passed(k, False).start()

        yield
        for copy in along:
            copy.wait_send()
        pl.when(same)(keep.wait)
        for copy in home:
            pl.when(jnp.logical_not(same))(copy.wait_send)
        for k in range(2):
            pl.when(jnp.logical_not(same))(passed(k, True).wait_send)
            pl.when(same)(passed(k, False).wait_send)
        for slot in range(4):
            y, c = slot // 2, slot % 2
            for i in range(2):
                came = remote(rows(slot, i), rows(slot, i), send.at[0], recv.at[slot, i], p.partner())
                if i == 0:
                    waited = jnp.logical_not(same) & (p.y == y)
                else:
                    waited = same & (p.y != y)
                mine = same & (part == slot)
                pl.when(jnp.logical_not(waited | mine))(came.wait_recv)


class PlaneScatter(Task):
    vmem_ins = (0,)
    vmem_outs = (0,)

    def __init__(self, partial):
        rows, depth = partial.shape[0] // 4, partial.shape[1]
        self.ins = (partial.reshape(4, rows, depth),)
        self.outs = (jax.ShapeDtypeStruct((rows, depth), f32),)
        self.scratch = (pltpu.VMEM((4, rows, depth), bf16), DMA((4,)), DMA((4,)))

    def steps(self, p, ins, outs, scratch):
        (parts,), (out,), (came, send, recv) = ins, outs, scratch
        head, ours = 2 * p.y + p.x, 2 * p.y + p.c

        def copy_to(part):
            target = p.device(x=p.c, y=part // 2, c=part % 2)
            return remote(parts.at[part], came.at[head], send.at[part], recv.at[head], target)

        for part in range(4):
            here = (p.x == p.c) & (part == ours)
            pl.when(jnp.logical_not(here))(copy_to(part).start)
        yield
        for part in range(4):
            here = (p.x == p.c) & (part == ours)
            pl.when(jnp.logical_not(here))(copy_to(part).wait_send)
            arrived = remote(parts.at[part], came.at[part], send.at[part], recv.at[part], p.partner())
            mine = (p.x == p.c) & (part == head)
            pl.when(jnp.logical_not(mine))(arrived.wait_recv)

        @pl.when(p.x == p.c)
        def _():
            came[head] = parts[ours]

        @pl.loop(0, out.shape[0] // 16)
        def _(i):
            at = pl.ds(pl.multiple_of(i * 16, 16), 16)
            low = came[0, at, :].astype(f32) + came[1, at, :].astype(f32)
            out[at, :] = low + (came[2, at, :].astype(f32) + came[3, at, :].astype(f32))


class HeadsForward(PlaneScatter):
    vmem_ins = (0, 1, 2, 3)
    vmem_outs = (0, 1)

    def __init__(self, partial, tokens, gain_out, gain_in):
        super().__init__(partial)
        depth = tokens.shape[1]
        self.ins += (tokens, gain_out.reshape(1, depth), gain_in.reshape(1, depth))
        self.outs += (jax.ShapeDtypeStruct(tokens.shape, bf16),)

    def steps(self, p, ins, outs, scratch):
        partial, tokens, gain_out, gain_in = ins
        summed, normed = outs
        yield from super().steps(p, (partial,), (summed,), scratch)

        @pl.loop(0, normed.shape[0] // 16)
        def _(i):
            at = pl.ds(pl.multiple_of(i * 16, 16), 16)
            middle = tokens[at, :].astype(f32) + normalize(summed[at, :], gain_out[...])
            normed[at, :] = normalize(middle, gain_in[...]).astype(bf16)


class HeadsBackward(PlaneGather):
    vmem_ins = (0, 1, 2, 3, 4, 5)
    vmem_outs = (0, 1, 2)

    def __init__(self, d_normed, projected, tokens, cotangent, gain_out, gain_in):
        super().__init__(tokens)
        depth = tokens.shape[1]
        gains = (gain_out.reshape(1, depth), gain_in.reshape(1, depth))
        self.ins = (d_normed, projected, tokens, cotangent) + gains
        self.outs += (
            jax.ShapeDtypeStruct(tokens.shape, f32),
            jax.ShapeDtypeStruct((2, 16, depth), f32),
        )
        self.scratch += (pltpu.VMEM(tokens.shape, bf16),)

    def steps(self, p, ins, outs, scratch):
        d_normed, projected, tokens, cotangent, gain_out, gain_in = ins
        whole, d_middle, sums = outs
        *sems, own = scratch
        sums[...] = jnp.zeros_like(sums)

        def back(values, gain, upstream):
            factor = factor_of(values)
            unit = values * factor
            scaled = upstream * (1.0 + gain)
            inner = jnp.mean(scaled * unit, axis=-1, keepdims=True)
            return (scaled - unit * inner) * factor, upstream * unit

        @pl.loop(0, own.shape[0] // 16)
        def _(i):
            at = pl.ds(pl.multiple_of(i * 16, 16), 16)
            values = projected[at, :]
            middle = tokens[at, :].astype(f32) + normalize(values, gain_out[...])
            part, by_in = back(middle, gain_in[...], d_normed[at, :])
            total = cotangent[at, :].astype(f32) + part
            d_middle[at, :] = total
            d_values, by_out = back(values, gain_out[...], total)
            own[at, :] = d_values.astype(bf16)
            sums[0] += by_out
            sums[1] += by_in

        yield from super().steps(p, (own,), (whole,), sems)


class PairGather(Task):
    vmem_ins = (0,)
    vmem_outs = (0,)

    def __init__(self, nz, own, trade):
        self.trade = trade
        self.ins = (own,)
        self.outs = (jax.ShapeDtypeStruct((nz, 2) + own.shape, bf16),)
        self.scratch = (DMA((2, nz)), DMA((2, nz)), DMA((nz,)), DMA((nz,)), DMA, DMA, DMA)

    def steps(self, p, ins, outs, scratch):
        (own,), (full,), (send, recv, x_send, x_recv, t_send, t_recv, local) = ins, outs, scratch
        nz = p.nz
        keep = pltpu.make_async_copy(own, full.at[p.z, p.c], local)
        line = LineGather(p, lambda z: full.at[z, p.c], send, recv)

        def across(z):
            here = full.at[z, p.c]
            return remote(here, here, x_send.at[z], x_recv.at[z], p.partner())

        if self.trade:
            same = p.c == p.x
            move = remote(own, full.at[p.z, p.x], t_send, t_recv, p.device(x=1 - p.x, c=1 - p.c))
            pl.when(same)(keep.start)
            pl.when(jnp.logical_not(same))(move.start)
            yield
            pl.when(same)(keep.wait)
            pl.when(jnp.logical_not(same))(move.wait_recv)
        else:
            keep.start()
            keep.wait()
        line.start(1)
        across(p.z).start()
        yield
        for s in range(1, nz):
            line.arrive(s)
            if s < nz - 1:
                line.start(s + 1)
            for came, z in line.newest(s):
                pl.when(came)(across(z).start)
            yield
        line.finish()
        if self.trade:
            pl.when(jnp.logical_not(same))(move.wait_send)
        for z in range(nz):
            across(z).wait()


class ZGather(Task):
    vmem_ins = (0,)
    vmem_outs = (0,)

    def __init__(self, nz, own):
        self.ins = (own,)
        self.outs = (jax.ShapeDtypeStruct((nz,) + own.shape, bf16),)
        self.scratch = (DMA((2, nz)), DMA((2, nz)), DMA)

    def steps(self, p, ins, outs, scratch):
        (own,), (full,), (send, recv, local) = ins, outs, scratch
        line = LineGather(p, lambda z: full.at[z], send, recv)
        keep = pltpu.make_async_copy(own, full.at[p.z], local)
        keep.start()
        keep.wait()
        line.start(1)
        yield
        for s in range(1, p.nz):
            line.arrive(s)
            if s < p.nz - 1:
                line.start(s + 1)
            yield
        line.finish()


class ZScatter(Task):
    vmem_outs = (0,)

    def __init__(self, nz, partial):
        rows, depth = partial.shape[0] // nz, partial.shape[1]
        self.ins = (partial.reshape(nz, rows, depth),)
        self.outs = (jax.ShapeDtypeStruct((rows, depth), f32),)
        line = pltpu.VMEM((nz - 1, rows, depth), bf16)
        self.scratch = (
            pltpu.VMEM((nz, rows, depth), bf16), line, line, DMA((2, nz)), DMA((2, nz)), DMA
        )

    def steps(self, p, ins, outs, scratch):
        (given,), (out,), (parts, up, down, send, recv, local) = ins, outs, scratch
        bring = pltpu.make_async_copy(given, parts, local)
        bring.start()
        bring.wait()
        line = LineScatter(p, lambda z: parts.at[z], up, down, send, recv)
        line.start(1)
        yield
        for t in range(1, p.nz):
            line.arrive(t)
            if t < p.nz - 1:
                line.start(t + 1)
            yield
        line.total(out)
        line.finish()


class PairScatter(Task):
    vmem_outs = (0,)

    def __init__(self, nz, given, trade):
        _, _, rows, width = given.shape
        self.trade = trade
        self.ins = (given,)
        self.outs = (jax.ShapeDtypeStruct((rows, width), bf16),)
        whole = pltpu.VMEM((nz, rows, width), bf16)
        line = pltpu.VMEM((nz - 1, rows, width), bf16)
        self.scratch = (
            whole, whole, line, line,
            DMA((nz,)), DMA((nz,)), DMA((2, nz)), DMA((2, nz)), DMA((nz,)), DMA, DMA, DMA,
        )

    def steps(self, p, ins, outs, scratch):
        (given,), (out,) = ins, outs
        parts, came, up, down, x_send, x_recv, send, recv, local, b_send, b_recv, b_local = scratch
        nz = p.nz
        order = [exclusive_or(p.z, i) for i in (3, 2, 1, 0)]

        def away(z):
            return remote(given.at[z, 1 - p.c], came.at[z], x_send.at[z], x_recv.at[z], p.partner())

        def bring(z):
            return pltpu.make_async_copy(given.at[z, p.c], parts.at[z], local.at[z])

        for z in order:
            away(z).start()
            bring(z).start()
        yield
        for z in order:
            away(z).wait_recv()
            bring(z).wait()
            add_rows(parts.at[z], parts.at[z], came.at[z])
        line = LineScatter(p, lambda z: parts.at[z], up, down, send, recv)
        line.start(1)
        yield
        for t in range(1, nz):
            line.arrive(t)
            if t < nz - 1:
                line.start(t + 1)
            yield
        if not self.trade:
            line.total(out)
        else:
            line.total(came.at[0])
            same = p.c == p.x
            back = remote(came.at[0], out, b_send, b_recv, p.device(x=1 - p.x, c=1 - p.c))
            keep = pltpu.make_async_copy(came.at[0], out, b_local)
            pl.when(same)(keep.start)
            pl.when(jnp.logical_not(same))(back.start)
            yield
            pl.when(same)(keep.wait)
            pl.when(jnp.logical_not(same))(back.wait)
        for z in order:
            away(z).wait_send()
        line.finish()


class Deal:
    def __init__(self, p, shard, place, quarter, send, recv):
        self.p, self.shard, self.place, self.quarter = p, shard, place, quarter
        self.send, self.recv = send, recv
        self.per_core = p.nz // 2

    def piece(self, piece, half):
        columns = pl.ds(piece * self.quarter, self.quarter)
        return self.shard.at[half, :, columns]

    def away(self, piece, half):
        p = self.p
        z = p.c * self.per_core + piece
        return z, remote(
            self.piece(piece, half),
            self.place(p.z, half),
            self.send.at[2 * piece + half],
            self.recv.at[p.z],
            p.device(z=z, c=half),
        )

    def local(self, piece):
        p = self.p
        columns = pl.ds(piece * self.quarter, self.quarter)
        return pltpu.make_async_copy(
            self.shard.at[p.c, :, columns], self.place(p.z, p.c), self.recv.at[p.z]
        )

    def start(self, in_plane):
        p = self.p
        for piece in range(self.per_core):
            for half in range(2):
                z, copy = self.away(piece, half)
                if in_plane:
                    pl.when((z == p.z) & (p.c != half))(copy.start)
                    pl.when((z == p.z) & (p.c == half))(self.local(piece).start)
                else:
                    pl.when(z != p.z)(copy.start)

    def arrive(self, source):
        p = self.p
        here = self.place(source, p.c)
        ours = (source == p.z) & (p.c == p.z // self.per_core)
        came = remote(here, here, self.send.at[0], self.recv.at[source], p.partner())
        pl.when(jnp.logical_not(ours))(came.wait_recv)
        pl.when(ours)(self.local(0).wait)

    def finish(self):
        p = self.p
        for piece in range(self.per_core):
            for half in range(2):
                z, copy = self.away(piece, half)
                here = (z == p.z) & (p.c == half)
                pl.when(jnp.logical_not(here))(copy.wait_send)


class DealTask(Task):
    vmem_outs = (0,)

    def __init__(self, nz, shard):
        rows, units = shard.shape
        self.ins = (shard.reshape(2, rows // 2, units),)
        self.outs = (jax.ShapeDtypeStruct((nz, rows // 2, 2 * units // nz), bf16),)
        self.scratch = (DMA((nz,)), DMA((nz,)))

    def steps(self, p, ins, outs, scratch):
        (shard,), (pieces,), (send, recv) = ins, outs, scratch
        deal = Deal(p, shard, lambda z, half: pieces.at[z], pieces.shape[-1], send, recv)
        deal.start(False)
        deal.start(True)
        yield
        for i in range(p.nz):
            deal.arrive(exclusive_or(p.z, i))
        deal.finish()


class Copies(Task):
    def __init__(self, nz, given, dealt):
        self.dealt = dealt
        if dealt:
            _, half, quarter = given.shape
            self.ins = (given,)
        else:
            rows, units = given.shape
            half, quarter = rows // 2, 2 * units // nz
            self.ins = (given.reshape(2, half, units),)
        self.outs = (jax.ShapeDtypeStruct((nz * 4 * half, 2 * quarter), bf16),)
        self.scratch = (pltpu.VMEM(self.outs[0].shape, bf16), DMA, *copy_sems(nz))

    def steps(self, p, ins, outs, scratch):
        full, done, *sems = scratch
        yield from copy_steps(p, ins[0], full, sems, self.dealt)
        store = pltpu.make_async_copy(full, outs[0], done)
        store.start()
        yield
        store.wait()


def copy_sems(nz):
    one, two = DMA((nz,)), DMA((nz, 2))
    return (one, one, one, one, two, two, two, two)


def copy_steps(p, given, full, sems, dealt):
    d_send, d_recv, f_send, f_recv, s_send, s_recv, x_send, x_recv = sems
    nz = p.nz
    quarter, half = full.shape[1] // 2, full.shape[0] // (4 * nz)

    def strip(z, x, c):
        return pl.ds(pl.multiple_of(((z * 2 + x) * 2 + c) * half, half), half)

    def place(z, x, c, y):
        return full.at[strip(z, x, c), pl.ds(pl.multiple_of(y * quarter, 128), quarter)]

    fx, fy = p.x + (1 - 2 * p.x) * (1 - p.c), p.y + (1 - 2 * p.y) * p.c
    sx, sy = p.x + (1 - 2 * p.x) * p.c, p.y + (1 - 2 * p.y) * (1 - p.c)

    def own(z):
        return given.at[z] if dealt else place(z, p.x, p.c, p.y)

    def first(z):
        target = p.device(x=fx, y=fy)
        return remote(own(z), place(z, p.x, p.c, p.y), f_send.at[z], f_recv.at[z], target)

    def second(z, which):
        x, y = (fx, fy) if which else (p.x, p.y)
        here = place(z, x, p.c, y)
        src = here if which else own(z)
        target = p.device(x=sx, y=sy)
        return remote(src, here, s_send.at[z, which], s_recv.at[z, which], target)

    def across(z, x):
        here = full.at[strip(z, x, p.c)]
        return remote(here, here, x_send.at[z, x], x_recv.at[z, x], p.partner())

    def keep(z):
        return pltpu.make_async_copy(given.at[z], place(z, p.x, p.c, p.y), d_send.at[z])

    order = [exclusive_or(p.z, i) for i in range(nz)]
    if dealt:
        for z in order:
            first(z).start()
            second(z, 0).start()
            keep(z).start()
        for z in order:
            keep(z).wait()
        yield
    else:
        deal = Deal(p, given, lambda z, c: place(z, p.x, c, p.y), quarter, d_send, d_recv)
        deal.start(True)
        yield
        deal.arrive(order[0])
        first(order[0]).start()
        second(order[0], 0).start()
        yield
        deal.start(False)
        yield
        for z in order[1:]:
            deal.arrive(z)
            first(z).start()
            second(z, 0).start()
            yield
    for z in order:
        first(z).wait_recv()
        second(z, 1).start()
        yield
    for z in order:
        second(z, 0).wait_recv()
        second(z, 1).wait_recv()
        across(z, 0).start()
        across(z, 1).start()
        yield
    for z in range(nz):
        first(z).wait_send()
        for i in range(2):
            second(z, i).wait_send()
            across(z, i).wait()
    if not dealt:
        deal.finish()


class DealBack:
    def __init__(self, p, source, out, quarter, send, recv):
        self.p, self.source, self.out, self.quarter = p, source, out, quarter
        self.send, self.recv = send, recv
        self.per_core = p.nz // 2
        self.owner = p.z // self.per_core

    def out_at(self, z, half):
        start = pl.multiple_of(lax.rem(z, self.per_core) * self.quarter, 128)
        return self.out.at[half, :, pl.ds(start, self.quarter)]

    def away(self, z):
        p = self.p
        return remote(
            self.source(z),
            self.out_at(p.z, p.c),
            self.send.at[z],
            self.recv.at[2 * lax.rem(p.z, self.per_core) + p.c],
            p.device(z=z, c=self.owner),
        )

    def keep(self, z):
        p = self.p
        return pltpu.make_async_copy(
            self.source(z),
            self.out_at(p.z, p.c),
            self.recv.at[2 * lax.rem(p.z, self.per_core) + p.c],
        )

    def start(self, z):
        p = self.p
        here = (z == p.z) & (p.c == self.owner)
        pl.when(jnp.logical_not(here))(self.away(z).start)
        pl.when(here)(self.keep(z).start)

    def finish(self):
        p = self.p
        for piece in range(self.per_core):
            for half in range(2):
                z = p.c * self.per_core + piece
                place = self.out_at(z, half)
                came = remote(
                    place, place, self.send.at[0], self.recv.at[2 * piece + half], p.partner()
                )
                ours = (z == p.z) & (p.c == half)
                pl.when(jnp.logical_not(ours))(came.wait_recv)
        for z in range(p.nz):
            here = (z == p.z) & (p.c == self.owner)
            pl.when(jnp.logical_not(here))(self.away(z).wait_send)
            pl.when(here)(self.keep(z).wait)


class DealBackTask(Task):
    vmem_outs = (0,)

    def __init__(self, nz, sums):
        _, half, quarter = sums.shape
        self.ins = (sums,)
        self.outs = (jax.ShapeDtypeStruct((2, half, nz // 2 * quarter), bf16),)
        self.scratch = (DMA((nz,)), DMA((nz,)))

    def steps(self, p, ins, outs, scratch):
        (sums,), (out,), (send, recv) = ins, outs, scratch
        deal = DealBack(p, lambda z: sums.at[z], out, sums.shape[-1], send, recv)
        for i in (3, 2, 1, 0):
            deal.start(exclusive_or(p.z, i))
        yield
        deal.finish()


class Sums(Task):
    def __init__(self, nz, grad, deal):
        depth, width = grad.shape
        half, quarter = depth // (4 * nz), width // 2
        self.deal = deal
        self.ins = (grad.reshape(nz, 2, 2, half, width),)
        if deal:
            self.outs = (jax.ShapeDtypeStruct((2, half, nz // 2 * quarter), bf16),)
        else:
            self.outs = (jax.ShapeDtypeStruct((nz, half, quarter), bf16),)
            self.vmem_outs = (0,)
        whole = pltpu.VMEM((nz, 2, half, width), bf16)
        self.scratch = (
            whole,
            whole,
            pltpu.VMEM((nz, 2, half, quarter), bf16),
            pltpu.VMEM((nz, half, quarter), bf16),
            DMA((nz, 2)), DMA((nz, 2)), DMA((nz, 2)), DMA((nz, 2)), DMA((nz, 2)),
            DMA((nz,)), DMA((nz,)), DMA((nz,)), DMA((nz,)),
        )

    def steps(self, p, ins, outs, scratch):
        (given,), (out,) = ins, outs
        mine, came, first_in, second_in, *sems = scratch
        local, c_send, c_recv, f_send, f_recv, s_send, s_recv, d_send, d_recv = sems
        nz, quarter = p.nz, given.shape[4] // 2
        order = [exclusive_or(p.z, i) for i in (3, 2, 1, 0)]

        def bring(z, x):
            return pltpu.make_async_copy(given.at[z, x, p.c], mine.at[z, x], local.at[z, x])

        def across(z, x):
            src = given.at[z, x, 1 - p.c]
            return remote(src, came.at[z, x], c_send.at[z, x], c_recv.at[z, x], p.partner())

        def place(z, x, y):
            return mine.at[z, x, :, pl.ds(pl.multiple_of(y * quarter, 128), quarter)]

        fx, fy = p.x + (1 - 2 * p.x) * p.c, p.y + (1 - 2 * p.y) * (1 - p.c)
        sx, sy = p.x + (1 - 2 * p.x) * (1 - p.c), p.y + (1 - 2 * p.y) * p.c

        def first(z, which):
            x, y = (1 - p.x, 1 - p.y) if which else (fx, fy)
            target = p.device(x=fx, y=fy)
            return remote(
                place(z, x, y), first_in.at[z, which], f_send.at[z, which], f_recv.at[z, which], target
            )

        def second(z):
            target = p.device(x=sx, y=sy)
            return remote(place(z, sx, sy), second_in.at[z], s_send.at[z], s_recv.at[z], target)

        back = DealBack(p, lambda z: place(z, p.x, p.y), out, quarter, d_send, d_recv)
        for z in order:
            for x in range(2):
                across(z, x).start()
                bring(z, x).start()
        yield
        def over_core(z):
            for x in range(2):
                across(z, x).wait_recv()
                bring(z, x).wait()
                add_rows(mine.at[z, x], mine.at[z, x], came.at[z, x])
            for which in (1, 0):
                first(z, which).start()

        def over_first(z):
            for which in (1, 0):
                at = place(z, sx, sy) if which else place(z, p.x, p.y)
                first(z, which).wait_recv()
                add_rows(at, at, first_in.at[z, which])
                if which:
                    second(z).start()

        def over_second(z):
            second(z).wait_recv()
            at = place(z, p.x, p.y)
            if self.deal:
                add_rows(at, at, second_in.at[z])
                back.start(z)
            else:
                add_rows(out.at[z], at, second_in.at[z])

        over_core(order[0])
        yield
        for i in range(nz + 1):
            if i + 1 < nz:
                over_core(order[i + 1])
                yield
            if i < nz:
                over_first(order[i])
                yield
            if i >= 1:
                over_second(order[i - 1])
                yield
        if self.deal:
            back.finish()
        for z in range(nz):
            second(z).wait_send()
            for i in range(2):
                first(z, i).wait_send()
                across(z, i).wait_send()


class FeedForward(Task):
    vmem_ins = (0, 1, 2)
    vmem_outs = (0, 1)
    spare = 10

    def __init__(self, nz, own, cotangent, gain, gate, up, down_pieces):
        rows, depth = own.shape
        units = gate.shape[1]
        self.rows, self.depth, self.units = rows, depth, units
        self.ins = (own, cotangent, gain.reshape(1, depth), gate, up, down_pieces)
        wide = jax.ShapeDtypeStruct((depth, units), bf16)
        exact = jax.ShapeDtypeStruct((rows, depth), f32)
        self.outs = (exact, exact, wide, wide, wide)
        weight = pltpu.VMEM((depth, units), bf16)
        tokens = pltpu.VMEM((nz * rows, depth), bf16)
        inner = pltpu.VMEM((nz * rows, units), bf16)
        line = pltpu.VMEM((2, nz - 1, rows // 2, depth), bf16)
        self.scratch = (
            weight, weight, weight, tokens, tokens, inner, inner, inner, tokens, line, line,
            DMA((8, 2, nz)), DMA((8, 2, nz)), DMA((8,)), *copy_sems(nz),
        )

    def steps(self, p, ins, outs, scratch):
        own, cotangent, gain, gate_in, up_in, down_in = ins
        ff_out, dn_out, grad_gate, grad_up, grad_down = outs
        gate, up, down, normed, d_ff, hidden, gated, upped, parts, above, below, *sems = scratch
        send, recv, local, *down_sems = sems
        copies = copy_steps(p, down_in, down, down_sems, True)
        nz, depth, units = p.nz, self.depth, self.units
        part = self.rows // 2
        half_rows = nz * part
        tile = units // 3

        def entry(buffer, half):
            return lambda z: buffer.at[pl.ds(pl.multiple_of(half * half_rows + z * part, part), part)]

        gathers, scatters = [], []
        for i, buffer in enumerate((normed, d_ff)):
            for half in range(2):
                k = 4 * i + half
                gathers.append(LineGather(p, entry(buffer, half), send.at[k], recv.at[k]))
                scatters.append(
                    LineScatter(
                        p, entry(parts, half), above.at[half], below.at[half], send.at[k + 2], recv.at[k + 2]
                    )
                )

        loads = [
            pltpu.make_async_copy(src, dst, local.at[i])
            for i, (src, dst) in enumerate(((gate_in, gate), (up_in, up)))
        ]

        def gelu(v):
            bent = jnp.tanh(math.sqrt(2.0 / math.pi) * (v + 0.044715 * (v * v * v)))
            return 0.5 * v * (1.0 + bent), bent

        def columns(i):
            return pl.ds(pl.multiple_of(i * tile, 128), tile)

        def hide(half, low, high):
            rows = slice(half * half_rows, (half + 1) * half_rows)

            @pl.loop(low, high)
            def _(i):
                at = columns(i)
                gate_lin = jnp.dot(normed[rows, :], gate[:, at], preferred_element_type=f32)
                up_lin = jnp.dot(normed[rows, :], up[:, at], preferred_element_type=f32)
                hidden[rows, at] = (gelu(gate_lin)[0] * up_lin).astype(bf16)
                gated[rows, at] = gate_lin.astype(bf16)
                upped[rows, at] = up_lin.astype(bf16)

        def project(half):
            rows = slice(half * half_rows, (half + 1) * half_rows)

            @pl.loop(0, depth // tile)
            def _(i):
                at = columns(i)
                parts[rows, at] = contract(hidden[rows, :], down[at, :], 1, 1).astype(bf16)

        def hide_back(half, low, high):
            rows = slice(half * half_rows, (half + 1) * half_rows)

            @pl.loop(low, high)
            def _(i):
                at = columns(i)
                d_hidden = jnp.dot(d_ff[rows, :], down[:, at], preferred_element_type=f32)
                v, u = gated[rows, at].astype(f32), upped[rows, at].astype(f32)
                value, bent = gelu(v)
                slope = 0.5 * (1.0 + bent) + (0.5 * math.sqrt(2.0 / math.pi)) * v * (
                    1.0 - bent * bent
                ) * (1.0 + (3.0 * 0.044715) * (v * v))
                gated[rows, at] = (d_hidden * u * slope).astype(bf16)
                upped[rows, at] = (d_hidden * value).astype(bf16)

        def project_back(half):
            rows = slice(half * half_rows, (half + 1) * half_rows)

            @pl.loop(0, depth // tile)
            def _(i):
                at = columns(i)
                total = contract(gated[rows, :], gate[at, :], 1, 1)
                parts[rows, at] = (total + contract(upped[rows, :], up[at, :], 1, 1)).astype(bf16)

        def turn_back(half):
            start = half * half_rows + p.z * part

            @pl.loop(0, part // 16)
            def _(i):
                at = pl.ds(pl.multiple_of(half * part + i * 16, 16), 16)
                values = ff_out[at, :]
                scaled = cotangent[at, :].astype(f32) * (1.0 + gain[...])
                factor = factor_of(values)
                unit = values * factor
                mean = jnp.mean(scaled * unit, axis=-1, keepdims=True)
                here = pl.ds(pl.multiple_of(start + i * 16, 16), 16)
                d_ff[here, :] = ((scaled - unit * mean) * factor).astype(bf16)

        def weigh(left, right, out, low, high):
            @pl.loop(low, high)
            def _(i):
                at = pl.ds(pl.multiple_of(i * 256, 128), 256)
                out[at, :] = contract(left[:, at], right[...], 0, 0).astype(bf16)

        def store(i, src, dst):
            return pltpu.make_async_copy(src, dst, local.at[3 + i])

        blocks = depth // 256
        one, two, one_back, two_back = gathers
        sum_one, sum_two, sum_one_back, sum_two_back = scatters
        keep = [
            pltpu.make_async_copy(own.at[pl.ds(half * part, part)], entry(normed, half)(p.z), local.at[6 + half])
            for half in range(2)
        ]
        keep[0].start()
        keep[1].start()
        keep[0].wait()
        one.start(1)
        keep[1].wait()
        next(copies)
        for load in loads:
            load.start()
        one.arrive(1)
        one.start(2)
        two.start(1)
        one.arrive(2)
        one.start(3)
        for _ in range(nz):
            next(copies)
        one.arrive(3)
        two.arrive(1)
        two.start(2)
        for load in loads:
            load.wait()
        hide(0, 0, 1)
        two.arrive(2)
        two.start(3)
        hide(0, 1, 3)
        two.arrive(3)
        hide(1, 0, 1)
        for _ in copies:
            pass
        project(0)
        sum_one.start(1)
        hide(1, 1, 3)
        sum_one.arrive(1)
        sum_one.start(2)
        project(1)
        sum_two.start(1)
        sum_one.arrive(2)
        sum_one.start(3)
        sum_two.arrive(1)
        sum_two.start(2)
        sum_one.arrive(3)
        sum_one.total(ff_out.at[pl.ds(0, part)])
        turn_back(0)
        one_back.start(1)
        sum_two.arrive(2)
        sum_two.start(3)
        one_back.arrive(1)
        one_back.start(2)
        sum_two.arrive(3)
        sum_two.total(ff_out.at[pl.ds(part, part)])
        turn_back(1)
        one_back.arrive(2)
        one_back.start(3)
        two_back.start(1)
        one_back.arrive(3)
        hide_back(0, 0, 3)
        two_back.arrive(1)
        two_back.start(2)
        sum_one.finish()
        project_back(0)
        sum_one_back.start(1)
        two_back.arrive(2)
        two_back.start(3)
        two_back.arrive(3)
        hide_back(1, 0, 3)
        sum_one_back.arrive(1)
        sum_one_back.start(2)
        sum_two.finish()
        project_back(1)
        sum_two_back.start(1)
        weigh(d_ff, hidden, down, 0, blocks)
        store(0, down, grad_down).start()
        sum_one_back.arrive(2)
        sum_two_back.arrive(1)
        sum_two_back.start(2)
        sum_one_back.start(3)
        weigh(normed, gated, gate, 0, blocks)
        store(1, gate, grad_gate).start()
        sum_two_back.arrive(2)
        sum_two_back.start(3)
        weigh(normed, upped, up, 0, blocks)
        store(2, up, grad_up).start()
        sum_one_back.arrive(3)
        sum_one_back.total(dn_out.at[pl.ds(0, part)])
        sum_two_back.arrive(3)
        sum_two_back.total(dn_out.at[pl.ds(part, part)])
        for gather in gathers:
            gather.finish()
        sum_one_back.finish()
        sum_two_back.finish()
        store(0, down, grad_down).wait()
        store(1, gate, grad_gate).wait()
        store(2, up, grad_up).wait()
        yield


class SumAll(Task):
    vmem_ins = (0,)
    vmem_outs = (0,)

    def __init__(self, values):
        self.ins = (values,)
        self.outs = (jax.ShapeDtypeStruct(values.shape, f32),)
        stage = pltpu.VMEM((5,) + values.shape, f32)
        self.scratch = (stage, stage, DMA((5,)), DMA((5,)))

    def steps(self, p, ins, outs, scratch):
        (given,), (out,), (stage, came, send, recv) = ins, outs, scratch
        targets = [
            p.partner(),
            p.device(y=1 - p.y),
            p.device(x=1 - p.x),
            p.device(z=exclusive_or(p.z, 1)),
            p.device(z=exclusive_or(p.z, 2)),
        ]
        stage[0] = given[...]
        for i, target in enumerate(targets):
            copy = remote(stage.at[i], came.at[i], send.at[i], recv.at[i], target)
            copy.start()
            yield
            copy.wait()
            total = stage[i] + came[i]
            if i < 4:
                stage[i + 1] = total
            else:
                out[...] = total


def run_tasks(nz, number, tasks, order="", every=False):
    counts = [(len(t.ins), len(t.outs), len(t.scratch)) for t in tasks]

    def split(refs, which):
        found = []
        for count in counts:
            found.append(refs[: count[which]])
            refs = refs[count[which] :]
        return found, refs

    def body(*refs):
        ins, refs = split(refs, 0)
        outs, refs = split(refs, 1)
        scratch, refs = split(refs, 2)
        p = Spot(nz)
        p.greet()
        running = [t.steps(p, *given) for t, *given in zip(tasks, ins, outs, scratch)]
        done = [False] * len(tasks)
        for digit in order:
            i = int(digit)
            if not done[i]:
                done[i] = next(running[i], "end") == "end"
        while not all(done):
            for i, steps in enumerate(running):
                if not done[i]:
                    done[i] = next(steps, "end") == "end"

    sent = sum(x.size * 2 for t in tasks for x in t.ins)
    spare = max(t.spare for t in tasks) * 2**20
    held = [s for t in tasks for s in t.scratch if getattr(s, "memory_space", None) == pltpu.VMEM]
    held += [t.ins[i] for t in tasks for i in t.vmem_ins] + [t.outs[i] for t in tasks for i in t.vmem_outs]
    vmem = sum(math.prod(s.shape) * jnp.dtype(s.dtype).itemsize for s in held)
    results = pl.pallas_call(
        body,
        out_shape=[o for t in tasks for o in t.outs],
        in_specs=[in_vmem if i in t.vmem_ins else anywhere for t in tasks for i in range(len(t.ins))],
        out_specs=[
            in_vmem if i in t.vmem_outs else anywhere for t in tasks for i in range(len(t.outs))
        ],
        scratch_shapes=[s for t in tasks for s in t.scratch],
        compiler_params=pltpu.CompilerParams(
            collective_id=number, has_side_effects=True, vmem_limit_bytes=vmem + spare
        ),
        cost_estimate=pl.CostEstimate(
            flops=0, bytes_accessed=sent, transcendentals=0, remote_bytes_transferred=sent
        ),
    )(*[x for t in tasks for x in t.ins])
    found, _ = split(list(results), 1)
    if every:
        return found
    return found[0] if len(tasks) == 1 else [f[0] for f in found]


START_ORDER = "10222102221222213222222131"
FINISH_ORDER = "0103111101131101132220113222022322222"
KV_ORDER = "0120122021220221222011222"


class Kernels:
    def __init__(self, at):
        self.at = at
        self.blocks, self.nz = at.blocks, at.nz
        self.block = 2 * at.z + at.c
        self.number = 0

    def run(self, tasks, order=""):
        self.number += 1
        return run_tasks(self.nz, self.number, tasks, order)

    def flat(self, whole):
        return whole.reshape(-1, whole.shape[-1])

    def start(self, own, qkv_shard, gate, up):
        nz = self.nz
        tasks = [
            PlaneGather(own),
            PairGather(nz, qkv_shard, True),
            Copies(nz, gate, False),
            DealTask(nz, up),
        ]
        rows, qkv, gate_full, pieces = self.run(tasks, START_ORDER)
        return self.flat(rows), self.flat(qkv), gate_full, pieces

    def gather_kv(self, own, out_shard, pieces):
        nz = self.nz
        whole, out, up = self.run(
            [PairGather(nz, own, False), PairGather(nz, out_shard, True), Copies(nz, pieces, True)],
            "1021" + "012" + "0222" + "1" + "2222" + "02" + "1",
        )
        return whole.reshape((self.blocks,) + own.shape), self.flat(out), up

    def heads_forward(self, partial, tokens, gain_out, gain_in, down):
        task = HeadsForward(partial, tokens, gain_out, gain_in)
        self.number += 1
        (summed, normed), (pieces,) = run_tasks(
            self.nz, self.number, [task, DealTask(self.nz, down)], "01", True
        )
        return summed, normed, pieces

    def feed_forward(self, own, cotangent, gain, gate, up, down):
        task = FeedForward(self.nz, own, cotangent, gain, gate, up, down)
        self.number += 1
        return run_tasks(self.nz, self.number, [task])

    def heads_backward(self, *given):
        whole, d_middle, sums = self.run([HeadsBackward(*given)])
        return self.flat(whole), d_middle, jnp.sum(sums, axis=1)

    def scatter_kv_sums(self, parts, out_grad, grad):
        nz = self.nz
        given = parts.reshape((nz, 2) + parts.shape[1:])
        rows = out_grad.shape[0] // self.blocks
        out_given = out_grad.reshape(nz, 2, rows, out_grad.shape[1])
        kv, out, sums = self.run(
            [PairScatter(nz, given, False), PairScatter(nz, out_given, True), Sums(nz, grad, False)],
            KV_ORDER,
        )
        return kv, out, sums

    def scatter_heads_back(self, partial, sums):
        rows, shard = self.run([PlaneScatter(partial), DealBackTask(self.nz, sums)], "01")
        return rows, self.flat(shard)

    def finish(self, qkv_grad, gate_grad, up_grad, gains):
        rows = qkv_grad.shape[0] // self.blocks
        given = qkv_grad.reshape(self.nz, 2, rows, qkv_grad.shape[1])
        qkv, gate, up, total = self.run(
            [
                PairScatter(self.nz, given, True),
                Sums(self.nz, gate_grad, True),
                Sums(self.nz, up_grad, True),
                SumAll(gains.reshape(8, -1)),
            ],
            FINISH_ORDER,
        )
        return qkv, self.flat(gate), self.flat(up), total.reshape(gains.shape)


def project_kernel(info, normed_ref, weight_ref, q_ref, kv_ref, cos_ref, sin_ref):
    rows, half = cos_ref.shape
    dim = 2 * half
    heads = q_ref.shape[0]
    blocks = (info.shape[0] - 2) // 2
    me, prompts = info[2 * blocks], info[2 * blocks + 1]
    first = jnp.minimum(info[blocks + me], prompts) * rows
    positions = (lax.broadcasted_iota(jnp.int32, (rows, half), 0) + first).astype(f32)
    index = lax.broadcasted_iota(jnp.int32, (rows, half), 1).astype(f32)
    angles = positions * jnp.exp(index * (-2.0 * math.log(10000.0) / dim))
    cos_ref[...] = jnp.cos(angles)
    sin_ref[...] = jnp.sin(angles)
    for i in range(heads + 2):
        columns = slice(i * dim, (i + 1) * dim)
        linear = jnp.dot(normed_ref[...], weight_ref[:, columns], preferred_element_type=f32)
        if i <= heads:
            linear = rotate(linear, cos_ref[...], sin_ref[...])
        if i < heads:
            q_ref[i] = linear.astype(bf16)
        else:
            kv_ref[:, (i - heads) * dim : (i - heads + 1) * dim] = linear.astype(bf16)


def project(info, normed, weight):
    rows = normed.shape[0]
    heads = weight.shape[1] // HEAD_DIM - 2
    table = jax.ShapeDtypeStruct((rows, HEAD_DIM // 2), f32)
    return pl.pallas_call(
        project_kernel,
        in_specs=[pl.BlockSpec(memory_space=pltpu.SMEM), in_vmem, in_vmem],
        out_specs=[in_vmem] * 4,
        out_shape=[
            jax.ShapeDtypeStruct((heads, rows, HEAD_DIM), bf16),
            jax.ShapeDtypeStruct((rows, 2 * HEAD_DIM), bf16),
            table,
            table,
        ],
        compiler_params=pltpu.CompilerParams(vmem_limit_bytes=24 * 2**20),
        cost_estimate=pl.CostEstimate(
            flops=2 * rows * weight.size, bytes_accessed=2 * weight.size, transcendentals=0
        ),
    )(info, normed, weight)


def project_back_kernel(dq_ref, dkv_ref, cos_ref, sin_ref, weight_ref, lin_ref, out_ref):
    heads, rows, dim = dq_ref.shape
    cosine, sine = cos_ref[...], -sin_ref[...]
    for i in range(heads):
        lin_ref[:, i * dim : (i + 1) * dim] = rotate(dq_ref[i], cosine, sine).astype(bf16)
    start = heads * dim
    d_key = rotate(dkv_ref[:, :dim].astype(f32), cosine, sine)
    lin_ref[:, start : start + dim] = d_key.astype(bf16)
    lin_ref[:, start + dim :] = dkv_ref[:, dim:].astype(bf16)
    depth = weight_ref.shape[0]
    tile = 384

    @pl.loop(0, depth // tile)
    def _(i):
        at = pl.ds(pl.multiple_of(i * tile, 128), tile)
        out_ref[:, at] = contract(lin_ref[...], weight_ref[at, :], 1, 1).astype(bf16)


def project_back(d_query, d_kv, cosine, sine_table, weight):
    rows = d_kv.shape[0]
    depth, width = weight.shape
    return pl.pallas_call(
        project_back_kernel,
        in_specs=[in_vmem] * 5,
        out_specs=[in_vmem] * 2,
        out_shape=[
            jax.ShapeDtypeStruct((rows, width), bf16),
            jax.ShapeDtypeStruct((rows, depth), bf16),
        ],
        compiler_params=pltpu.CompilerParams(vmem_limit_bytes=24 * 2**20),
        cost_estimate=pl.CostEstimate(
            flops=2 * rows * weight.size, bytes_accessed=2 * weight.size, transcendentals=0
        ),
    )(d_query, d_kv, cosine, sine_table, weight)


def causal_mask(rows):
    shape = (rows, rows)
    return lax.broadcasted_iota(jnp.int32, shape, 1) <= lax.broadcasted_iota(jnp.int32, shape, 0)


def kind_of(info, step):
    blocks = pl.num_programs(0)
    me, prompts = info[2 * blocks], info[2 * blocks + 1]
    role = info[blocks + step]
    reads = (info[step] == info[me]) & (role < prompts) & (role < info[blocks + me])
    return jnp.where(step == me, 2, jnp.where(reads, 1, 0))


def forward_kernel(info, q_ref, kv_ref, out_ref, exact_ref, inv_ref, acc, total):
    step, last = pl.program_id(0), pl.num_programs(0) - 1
    heads, rows, dim = q_ref.shape
    kind = kind_of(info, step)

    @pl.when(step == 0)
    def _():
        acc[...] = jnp.zeros_like(acc)
        total[...] = jnp.zeros_like(total)

    def work(own):
        for head in range(heads):
            raw = contract(q_ref[head], kv_ref[0, :, :dim], 1, 1)
            weights = jnp.exp(softcap * jnp.tanh(raw * (score_scale / softcap)))
            if own:
                weights = jnp.where(causal_mask(rows), weights, 0.0)
            total[head] += jnp.sum(weights, axis=-1, keepdims=True)
            acc[head] += contract(weights.astype(bf16), kv_ref[0, :, dim:], 1, 0)

    @pl.when(kind == 1)
    def _():
        work(False)

    @pl.when(kind == 2)
    def _():
        work(True)

    @pl.when(step == last)
    def _():
        for head in range(heads):
            inverse = 1.0 / total[head]
            value = acc[head] * inverse
            inv_ref[head] = inverse
            exact_ref[:, head * dim : (head + 1) * dim] = value
            out_ref[:, head * dim : (head + 1) * dim] = value.astype(bf16)


def whole2(step, info):
    return (0, 0)


def whole3(step, info):
    return (0, 0, 0)


def by_step(step, info):
    return (step, 0, 0)


def attend(info, queries, all_kv):
    heads, rows, dim = queries.shape
    return pl.pallas_call(
        forward_kernel,
        grid_spec=pltpu.PrefetchScalarGridSpec(
            num_scalar_prefetch=1,
            grid=(all_kv.shape[0],),
            in_specs=[
                pl.BlockSpec((heads, rows, dim), whole3),
                pl.BlockSpec((1, rows, 2 * dim), by_step),
            ],
            out_specs=[
                pl.BlockSpec((rows, heads * dim), whole2),
                pl.BlockSpec((rows, heads * dim), whole2),
                pl.BlockSpec((heads, rows, 1), whole3),
            ],
            scratch_shapes=[
                pltpu.VMEM((heads, rows, dim), f32),
                pltpu.VMEM((heads, rows, 1), f32),
            ],
        ),
        out_shape=[
            jax.ShapeDtypeStruct((rows, heads * dim), bf16),
            jax.ShapeDtypeStruct((rows, heads * dim), f32),
            jax.ShapeDtypeStruct((heads, rows, 1), f32),
        ],
        compiler_params=pltpu.CompilerParams(vmem_limit_bytes=24 * 2**20),
        cost_estimate=pl.CostEstimate(
            flops=3 * 4 * heads * rows * rows * dim,
            bytes_accessed=8 * rows * dim * heads,
            transcendentals=6 * heads * rows * rows,
        ),
    )(info, queries, all_kv)


def backward_kernel(info, q_ref, kv_ref, up_ref, exact_ref, inv_ref, dq_ref, dkv_ref):
    step = pl.program_id(0)
    heads, rows, dim = q_ref.shape
    kind = kind_of(info, step)

    @pl.when(step == 0)
    def _():
        dq_ref[...] = jnp.zeros_like(dq_ref)

    def work(own):
        dk = jnp.zeros((rows, dim), f32)
        dv = jnp.zeros((rows, dim), f32)
        for head in range(heads):
            columns = slice(head * dim, (head + 1) * dim)
            up = up_ref[:, columns]
            delta = jnp.sum(up.astype(f32) * exact_ref[:, columns], axis=-1, keepdims=True)
            raw = contract(q_ref[head], kv_ref[0, :, :dim], 1, 1)
            bounded = jnp.tanh(raw * (score_scale / softcap))
            probs = jnp.exp(softcap * bounded) * inv_ref[head]
            if own:
                probs = jnp.where(causal_mask(rows), probs, 0.0)
            d_probs = contract(up, kv_ref[0, :, dim:], 1, 1)
            d_raw = probs * (d_probs - delta) * ((1.0 - bounded * bounded) * score_scale)
            d_raw = d_raw.astype(bf16)
            dq_ref[head] += contract(d_raw, kv_ref[0, :, :dim], 1, 0)
            dk += contract(d_raw, q_ref[head], 0, 0)
            dv += contract(probs.astype(bf16), up, 0, 0)
        dkv_ref[0, :, :dim] = dk.astype(bf16)
        dkv_ref[0, :, dim:] = dv.astype(bf16)

    @pl.when(kind == 1)
    def _():
        work(False)

    @pl.when(kind == 0)
    def _():
        dkv_ref[...] = jnp.zeros_like(dkv_ref)

    @pl.when(kind == 2)
    def _():
        work(True)


def attend_back(info, queries, all_kv, upstream, exact, inverse):
    heads, rows, dim = queries.shape
    blocks = all_kv.shape[0]
    return pl.pallas_call(
        backward_kernel,
        grid_spec=pltpu.PrefetchScalarGridSpec(
            num_scalar_prefetch=1,
            grid=(blocks,),
            in_specs=[
                pl.BlockSpec((heads, rows, dim), whole3),
                pl.BlockSpec((1, rows, 2 * dim), by_step),
                pl.BlockSpec((rows, heads * dim), whole2),
                pl.BlockSpec((rows, heads * dim), whole2),
                pl.BlockSpec((heads, rows, 1), whole3),
            ],
            out_specs=[
                pl.BlockSpec((heads, rows, dim), whole3),
                pl.BlockSpec((1, rows, 2 * dim), by_step),
            ],
        ),
        out_shape=[
            jax.ShapeDtypeStruct((heads, rows, dim), f32),
            jax.ShapeDtypeStruct((blocks, rows, 2 * dim), bf16),
        ],
        compiler_params=pltpu.CompilerParams(vmem_limit_bytes=24 * 2**20),
        cost_estimate=pl.CostEstimate(
            flops=3 * 10 * heads * rows * rows * dim,
            bytes_accessed=16 * rows * dim * heads,
            transcendentals=6 * heads * rows * rows,
        ),
    )(info, queries, all_kv, upstream, exact, inverse)


def on_device(
    tokens,
    cotangent,
    norm_attn_in,
    w_query,
    w_key,
    w_value,
    w_out,
    norm_attn_out,
    norm_ff_in,
    w_gate,
    w_up,
    w_down,
    norm_ff_out,
    block_group,
    block_role,
):
    at = Place()
    own_rows, depth = tokens.shape
    shard_rows, units = w_gate.shape
    regular = at.nz == 4 and shard_rows % 32 == 0 and units == depth and units % 768 == 0
    comm = Kernels(at) if regular else Permutes(at)
    blocks = at.blocks
    info = jnp.concatenate(
        [block_group, block_role, jnp.stack([comm.block, blocks // 4]).astype(jnp.int32)]
    )

    token_f32 = tokens.astype(f32)
    heads_width = w_query.shape[1]
    normed_one, qkv_full, gate_full, up_pieces = comm.start(
        normalize(token_f32, norm_attn_in).astype(bf16),
        jnp.concatenate([w_query, w_key, w_value], axis=1),
        w_gate,
        w_up,
    )
    queries, own_kv, cosine, sine_table = project(info, normed_one, qkv_full)
    all_kv, out_full, up_full = comm.gather_kv(own_kv, w_out.T, up_pieces)
    attn_rows, attended, inverse = attend(info, queries, all_kv)
    attn_proj, normed_two, down_pieces = comm.heads_forward(
        contract(attn_rows, out_full, 1, 1).astype(bf16), tokens, norm_attn_out, norm_ff_in, w_down.T
    )

    ff_proj, d_normed_two, gate_sum, up_sum, down_sum = comm.feed_forward(
        normed_two, cotangent, norm_ff_out, gate_full, up_full, down_pieces
    )
    middle = token_f32 + normalize(attn_proj, norm_attn_out)
    layer_out = middle + normalize(ff_proj, norm_ff_out)
    upstream = cotangent.astype(f32)
    _, grad_ff_out = normalize_back(ff_proj, norm_ff_out, upstream)

    d_proj_rows, d_middle, inner_gains = comm.heads_backward(
        d_normed_two, attn_proj, tokens, cotangent, norm_attn_out, norm_ff_in
    )
    d_attended = contract(d_proj_rows, out_full, 1, 0).astype(bf16)
    d_query, d_kv_parts = attend_back(info, queries, all_kv, d_attended, attended, inverse)
    d_kv, grad_out, down_sums = comm.scatter_kv_sums(
        d_kv_parts, contract(d_proj_rows, attn_rows, 0, 0).astype(bf16), down_sum
    )
    d_qkv_lin, d_partial = project_back(d_query, d_kv, cosine, sine_table, qkv_full)
    d_normed_one, grad_down = comm.scatter_heads_back(d_partial, down_sums)
    d_token_part, grad_attn_in = normalize_back(token_f32, norm_attn_in, d_normed_one)
    input_grad = (d_middle + d_token_part).astype(bf16)
    grad_qkv, grad_gate, grad_up, gains = comm.finish(
        contract(normed_one, d_qkv_lin, 0, 0).astype(bf16),
        gate_sum,
        up_sum,
        jnp.stack([grad_attn_in, inner_gains[0], inner_gains[1], grad_ff_out]),
    )
    grad_qkv, grad_gate, grad_up = [g.astype(f32) for g in (grad_qkv, grad_gate, grad_up)]
    return (
        layer_out.astype(bf16),
        input_grad,
        gains[0],
        grad_qkv[:, :heads_width],
        grad_qkv[:, heads_width : heads_width + HEAD_DIM],
        grad_qkv[:, heads_width + HEAD_DIM :],
        grad_out.astype(f32).T,
        gains[1],
        gains[2],
        grad_gate,
        grad_up,
        grad_down.astype(f32).T,
        gains[3],
    )


def solution(mesh):
    rows, weight, turned = P(("blk", "heads"), None), P("blk", "heads"), P("heads", "blk")
    return jax.shard_map(
        on_device,
        mesh=mesh,
        in_specs=(
            rows, rows, P(), weight, weight, weight, turned, P(), P(), weight, weight, turned,
            P(), P(), P(),
        ),
        out_specs=(
            rows, rows, P(), weight, weight, weight, turned, P(), P(), weight, weight, turned, P(),
        ),
        check_vma=False,
    )
```

```python
import math

import jax
import jax.numpy as jnp
from jax import lax
from jax.experimental import pallas as pl
from jax.experimental.pallas import tpu as pltpu
from jax.sharding import PartitionSpec as P

HEAD_DIM = 256


softcap = 50.0
epsilon = 1e-06
score_scale = HEAD_DIM ** (-0.5)
bf16 = jnp.bfloat16
f32 = jnp.float32


def contract(left_side, right_side, left_dim, right_dim):
    return lax.dot_general(
        left_side,
        right_side,
        (((left_dim,), (right_dim,)), ((), ())),
        preferred_element_type=f32,
    )


def factor_of(values):
    return lax.rsqrt(jnp.mean(values * values, axis=-1, keepdims=True) + epsilon)


def normalize(values, weight_gain):
    return values * factor_of(values) * (1.0 + weight_gain)


def normalize_back(values, weight_gain, upstream):
    factor = factor_of(values)
    unit = values * factor
    scaled = upstream * (1.0 + weight_gain)
    inner = jnp.mean(scaled * unit, axis=-1, keepdims=True)
    return (scaled - unit * inner) * factor, jnp.sum(upstream * unit, axis=0)


def rotate(tensor, cosine, sine_table):
    half_dim = HEAD_DIM // 2
    first_half = tensor[..., :half_dim]
    second_half = tensor[..., half_dim:]
    return jnp.concatenate(
        [
            first_half * cosine - second_half * sine_table,
            second_half * cosine + first_half * sine_table,
        ],
        axis=-1,
    )


def swap_core(v):
    return lax.ppermute(v, "heads", [(i, i ^ 1) for i in range(4)])


def swap_y(v):
    return lax.ppermute(v, "heads", [(i, i ^ 2) for i in range(4)])


def swap_x(v):
    blocks = lax.axis_size("blk")
    return lax.ppermute(v, "blk", [(i, i ^ 1) for i in range(blocks)])


def pair_up(own, other, place, axis):
    first = jnp.where(place == 0, own, other)
    second = jnp.where(place == 0, other, own)
    return jnp.concatenate([first, second], axis=axis)


def shift_z(v, step, senders):
    pairs = []
    for z in senders:
        for x in range(2):
            pairs.append((2 * z + x, 2 * (z + step) + x))
    return lax.ppermute(v, "blk", pairs)


class Place:
    def __init__(self):
        self.blocks = lax.axis_size("blk")
        self.nz = self.blocks // 2
        self.b = lax.axis_index("blk")
        self.h = lax.axis_index("heads")
        self.z, self.x = self.b // 2, self.b % 2
        self.y, self.c = self.h // 2, self.h % 2


def gather_z(at, unit):
    nz = at.nz
    up, down = unit, unit
    ups, downs = [None], [None]
    for s in range(1, nz):
        up = shift_z(up, 1, range(s - 1, nz - 1))
        down = shift_z(down, -1, range(1, nz - s + 1))
        ups.append(up)
        downs.append(down)
    return [unit] + [jnp.where(at.z >= s, ups[s], downs[nz - s]) for s in range(1, nz)]


def scatter_z(at, parts):
    nz = at.nz
    up = down = None
    for t in range(1, nz):
        k = nz - t
        send_up = parts[nz - k].astype(f32)
        send_down = parts[k].astype(f32)
        if up is not None:
            send_up = send_up + up.astype(f32)
            send_down = send_down + down.astype(f32)
        up = shift_z(send_up.astype(bf16), 1, range(0, nz - k))
        down = shift_z(send_down.astype(bf16), -1, range(k, nz))
    return parts[0].astype(f32) + (up.astype(f32) + down.astype(f32))


def deal_z(at, parts):
    nz = at.nz
    got = [parts[0]]
    for s in range(1, nz):
        up = shift_z(parts[nz - s], s, range(0, nz - s))
        down = shift_z(parts[nz - s], s - nz, range(nz - s, nz))
        got.append(jnp.where(at.z >= s, up, down))
    return got


def turn(at, whole):
    return [
        lax.dynamic_index_in_dim(whole, (at.z - s) % at.nz, 0, keepdims=False)
        for s in range(at.nz)
    ]


def unturn(at, parts):
    whole = jnp.zeros((at.nz,) + parts[0].shape, parts[0].dtype)
    for s, part in enumerate(parts):
        whole = lax.dynamic_update_index_in_dim(whole, part, (at.z - s) % at.nz, 0)
    return whole


def gather_zx(at, unit):
    got = []
    for part in gather_z(at, unit):
        got.append(pair_up(part[None], swap_x(part)[None], at.x, 0))
    return unturn(at, got)


def gather_xz(at, unit):
    both = pair_up(unit[None], swap_x(unit)[None], at.x, 0)
    return unturn(at, gather_z(at, both))


def pick(pair, place):
    mine = jnp.where(place == 0, pair[0], pair[1])
    other = jnp.where(place == 0, pair[1], pair[0])
    return mine, other


def scatter_zx(at, parts):
    total = scatter_z(at, parts)
    mine, other = pick(total, at.x)
    return mine + swap_x(other.astype(bf16)).astype(f32)


def scatter_xz(at, parts):
    sums = []
    for part in parts:
        mine, other = pick(part, at.x)
        sums.append(mine.astype(f32) + swap_x(other.astype(bf16)).astype(f32))
    return scatter_z(at, sums)


def rows_to_block(at, own):
    both = pair_up(own, swap_core(own), at.c, 0)
    pair = pair_up(both[None], swap_y(both)[None], at.y, 0)
    return pair.reshape(4 * own.shape[0], own.shape[1])


def rows_from_block(at, partial_sum):
    rows = partial_sum.shape[0] // 4
    parts = partial_sum.reshape(2, 2, rows, partial_sum.shape[1])
    mine, other = pick(parts.swapaxes(0, 1), at.c)
    total = mine + swap_core(other.astype(bf16)).astype(f32)
    mine, other = pick(total, at.y)
    return mine + swap_y(other.astype(bf16)).astype(f32)


def spread_weight(at, shard):
    rows, units = shard.shape
    half = rows // 2
    keep, send = pick(shard.reshape(2, half, units), at.c)
    wide = pair_up(keep[None], swap_core(send)[None], at.c, 0)
    quarter = 2 * units // at.nz
    per_core = units // quarter
    pieces = wide.reshape(2, half, per_core, quarter).transpose(0, 2, 1, 3)
    pieces = pieces.reshape(at.nz, half, quarter)
    got = unturn(at, deal_z(at, turn(at, pieces)))
    got = pair_up(got[:, None], swap_x(got)[:, None], at.x, 1)
    got = pair_up(got, swap_y(got), at.y, 3)
    got = pair_up(got[:, :, None], swap_core(got)[:, :, None], at.c, 2)
    return got.reshape(at.blocks * rows, 2 * quarter)


def collect_weight(at, grad):
    depth, width = grad.shape
    half, quarter = depth // (2 * at.blocks), width // 2
    parts = grad.reshape(at.nz, 2, 2, half, width)
    mine, other = pick(parts.transpose(2, 0, 1, 3, 4), at.c)
    total = mine + swap_core(other.astype(bf16)).astype(f32)
    mine, other = pick((total[..., :quarter], total[..., quarter:]), at.y)
    total = mine + swap_y(other.astype(bf16)).astype(f32)
    mine, other = pick((total[:, 0], total[:, 1]), at.x)
    total = mine + swap_x(other.astype(bf16)).astype(f32)
    got = unturn(at, deal_z(at, turn(at, total.astype(bf16))))
    per_core = at.nz // 2
    wide = got.reshape(2, per_core, half, quarter).transpose(0, 2, 1, 3)
    wide = wide.reshape(2, half, per_core * quarter)
    mine, other = pick(wide, at.c)
    rows = pair_up(mine, swap_core(other), at.c, 0)
    return rows.astype(f32)


def sum_all(at, values):
    total = values
    for bit in (1, 2):
        total = total + lax.ppermute(total, "heads", [(i, i ^ bit) for i in range(4)])
    bit = 1
    while bit < at.blocks:
        total = total + lax.ppermute(total, "blk", [(i, i ^ bit) for i in range(at.blocks)])
        bit *= 2
    return total


class Permutes:
    def __init__(self, at):
        self.at = at
        self.block, self.blocks, self.nz = at.b, at.blocks, at.nz

    def split(self, whole):
        return turn(self.at, whole.reshape((self.nz, whole.shape[0] // self.nz) + whole.shape[1:]))

    def start(self, own, qkv_shard, gate, up):
        at = self.at
        qkv_full = gather_zx(at, qkv_shard).reshape(own.shape[1], -1)
        return rows_to_block(at, own), qkv_full, spread_weight(at, gate), spread_weight(at, up)

    def gather_kv(self, own, out_shard, up):
        out_full = gather_zx(self.at, out_shard).reshape(-1, out_shard.shape[1])
        return gather_zx(self.at, own).reshape((self.blocks,) + own.shape), out_full, up

    def heads_forward(self, partial, tokens, gain_out, gain_in, down):
        summed = rows_from_block(self.at, partial)
        middle = tokens.astype(f32) + normalize(summed, gain_out)
        return summed, normalize(middle, gain_in).astype(bf16), spread_weight(self.at, down)

    def gather_z(self, own):
        whole = unturn(self.at, gather_z(self.at, own))
        return whole.reshape(-1, own.shape[1])

    def scatter_z(self, partial):
        return scatter_z(self.at, self.split(partial))

    def feed_forward(self, own, cotangent, gain, gate, up, down):
        normed = self.gather_z(own)
        gate_lin = jnp.dot(normed, gate, preferred_element_type=f32)
        up_lin = jnp.dot(normed, up, preferred_element_type=f32)
        hidden = (jax.nn.gelu(gate_lin, approximate=True) * up_lin).astype(bf16)
        ff_proj = self.scatter_z(contract(hidden, down, 1, 1).astype(bf16))
        d_ff, _ = normalize_back(ff_proj, gain, cotangent.astype(f32))
        d_ff_rows = self.gather_z(d_ff.astype(bf16))
        d_hidden = contract(d_ff_rows, down, 1, 0)
        _, glu_back = jax.vjp(
            lambda gate_in, up_in: jax.nn.gelu(gate_in, approximate=True) * up_in, gate_lin, up_lin
        )
        d_gate, d_up = [d.astype(bf16) for d in glu_back(d_hidden)]
        d_partial = contract(d_gate, gate, 1, 1) + contract(d_up, up, 1, 1)
        d_normed = self.scatter_z(d_partial.astype(bf16))
        grads = [
            contract(left, right, 0, 0).astype(bf16)
            for left, right in ((normed, d_gate), (normed, d_up), (d_ff_rows, hidden))
        ]
        return [ff_proj, d_normed] + grads

    def heads_backward(self, d_normed, projected, tokens, cotangent, gain_out, gain_in):
        middle = tokens.astype(f32) + normalize(projected, gain_out)
        part, by_in = normalize_back(middle, gain_in, d_normed)
        d_middle = cotangent.astype(f32) + part
        d_projected, by_out = normalize_back(projected, gain_out, d_middle)
        rows = rows_to_block(self.at, d_projected.astype(bf16))
        return rows, d_middle, jnp.stack([by_out, by_in])

    def scatter_pairs(self, grad):
        rows = grad.shape[0] // self.blocks
        return scatter_xz(self.at, self.split(grad.reshape(self.blocks, rows, -1)))

    def scatter_kv_sums(self, parts, out_grad, grad):
        kv = scatter_xz(self.at, self.split(parts))
        return kv, self.scatter_pairs(out_grad), collect_weight(self.at, grad)

    def scatter_heads_back(self, partial, sums):
        return rows_from_block(self.at, partial), sums

    def finish(self, qkv_grad, gate_grad, up_grad, gains):
        gate, up = collect_weight(self.at, gate_grad), collect_weight(self.at, up_grad)
        return self.scatter_pairs(qkv_grad), gate, up, sum_all(self.at, gains)


MESH = pl.DeviceIdType.MESH
DMA = pltpu.SemaphoreType.DMA
anywhere = pl.BlockSpec(memory_space=pl.ANY)
in_vmem = pl.BlockSpec(memory_space=pltpu.VMEM)


def remote(src, dst, send_sem, recv_sem, target):
    return pltpu.make_async_remote_copy(
        src_ref=src,
        dst_ref=dst,
        send_sem=send_sem,
        recv_sem=recv_sem,
        device_id=target,
        device_id_type=MESH,
    )


def flip(bit, by):
    return 1 - bit if by else bit


def exclusive_or(z, i):
    low, high = lax.rem(z, 2), lax.rem(z // 2, 2)
    rest = z - 2 * high - low
    return rest + 2 * flip(high, i // 2) + flip(low, i % 2)


class Spot:
    def __init__(self, nz):
        self.nz = nz
        h, b = lax.axis_index("heads"), lax.axis_index("blk")
        self.y, self.c = h // 2, h % 2
        self.z, self.x = b // 2, b % 2

    def device(self, z=None, x=None, y=None, c=None):
        z = self.z if z is None else z
        x = self.x if x is None else x
        y = self.y if y is None else y
        c = self.c if c is None else c
        return (2 * y + c, 2 * z + x)

    def partner(self):
        return self.device(c=1 - self.c)

    def greet(self):
        found = []
        for dx, dy, dc in [(0, 0, 1), (1, 0, 0), (1, 0, 1), (0, 1, 0), (0, 1, 1), (1, 1, 0), (1, 1, 1)]:
            found.append(self.device(x=flip(self.x, dx), y=flip(self.y, dy), c=flip(self.c, dc)))
        for s in range(1, self.nz):
            z = lax.rem(self.z + s, self.nz)
            found += [self.device(z=z), self.device(z=z, c=1 - self.c)]
        barrier = pltpu.get_barrier_semaphore()
        for device in found:
            pl.semaphore_signal(barrier, inc=1, device_id=device, device_id_type=MESH)
        pl.semaphore_wait(barrier, len(found))


def row_step(rows):
    return next(step for step in (48, 32, 16) if rows % step == 0)


def add_rows(out, left, right):
    rows = left.shape[0]
    step = row_step(rows)

    @pl.loop(0, rows // step)
    def _(i):
        at = pl.ds(pl.multiple_of(i * step, step), step)
        out[at, :] = (left[at, :].astype(f32) + right[at, :].astype(f32)).astype(out.dtype)


class LineGather:
    def __init__(self, spot, entry, send, recv):
        self.spot, self.entry = spot, entry
        self.send, self.recv = send, recv

    def copies(self, s):
        p, nz = self.spot, self.spot.nz
        up_at = lax.rem(p.z - s + 1 + nz, nz)
        down_at = lax.rem(p.z + s - 1, nz)
        up = remote(
            self.entry(up_at),
            self.entry(up_at),
            self.send.at[0, s],
            self.recv.at[0, s],
            p.device(z=lax.rem(p.z + 1, nz)),
        )
        down = remote(
            self.entry(down_at),
            self.entry(down_at),
            self.send.at[1, s],
            self.recv.at[1, s],
            p.device(z=lax.rem(p.z + nz - 1, nz)),
        )
        return (
            ((p.z >= s - 1) & (p.z < nz - 1), p.z >= s, up),
            ((p.z <= nz - s) & (p.z > 0), p.z <= nz - 1 - s, down),
        )

    def start(self, s):
        for sends, _, copy in self.copies(s):
            pl.when(sends)(copy.start)

    def arrive(self, s):
        for _, receives, copy in self.copies(s):
            pl.when(receives)(copy.wait_recv)

    def finish(self):
        for s in range(1, self.spot.nz):
            for sends, _, copy in self.copies(s):
                pl.when(sends)(copy.wait_send)

    def newest(self, s):
        p, nz = self.spot, self.spot.nz
        return (
            (p.z >= s, lax.rem(p.z - s + nz, nz)),
            (p.z <= nz - 1 - s, lax.rem(p.z + s, nz)),
        )


class LineScatter:
    def __init__(self, spot, parts, up, down, send, recv):
        self.spot, self.parts, self.up, self.down = spot, parts, up, down
        self.send, self.recv = send, recv

    def copies(self, t):
        p, nz = self.spot, self.spot.nz
        k = nz - t
        up = remote(
            self.parts(lax.rem(p.z + k, nz)),
            self.up.at[t - 1],
            self.send.at[0, t],
            self.recv.at[0, t],
            p.device(z=lax.rem(p.z + 1, nz)),
        )
        down = remote(
            self.parts(lax.rem(p.z - k + nz, nz)),
            self.down.at[t - 1],
            self.send.at[1, t],
            self.recv.at[1, t],
            p.device(z=lax.rem(p.z + nz - 1, nz)),
        )
        return (
            (p.z <= nz - 1 - k, (p.z >= 1) & (p.z <= t), up),
            (p.z >= k, (p.z <= nz - 2) & (p.z >= nz - 1 - t), down),
        )

    def start(self, t):
        for sends, _, copy in self.copies(t):
            pl.when(sends)(copy.start)

    def arrive(self, t):
        p, nz = self.spot, self.spot.nz
        k = nz - t
        for way, (_, receives, copy) in enumerate(self.copies(t)):

            @pl.when(receives)
            def _(way=way, copy=copy):
                copy.wait_recv()
                if t < nz - 1:
                    index = lax.rem(p.z + k - 1, nz) if way == 0 else lax.rem(p.z - k + 1 + nz, nz)
                    came = (self.up if way == 0 else self.down).at[t - 1]
                    add_rows(self.parts(index), self.parts(index), came)

    def finish(self):
        for t in range(1, self.spot.nz):
            for sends, _, copy in self.copies(t):
                pl.when(sends)(copy.wait_send)

    def total(self, out):
        p, last = self.spot, self.spot.nz - 2
        mine = self.parts(p.z)
        inner = (p.z > 0) & (p.z < p.nz - 1)

        @pl.when(p.z == 0)
        def _():
            add_rows(out, mine, self.down.at[last])

        @pl.when(p.z == p.nz - 1)
        def _():
            add_rows(out, mine, self.up.at[last])

        step = row_step(out.shape[0])

        @pl.when(inner)
        def _():
            @pl.loop(0, out.shape[0] // step)
            def _(i):
                at = pl.ds(pl.multiple_of(i * step, step), step)
                sides = self.up[last, at, :].astype(f32) + self.down[last, at, :].astype(f32)
                out[at, :] = (mine[at, :].astype(f32) + sides).astype(out.dtype)


class Task:
    ins = ()
    outs = ()
    scratch = ()
    vmem_ins = ()
    vmem_outs = ()
    spare = 5

    def steps(self, p, ins, outs, scratch):
        raise NotImplementedError


class PlaneGather(Task):
    vmem_ins = (0,)
    vmem_outs = (0,)

    def __init__(self, own):
        self.ins = (own,)
        self.outs = (jax.ShapeDtypeStruct((4,) + own.shape, bf16),)
        self.scratch = (DMA((6,)), DMA((4, 2)), DMA((2,)), DMA)

    def steps(self, p, ins, outs, scratch):
        (own,), (whole,), (send, recv, on_send, local) = ins, outs, scratch
        part, half = 2 * p.y + p.c, own.shape[0] // 2
        same = p.c == p.x

        def rows(of, i):
            return whole.at[of, pl.ds(i * half, half)]

        def piece(i):
            return own.at[pl.ds(i * half, half)]

        along = [
            remote(piece(i), rows(part, i), send.at[2 * k + i], recv.at[part, i], target)
            for k, target in enumerate((p.device(x=1 - p.x, c=p.x), p.device(y=1 - p.y, c=p.x)))
            for i in range(2)
        ]
        home = [
            remote(piece(i), rows(part, i), send.at[4 + i], recv.at[part, i], p.device(c=1 - p.c))
            for i in range(2)
        ]
        keep = pltpu.make_async_copy(own, whole.at[part], local)

        def passed(k, by_x):
            if by_x:
                here = rows(2 * p.y + k, 0)
                return remote(here, here, on_send.at[k], recv.at[2 * p.y + k, 0], p.device(y=1 - p.y))
            here = rows(2 * (1 - p.y) + k, 1)
            return remote(
                here, here, on_send.at[k], recv.at[2 * (1 - p.y) + k, 1], p.device(x=1 - p.x)
            )

        along[0].start()
        along[3].start()
        along[1].start()
        along[2].start()
        pl.when(same)(keep.start)
        for copy in home:
            pl.when(jnp.logical_not(same))(copy.start)
        yield
        for k in range(2):

            @pl.when(jnp.logical_not(same))
            def _(k=k):
                passed(k, True).wait_recv()
                passed(k, True).start()

            @pl.when(same)
            def _(k=k):
                passed(k, False).wait_recv()
                passed(k, False).start()

        yield
        for copy in along:
            copy.wait_send()
        pl.when(same)(keep.wait)
        for copy in home:
            pl.when(jnp.logical_not(same))(copy.wait_send)
        for k in range(2):
            pl.when(jnp.logical_not(same))(passed(k, True).wait_send)
            pl.when(same)(passed(k, False).wait_send)
        for slot in range(4):
            y, c = slot // 2, slot % 2
            for i in range(2):
                came = remote(rows(slot, i), rows(slot, i), send.at[0], recv.at[slot, i], p.partner())
                if i == 0:
                    waited = jnp.logical_not(same) & (p.y == y)
                else:
                    waited = same & (p.y != y)
                mine = same & (part == slot)
                pl.when(jnp.logical_not(waited | mine))(came.wait_recv)


class PlaneScatter(Task):
    vmem_ins = (0,)
    vmem_outs = (0,)

    def __init__(self, partial):
        rows, depth = partial.shape[0] // 4, partial.shape[1]
        self.ins = (partial.reshape(4, rows, depth),)
        self.outs = (jax.ShapeDtypeStruct((rows, depth), f32),)
        self.scratch = (pltpu.VMEM((4, rows, depth), bf16), DMA((4,)), DMA((4,)))

    def steps(self, p, ins, outs, scratch):
        (parts,), (out,), (came, send, recv) = ins, outs, scratch
        head, ours = 2 * p.y + p.x, 2 * p.y + p.c

        def copy_to(part):
            target = p.device(x=p.c, y=part // 2, c=part % 2)
            return remote(parts.at[part], came.at[head], send.at[part], recv.at[head], target)

        for part in range(4):
            here = (p.x == p.c) & (part == ours)
            pl.when(jnp.logical_not(here))(copy_to(part).start)
        yield
        for part in range(4):
            here = (p.x == p.c) & (part == ours)
            pl.when(jnp.logical_not(here))(copy_to(part).wait_send)
            arrived = remote(parts.at[part], came.at[part], send.at[part], recv.at[part], p.partner())
            mine = (p.x == p.c) & (part == head)
            pl.when(jnp.logical_not(mine))(arrived.wait_recv)

        @pl.when(p.x == p.c)
        def _():
            came[head] = parts[ours]

        @pl.loop(0, out.shape[0] // 16)
        def _(i):
            at = pl.ds(pl.multiple_of(i * 16, 16), 16)
            low = came[0, at, :].astype(f32) + came[1, at, :].astype(f32)
            out[at, :] = low + (came[2, at, :].astype(f32) + came[3, at, :].astype(f32))


class HeadsForward(PlaneScatter):
    vmem_ins = (0, 1, 2, 3)
    vmem_outs = (0, 1)

    def __init__(self, partial, tokens, gain_out, gain_in):
        super().__init__(partial)
        depth = tokens.shape[1]
        self.ins += (tokens, gain_out.reshape(1, depth), gain_in.reshape(1, depth))
        self.outs += (jax.ShapeDtypeStruct(tokens.shape, bf16),)

    def steps(self, p, ins, outs, scratch):
        partial, tokens, gain_out, gain_in = ins
        summed, normed = outs
        yield from super().steps(p, (partial,), (summed,), scratch)

        @pl.loop(0, normed.shape[0] // 16)
        def _(i):
            at = pl.ds(pl.multiple_of(i * 16, 16), 16)
            middle = tokens[at, :].astype(f32) + normalize(summed[at, :], gain_out[...])
            normed[at, :] = normalize(middle, gain_in[...]).astype(bf16)


class HeadsBackward(PlaneGather):
    vmem_ins = (0, 1, 2, 3, 4, 5)
    vmem_outs = (0, 1, 2)

    def __init__(self, d_normed, projected, tokens, cotangent, gain_out, gain_in):
        super().__init__(tokens)
        depth = tokens.shape[1]
        gains = (gain_out.reshape(1, depth), gain_in.reshape(1, depth))
        self.ins = (d_normed, projected, tokens, cotangent) + gains
        self.outs += (
            jax.ShapeDtypeStruct(tokens.shape, f32),
            jax.ShapeDtypeStruct((2, 16, depth), f32),
        )
        self.scratch += (pltpu.VMEM(tokens.shape, bf16),)

    def steps(self, p, ins, outs, scratch):
        d_normed, projected, tokens, cotangent, gain_out, gain_in = ins
        whole, d_middle, sums = outs
        *sems, own = scratch
        sums[...] = jnp.zeros_like(sums)

        def back(values, gain, upstream):
            factor = factor_of(values)
            unit = values * factor
            scaled = upstream * (1.0 + gain)
            inner = jnp.mean(scaled * unit, axis=-1, keepdims=True)
            return (scaled - unit * inner) * factor, upstream * unit

        @pl.loop(0, own.shape[0] // 16)
        def _(i):
            at = pl.ds(pl.multiple_of(i * 16, 16), 16)
            values = projected[at, :]
            middle = tokens[at, :].astype(f32) + normalize(values, gain_out[...])
            part, by_in = back(middle, gain_in[...], d_normed[at, :])
            total = cotangent[at, :].astype(f32) + part
            d_middle[at, :] = total
            d_values, by_out = back(values, gain_out[...], total)
            own[at, :] = d_values.astype(bf16)
            sums[0] += by_out
            sums[1] += by_in

        yield from super().steps(p, (own,), (whole,), sems)


class PairGather(Task):
    vmem_ins = (0,)
    vmem_outs = (0,)

    def __init__(self, nz, own, trade):
        self.trade = trade
        self.ins = (own,)
        self.outs = (jax.ShapeDtypeStruct((nz, 2) + own.shape, bf16),)
        self.scratch = (DMA((2, nz)), DMA((2, nz)), DMA((nz,)), DMA((nz,)), DMA, DMA, DMA)

    def steps(self, p, ins, outs, scratch):
        (own,), (full,), (send, recv, x_send, x_recv, t_send, t_recv, local) = ins, outs, scratch
        nz = p.nz
        keep = pltpu.make_async_copy(own, full.at[p.z, p.c], local)
        line = LineGather(p, lambda z: full.at[z, p.c], send, recv)

        def across(z):
            here = full.at[z, p.c]
            return remote(here, here, x_send.at[z], x_recv.at[z], p.partner())

        if self.trade:
            same = p.c == p.x
            move = remote(own, full.at[p.z, p.x], t_send, t_recv, p.device(x=1 - p.x, c=1 - p.c))
            pl.when(same)(keep.start)
            pl.when(jnp.logical_not(same))(move.start)
            yield
            pl.when(same)(keep.wait)
            pl.when(jnp.logical_not(same))(move.wait_recv)
        else:
            keep.start()
            keep.wait()
        line.start(1)
        across(p.z).start()
        yield
        for s in range(1, nz):
            line.arrive(s)
            if s < nz - 1:
                line.start(s + 1)
            for came, z in line.newest(s):
                pl.when(came)(across(z).start)
            yield
        line.finish()
        if self.trade:
            pl.when(jnp.logical_not(same))(move.wait_send)
        for z in range(nz):
            across(z).wait()


class ZGather(Task):
    vmem_ins = (0,)
    vmem_outs = (0,)

    def __init__(self, nz, own):
        self.ins = (own,)
        self.outs = (jax.ShapeDtypeStruct((nz,) + own.shape, bf16),)
        self.scratch = (DMA((2, nz)), DMA((2, nz)), DMA)

    def steps(self, p, ins, outs, scratch):
        (own,), (full,), (send, recv, local) = ins, outs, scratch
        line = LineGather(p, lambda z: full.at[z], send, recv)
        keep = pltpu.make_async_copy(own, full.at[p.z], local)
        keep.start()
        keep.wait()
        line.start(1)
        yield
        for s in range(1, p.nz):
            line.arrive(s)
            if s < p.nz - 1:
                line.start(s + 1)
            yield
        line.finish()


class ZScatter(Task):
    vmem_outs = (0,)

    def __init__(self, nz, partial):
        rows, depth = partial.shape[0] // nz, partial.shape[1]
        self.ins = (partial.reshape(nz, rows, depth),)
        self.outs = (jax.ShapeDtypeStruct((rows, depth), f32),)
        line = pltpu.VMEM((nz - 1, rows, depth), bf16)
        self.scratch = (
            pltpu.VMEM((nz, rows, depth), bf16), line, line, DMA((2, nz)), DMA((2, nz)), DMA
        )

    def steps(self, p, ins, outs, scratch):
        (given,), (out,), (parts, up, down, send, recv, local) = ins, outs, scratch
        bring = pltpu.make_async_copy(given, parts, local)
        bring.start()
        bring.wait()
        line = LineScatter(p, lambda z: parts.at[z], up, down, send, recv)
        line.start(1)
        yield
        for t in range(1, p.nz):
            line.arrive(t)
            if t < p.nz - 1:
                line.start(t + 1)
            yield
        line.total(out)
        line.finish()


class PairScatter(Task):
    vmem_outs = (0,)

    def __init__(self, nz, given, trade):
        _, _, rows, width = given.shape
        self.trade = trade
        self.ins = (given,)
        self.outs = (jax.ShapeDtypeStruct((rows, width), bf16),)
        whole = pltpu.VMEM((nz, rows, width), bf16)
        line = pltpu.VMEM((nz - 1, rows, width), bf16)
        self.scratch = (
            whole, whole, line, line,
            DMA((nz,)), DMA((nz,)), DMA((2, nz)), DMA((2, nz)), DMA((nz,)), DMA, DMA, DMA,
        )

    def steps(self, p, ins, outs, scratch):
        (given,), (out,) = ins, outs
        parts, came, up, down, x_send, x_recv, send, recv, local, b_send, b_recv, b_local = scratch
        nz = p.nz
        order = [exclusive_or(p.z, i) for i in (3, 2, 1, 0)]

        def away(z):
            return remote(given.at[z, 1 - p.c], came.at[z], x_send.at[z], x_recv.at[z], p.partner())

        def bring(z):
            return pltpu.make_async_copy(given.at[z, p.c], parts.at[z], local.at[z])

        for z in order:
            away(z).start()
            bring(z).start()
        yield
        for z in order:
            away(z).wait_recv()
            bring(z).wait()
            add_rows(parts.at[z], parts.at[z], came.at[z])
        line = LineScatter(p, lambda z: parts.at[z], up, down, send, recv)
        line.start(1)
        yield
        for t in range(1, nz):
            line.arrive(t)
            if t < nz - 1:
                line.start(t + 1)
            yield
        if not self.trade:
            line.total(out)
        else:
            line.total(came.at[0])
            same = p.c == p.x
            back = remote(came.at[0], out, b_send, b_recv, p.device(x=1 - p.x, c=1 - p.c))
            keep = pltpu.make_async_copy(came.at[0], out, b_local)
            pl.when(same)(keep.start)
            pl.when(jnp.logical_not(same))(back.start)
            yield
            pl.when(same)(keep.wait)
            pl.when(jnp.logical_not(same))(back.wait)
        for z in order:
            away(z).wait_send()
        line.finish()


class Deal:
    def __init__(self, p, shard, place, quarter, send, recv):
        self.p, self.shard, self.place, self.quarter = p, shard, place, quarter
        self.send, self.recv = send, recv
        self.per_core = p.nz // 2

    def piece(self, piece, half):
        columns = pl.ds(piece * self.quarter, self.quarter)
        return self.shard.at[half, :, columns]

    def away(self, piece, half):
        p = self.p
        z = p.c * self.per_core + piece
        return z, remote(
            self.piece(piece, half),
            self.place(p.z, half),
            self.send.at[2 * piece + half],
            self.recv.at[p.z],
            p.device(z=z, c=half),
        )

    def local(self, piece):
        p = self.p
        columns = pl.ds(piece * self.quarter, self.quarter)
        return pltpu.make_async_copy(
            self.shard.at[p.c, :, columns], self.place(p.z, p.c), self.recv.at[p.z]
        )

    def start(self, in_plane):
        p = self.p
        for piece in range(self.per_core):
            for half in range(2):
                z, copy = self.away(piece, half)
                if in_plane:
                    pl.when((z == p.z) & (p.c != half))(copy.start)
                    pl.when((z == p.z) & (p.c == half))(self.local(piece).start)
                else:
                    pl.when(z != p.z)(copy.start)

    def arrive(self, source):
        p = self.p
        here = self.place(source, p.c)
        ours = (source == p.z) & (p.c == p.z // self.per_core)
        came = remote(here, here, self.send.at[0], self.recv.at[source], p.partner())
        pl.when(jnp.logical_not(ours))(came.wait_recv)
        pl.when(ours)(self.local(0).wait)

    def finish(self):
        p = self.p
        for piece in range(self.per_core):
            for half in range(2):
                z, copy = self.away(piece, half)
                here = (z == p.z) & (p.c == half)
                pl.when(jnp.logical_not(here))(copy.wait_send)


class DealTask(Task):
    vmem_outs = (0,)

    def __init__(self, nz, shard):
        rows, units = shard.shape
        self.ins = (shard.reshape(2, rows // 2, units),)
        self.outs = (jax.ShapeDtypeStruct((nz, rows // 2, 2 * units // nz), bf16),)
        self.scratch = (DMA((nz,)), DMA((nz,)))

    def steps(self, p, ins, outs, scratch):
        (shard,), (pieces,), (send, recv) = ins, outs, scratch
        deal = Deal(p, shard, lambda z, half: pieces.at[z], pieces.shape[-1], send, recv)
        deal.start(False)
        deal.start(True)
        yield
        for i in range(p.nz):
            deal.arrive(exclusive_or(p.z, i))
        deal.finish()


class Copies(Task):
    def __init__(self, nz, given, dealt):
        self.dealt = dealt
        if dealt:
            _, half, quarter = given.shape
            self.ins = (given,)
        else:
            rows, units = given.shape
            half, quarter = rows // 2, 2 * units // nz
            self.ins = (given.reshape(2, half, units),)
        self.outs = (jax.ShapeDtypeStruct((nz * 4 * half, 2 * quarter), bf16),)
        self.scratch = (pltpu.VMEM(self.outs[0].shape, bf16), DMA, *copy_sems(nz))

    def steps(self, p, ins, outs, scratch):
        full, done, *sems = scratch
        yield from copy_steps(p, ins[0], full, sems, self.dealt)
        store = pltpu.make_async_copy(full, outs[0], done)
        store.start()
        yield
        store.wait()


def copy_sems(nz):
    one, two = DMA((nz,)), DMA((nz, 2))
    return (one, one, one, one, two, two, two, two)


def copy_steps(p, given, full, sems, dealt):
    d_send, d_recv, f_send, f_recv, s_send, s_recv, x_send, x_recv = sems
    nz = p.nz
    quarter, half = full.shape[1] // 2, full.shape[0] // (4 * nz)

    def strip(z, x, c):
        return pl.ds(pl.multiple_of(((z * 2 + x) * 2 + c) * half, half), half)

    def place(z, x, c, y):
        return full.at[strip(z, x, c), pl.ds(pl.multiple_of(y * quarter, 128), quarter)]

    fx, fy = p.x + (1 - 2 * p.x) * (1 - p.c), p.y + (1 - 2 * p.y) * p.c
    sx, sy = p.x + (1 - 2 * p.x) * p.c, p.y + (1 - 2 * p.y) * (1 - p.c)

    def own(z):
        return given.at[z] if dealt else place(z, p.x, p.c, p.y)

    def first(z):
        target = p.device(x=fx, y=fy)
        return remote(own(z), place(z, p.x, p.c, p.y), f_send.at[z], f_recv.at[z], target)

    def second(z, which):
        x, y = (fx, fy) if which else (p.x, p.y)
        here = place(z, x, p.c, y)
        src = here if which else own(z)
        target = p.device(x=sx, y=sy)
        return remote(src, here, s_send.at[z, which], s_recv.at[z, which], target)

    def across(z, x):
        here = full.at[strip(z, x, p.c)]
        return remote(here, here, x_send.at[z, x], x_recv.at[z, x], p.partner())

    def keep(z):
        return pltpu.make_async_copy(given.at[z], place(z, p.x, p.c, p.y), d_send.at[z])

    order = [exclusive_or(p.z, i) for i in range(nz)]
    if dealt:
        for z in order:
            first(z).start()
            second(z, 0).start()
            keep(z).start()
        for z in order:
            keep(z).wait()
        yield
    else:
        deal = Deal(p, given, lambda z, c: place(z, p.x, c, p.y), quarter, d_send, d_recv)
        deal.start(True)
        yield
        deal.arrive(order[0])
        first(order[0]).start()
        second(order[0], 0).start()
        yield
        deal.start(False)
        yield
        for z in order[1:]:
            deal.arrive(z)
            first(z).start()
            second(z, 0).start()
            yield
    for z in order:
        first(z).wait_recv()
        second(z, 1).start()
        yield
    for z in order:
        second(z, 0).wait_recv()
        second(z, 1).wait_recv()
        across(z, 0).start()
        across(z, 1).start()
        yield
    for z in range(nz):
        first(z).wait_send()
        for i in range(2):
            second(z, i).wait_send()
            across(z, i).wait()
    if not dealt:
        deal.finish()


class DealBack:
    def __init__(self, p, source, out, quarter, send, recv):
        self.p, self.source, self.out, self.quarter = p, source, out, quarter
        self.send, self.recv = send, recv
        self.per_core = p.nz // 2
        self.owner = p.z // self.per_core

    def out_at(self, z, half):
        start = pl.multiple_of(lax.rem(z, self.per_core) * self.quarter, 128)
        return self.out.at[half, :, pl.ds(start, self.quarter)]

    def away(self, z):
        p = self.p
        return remote(
            self.source(z),
            self.out_at(p.z, p.c),
            self.send.at[z],
            self.recv.at[2 * lax.rem(p.z, self.per_core) + p.c],
            p.device(z=z, c=self.owner),
        )

    def keep(self, z):
        p = self.p
        return pltpu.make_async_copy(
            self.source(z),
            self.out_at(p.z, p.c),
            self.recv.at[2 * lax.rem(p.z, self.per_core) + p.c],
        )

    def start(self, z):
        p = self.p
        here = (z == p.z) & (p.c == self.owner)
        pl.when(jnp.logical_not(here))(self.away(z).start)
        pl.when(here)(self.keep(z).start)

    def finish(self):
        p = self.p
        for piece in range(self.per_core):
            for half in range(2):
                z = p.c * self.per_core + piece
                place = self.out_at(z, half)
                came = remote(
                    place, place, self.send.at[0], self.recv.at[2 * piece + half], p.partner()
                )
                ours = (z == p.z) & (p.c == half)
                pl.when(jnp.logical_not(ours))(came.wait_recv)
        for z in range(p.nz):
            here = (z == p.z) & (p.c == self.owner)
            pl.when(jnp.logical_not(here))(self.away(z).wait_send)
            pl.when(here)(self.keep(z).wait)


class DealBackTask(Task):
    vmem_outs = (0,)

    def __init__(self, nz, sums):
        _, half, quarter = sums.shape
        self.ins = (sums,)
        self.outs = (jax.ShapeDtypeStruct((2, half, nz // 2 * quarter), bf16),)
        self.scratch = (DMA((nz,)), DMA((nz,)))

    def steps(self, p, ins, outs, scratch):
        (sums,), (out,), (send, recv) = ins, outs, scratch
        deal = DealBack(p, lambda z: sums.at[z], out, sums.shape[-1], send, recv)
        for i in (3, 2, 1, 0):
            deal.start(exclusive_or(p.z, i))
        yield
        deal.finish()


class Sums(Task):
    def __init__(self, nz, grad, deal):
        depth, width = grad.shape
        half, quarter = depth // (4 * nz), width // 2
        self.deal = deal
        self.ins = (grad.reshape(nz, 2, 2, half, width),)
        if deal:
            self.outs = (jax.ShapeDtypeStruct((2, half, nz // 2 * quarter), bf16),)
        else:
            self.outs = (jax.ShapeDtypeStruct((nz, half, quarter), bf16),)
            self.vmem_outs = (0,)
        whole = pltpu.VMEM((nz, 2, half, width), bf16)
        self.scratch = (
            whole,
            whole,
            pltpu.VMEM((nz, 2, half, quarter), bf16),
            pltpu.VMEM((nz, half, quarter), bf16),
            DMA((nz, 2)), DMA((nz, 2)), DMA((nz, 2)), DMA((nz, 2)), DMA((nz, 2)),
            DMA((nz,)), DMA((nz,)), DMA((nz,)), DMA((nz,)),
        )

    def steps(self, p, ins, outs, scratch):
        (given,), (out,) = ins, outs
        mine, came, first_in, second_in, *sems = scratch
        local, c_send, c_recv, f_send, f_recv, s_send, s_recv, d_send, d_recv = sems
        nz, quarter = p.nz, given.shape[4] // 2
        order = [exclusive_or(p.z, i) for i in (3, 2, 1, 0)]

        def bring(z, x):
            return pltpu.make_async_copy(given.at[z, x, p.c], mine.at[z, x], local.at[z, x])

        def across(z, x):
            src = given.at[z, x, 1 - p.c]
            return remote(src, came.at[z, x], c_send.at[z, x], c_recv.at[z, x], p.partner())

        def place(z, x, y):
            return mine.at[z, x, :, pl.ds(pl.multiple_of(y * quarter, 128), quarter)]

        fx, fy = p.x + (1 - 2 * p.x) * p.c, p.y + (1 - 2 * p.y) * (1 - p.c)
        sx, sy = p.x + (1 - 2 * p.x) * (1 - p.c), p.y + (1 - 2 * p.y) * p.c

        def first(z, which):
            x, y = (1 - p.x, 1 - p.y) if which else (fx, fy)
            target = p.device(x=fx, y=fy)
            return remote(
                place(z, x, y), first_in.at[z, which], f_send.at[z, which], f_recv.at[z, which], target
            )

        def second(z):
            target = p.device(x=sx, y=sy)
            return remote(place(z, sx, sy), second_in.at[z], s_send.at[z], s_recv.at[z], target)

        back = DealBack(p, lambda z: place(z, p.x, p.y), out, quarter, d_send, d_recv)
        for z in order:
            for x in range(2):
                across(z, x).start()
                bring(z, x).start()
        yield
        def over_core(z):
            for x in range(2):
                across(z, x).wait_recv()
                bring(z, x).wait()
                add_rows(mine.at[z, x], mine.at[z, x], came.at[z, x])
            for which in (1, 0):
                first(z, which).start()

        def over_first(z):
            for which in (1, 0):
                at = place(z, sx, sy) if which else place(z, p.x, p.y)
                first(z, which).wait_recv()
                add_rows(at, at, first_in.at[z, which])
                if which:
                    second(z).start()

        def over_second(z):
            second(z).wait_recv()
            at = place(z, p.x, p.y)
            if self.deal:
                add_rows(at, at, second_in.at[z])
                back.start(z)
            else:
                add_rows(out.at[z], at, second_in.at[z])

        over_core(order[0])
        yield
        for i in range(nz + 1):
            if i + 1 < nz:
                over_core(order[i + 1])
                yield
            if i < nz:
                over_first(order[i])
                yield
            if i >= 1:
                over_second(order[i - 1])
                yield
        if self.deal:
            back.finish()
        for z in range(nz):
            second(z).wait_send()
            for i in range(2):
                first(z, i).wait_send()
                across(z, i).wait_send()


class FeedForward(Task):
    vmem_ins = (0, 1, 2)
    vmem_outs = (0, 1)
    spare = 10

    def __init__(self, nz, own, cotangent, gain, gate, up, down_pieces):
        rows, depth = own.shape
        units = gate.shape[1]
        self.rows, self.depth, self.units = rows, depth, units
        self.ins = (own, cotangent, gain.reshape(1, depth), gate, up, down_pieces)
        wide = jax.ShapeDtypeStruct((depth, units), bf16)
        exact = jax.ShapeDtypeStruct((rows, depth), f32)
        self.outs = (exact, exact, wide, wide, wide)
        weight = pltpu.VMEM((depth, units), bf16)
        tokens = pltpu.VMEM((nz * rows, depth), bf16)
        inner = pltpu.VMEM((nz * rows, units), bf16)
        line = pltpu.VMEM((2, nz - 1, rows // 2, depth), bf16)
        self.scratch = (
            weight, weight, weight, tokens, tokens, inner, inner, inner, tokens, line, line,
            DMA((8, 2, nz)), DMA((8, 2, nz)), DMA((8,)), *copy_sems(nz),
        )

    def steps(self, p, ins, outs, scratch):
        own, cotangent, gain, gate_in, up_in, down_in = ins
        ff_out, dn_out, grad_gate, grad_up, grad_down = outs
        gate, up, down, normed, d_ff, hidden, gated, upped, parts, above, below, *sems = scratch
        send, recv, local, *down_sems = sems
        copies = copy_steps(p, down_in, down, down_sems, True)
        nz, depth, units = p.nz, self.depth, self.units
        part = self.rows // 2
        half_rows = nz * part
        tile = units // 3

        def entry(buffer, half):
            return lambda z: buffer.at[pl.ds(pl.multiple_of(half * half_rows + z * part, part), part)]

        gathers, scatters = [], []
        for i, buffer in enumerate((normed, d_ff)):
            for half in range(2):
                k = 4 * i + half
                gathers.append(LineGather(p, entry(buffer, half), send.at[k], recv.at[k]))
                scatters.append(
                    LineScatter(
                        p, entry(parts, half), above.at[half], below.at[half], send.at[k + 2], recv.at[k + 2]
                    )
                )

        loads = [
            pltpu.make_async_copy(src, dst, local.at[i])
            for i, (src, dst) in enumerate(((gate_in, gate), (up_in, up)))
        ]

        def gelu(v):
            bent = jnp.tanh(math.sqrt(2.0 / math.pi) * (v + 0.044715 * (v * v * v)))
            return 0.5 * v * (1.0 + bent), bent

        def columns(i):
            return pl.ds(pl.multiple_of(i * tile, 128), tile)

        def hide(half, low, high):
            rows = slice(half * half_rows, (half + 1) * half_rows)

            @pl.loop(low, high)
            def _(i):
                at = columns(i)
                gate_lin = jnp.dot(normed[rows, :], gate[:, at], preferred_element_type=f32)
                up_lin = jnp.dot(normed[rows, :], up[:, at], preferred_element_type=f32)
                hidden[rows, at] = (gelu(gate_lin)[0] * up_lin).astype(bf16)
                gated[rows, at] = gate_lin.astype(bf16)
                upped[rows, at] = up_lin.astype(bf16)

        def project(half):
            rows = slice(half * half_rows, (half + 1) * half_rows)

            @pl.loop(0, depth // tile)
            def _(i):
                at = columns(i)
                parts[rows, at] = contract(hidden[rows, :], down[at, :], 1, 1).astype(bf16)

        def hide_back(half, low, high):
            rows = slice(half * half_rows, (half + 1) * half_rows)

            @pl.loop(low, high)
            def _(i):
                at = columns(i)
                d_hidden = jnp.dot(d_ff[rows, :], down[:, at], preferred_element_type=f32)
                v, u = gated[rows, at].astype(f32), upped[rows, at].astype(f32)
                value, bent = gelu(v)
                slope = 0.5 * (1.0 + bent) + (0.5 * math.sqrt(2.0 / math.pi)) * v * (
                    1.0 - bent * bent
                ) * (1.0 + (3.0 * 0.044715) * (v * v))
                gated[rows, at] = (d_hidden * u * slope).astype(bf16)
                upped[rows, at] = (d_hidden * value).astype(bf16)

        def project_back(half):
            rows = slice(half * half_rows, (half + 1) * half_rows)

            @pl.loop(0, depth // tile)
            def _(i):
                at = columns(i)
                total = contract(gated[rows, :], gate[at, :], 1, 1)
                parts[rows, at] = (total + contract(upped[rows, :], up[at, :], 1, 1)).astype(bf16)

        def turn_back(half):
            start = half * half_rows + p.z * part

            @pl.loop(0, part // 16)
            def _(i):
                at = pl.ds(pl.multiple_of(half * part + i * 16, 16), 16)
                values = ff_out[at, :]
                scaled = cotangent[at, :].astype(f32) * (1.0 + gain[...])
                factor = factor_of(values)
                unit = values * factor
                mean = jnp.mean(scaled * unit, axis=-1, keepdims=True)
                here = pl.ds(pl.multiple_of(start + i * 16, 16), 16)
                d_ff[here, :] = ((scaled - unit * mean) * factor).astype(bf16)

        def weigh(left, right, out, low, high):
            @pl.loop(low, high)
            def _(i):
                at = pl.ds(pl.multiple_of(i * 256, 128), 256)
                out[at, :] = contract(left[:, at], right[...], 0, 0).astype(bf16)

        def store(i, src, dst):
            return pltpu.make_async_copy(src, dst, local.at[3 + i])

        blocks = depth // 256
        one, two, one_back, two_back = gathers
        sum_one, sum_two, sum_one_back, sum_two_back = scatters
        keep = [
            pltpu.make_async_copy(own.at[pl.ds(half * part, part)], entry(normed, half)(p.z), local.at[6 + half])
            for half in range(2)
        ]
        keep[0].start()
        keep[1].start()
        keep[0].wait()
        one.start(1)
        keep[1].wait()
        next(copies)
        for load in loads:
            load.start()
        two.start(1)
        one.arrive(1)
        one.start(2)
        two.arrive(1)
        one.arrive(2)
        two.start(2)
        one.start(3)
        for _ in range(nz):
            next(copies)
        one.arrive(3)
        for load in loads:
            load.wait()
        hide(0, 0, 1)
        two.arrive(2)
        hide(0, 1, 2)
        two.start(3)
        two.arrive(3)
        hide(0, 2, 3)
        for _ in copies:
            pass
        project(0)
        sum_one.start(1)
        hide(1, 0, 2)
        sum_one.arrive(1)
        sum_one.start(2)
        hide(1, 2, 3)
        project(1)
        sum_two.start(1)
        sum_one.arrive(2)
        sum_one.start(3)
        sum_two.arrive(1)
        sum_two.start(2)
        sum_one.arrive(3)
        sum_one.total(ff_out.at[pl.ds(0, part)])
        turn_back(0)
        one_back.start(1)
        sum_two.arrive(2)
        sum_two.start(3)
        one_back.arrive(1)
        one_back.start(2)
        sum_two.arrive(3)
        one_back.arrive(2)
        one_back.start(3)
        sum_two.total(ff_out.at[pl.ds(part, part)])
        turn_back(1)
        two_back.start(1)
        one_back.arrive(3)
        hide_back(0, 0, 3)
        two_back.arrive(1)
        two_back.start(2)
        sum_one.finish()
        project_back(0)
        two_back.arrive(2)
        two_back.start(3)
        sum_one_back.start(1)
        two_back.arrive(3)
        hide_back(1, 0, 3)
        sum_one_back.arrive(1)
        sum_one_back.start(2)
        sum_two.finish()
        project_back(1)
        sum_two_back.start(1)
        weigh(d_ff, hidden, down, 0, blocks)
        store(0, down, grad_down).start()
        sum_one_back.arrive(2)
        sum_two_back.arrive(1)
        sum_two_back.start(2)
        sum_one_back.start(3)
        weigh(normed, gated, gate, 0, blocks)
        store(1, gate, grad_gate).start()
        sum_two_back.arrive(2)
        sum_two_back.start(3)
        weigh(normed, upped, up, 0, blocks)
        store(2, up, grad_up).start()
        sum_one_back.arrive(3)
        sum_one_back.total(dn_out.at[pl.ds(0, part)])
        sum_two_back.arrive(3)
        sum_two_back.total(dn_out.at[pl.ds(part, part)])
        for gather in gathers:
            gather.finish()
        sum_one_back.finish()
        sum_two_back.finish()
        store(0, down, grad_down).wait()
        store(1, gate, grad_gate).wait()
        store(2, up, grad_up).wait()
        yield


class SumAll(Task):
    vmem_ins = (0,)
    vmem_outs = (0,)

    def __init__(self, values):
        self.ins = (values,)
        self.outs = (jax.ShapeDtypeStruct(values.shape, f32),)
        stage = pltpu.VMEM((5,) + values.shape, f32)
        self.scratch = (stage, stage, DMA((5,)), DMA((5,)))

    def steps(self, p, ins, outs, scratch):
        (given,), (out,), (stage, came, send, recv) = ins, outs, scratch
        targets = [
            p.partner(),
            p.device(y=1 - p.y),
            p.device(x=1 - p.x),
            p.device(z=exclusive_or(p.z, 1)),
            p.device(z=exclusive_or(p.z, 2)),
        ]
        stage[0] = given[...]
        for i, target in enumerate(targets):
            copy = remote(stage.at[i], came.at[i], send.at[i], recv.at[i], target)
            copy.start()
            yield
            copy.wait()
            total = stage[i] + came[i]
            if i < 4:
                stage[i + 1] = total
            else:
                out[...] = total


def run_tasks(nz, number, tasks, order="", every=False):
    counts = [(len(t.ins), len(t.outs), len(t.scratch)) for t in tasks]

    def split(refs, which):
        found = []
        for count in counts:
            found.append(refs[: count[which]])
            refs = refs[count[which] :]
        return found, refs

    def body(*refs):
        ins, refs = split(refs, 0)
        outs, refs = split(refs, 1)
        scratch, refs = split(refs, 2)
        p = Spot(nz)
        p.greet()
        running = [t.steps(p, *given) for t, *given in zip(tasks, ins, outs, scratch)]
        done = [False] * len(tasks)
        for digit in order:
            i = int(digit)
            if not done[i]:
                done[i] = next(running[i], "end") == "end"
        while not all(done):
            for i, steps in enumerate(running):
                if not done[i]:
                    done[i] = next(steps, "end") == "end"

    sent = sum(x.size * 2 for t in tasks for x in t.ins)
    spare = max(t.spare for t in tasks) * 2**20
    held = [s for t in tasks for s in t.scratch if getattr(s, "memory_space", None) == pltpu.VMEM]
    held += [t.ins[i] for t in tasks for i in t.vmem_ins] + [t.outs[i] for t in tasks for i in t.vmem_outs]
    vmem = sum(math.prod(s.shape) * jnp.dtype(s.dtype).itemsize for s in held)
    results = pl.pallas_call(
        body,
        out_shape=[o for t in tasks for o in t.outs],
        in_specs=[in_vmem if i in t.vmem_ins else anywhere for t in tasks for i in range(len(t.ins))],
        out_specs=[
            in_vmem if i in t.vmem_outs else anywhere for t in tasks for i in range(len(t.outs))
        ],
        scratch_shapes=[s for t in tasks for s in t.scratch],
        compiler_params=pltpu.CompilerParams(
            collective_id=number, has_side_effects=True, vmem_limit_bytes=vmem + spare
        ),
        cost_estimate=pl.CostEstimate(
            flops=0, bytes_accessed=sent, transcendentals=0, remote_bytes_transferred=sent
        ),
    )(*[x for t in tasks for x in t.ins])
    found, _ = split(list(results), 1)
    if every:
        return found
    return found[0] if len(tasks) == 1 else [f[0] for f in found]


START_ORDER = "10222102221222213222222131"
FINISH_ORDER = "0103111101131101132220113222022322222"
KV_ORDER = "0120122021220221222011222"


class Kernels:
    def __init__(self, at):
        self.at = at
        self.blocks, self.nz = at.blocks, at.nz
        self.block = 2 * at.z + at.c
        self.number = 0

    def run(self, tasks, order=""):
        self.number += 1
        return run_tasks(self.nz, self.number, tasks, order)

    def flat(self, whole):
        return whole.reshape(-1, whole.shape[-1])

    def start(self, own, qkv_shard, gate, up):
        nz = self.nz
        tasks = [
            PlaneGather(own),
            PairGather(nz, qkv_shard, True),
            Copies(nz, gate, False),
            DealTask(nz, up),
        ]
        rows, qkv, gate_full, pieces = self.run(tasks, START_ORDER)
        return self.flat(rows), self.flat(qkv), gate_full, pieces

    def gather_kv(self, own, out_shard, pieces):
        nz = self.nz
        whole, out, up = self.run(
            [PairGather(nz, own, False), PairGather(nz, out_shard, True), Copies(nz, pieces, True)],
            "1021" + "012" + "0222" + "1" + "2222" + "02" + "1",
        )
        return whole.reshape((self.blocks,) + own.shape), self.flat(out), up

    def heads_forward(self, partial, tokens, gain_out, gain_in, down):
        task = HeadsForward(partial, tokens, gain_out, gain_in)
        self.number += 1
        (summed, normed), (pieces,) = run_tasks(
            self.nz, self.number, [task, DealTask(self.nz, down)], "01", True
        )
        return summed, normed, pieces

    def feed_forward(self, own, cotangent, gain, gate, up, down):
        task = FeedForward(self.nz, own, cotangent, gain, gate, up, down)
        self.number += 1
        return run_tasks(self.nz, self.number, [task])

    def heads_backward(self, *given):
        whole, d_middle, sums = self.run([HeadsBackward(*given)])
        return self.flat(whole), d_middle, jnp.sum(sums, axis=1)

    def scatter_kv_sums(self, parts, out_grad, grad):
        nz = self.nz
        given = parts.reshape((nz, 2) + parts.shape[1:])
        rows = out_grad.shape[0] // self.blocks
        out_given = out_grad.reshape(nz, 2, rows, out_grad.shape[1])
        kv, out, sums = self.run(
            [PairScatter(nz, given, False), PairScatter(nz, out_given, True), Sums(nz, grad, False)],
            KV_ORDER,
        )
        return kv, out, sums

    def scatter_heads_back(self, partial, sums):
        rows, shard = self.run([PlaneScatter(partial), DealBackTask(self.nz, sums)], "01")
        return rows, self.flat(shard)

    def finish(self, qkv_grad, gate_grad, up_grad, gains):
        rows = qkv_grad.shape[0] // self.blocks
        given = qkv_grad.reshape(self.nz, 2, rows, qkv_grad.shape[1])
        qkv, gate, up, total = self.run(
            [
                PairScatter(self.nz, given, True),
                Sums(self.nz, gate_grad, True),
                Sums(self.nz, up_grad, True),
                SumAll(gains.reshape(8, -1)),
            ],
            FINISH_ORDER,
        )
        return qkv, self.flat(gate), self.flat(up), total.reshape(gains.shape)


def project_kernel(info, normed_ref, weight_ref, q_ref, kv_ref, cos_ref, sin_ref):
    rows, half = cos_ref.shape
    dim = 2 * half
    heads = q_ref.shape[0]
    blocks = (info.shape[0] - 2) // 2
    me, prompts = info[2 * blocks], info[2 * blocks + 1]
    first = jnp.minimum(info[blocks + me], prompts) * rows
    positions = (lax.broadcasted_iota(jnp.int32, (rows, half), 0) + first).astype(f32)
    index = lax.broadcasted_iota(jnp.int32, (rows, half), 1).astype(f32)
    angles = positions * jnp.exp(index * (-2.0 * math.log(10000.0) / dim))
    cos_ref[...] = jnp.cos(angles)
    sin_ref[...] = jnp.sin(angles)
    for i in range(heads + 2):
        columns = slice(i * dim, (i + 1) * dim)
        linear = jnp.dot(normed_ref[...], weight_ref[:, columns], preferred_element_type=f32)
        if i <= heads:
            linear = rotate(linear, cos_ref[...], sin_ref[...])
        if i < heads:
            q_ref[i] = linear.astype(bf16)
        else:
            kv_ref[:, (i - heads) * dim : (i - heads + 1) * dim] = linear.astype(bf16)


def project(info, normed, weight):
    rows = normed.shape[0]
    heads = weight.shape[1] // HEAD_DIM - 2
    table = jax.ShapeDtypeStruct((rows, HEAD_DIM // 2), f32)
    return pl.pallas_call(
        project_kernel,
        in_specs=[pl.BlockSpec(memory_space=pltpu.SMEM), in_vmem, in_vmem],
        out_specs=[in_vmem] * 4,
        out_shape=[
            jax.ShapeDtypeStruct((heads, rows, HEAD_DIM), bf16),
            jax.ShapeDtypeStruct((rows, 2 * HEAD_DIM), bf16),
            table,
            table,
        ],
        compiler_params=pltpu.CompilerParams(vmem_limit_bytes=24 * 2**20),
        cost_estimate=pl.CostEstimate(
            flops=2 * rows * weight.size, bytes_accessed=2 * weight.size, transcendentals=0
        ),
    )(info, normed, weight)


def project_back_kernel(dq_ref, dkv_ref, cos_ref, sin_ref, weight_ref, lin_ref, out_ref):
    heads, rows, dim = dq_ref.shape
    cosine, sine = cos_ref[...], -sin_ref[...]
    for i in range(heads):
        lin_ref[:, i * dim : (i + 1) * dim] = rotate(dq_ref[i], cosine, sine).astype(bf16)
    start = heads * dim
    d_key = rotate(dkv_ref[:, :dim].astype(f32), cosine, sine)
    lin_ref[:, start : start + dim] = d_key.astype(bf16)
    lin_ref[:, start + dim :] = dkv_ref[:, dim:].astype(bf16)
    depth = weight_ref.shape[0]
    tile = 384

    @pl.loop(0, depth // tile)
    def _(i):
        at = pl.ds(pl.multiple_of(i * tile, 128), tile)
        out_ref[:, at] = contract(lin_ref[...], weight_ref[at, :], 1, 1).astype(bf16)


def project_back(d_query, d_kv, cosine, sine_table, weight):
    rows = d_kv.shape[0]
    depth, width = weight.shape
    return pl.pallas_call(
        project_back_kernel,
        in_specs=[in_vmem] * 5,
        out_specs=[in_vmem] * 2,
        out_shape=[
            jax.ShapeDtypeStruct((rows, width), bf16),
            jax.ShapeDtypeStruct((rows, depth), bf16),
        ],
        compiler_params=pltpu.CompilerParams(vmem_limit_bytes=24 * 2**20),
        cost_estimate=pl.CostEstimate(
            flops=2 * rows * weight.size, bytes_accessed=2 * weight.size, transcendentals=0
        ),
    )(d_query, d_kv, cosine, sine_table, weight)


def causal_mask(rows):
    shape = (rows, rows)
    return lax.broadcasted_iota(jnp.int32, shape, 1) <= lax.broadcasted_iota(jnp.int32, shape, 0)


def kind_of(info, step):
    blocks = pl.num_programs(0)
    me, prompts = info[2 * blocks], info[2 * blocks + 1]
    role = info[blocks + step]
    reads = (info[step] == info[me]) & (role < prompts) & (role < info[blocks + me])
    return jnp.where(step == me, 2, jnp.where(reads, 1, 0))


def forward_kernel(info, q_ref, kv_ref, out_ref, exact_ref, inv_ref, acc, total):
    step, last = pl.program_id(0), pl.num_programs(0) - 1
    heads, rows, dim = q_ref.shape
    kind = kind_of(info, step)

    @pl.when(step == 0)
    def _():
        acc[...] = jnp.zeros_like(acc)
        total[...] = jnp.zeros_like(total)

    def work(own):
        for head in range(heads):
            raw = contract(q_ref[head], kv_ref[0, :, :dim], 1, 1)
            weights = jnp.exp(softcap * jnp.tanh(raw * (score_scale / softcap)))
            if own:
                weights = jnp.where(causal_mask(rows), weights, 0.0)
            total[head] += jnp.sum(weights, axis=-1, keepdims=True)
            acc[head] += contract(weights.astype(bf16), kv_ref[0, :, dim:], 1, 0)

    @pl.when(kind == 1)
    def _():
        work(False)

    @pl.when(kind == 2)
    def _():
        work(True)

    @pl.when(step == last)
    def _():
        for head in range(heads):
            inverse = 1.0 / total[head]
            value = acc[head] * inverse
            inv_ref[head] = inverse
            exact_ref[:, head * dim : (head + 1) * dim] = value
            out_ref[:, head * dim : (head + 1) * dim] = value.astype(bf16)


def whole2(step, info):
    return (0, 0)


def whole3(step, info):
    return (0, 0, 0)


def by_step(step, info):
    return (step, 0, 0)


def attend(info, queries, all_kv):
    heads, rows, dim = queries.shape
    return pl.pallas_call(
        forward_kernel,
        grid_spec=pltpu.PrefetchScalarGridSpec(
            num_scalar_prefetch=1,
            grid=(all_kv.shape[0],),
            in_specs=[
                pl.BlockSpec((heads, rows, dim), whole3),
                pl.BlockSpec((1, rows, 2 * dim), by_step),
            ],
            out_specs=[
                pl.BlockSpec((rows, heads * dim), whole2),
                pl.BlockSpec((rows, heads * dim), whole2),
                pl.BlockSpec((heads, rows, 1), whole3),
            ],
            scratch_shapes=[
                pltpu.VMEM((heads, rows, dim), f32),
                pltpu.VMEM((heads, rows, 1), f32),
            ],
        ),
        out_shape=[
            jax.ShapeDtypeStruct((rows, heads * dim), bf16),
            jax.ShapeDtypeStruct((rows, heads * dim), f32),
            jax.ShapeDtypeStruct((heads, rows, 1), f32),
        ],
        compiler_params=pltpu.CompilerParams(vmem_limit_bytes=24 * 2**20),
        cost_estimate=pl.CostEstimate(
            flops=3 * 4 * heads * rows * rows * dim,
            bytes_accessed=8 * rows * dim * heads,
            transcendentals=6 * heads * rows * rows,
        ),
    )(info, queries, all_kv)


def backward_kernel(info, q_ref, kv_ref, up_ref, exact_ref, inv_ref, dq_ref, dkv_ref):
    step = pl.program_id(0)
    heads, rows, dim = q_ref.shape
    kind = kind_of(info, step)

    @pl.when(step == 0)
    def _():
        dq_ref[...] = jnp.zeros_like(dq_ref)

    def work(own):
        dk = jnp.zeros((rows, dim), f32)
        dv = jnp.zeros((rows, dim), f32)
        for head in range(heads):
            columns = slice(head * dim, (head + 1) * dim)
            up = up_ref[:, columns]
            delta = jnp.sum(up.astype(f32) * exact_ref[:, columns], axis=-1, keepdims=True)
            raw = contract(q_ref[head], kv_ref[0, :, :dim], 1, 1)
            bounded = jnp.tanh(raw * (score_scale / softcap))
            probs = jnp.exp(softcap * bounded) * inv_ref[head]
            if own:
                probs = jnp.where(causal_mask(rows), probs, 0.0)
            d_probs = contract(up, kv_ref[0, :, dim:], 1, 1)
            d_raw = probs * (d_probs - delta) * ((1.0 - bounded * bounded) * score_scale)
            d_raw = d_raw.astype(bf16)
            dq_ref[head] += contract(d_raw, kv_ref[0, :, :dim], 1, 0)
            dk += contract(d_raw, q_ref[head], 0, 0)
            dv += contract(probs.astype(bf16), up, 0, 0)
        dkv_ref[0, :, :dim] = dk.astype(bf16)
        dkv_ref[0, :, dim:] = dv.astype(bf16)

    @pl.when(kind == 1)
    def _():
        work(False)

    @pl.when(kind == 0)
    def _():
        dkv_ref[...] = jnp.zeros_like(dkv_ref)

    @pl.when(kind == 2)
    def _():
        work(True)


def attend_back(info, queries, all_kv, upstream, exact, inverse):
    heads, rows, dim = queries.shape
    blocks = all_kv.shape[0]
    return pl.pallas_call(
        backward_kernel,
        grid_spec=pltpu.PrefetchScalarGridSpec(
            num_scalar_prefetch=1,
            grid=(blocks,),
            in_specs=[
                pl.BlockSpec((heads, rows, dim), whole3),
                pl.BlockSpec((1, rows, 2 * dim), by_step),
                pl.BlockSpec((rows, heads * dim), whole2),
                pl.BlockSpec((rows, heads * dim), whole2),
                pl.BlockSpec((heads, rows, 1), whole3),
            ],
            out_specs=[
                pl.BlockSpec((heads, rows, dim), whole3),
                pl.BlockSpec((1, rows, 2 * dim), by_step),
            ],
        ),
        out_shape=[
            jax.ShapeDtypeStruct((heads, rows, dim), f32),
            jax.ShapeDtypeStruct((blocks, rows, 2 * dim), bf16),
        ],
        compiler_params=pltpu.CompilerParams(vmem_limit_bytes=24 * 2**20),
        cost_estimate=pl.CostEstimate(
            flops=3 * 10 * heads * rows * rows * dim,
            bytes_accessed=16 * rows * dim * heads,
            transcendentals=6 * heads * rows * rows,
        ),
    )(info, queries, all_kv, upstream, exact, inverse)


def on_device(
    tokens,
    cotangent,
    norm_attn_in,
    w_query,
    w_key,
    w_value,
    w_out,
    norm_attn_out,
    norm_ff_in,
    w_gate,
    w_up,
    w_down,
    norm_ff_out,
    block_group,
    block_role,
):
    at = Place()
    own_rows, depth = tokens.shape
    shard_rows, units = w_gate.shape
    regular = at.nz == 4 and shard_rows % 32 == 0 and units == depth and units % 768 == 0
    comm = Kernels(at) if regular else Permutes(at)
    blocks = at.blocks
    info = jnp.concatenate(
        [block_group, block_role, jnp.stack([comm.block, blocks // 4]).astype(jnp.int32)]
    )

    token_f32 = tokens.astype(f32)
    heads_width = w_query.shape[1]
    normed_one, qkv_full, gate_full, up_pieces = comm.start(
        normalize(token_f32, norm_attn_in).astype(bf16),
        jnp.concatenate([w_query, w_key, w_value], axis=1),
        w_gate,
        w_up,
    )
    queries, own_kv, cosine, sine_table = project(info, normed_one, qkv_full)
    all_kv, out_full, up_full = comm.gather_kv(own_kv, w_out.T, up_pieces)
    attn_rows, attended, inverse = attend(info, queries, all_kv)
    attn_proj, normed_two, down_pieces = comm.heads_forward(
        contract(attn_rows, out_full, 1, 1).astype(bf16), tokens, norm_attn_out, norm_ff_in, w_down.T
    )

    ff_proj, d_normed_two, gate_sum, up_sum, down_sum = comm.feed_forward(
        normed_two, cotangent, norm_ff_out, gate_full, up_full, down_pieces
    )
    middle = token_f32 + normalize(attn_proj, norm_attn_out)
    layer_out = middle + normalize(ff_proj, norm_ff_out)
    upstream = cotangent.astype(f32)
    _, grad_ff_out = normalize_back(ff_proj, norm_ff_out, upstream)

    d_proj_rows, d_middle, inner_gains = comm.heads_backward(
        d_normed_two, attn_proj, tokens, cotangent, norm_attn_out, norm_ff_in
    )
    d_attended = contract(d_proj_rows, out_full, 1, 0).astype(bf16)
    d_query, d_kv_parts = attend_back(info, queries, all_kv, d_attended, attended, inverse)
    d_kv, grad_out, down_sums = comm.scatter_kv_sums(
        d_kv_parts, contract(d_proj_rows, attn_rows, 0, 0).astype(bf16), down_sum
    )
    d_qkv_lin, d_partial = project_back(d_query, d_kv, cosine, sine_table, qkv_full)
    d_normed_one, grad_down = comm.scatter_heads_back(d_partial, down_sums)
    d_token_part, grad_attn_in = normalize_back(token_f32, norm_attn_in, d_normed_one)
    input_grad = (d_middle + d_token_part).astype(bf16)
    grad_qkv, grad_gate, grad_up, gains = comm.finish(
        contract(normed_one, d_qkv_lin, 0, 0).astype(bf16),
        gate_sum,
        up_sum,
        jnp.stack([grad_attn_in, inner_gains[0], inner_gains[1], grad_ff_out]),
    )
    grad_qkv, grad_gate, grad_up = [g.astype(f32) for g in (grad_qkv, grad_gate, grad_up)]
    return (
        layer_out.astype(bf16),
        input_grad,
        gains[0],
        grad_qkv[:, :heads_width],
        grad_qkv[:, heads_width : heads_width + HEAD_DIM],
        grad_qkv[:, heads_width + HEAD_DIM :],
        grad_out.astype(f32).T,
        gains[1],
        gains[2],
        grad_gate,
        grad_up,
        grad_down.astype(f32).T,
        gains[3],
    )


def solution(mesh):
    rows, weight, turned = P(("blk", "heads"), None), P("blk", "heads"), P("heads", "blk")
    return jax.shard_map(
        on_device,
        mesh=mesh,
        in_specs=(
            rows, rows, P(), weight, weight, weight, turned, P(), P(), weight, weight, turned,
            P(), P(), P(),
        ),
        out_specs=(
            rows, rows, P(), weight, weight, weight, turned, P(), P(), weight, weight, turned, P(),
        ),
        check_vma=False,
    )
```
